32 devices in a mesh: dp: 16 (over z, y, x), head: 2 (over core).
Axes of the slice: x: 2, y: 2, z: 4, core: 2. Of those that a mesh axis runs over, the one named last changes fastest.
Arguments:
- tokens: bfloat16 [32768, 768], P(('dp', 'head')), may hold values from -6 to 6
- lengths: int32 [16, 32], P('dp'), may hold values from 1 to 512, 2048 in all within a row
- w_qkv: bfloat16 [768, 3, 768], P(None, None, 'head'), may hold values from -0.21875 to 0.21875
- bias_qv: float32 [768, 2], P('head'), may hold values from -4 to 4
- w_out: bfloat16 [768, 768], replicated, may hold values from -0.625 to 0.625
- bias_out: float32 [768], replicated, may hold values from -4 to 4
- ln1_gain: float32 [768], replicated, may hold values from 0.5 to 1.5
- ln1_bias: float32 [768], replicated, may hold values from -4 to 4
- w_in: bfloat16 [768, 3072], replicated, may hold values from -0.21875 to 0.21875
- bias_in: float32 [3072], replicated, may hold values from -4 to 4
- w_down: bfloat16 [3072, 768], replicated, may hold values from -0.109375 to 0.109375
- bias_down: float32 [768], replicated, may hold values from -4 to 4
- ln2_gain: float32 [768], replicated, may hold values from 0.5 to 1.5
- ln2_bias: float32 [768], replicated, may hold values from -4 to 4
- term_w: float32 [768], replicated, may hold values from -0.21875 to 0.21875
- term_bias: float32 [1], replicated, may hold values from -3 to 3
- grad_hidden: float32 [32768, 768], P(('dp', 'head')), may hold values from -6 to 6
- grad_term: float32 [32768], P(('dp', 'head')), may hold values from -6 to 6
Outputs:
- hidden_out: bfloat16 [32768, 768], P(('dp', 'head'))
- term_weight: float32 [32768], P(('dp', 'head'))
- grad_tokens: float32 [32768, 768], P(('dp', 'head'))
- grad_w_qkv: float32 [768, 3, 768], P('dp', None, 'head')
- grad_bias_qv: float32 [768, 2], P(('dp', 'head'))
- grad_w_out: float32 [768, 768], P(('dp', 'head'))
- grad_bias_out: float32 [768], P(('dp', 'head'))
- grad_ln1_gain: float32 [768], P(('dp', 'head'))
- grad_ln1_bias: float32 [768], P(('dp', 'head'))
- grad_w_in: float32 [768, 3072], P(('dp', 'head'))
- grad_bias_in: float32 [3072], P(('dp', 'head'))
- grad_w_down: float32 [3072, 768], P(('dp', 'head'))
- grad_bias_down: float32 [768], P(('dp', 'head'))
- grad_ln2_gain: float32 [768], P(('dp', 'head'))
- grad_ln2_bias: float32 [768], P(('dp', 'head'))
- grad_term_w: float32 [768], P(('dp', 'head'))
- grad_term_bias: float32 [1], replicated
The draws below stay inside these ranges and needn't reach their ends.
Inputs may be any that keep to these rules, and one draw needn't show every extreme that they name: `lengths`: each row lists the 32 passages packed in order into one row of 2048 tokens; a row sums to 2048 and its largest length is exactly 512.
All inputs are finite; a program needn't handle non-finite values.
Results may differ from the reference program's by a relative error of at most 0.012.
The reference program's roundings to bfloat16 on the way count: a program that leaves them out, or rounds other values in their place, can miss the bound.
Values may be sent and summed in bfloat16 or wider, within the bound.
A program may use at most 256 MiB of HBM per device.

```python
import math
import jax
import jax.numpy as jnp
import numpy as np
from jax import lax

MODEL_DIM = 768
HEAD_COUNT = 12
HEAD_DIM = 64
FFN_DIM = 3072
ROW_LEN = 2048
LONGEST = 512
PASSAGES = 32
TOKENS = 32768
N_DP = 16


def levels(key, shape, split, low, largest):
    def one(dim, blocks):
        steps = jax.random.uniform(jax.random.fold_in(jax.random.fold_in(key, 6), dim), (blocks,), jnp.float32, low / len(split), largest / len(split))
        return jnp.repeat(jnp.exp(steps), shape[dim] // blocks).reshape((-1,) + (1,) * (len(shape) - dim - 1))

    factor_of = one(*split[0])
    for cut in split[1:]:
        factor_of = factor_of * one(*cut)
    return factor_of


def length_profile(count, total, most, lean):
    loads = [(1 << 20) // math.isqrt(standing ** lean) + 1 for standing in range(2, count + 1)]
    surplus, counts = total - most - (count - 1), [1] * (count - 1)
    while surplus > 0:
        movable = [i for i in range(count - 1) if counts[i] < most]
        mass, remaining = sum([loads[i] for i in movable]), surplus
        for i in movable:
            addition = min(most - counts[i], max(1, remaining * loads[i] // mass), surplus)
            counts[i] = counts[i] + addition
            surplus = surplus - addition
    return np.array([most] + counts)


def uneven(stream_key, count, total, reach, lean):
    if count == 2:
        one = jax.random.randint(stream_key, (), max(1, total - reach), min(reach, total - 1) + 1)
        return jnp.stack([one, total - one])
    tallies = jnp.asarray(length_profile(count, total, reach, lean), jnp.int32)
    twos = (count - 1) // 2
    giver, receiver = tallies[1:1 + 2 * twos:2], tallies[2:2 + 2 * twos:2]
    slack = jnp.minimum(giver - 1, reach - receiver)
    moved = jax.random.randint(jax.random.fold_in(stream_key, 1), (twos,), 0, 1 << 20) % (slack + 1)
    tallies = tallies.at[1:1 + 2 * twos:2].set(giver - moved).at[2:2 + 2 * twos:2].set(receiver + moved)
    return tallies[jax.random.permutation(jax.random.fold_in(stream_key, 2), count)]


def scatter_about(key, shape, deviation, reach, split=(), kind=jnp.bfloat16):
    entries = jax.random.normal(key, shape, jnp.float32) * deviation
    if len(split) > 0:
        entries = levels(key, shape, split, -0.22, 0.18) * entries
    return jnp.clip(entries, min=-reach, max=reach).astype(kind)


def setup_inputs(seed: int = 0) -> dict:
    key_list = jax.random.split(jax.random.key(seed), 19)
    tokens = scatter_about(key_list[0], (TOKENS, MODEL_DIM), 1.0, 6.0, ((0, 32),))
    lengths = jax.vmap(lambda own: uneven(own, PASSAGES, ROW_LEN, LONGEST, 2))(jax.random.split(key_list[1], N_DP)).reshape((N_DP, PASSAGES)).astype(jnp.int32)
    w_qkv = scatter_about(key_list[2], (MODEL_DIM, 3, MODEL_DIM), MODEL_DIM ** -0.5, 0.21875, ((2, 2),))
    bias_qv = scatter_about(key_list[3], (MODEL_DIM, 2), 0.3, 4.0, ((0, 2),), jnp.float32)
    w_out = scatter_about(key_list[4], (MODEL_DIM, MODEL_DIM), (MODEL_DIM // 8) ** -0.5, 0.625)
    bias_out = scatter_about(key_list[5], (MODEL_DIM,), 0.3, 4.0, (), jnp.float32)
    ln1_gain = jnp.clip(1.0 + 0.1 * jax.random.normal(key_list[6], (MODEL_DIM,), jnp.float32), 0.5, 1.5)
    ln1_bias = scatter_about(key_list[7], (MODEL_DIM,), 0.3, 4.0, (), jnp.float32)
    w_in = scatter_about(key_list[8], (MODEL_DIM, FFN_DIM), MODEL_DIM ** -0.5, 0.21875)
    bias_in = scatter_about(key_list[9], (FFN_DIM,), 0.3, 4.0, (), jnp.float32)
    w_down = scatter_about(key_list[10], (FFN_DIM, MODEL_DIM), FFN_DIM ** -0.5, 0.109375)
    bias_down = scatter_about(key_list[11], (MODEL_DIM,), 0.3, 4.0, (), jnp.float32)
    ln2_gain = jnp.clip(1.0 + 0.1 * jax.random.normal(key_list[12], (MODEL_DIM,), jnp.float32), 0.5, 1.5)
    ln2_bias = scatter_about(key_list[13], (MODEL_DIM,), 0.3, 4.0, (), jnp.float32)
    term_w = scatter_about(key_list[14], (MODEL_DIM,), MODEL_DIM ** -0.5, 0.21875, (), jnp.float32)
    term_bias = scatter_about(key_list[15], (1,), 0.5, 3.0, (), jnp.float32)
    grad_hidden = scatter_about(key_list[16], (TOKENS, MODEL_DIM), 1.0, 6.0, ((0, 32),), jnp.float32)
    grad_term = scatter_about(key_list[17], (TOKENS,), 1.0, 6.0, ((0, 32),), jnp.float32)
    return dict(tokens=tokens, lengths=lengths, w_qkv=w_qkv, bias_qv=bias_qv, w_out=w_out, bias_out=bias_out, ln1_gain=ln1_gain, ln1_bias=ln1_bias, w_in=w_in, bias_in=bias_in, w_down=w_down, bias_down=bias_down, ln2_gain=ln2_gain, ln2_bias=ln2_bias, term_w=term_w, term_bias=term_bias, grad_hidden=grad_hidden, grad_term=grad_term)


highest = lax.Precision.HIGHEST
norm_eps = 1e-06

@jax.custom_vjp
def low(v):
    return lax.optimization_barrier(v.astype(jnp.bfloat16)).astype(jnp.float32)

@jax.custom_vjp
def low_back(v):
    return v

def low_keep(v):
    return (low(v), None)

def low_pass(kept, grad):
    return (grad,)

def back_keep(v):
    return (v, None)

def back_low(kept, grad):
    return (low(grad),)
low.defvjp(low_keep, low_pass)
low_back.defvjp(back_keep, back_low)

def segment_ids(lengths, row_len):
    boundary = jnp.cumsum(lengths, axis=-1)
    places = jnp.arange(row_len, dtype=jnp.int32)
    return lax.optimization_barrier(jnp.sum((places[None, :, None] >= boundary[:, None, :]).astype(jnp.int32), axis=-1))

def layer_norm(resid, gain, shift):
    center = resid - lax.optimization_barrier(jnp.mean(resid, axis=-1, keepdims=True))
    spread = lax.optimization_barrier(jnp.mean(center * center, axis=-1, keepdims=True))
    return center * lax.rsqrt(spread + norm_eps) * gain + shift

def attend(queries, key_rows, value_rows, segment):
    row_len = queries.shape[0]
    block_rows = min(512, row_len)
    block_count = row_len // block_rows
    key_heads = key_rows.reshape(row_len, HEAD_COUNT, HEAD_DIM)
    value_heads = value_rows.reshape(row_len, HEAD_COUNT, HEAD_DIM)
    query_blocks = queries.reshape(block_count, block_rows, HEAD_COUNT, HEAD_DIM)
    segment_blocks = segment.reshape(block_count, block_rows)

    def one_block(block_items):
        query_part, segment_part = block_items
        scores = jnp.einsum('qhe,khe->hqk', query_part, key_heads, precision=highest)
        scores = low_back(scores)
        allowed = (segment_part[:, None] == segment[None, :])[None]
        scores = jnp.where(allowed, scores, -1e+30)
        row_max = lax.optimization_barrier(jnp.max(scores, axis=-1, keepdims=True))
        powers = jnp.exp(scores - row_max)
        attn_probs = powers / lax.optimization_barrier(jnp.sum(powers, axis=-1, keepdims=True))
        return jnp.einsum('hqk,khe->qhe', low(attn_probs), value_heads, precision=highest)
    output = lax.map(jax.checkpoint(one_block), (query_blocks, segment_blocks))
    return output.reshape(row_len, MODEL_DIM)

def forward(params, inputs, segment):
    w_qkv, bias_qv, w_out, bias_out, ln1_gain, ln1_bias, w_in, bias_in, w_down, bias_down, ln2_gain, ln2_bias, term_w, term_bias = params
    projected = jnp.einsum('td,dce->tce', inputs, w_qkv, precision=highest)
    queries = low(low_back((projected[:, 0] + bias_qv[:, 0]) * HEAD_DIM ** (-0.5)))
    key_rows = low(low_back(projected[:, 1]))
    value_rows = low(low_back(projected[:, 2] + bias_qv[:, 1]))
    attended = low_back(low(attend(queries, key_rows, value_rows, segment)))
    branch = low_back(jnp.dot(attended, w_out, precision=highest) + bias_out)
    normed_one = layer_norm(inputs + branch, ln1_gain, ln1_bias)
    hidden_pre = low_back(jnp.dot(low(normed_one), w_in, precision=highest) + bias_in)
    activated = low(jax.nn.gelu(hidden_pre, approximate=False))
    ffn_out = low_back(jnp.dot(activated, w_down, precision=highest) + bias_down)
    normed_two = layer_norm(normed_one + ffn_out, ln2_gain, ln2_bias)
    term_logit = jnp.dot(normed_two, term_w, precision=highest) + term_bias[0]
    return (normed_two, jax.nn.softplus(term_logit))

def reference(tokens, lengths, w_qkv, bias_qv, w_out, bias_out, ln1_gain, ln1_bias, w_in, bias_in, w_down, bias_down, ln2_gain, ln2_bias, term_w, term_bias, grad_hidden, grad_term):
    params = tuple((weight.astype(jnp.float32) for weight in (w_qkv, bias_qv, w_out, bias_out, ln1_gain, ln1_bias, w_in, bias_in, w_down, bias_down, ln2_gain, ln2_bias, term_w, term_bias)))
    segments = segment_ids(lengths, ROW_LEN)
    inputs = tokens.astype(jnp.float32).reshape(N_DP, ROW_LEN, MODEL_DIM)
    cot_hidden = grad_hidden.astype(jnp.float32).reshape(N_DP, ROW_LEN, MODEL_DIM)
    cot_term = grad_term.astype(jnp.float32).reshape(N_DP, ROW_LEN)

    def group_step(totals, group_items):
        group_in, group_seg, group_hid, group_term = group_items
        results, pullback = jax.vjp(lambda weights, group_rows: forward(weights, group_rows, group_seg), params, group_in)
        weight_grads, input_grad = pullback((group_hid, group_term))
        totals = jax.tree.map(jnp.add, totals, weight_grads)
        return (totals, (results[0].astype(jnp.bfloat16), results[1], input_grad))
    starting = jax.tree.map(jnp.zeros_like, params)
    totals, (hidden_out, term_weight, grad_tokens) = lax.scan(group_step, starting, (inputs, segments, cot_hidden, cot_term))
    return (hidden_out.reshape(TOKENS, MODEL_DIM), term_weight.reshape(TOKENS), grad_tokens.reshape(TOKENS, MODEL_DIM), totals[0], totals[1], totals[2], totals[3], totals[4], totals[5], totals[6], totals[7], totals[8], totals[9], totals[10], totals[11], totals[12], totals[13])
```

```python
from functools import partial

import jax
import jax.numpy as jnp
from jax import lax
from jax.experimental import pallas as pl
from jax.experimental.pallas import tpu as pltpu
from jax.sharding import PartitionSpec as P

HEAD_DIM = 64
LANES = 128
Q_ROWS = 256
WIDTHS = (2, 3, 4, 5, 6, 8, 10)
AXES = ("dp", "head")

f32 = jnp.float32
bf16 = jnp.bfloat16
highest = lax.Precision.HIGHEST
norm_eps = 1e-06
NT = (((1,), (1,)), ((), ()))
TN = (((0,), (0,)), ((), ()))


def layer_norm(resid, gain, shift):
    center = resid - jnp.mean(resid, axis=-1, keepdims=True)
    spread = jnp.mean(center * center, axis=-1, keepdims=True)
    return center * lax.rsqrt(spread + norm_eps) * gain + shift


def key_range(lengths_ref, first, rows, row_len):
    start = jnp.int32(0)
    low = jnp.int32(0)
    high = jnp.int32(row_len)
    for j in range(lengths_ref.shape[1]):
        end = start + lengths_ref[0, j]
        low = jnp.where(start <= first, start, low)
        high = jnp.where(end >= first + rows, jnp.minimum(high, end), high)
        start = end
    low_block = low // LANES
    count = (high + LANES - 1) // LANES - low_block
    return low_block, count


def by_width(lengths_ref, first, rows, row_len, body):
    blocks = row_len // LANES
    low_block, count = key_range(lengths_ref, first, rows, row_len)
    widths = sorted({min(w, blocks) for w in WIDTHS})
    below = 0
    for width in widths:

        @pl.when((count > below) & (count <= width))
        def _(width=width):
            begin = jnp.minimum(low_block, blocks - width)
            body(pl.multiple_of(begin * LANES, LANES), width * LANES)

        below = width


def attend_kernel(lengths_ref, q_ref, k_ref, v_ref, segc_ref, segr_ref, o_ref, log_ref, mask_ref, cols_ref):
    rows, local_dim = q_ref.shape
    row_len = k_ref.shape[0]
    first = pl.program_id(0) * rows
    lane = lax.broadcasted_iota(jnp.int32, (rows, LANES), 1)

    def body(begin, width):
        same = segc_ref[:, 0:1] == segr_ref[0:1, pl.ds(begin, width)]
        mask_ref[:, :width] = jnp.where(same, 0.0, -1e30)

        def pair_step(pair, carry):
            cols = pl.ds(pl.multiple_of(pair * LANES, LANES), LANES)
            q_pair = q_ref[:, cols]
            k_pair = k_ref[pl.ds(begin, width), cols]
            v_pair = v_ref[pl.ds(begin, width), cols]
            outs = []
            for h in range(2):
                mine = (lane // HEAD_DIM) == h
                q_one = jnp.where(mine, q_pair, jnp.zeros_like(q_pair))
                scores = lax.dot_general(q_one, k_pair, NT, preferred_element_type=f32)
                scores = scores + mask_ref[:, :width]
                row_max = jnp.max(scores, axis=1, keepdims=True)
                powers = jnp.exp(scores - row_max)
                total = jnp.sum(powers, axis=1, keepdims=True)
                probs = (powers * (1.0 / total)).astype(bf16)
                outs.append(jnp.dot(probs, v_pair, preferred_element_type=f32))
                log_total = row_max + jnp.log(total)
                cols_ref[...] = jnp.where(lane == 2 * pair + h, log_total, cols_ref[...])
            o_ref[:, cols] = jnp.where(lane < HEAD_DIM, outs[0], outs[1]).astype(bf16)
            return carry

        lax.fori_loop(0, local_dim // LANES, pair_step, 0)

    by_width(lengths_ref, first, rows, row_len, body)
    log_ref[...] = cols_ref[...].T[: log_ref.shape[0]]


def attend(lengths, queries, key_rows, value_rows, seg_col, seg_row):
    row_len, local_dim = queries.shape
    rows = min(Q_ROWS, row_len)
    whole = pl.BlockSpec((row_len, local_dim), lambda i, n: (0, 0))
    block = pl.BlockSpec((rows, local_dim), lambda i, n: (i, 0))
    return pl.pallas_call(
        attend_kernel,
        grid_spec=pltpu.PrefetchScalarGridSpec(
            num_scalar_prefetch=1,
            grid=(row_len // rows,),
            in_specs=[
                block,
                whole,
                whole,
                pl.BlockSpec((rows, LANES), lambda i, n: (i, 0)),
                pl.BlockSpec((8, row_len), lambda i, n: (0, 0)),
            ],
            out_specs=[block, pl.BlockSpec((8, rows), lambda i, n: (0, i))],
            scratch_shapes=[
                pltpu.VMEM((rows, max(WIDTHS) * LANES), f32),
                pltpu.VMEM((rows, LANES), f32),
            ],
        ),
        out_shape=[
            jax.ShapeDtypeStruct((row_len, local_dim), bf16),
            jax.ShapeDtypeStruct((8, row_len), f32),
        ],
        compiler_params=pltpu.CompilerParams(vmem_limit_bytes=48 * 2**20),
        cost_estimate=pl.CostEstimate(flops=20_000_000_000, bytes_accessed=8_000_000, transcendentals=0),
    )(lengths, queries, key_rows, value_rows, seg_col, seg_row)


def attend_back_kernel(
    lengths_ref, q_ref, k_ref, v_ref, g_ref, log_ref, segc_ref, segr_ref, raw_ref, sums_ref, mask_ref, dk_ref, dv_ref
):
    rows, local_dim = q_ref.shape
    row_len = k_ref.shape[0]
    step = pl.program_id(0)
    first = step * rows
    lane = lax.broadcasted_iota(jnp.int32, (rows, LANES), 1)

    @pl.when(step == 0)
    def _():
        dk_ref[...] = jnp.zeros_like(dk_ref)
        dv_ref[...] = jnp.zeros_like(dv_ref)

    def body(begin, width):
        keys = pl.ds(begin, width)
        same = segc_ref[keys, 0:1] == segr_ref[0:1, :]
        mask_ref[:width, :] = jnp.where(same, 0.0, -1e30)

        def pair_step(pair, carry):
            cols = pl.ds(pl.multiple_of(pair * LANES, LANES), LANES)
            q_pair, g_pair = q_ref[:, cols], g_ref[:, cols]
            k_pair, v_pair = k_ref[keys, cols], v_ref[keys, cols]
            dq = []
            dk = dv = None
            for h in range(2):
                mine = (lane // HEAD_DIM) == h
                q_one = jnp.where(mine, q_pair, jnp.zeros_like(q_pair))
                g_one = jnp.where(mine, g_pair, jnp.zeros_like(g_pair))
                scores = lax.dot_general(k_pair, q_one, NT, preferred_element_type=f32)
                probs = jnp.exp(scores + mask_ref[:width, :] - log_ref[pl.ds(2 * pair + h, 1), :])
                dv_one = jnp.dot(probs.astype(bf16), g_one, preferred_element_type=f32)
                prob_grad = lax.dot_general(v_pair, g_one, NT, preferred_element_type=f32)
                inner = jnp.sum(probs * prob_grad, axis=0, keepdims=True)
                score_grad = (probs * (prob_grad - inner)).astype(bf16)
                dk_one = jnp.dot(score_grad, q_one, preferred_element_type=f32)
                dq.append(lax.dot_general(score_grad, k_pair, TN, preferred_element_type=f32))
                dk = dk_one if dk is None else dk + dk_one
                dv = dv_one if dv is None else dv + dv_one
            dk_ref[keys, cols] += dk
            dv_ref[keys, cols] += dv
            dq_low = jnp.where(lane < HEAD_DIM, dq[0], dq[1]).astype(bf16)
            raw_ref[pl.ds(pl.multiple_of(first, rows), rows), cols] = dq_low * jnp.asarray(HEAD_DIM**-0.5, bf16)
            return carry

        lax.fori_loop(0, local_dim // LANES, pair_step, 0)

    by_width(lengths_ref, first, rows, row_len, body)

    @pl.when(step == pl.num_programs(0) - 1)
    def _():
        raw_ref[:, local_dim : 2 * local_dim] = dk_ref[...].astype(bf16)
        raw_ref[:, 2 * local_dim :] = dv_ref[...].astype(bf16)
        sums_ref[...] = jnp.sum(raw_ref[...].astype(f32), axis=0, keepdims=True)


def attend_back(lengths, queries, key_rows, value_rows, grads, logs, seg_col, seg_row):
    row_len, local_dim = queries.shape
    rows = min(Q_ROWS, row_len)
    whole = pl.BlockSpec((row_len, local_dim), lambda i, n: (0, 0))
    block = pl.BlockSpec((rows, local_dim), lambda i, n: (i, 0))
    return pl.pallas_call(
        attend_back_kernel,
        grid_spec=pltpu.PrefetchScalarGridSpec(
            num_scalar_prefetch=1,
            grid=(row_len // rows,),
            in_specs=[
                block,
                whole,
                whole,
                block,
                pl.BlockSpec((8, rows), lambda i, n: (0, i)),
                pl.BlockSpec((row_len, LANES), lambda i, n: (0, 0)),
                pl.BlockSpec((8, rows), lambda i, n: (0, i)),
            ],
            out_specs=[
                pl.BlockSpec((row_len, 3 * local_dim), lambda i, n: (0, 0)),
                pl.BlockSpec((1, 3 * local_dim), lambda i, n: (0, 0)),
            ],
            scratch_shapes=[
                pltpu.VMEM((max(WIDTHS) * LANES, rows), f32),
                pltpu.VMEM((row_len, local_dim), f32),
                pltpu.VMEM((row_len, local_dim), f32),
            ],
        ),
        out_shape=[
            jax.ShapeDtypeStruct((row_len, 3 * local_dim), bf16),
            jax.ShapeDtypeStruct((1, 3 * local_dim), f32),
        ],
        compiler_params=pltpu.CompilerParams(vmem_limit_bytes=56 * 2**20),
        cost_estimate=pl.CostEstimate(flops=40_000_000_000, bytes_accessed=12_000_000, transcendentals=0),
    )(lengths, queries, key_rows, value_rows, grads, logs, seg_col, seg_row)


def take(array, index, axis=0):
    return lax.dynamic_index_in_dim(array, index, axis, keepdims=False)


class Links:
    def __init__(self, n_dp):
        self.n_dp = n_dp
        self.bits = n_dp.bit_length() - 1
        self.dp = lax.axis_index("dp")
        self.head = lax.axis_index("head")

    def bit(self, which):
        return (self.dp >> which) & 1

    def permute(self, array, partner):
        pairs = []
        for d in range(self.n_dp):
            for h in range(2):
                to_d, to_h = partner(d, h)
                pairs.append((2 * d + h, 2 * to_d + to_h))
        return lax.ppermute(array, AXES, pairs)

    def swap_head(self, array):
        return self.permute(array, lambda d, h: (d, 1 - h))

    def swap_bit(self, array, which):
        return self.permute(array, lambda d, h: (d ^ (1 << which), h))

    def scatter_heads(self, blocks):
        got = self.swap_head(take(blocks, 1 - self.head, 1))
        return (take(blocks, self.head, 1).astype(f32) + got.astype(f32)).astype(bf16)

    def scatter_dp(self, blocks):
        tail = blocks.shape[1:]
        b0, b1 = self.bit(0), self.bit(1)
        first = self.head == 0
        blocks = blocks.reshape((self.n_dp // 4, 4) + tail)

        def two(one, other):
            i = jnp.where(first, one, 2 * other)
            j = jnp.where(first, 2 + one, 2 * other + 1)
            return jnp.stack([take(blocks, i, 1), take(blocks, j, 1)], axis=1)

        got = self.permute(two(1 - b0, 1 - b1), lambda d, h: (d ^ (1 if h == 0 else 2), h))
        blocks = (two(b0, b1).astype(f32) + got.astype(f32)).astype(bf16)
        mine = jnp.where(first, b1, b0)
        got = self.permute(take(blocks, 1 - mine, 1), lambda d, h: (d ^ (2 if h == 0 else 1), h))
        blocks = take(blocks, mine, 1).astype(f32) + got.astype(f32)
        for which in range(2, self.bits):
            blocks = blocks.reshape((-1, 2) + tail)
            mine = self.bit(which)
            got = self.swap_bit(take(blocks, 1 - mine, 1).astype(bf16), which)
            blocks = take(blocks, mine, 1) + got.astype(f32)
        return blocks.reshape(tail)

    def total(self, array):
        array = array + self.swap_head(array)
        for which in range(self.bits):
            array = array + self.swap_bit(array, which)
        return array


def shards(
    n_dp,
    tokens,
    lengths,
    w_qkv,
    bias_qv,
    w_out,
    bias_out,
    ln1_gain,
    ln1_bias,
    w_in,
    bias_in,
    w_down,
    bias_down,
    ln2_gain,
    ln2_bias,
    term_w,
    term_bias,
    grad_hidden,
    grad_term,
):
    links = Links(n_dp)
    head = links.head
    half, model_dim = tokens.shape
    row_len = 2 * half
    local_dim = w_qkv.shape[2]
    ffn_dim = w_in.shape[1]
    query_scale = HEAD_DIM ** (-0.5)

    boundary = jnp.cumsum(lengths[0])
    places = jnp.arange(row_len, dtype=jnp.int32)
    segment = jnp.sum((places[:, None] >= boundary[None, :]).astype(jnp.int32), axis=-1)
    seg_col = jnp.broadcast_to(segment[:, None], (row_len, LANES))
    seg_row = jnp.broadcast_to(segment[None, :], (8, row_len))

    def both(mine, theirs, axis):
        return jnp.where(
            head == 0,
            jnp.concatenate([mine, theirs], axis=axis),
            jnp.concatenate([theirs, mine], axis=axis),
        )

    group_rows = both(tokens, links.swap_head(tokens), 0)
    w_flat = w_qkv.reshape(model_dim, 3 * local_dim)
    projected = jnp.dot(group_rows, w_flat, preferred_element_type=f32)
    queries = ((projected[:, :local_dim] + bias_qv[:, 0]) * query_scale).astype(bf16)
    key_rows = projected[:, local_dim : 2 * local_dim].astype(bf16)
    value_rows = (projected[:, 2 * local_dim :] + bias_qv[:, 1]).astype(bf16)
    attended, logs = attend(lengths, queries, key_rows, value_rows, seg_col, seg_row)

    def my_half(rows):
        return lax.dynamic_slice_in_dim(rows, head * half, half, 0)

    def their_half(rows):
        return lax.dynamic_slice_in_dim(rows, (1 - head) * half, half, 0)

    token_mixed = both(my_half(attended), links.swap_head(their_half(attended)), 1)

    inputs = tokens.astype(f32)
    branch = jnp.dot(token_mixed, w_out, preferred_element_type=f32) + bias_out
    normed_one, norm_one_back = jax.vjp(layer_norm, inputs + branch, ln1_gain, ln1_bias)
    normed_low = normed_one.astype(bf16)
    hidden_pre = jnp.dot(normed_low, w_in, preferred_element_type=f32) + bias_in
    activated, gelu_back = jax.vjp(partial(jax.nn.gelu, approximate=False), hidden_pre)
    active_low = activated.astype(bf16)
    ffn_out = jnp.dot(active_low, w_down, preferred_element_type=f32) + bias_down
    normed_two, norm_two_back = jax.vjp(layer_norm, normed_one + ffn_out, ln2_gain, ln2_bias)
    term_logit = jnp.dot(normed_two, term_w, precision=highest) + term_bias[0]
    term_weight = jax.nn.softplus(term_logit)
    logit_grad = grad_term * jax.nn.sigmoid(term_logit)
    two_grad = grad_hidden + logit_grad[:, None] * term_w[None, :]
    term_w_local = jnp.dot(logit_grad, normed_two, precision=highest)
    term_bias_local = jnp.sum(logit_grad)
    resid_two_grad, gain_two_grad, shift_two_grad = norm_two_back(two_grad)
    ffn_grad = resid_two_grad.astype(bf16)
    down_local = lax.dot_general(active_low, ffn_grad, TN, preferred_element_type=f32).astype(bf16)
    bias_down_local = jnp.sum(ffn_grad.astype(f32), axis=0)
    active_grad = lax.dot_general(ffn_grad, w_down, NT, preferred_element_type=f32)
    (pre_grad,) = gelu_back(active_grad)
    pre_low = pre_grad.astype(bf16)
    in_local = lax.dot_general(normed_low, pre_low, TN, preferred_element_type=f32).astype(bf16)
    bias_in_local = jnp.sum(pre_low.astype(f32), axis=0)
    one_grad = resid_two_grad + lax.dot_general(pre_low, w_in, NT, preferred_element_type=f32)
    resid_one_grad, gain_one_grad, shift_one_grad = norm_one_back(one_grad)
    branch_low = resid_one_grad.astype(bf16)
    out_local = lax.dot_general(token_mixed, branch_low, TN, preferred_element_type=f32).astype(bf16)
    bias_out_local = jnp.sum(branch_low.astype(f32), axis=0)
    mixed_grad = lax.dot_general(branch_low, w_out, NT, preferred_element_type=f32).astype(bf16)

    my_cols = lax.dynamic_slice_in_dim(mixed_grad, head * local_dim, local_dim, 1)
    their_cols = lax.dynamic_slice_in_dim(mixed_grad, (1 - head) * local_dim, local_dim, 1)
    head_grad = both(my_cols, links.swap_head(their_cols), 0)

    raw_grad, raw_sums = attend_back(lengths, queries, key_rows, value_rows, head_grad, logs, seg_col, seg_row)

    def blocks_of(partial_sum):
        rows, cols = partial_sum.shape
        return partial_sum.reshape(n_dp, 2, rows // (2 * n_dp), cols)

    grad_down = links.scatter_dp(links.scatter_heads(blocks_of(down_local)))
    grad_in = links.scatter_dp(links.scatter_heads(blocks_of(in_local)))
    grad_out = links.scatter_dp(links.scatter_heads(blocks_of(out_local)))

    input_grad = lax.dot_general(raw_grad, w_flat, NT, preferred_element_type=f32)
    received = links.swap_head(their_half(input_grad).astype(bf16))
    grad_tokens = resid_one_grad + my_half(input_grad) + received.astype(f32)
    qkv_local = lax.dot_general(group_rows, raw_grad, TN, preferred_element_type=f32).astype(bf16)
    grad_qkv = links.scatter_dp(qkv_local.reshape(n_dp, model_dim // n_dp, 3 * local_dim))
    grad_qkv = grad_qkv.reshape(model_dim // n_dp, 3, local_dim)

    vectors = jnp.stack(
        [
            bias_out_local,
            gain_one_grad,
            shift_one_grad,
            bias_down_local,
            gain_two_grad,
            shift_two_grad,
            term_w_local,
            jnp.full((model_dim,), term_bias_local),
        ]
    )
    vectors = jnp.concatenate([vectors, bias_in_local.reshape(-1, model_dim)])
    vectors = links.total(vectors)
    place = 2 * links.dp + head
    width = model_dim // (2 * n_dp)
    mine = lax.dynamic_slice_in_dim(vectors[:8], place * width, width, 1)
    in_width = ffn_dim // (2 * n_dp)
    bias_in_mine = lax.dynamic_slice_in_dim(vectors[8:].reshape(-1), place * in_width, in_width, 0)

    padded = lax.dynamic_update_slice(
        jnp.zeros((2, 2 * local_dim), f32),
        jnp.concatenate([raw_sums[:, :local_dim], raw_sums[:, 2 * local_dim :]]),
        (jnp.int32(0), head * local_dim),
    )
    bias_qv_mine = lax.dynamic_slice_in_dim(links.total(padded), place * width, width, 1).T

    return (
        normed_two.astype(bf16),
        term_weight,
        grad_tokens,
        grad_qkv,
        bias_qv_mine,
        grad_out,
        mine[0],
        mine[1],
        mine[2],
        grad_in,
        bias_in_mine,
        grad_down,
        mine[3],
        mine[4],
        mine[5],
        mine[6],
        vectors[7, :1],
    )


def solution(mesh):
    rows = P(AXES, None)
    return jax.shard_map(
        partial(shards, mesh.shape["dp"]),
        mesh=mesh,
        in_specs=(rows, P("dp", None), P(None, None, "head"), P("head", None))
        + (P(),) * 12
        + (rows, P(AXES)),
        out_specs=(
            rows,
            P(AXES),
            rows,
            P("dp", None, "head"),
            rows,
            rows,
            P(AXES),
            P(AXES),
            P(AXES),
            rows,
            P(AXES),
            rows,
            P(AXES),
            P(AXES),
            P(AXES),
            P(AXES),
            P(),
        ),
        check_vma=False,
    )
```

```python
from functools import partial

import jax
import jax.numpy as jnp
from jax import lax
from jax.experimental import pallas as pl
from jax.experimental.pallas import tpu as pltpu
from jax.sharding import PartitionSpec as P

HEAD_DIM = 64
LANES = 128
Q_ROWS = 256
WIDTHS = (2, 3, 4, 5, 6, 8, 10)
AXES = ("dp", "head")

f32 = jnp.float32
bf16 = jnp.bfloat16
norm_eps = 1e-06
NT = (((1,), (1,)), ((), ()))
TN = (((0,), (0,)), ((), ()))


def key_range(lengths_ref, first, rows, row_len):
    start = jnp.int32(0)
    low = jnp.int32(0)
    high = jnp.int32(row_len)
    for j in range(lengths_ref.shape[1]):
        end = start + lengths_ref[0, j]
        low = jnp.where(start <= first, start, low)
        high = jnp.where(end >= first + rows, jnp.minimum(high, end), high)
        start = end
    low_block = low // LANES
    count = (high + LANES - 1) // LANES - low_block
    return low_block, count


def by_width(lengths_ref, first, rows, row_len, body):
    blocks = row_len // LANES
    low_block, count = key_range(lengths_ref, first, rows, row_len)
    widths = sorted({min(w, blocks) for w in WIDTHS})
    below = 0
    for width in widths:

        @pl.when((count > below) & (count <= width))
        def _(width=width):
            begin = jnp.minimum(low_block, blocks - width)
            body(pl.multiple_of(begin * LANES, LANES), width * LANES)

        below = width


def attend_kernel(lengths_ref, q_ref, k_ref, v_ref, segc_ref, segr_ref, o_ref, log_ref, mask_ref, cols_ref):
    rows, local_dim = q_ref.shape
    row_len = k_ref.shape[0]
    first = pl.program_id(0) * rows
    lane = lax.broadcasted_iota(jnp.int32, (rows, LANES), 1)

    def body(begin, width):
        same = segc_ref[:, 0:1] == segr_ref[0:1, pl.ds(begin, width)]
        mask_ref[:, :width] = jnp.where(same, 0.0, -1e30)

        def pair_step(pair, carry):
            cols = pl.ds(pl.multiple_of(pair * LANES, LANES), LANES)
            q_pair = q_ref[:, cols]
            k_pair = k_ref[pl.ds(begin, width), cols]
            v_pair = v_ref[pl.ds(begin, width), cols]
            outs = []
            for h in range(2):
                mine = (lane // HEAD_DIM) == h
                q_one = jnp.where(mine, q_pair, jnp.zeros_like(q_pair))
                scores = lax.dot_general(q_one, k_pair, NT, preferred_element_type=f32)
                scores = scores + mask_ref[:, :width]
                row_max = jnp.max(scores, axis=1, keepdims=True)
                powers = jnp.exp(scores - row_max)
                total = jnp.sum(powers, axis=1, keepdims=True)
                probs = (powers * (1.0 / total)).astype(bf16)
                outs.append(jnp.dot(probs, v_pair, preferred_element_type=f32))
                log_total = row_max + jnp.log(total)
                cols_ref[...] = jnp.where(lane == 2 * pair + h, log_total, cols_ref[...])
            o_ref[:, cols] = jnp.where(lane < HEAD_DIM, outs[0], outs[1]).astype(bf16)
            return carry

        lax.fori_loop(0, local_dim // LANES, pair_step, 0)

    by_width(lengths_ref, first, rows, row_len, body)
    log_ref[...] = cols_ref[...].T[: log_ref.shape[0]]


def attend(lengths, queries, key_rows, value_rows, seg_col, seg_row):
    row_len, local_dim = queries.shape
    rows = min(Q_ROWS, row_len)
    whole = pl.BlockSpec((row_len, local_dim), lambda i, n: (0, 0))
    block = pl.BlockSpec((rows, local_dim), lambda i, n: (i, 0))
    return pl.pallas_call(
        attend_kernel,
        grid_spec=pltpu.PrefetchScalarGridSpec(
            num_scalar_prefetch=1,
            grid=(row_len // rows,),
            in_specs=[
                block,
                whole,
                whole,
                pl.BlockSpec((rows, LANES), lambda i, n: (i, 0)),
                pl.BlockSpec((8, row_len), lambda i, n: (0, 0)),
            ],
            out_specs=[block, pl.BlockSpec((8, rows), lambda i, n: (0, i))],
            scratch_shapes=[
                pltpu.VMEM((rows, max(WIDTHS) * LANES), f32),
                pltpu.VMEM((rows, LANES), f32),
            ],
        ),
        out_shape=[
            jax.ShapeDtypeStruct((row_len, local_dim), bf16),
            jax.ShapeDtypeStruct((8, row_len), f32),
        ],
        compiler_params=pltpu.CompilerParams(vmem_limit_bytes=48 * 2**20),
        cost_estimate=pl.CostEstimate(flops=20_000_000_000, bytes_accessed=8_000_000, transcendentals=0),
    )(lengths, queries, key_rows, value_rows, seg_col, seg_row)


def attend_back_kernel(
    first_pair, lengths_ref, q_ref, k_ref, v_ref, g_ref, log_ref, segc_ref, segr_ref, raw_ref, sums_ref, mask_ref, dk_ref, dv_ref
):
    rows, local_dim = q_ref.shape
    row_len = k_ref.shape[0]
    step = pl.program_id(0)
    first = step * rows
    lane = lax.broadcasted_iota(jnp.int32, (rows, LANES), 1)

    @pl.when(step == 0)
    def _():
        dk_ref[...] = jnp.zeros_like(dk_ref)
        dv_ref[...] = jnp.zeros_like(dv_ref)

    def body(begin, width):
        keys = pl.ds(begin, width)
        same = segc_ref[keys, 0:1] == segr_ref[0:1, :]
        mask_ref[:width, :] = jnp.where(same, 0.0, -1e30)

        def pair_step(pair, carry):
            cols = pl.ds(pl.multiple_of(pair * LANES, LANES), LANES)
            q_pair, g_pair = q_ref[:, cols], g_ref[:, cols]
            k_pair, v_pair = k_ref[keys, cols], v_ref[keys, cols]
            dq = []
            dk = dv = None
            for h in range(2):
                mine = (lane // HEAD_DIM) == h
                q_one = jnp.where(mine, q_pair, jnp.zeros_like(q_pair))
                g_one = jnp.where(mine, g_pair, jnp.zeros_like(g_pair))
                scores = lax.dot_general(k_pair, q_one, NT, preferred_element_type=f32)
                probs = jnp.exp(scores + mask_ref[:width, :] - log_ref[pl.ds(2 * (first_pair + pair) + h, 1), :])
                dv_one = jnp.dot(probs.astype(bf16), g_one, preferred_element_type=f32)
                prob_grad = lax.dot_general(v_pair, g_one, NT, preferred_element_type=f32)
                inner = jnp.sum(probs * prob_grad, axis=0, keepdims=True)
                score_grad = (probs * (prob_grad - inner)).astype(bf16)
                dk_one = jnp.dot(score_grad, q_one, preferred_element_type=f32)
                dq.append(lax.dot_general(score_grad, k_pair, TN, preferred_element_type=f32))
                dk = dk_one if dk is None else dk + dk_one
                dv = dv_one if dv is None else dv + dv_one
            dk_ref[keys, cols] += dk
            dv_ref[keys, cols] += dv
            dq_low = jnp.where(lane < HEAD_DIM, dq[0], dq[1]).astype(bf16)
            raw_ref[pl.ds(pl.multiple_of(first, rows), rows), cols] = dq_low * jnp.asarray(HEAD_DIM**-0.5, bf16)
            return carry

        lax.fori_loop(0, local_dim // LANES, pair_step, 0)

    by_width(lengths_ref, first, rows, row_len, body)

    @pl.when(step == pl.num_programs(0) - 1)
    def _():
        raw_ref[:, local_dim : 2 * local_dim] = dk_ref[...].astype(bf16)
        raw_ref[:, 2 * local_dim :] = dv_ref[...].astype(bf16)
        sums_ref[...] = jnp.sum(raw_ref[...].astype(f32), axis=0, keepdims=True)


def attend_back(lengths, queries, key_rows, value_rows, grads, logs, seg_col, seg_row, first_pair, pairs):
    row_len = queries.shape[0]
    local_dim = pairs * LANES
    place = first_pair // pairs
    rows = min(Q_ROWS, row_len)
    whole = pl.BlockSpec((row_len, local_dim), lambda i, n: (0, place))
    block = pl.BlockSpec((rows, local_dim), lambda i, n: (i, place))
    return pl.pallas_call(
        partial(attend_back_kernel, first_pair),
        grid_spec=pltpu.PrefetchScalarGridSpec(
            num_scalar_prefetch=1,
            grid=(row_len // rows,),
            in_specs=[
                block,
                whole,
                whole,
                block,
                pl.BlockSpec((8, rows), lambda i, n: (0, i)),
                pl.BlockSpec((row_len, LANES), lambda i, n: (0, 0)),
                pl.BlockSpec((8, rows), lambda i, n: (0, i)),
            ],
            out_specs=[
                pl.BlockSpec((row_len, 3 * local_dim), lambda i, n: (0, 0)),
                pl.BlockSpec((1, 3 * local_dim), lambda i, n: (0, 0)),
            ],
            scratch_shapes=[
                pltpu.VMEM((max(WIDTHS) * LANES, rows), f32),
                pltpu.VMEM((row_len, local_dim), f32),
                pltpu.VMEM((row_len, local_dim), f32),
            ],
        ),
        out_shape=[
            jax.ShapeDtypeStruct((row_len, 3 * local_dim), bf16),
            jax.ShapeDtypeStruct((1, 3 * local_dim), f32),
        ],
        compiler_params=pltpu.CompilerParams(vmem_limit_bytes=56 * 2**20),
        cost_estimate=pl.CostEstimate(flops=14_000_000_000 * pairs, bytes_accessed=4_000_000 * pairs, transcendentals=0),
    )(lengths, queries, key_rows, value_rows, grads, logs, seg_col, seg_row)


ERF_TOP = (0.00022905065861350646, 0.0034082910107109506, 0.050955695062380861, 0.18520832239976145, 1.128379143519084)
ERF_LOW = (
    -1.1791602954361697e-7,
    0.000023547966471313185,
    0.0010179625278914885,
    0.014070470171167667,
    0.11098505178285362,
    0.49746925110067538,
    1.0,
)
TILE = 256
CHUNK = 384


def polynomial(x, factors):
    value = jnp.full_like(x, factors[0])
    for factor in factors[1:]:
        value = value * x + factor
    return value


def gelu_both(x):
    scaled = jnp.clip(x * 0.7071067811865476, -3.832506856900711, 3.832506856900711)
    square = scaled * scaled
    erf = scaled * polynomial(square, ERF_TOP) / polynomial(square, ERF_LOW)
    cdf = 0.5 + 0.5 * erf
    density = jnp.exp(-0.5 * x * x) * 0.3989422804014327
    return x * cdf, cdf + x * density


def normalize(resid):
    center = resid - jnp.mean(resid, axis=-1, keepdims=True)
    scale = lax.rsqrt(jnp.mean(center * center, axis=-1, keepdims=True) + norm_eps)
    return center * scale, scale


def normalize_back(grad, normed, scale):
    shift = jnp.mean(grad, axis=-1, keepdims=True)
    slope = jnp.mean(grad * normed, axis=-1, keepdims=True)
    return scale * (grad - shift - normed * slope)


def column_sum(x):
    return jnp.sum(x.astype(f32), axis=0, keepdims=True)


def middle_kernel(
    mine_ref,
    theirs_ref,
    tokens_ref,
    hid_ref,
    term_ref,
    w_out_ref,
    w_in_ref,
    w_down_ref,
    vec_ref,
    bias_in_ref,
    term_bias_ref,
    hidden_ref,
    weight_ref,
    left_ref,
    right_ref,
    resid_ref,
    my_grad_ref,
    their_grad_ref,
    sums_ref,
    in_sums_ref,
    slope_ref,
):
    head = lax.axis_index("head")
    local_dim = mine_ref.shape[1]
    ffn_dim = w_in_ref.shape[1]
    bias_out, ln1_gain, ln1_bias = vec_ref[0:1], vec_ref[1:2], vec_ref[2:3]
    bias_down, ln2_gain, ln2_bias, term_w = vec_ref[3:4], vec_ref[4:5], vec_ref[5:6], vec_ref[6:7]

    @pl.when(pl.program_id(0) == 0)
    def _():
        sums_ref[...] = jnp.zeros_like(sums_ref)
        in_sums_ref[...] = jnp.zeros_like(in_sums_ref)

    model_dim = w_out_ref.shape[0]
    parts = ffn_dim // model_dim
    left_ref[parts + 1, :, pl.ds(pl.multiple_of(head * local_dim, LANES), local_dim)] = mine_ref[...]
    left_ref[parts + 1, :, pl.ds(pl.multiple_of((1 - head) * local_dim, LANES), local_dim)] = theirs_ref[...]
    branch = jnp.dot(left_ref[parts + 1], w_out_ref[...], preferred_element_type=f32) + bias_out
    normal_one, scale_one = normalize(tokens_ref[...].astype(f32) + branch)
    normed_one = normal_one * ln1_gain + ln1_bias
    normed_low = normed_one.astype(bf16)
    left_ref[parts] = normed_low
    resid = normed_one + bias_down
    for c in range(0, ffn_dim, CHUNK):
        cols = slice(c, c + CHUNK)
        pre = jnp.dot(normed_low, w_in_ref[:, cols], preferred_element_type=f32) + bias_in_ref[:, cols]
        value, slope = gelu_both(pre)
        value = value.astype(bf16)
        left_ref[c // model_dim, :, c % model_dim : c % model_dim + CHUNK] = value
        slope_ref[:, cols] = slope
        resid = resid + jnp.dot(value, w_down_ref[cols, :], preferred_element_type=f32)
    normal_two, scale_two = normalize(resid)
    normed_two = normal_two * ln2_gain + ln2_bias
    hidden_ref[...] = normed_two.astype(bf16)
    logit = jnp.sum(normed_two * term_w, axis=-1, keepdims=True) + term_bias_ref[0:1, 0:1]
    small = jnp.exp(-jnp.abs(logit))
    weight_ref[...] = jnp.maximum(logit, 0.0) + jnp.log1p(small)
    logit_grad = term_ref[...] * (jnp.where(logit >= 0.0, 1.0, small) / (1.0 + small))
    two_grad = hid_ref[...] + logit_grad * term_w
    resid_two = normalize_back(two_grad * ln2_gain, normal_two, scale_two)
    ffn_grad = resid_two.astype(bf16)
    right_ref[0] = ffn_grad
    one_grad = resid_two
    for c in range(0, ffn_dim, CHUNK):
        cols = slice(c, c + CHUNK)
        active_grad = lax.dot_general(ffn_grad, w_down_ref[cols, :], NT, preferred_element_type=f32)
        pre = (active_grad * slope_ref[:, cols]).astype(bf16)
        right_ref[1 + c // model_dim, :, c % model_dim : c % model_dim + CHUNK] = pre
        in_sums_ref[:, cols] += column_sum(pre)
        one_grad = one_grad + lax.dot_general(pre, w_in_ref[:, cols], NT, preferred_element_type=f32)
    resid_one = normalize_back(one_grad * ln1_gain, normal_one, scale_one)
    resid_ref[...] = resid_one
    branch_low = resid_one.astype(bf16)
    right_ref[parts + 1] = branch_low
    grads = lax.dot_general(branch_low, w_out_ref[...], NT, preferred_element_type=f32).astype(bf16)

    @pl.when(head == 0)
    def _():
        my_grad_ref[...] = grads[:, :local_dim]
        their_grad_ref[...] = grads[:, local_dim:]

    @pl.when(head == 1)
    def _():
        my_grad_ref[...] = grads[:, local_dim:]
        their_grad_ref[...] = grads[:, :local_dim]

    sums_ref[0:1] += column_sum(branch_low)
    sums_ref[1:2] += column_sum(one_grad * normal_one)
    sums_ref[2:3] += column_sum(one_grad)
    sums_ref[3:4] += column_sum(ffn_grad)
    sums_ref[4:5] += column_sum(two_grad * normal_two)
    sums_ref[5:6] += column_sum(two_grad)
    sums_ref[6:7] += column_sum(logit_grad * normed_two)
    sums_ref[7:8] += jnp.sum(logit_grad, axis=0, keepdims=True)


def middle(mine, theirs, tokens, grad_hidden, grad_term, w_out, w_in, w_down, vec, bias_in, term_bias):
    half, model_dim = tokens.shape
    local_dim = mine.shape[1]
    ffn_dim = w_in.shape[1]
    rows = min(TILE, half)

    def tile(cols):
        return pl.BlockSpec((rows, cols), lambda i: (i, 0))

    def whole(*shape):
        return pl.BlockSpec(shape, lambda i: (0, 0), pipeline_mode=pl.Buffered(1))

    stacked = pl.BlockSpec((ffn_dim // model_dim + 2, rows, model_dim), lambda i: (0, i, 0))
    stack = jax.ShapeDtypeStruct((ffn_dim // model_dim + 2, half, model_dim), bf16)

    def full(cols, kind):
        return jax.ShapeDtypeStruct((half, cols), kind)

    return pl.pallas_call(
        middle_kernel,
        grid=(half // rows,),
        in_specs=[
            tile(local_dim),
            tile(local_dim),
            tile(model_dim),
            tile(model_dim),
            tile(1),
            whole(model_dim, model_dim),
            whole(model_dim, ffn_dim),
            whole(ffn_dim, model_dim),
            whole(8, model_dim),
            whole(1, ffn_dim),
            whole(1, 1),
        ],
        out_specs=[
            tile(model_dim),
            tile(1),
            stacked,
            stacked,
            tile(model_dim),
            tile(local_dim),
            tile(local_dim),
            pl.BlockSpec((8, model_dim), lambda i: (0, 0)),
            pl.BlockSpec((1, ffn_dim), lambda i: (0, 0)),
        ],
        scratch_shapes=[pltpu.VMEM((rows, ffn_dim), f32)],
        out_shape=[
            full(model_dim, bf16),
            full(1, f32),
            stack,
            stack,
            full(model_dim, f32),
            full(local_dim, bf16),
            full(local_dim, bf16),
            jax.ShapeDtypeStruct((8, model_dim), f32),
            jax.ShapeDtypeStruct((1, ffn_dim), f32),
        ],
        compiler_params=pltpu.CompilerParams(vmem_limit_bytes=60 * 2**20),
        cost_estimate=pl.CostEstimate(flops=40_000_000_000, bytes_accessed=50_000_000, transcendentals=0),
    )(mine, theirs, tokens, grad_hidden, grad_term, w_out, w_in, w_down, vec, bias_in, term_bias)


def bit(place, which):
    return (place // 2**which) % 2


def flip(place, which):
    return place + (1 - 2 * bit(place, which)) * 2**which


def route(target, me, head):
    low, high = bit(target, 0), bit(target, 1)
    send = (1 - head) * ((low + bit(me, 0)) % 2) + head * ((high + bit(me, 1)) % 2)
    return send, 2 * (target // 4) + (1 - head) * high + head * low


def greet(partners):
    barrier = pltpu.get_barrier_semaphore()
    for partner in partners:
        pl.semaphore_signal(barrier, inc=1, device_id=partner, device_id_type=pl.DeviceIdType.MESH)
    pl.semaphore_wait(barrier, len(partners))


def remote(source, target, send_sem, recv_sem, partner):
    return pltpu.make_async_remote_copy(
        src_ref=source,
        dst_ref=target,
        send_sem=send_sem,
        recv_sem=recv_sem,
        device_id=partner,
        device_id_type=pl.DeviceIdType.MESH,
    )


def weights_kernel(
    n_dp,
    parts,
    left_ref,
    right_ref,
    my_cols_ref,
    their_cols_ref,
    vec_ref,
    keep_ref,
    send_ref,
    grads_ref,
    vec_out_ref,
    full_ref,
    recv_ref,
    both_ref,
    vec_recv_ref,
    send_sem,
    recv_sem,
    grad_send_sem,
    grad_recv_sem,
    vec_send_sem,
    vec_recv_sem,
    copy_sem,
):
    me, head = lax.axis_index("dp"), lax.axis_index("head")
    other = (me, 1 - head)
    step = pl.program_id(0)
    steps = 2 * parts + 1
    model_dim = left_ref.shape[2]
    cols = model_dim // 2
    half = my_cols_ref.shape[0]
    down_rows = parts * model_dim // n_dp
    rows = model_dim // n_dp
    my_rows = grads_ref.at[pl.ds(pl.multiple_of(head * half, half), half)]
    own_copy = pltpu.make_async_copy(my_cols_ref, my_rows, copy_sem.at[2])
    grad_copy = remote(their_cols_ref, my_rows, grad_send_sem, grad_recv_sem, other)
    vec_copy = remote(vec_ref, vec_recv_ref, vec_send_sem, vec_recv_sem, other)
    my_half = pl.ds(pl.multiple_of(head * cols, LANES), cols)
    other_half = pl.ds(pl.multiple_of((1 - head) * cols, LANES), cols)

    def exchange(k):
        return remote(full_ref.at[k % 2, :, other_half], recv_ref.at[k], send_sem.at[k], recv_sem.at[k], other)

    @pl.when(step == 0)
    def _():
        greet([other])
        grad_copy.start()
        vec_copy.start()
        own_copy.start()

    @pl.when(step >= 2)
    def _():
        exchange(step - 2).wait_send()

    full_ref[step % 2] = lax.dot_general(left_ref[0], right_ref[0], TN, preferred_element_type=f32).astype(bf16)
    exchange(step).start()

    def finish(k):
        exchange(k).wait_recv()

        def total(start, count):
            return (
                full_ref[k % 2, start : start + count, my_half].astype(f32)
                + recv_ref[k, start : start + count, :].astype(f32)
            ).astype(bf16)

        @pl.when(k < parts)
        def _():
            count = model_dim // down_rows
            for q in range(count):
                send, place = route(k * count + q, me, head)
                both_ref[send, place, :down_rows, :] = total(q * down_rows, down_rows)

        @pl.when(k >= parts)
        def _():
            start = pl.multiple_of(down_rows + (k - parts) * rows, 16)
            for d in range(n_dp):
                send, place = route(d, me, head)
                both_ref[send, place, pl.ds(start, rows), :] = total(d * rows, rows)

    @pl.when(step >= 1)
    def _():
        finish(step - 1)

    @pl.when(step == steps - 1)
    def _():
        finish(steps - 1)
        copies = [
            pltpu.make_async_copy(both_ref.at[0], keep_ref, copy_sem.at[0]),
            pltpu.make_async_copy(both_ref.at[1], send_ref, copy_sem.at[1]),
        ]
        for copy in copies:
            copy.start()
        vec_copy.wait()
        vec_out_ref[...] = vec_ref[...] + vec_recv_ref[...]
        grad_copy.wait()
        own_copy.wait()
        exchange(steps - 2).wait_send()
        exchange(steps - 1).wait_send()
        for copy in copies:
            copy.wait()


def weights(n_dp, left, right, my_cols, their_cols, vec):
    stack, half, model_dim = left.shape
    parts = stack - 2
    steps = 2 * parts + 1
    cols = model_dim // 2
    block_rows = (2 * parts + 1) * model_dim // n_dp
    anywhere = pl.BlockSpec(memory_space=pl.ANY)

    def left_map(j):
        return (jnp.where(j < parts, j, jnp.where(j < 2 * parts, parts, parts + 1)), 0, 0)

    def right_map(j):
        return (jnp.where(j < parts, 0, j - parts + 1), 0, 0)

    blocks = jax.ShapeDtypeStruct((n_dp // 2, block_rows, cols), bf16)
    return pl.pallas_call(
        partial(weights_kernel, n_dp, parts),
        grid=(steps,),
        in_specs=[
            pl.BlockSpec((1, half, model_dim), left_map),
            pl.BlockSpec((1, half, model_dim), right_map),
            anywhere,
            anywhere,
            pl.BlockSpec(vec.shape, lambda j: (0, 0)),
        ],
        out_specs=[anywhere, anywhere, anywhere, pl.BlockSpec(vec.shape, lambda j: (0, 0))],
        scratch_shapes=[
            pltpu.VMEM((2, model_dim, model_dim), bf16),
            pltpu.VMEM((steps, model_dim, cols), bf16),
            pltpu.VMEM((2,) + blocks.shape, bf16),
            pltpu.VMEM(vec.shape, f32),
            pltpu.SemaphoreType.DMA((steps,)),
            pltpu.SemaphoreType.DMA((steps,)),
            pltpu.SemaphoreType.DMA,
            pltpu.SemaphoreType.DMA,
            pltpu.SemaphoreType.DMA,
            pltpu.SemaphoreType.DMA,
            pltpu.SemaphoreType.DMA((3,)),
        ],
        out_shape=[
            blocks,
            blocks,
            jax.ShapeDtypeStruct((2 * half, my_cols.shape[1]), bf16),
            jax.ShapeDtypeStruct(vec.shape, f32),
        ],
        compiler_params=pltpu.CompilerParams(
            collective_id=0, has_side_effects=True, vmem_limit_bytes=48 * 2**20
        ),
        cost_estimate=pl.CostEstimate(flops=15_000_000_000, bytes_accessed=20_000_000, transcendentals=0),
    )(left, right, my_cols, their_cols, vec)


def halve_kernel(mine_ref, kept_ref, got_ref, keep_ref, send_ref):
    mine = mine_ref[0]
    total = (kept_ref[0].astype(f32) + got_ref[0].astype(f32)).astype(bf16)

    @pl.when(mine == 0)
    def _():
        keep_ref[0] = total[0]
        send_ref[0] = total[1]

    @pl.when(mine == 1)
    def _():
        keep_ref[0] = total[1]
        send_ref[0] = total[0]


def halve(mine, kept, got):
    count, rows, cols = kept.shape
    pair = pl.BlockSpec((1, 2, rows, cols), lambda i, n: (i, 0, 0, 0))
    one = pl.BlockSpec((1, rows, cols), lambda i, n: (i, 0, 0))
    shape = jax.ShapeDtypeStruct((count // 2, rows, cols), bf16)
    return pl.pallas_call(
        halve_kernel,
        grid_spec=pltpu.PrefetchScalarGridSpec(
            num_scalar_prefetch=1, grid=(count // 2,), in_specs=[pair, pair], out_specs=[one, one]
        ),
        out_shape=[shape, shape],
        cost_estimate=pl.CostEstimate(flops=1_000_000, bytes_accessed=6 * kept.size, transcendentals=0),
    )(mine[None], kept.reshape(count // 2, 2, rows, cols), got.reshape(count // 2, 2, rows, cols))


def projection_kernel(n_dp, rows_ref, raw_a_ref, raw_b_ref, keep_ref, send_ref, both_ref, sem):
    me, head = lax.axis_index("dp"), lax.axis_index("head")
    rows = both_ref.shape[2]
    local_dim = both_ref.shape[3] // 3
    begin = 0
    for raw_ref in (raw_a_ref, raw_b_ref):
        width = raw_ref.shape[1] // 3
        for c in range(3):
            grad = lax.dot_general(
                rows_ref[...], raw_ref[:, c * width : (c + 1) * width], TN, preferred_element_type=f32
            ).astype(bf16)
            start = c * local_dim + begin
            for d in range(n_dp):
                send, place = route(d, me, head)
                both_ref[send, place, :, start : start + width] = grad[d * rows : (d + 1) * rows]
        begin += width
    copies = [
        pltpu.make_async_copy(both_ref.at[0], keep_ref, sem.at[0]),
        pltpu.make_async_copy(both_ref.at[1], send_ref, sem.at[1]),
    ]
    for copy in copies:
        copy.start()
    for copy in copies:
        copy.wait()


def projection(n_dp, group_rows, raw_a, raw_b):
    model_dim = group_rows.shape[1]
    shape = (n_dp // 2, model_dim // n_dp, raw_a.shape[1] + raw_b.shape[1])
    anywhere = pl.BlockSpec(memory_space=pl.ANY)
    vmem = pl.BlockSpec(memory_space=pltpu.VMEM)
    return pl.pallas_call(
        partial(projection_kernel, n_dp),
        in_specs=[vmem] * 3,
        out_specs=[anywhere] * 2,
        scratch_shapes=[pltpu.VMEM((2,) + shape, bf16), pltpu.SemaphoreType.DMA((2,))],
        out_shape=[jax.ShapeDtypeStruct(shape, bf16)] * 2,
        compiler_params=pltpu.CompilerParams(vmem_limit_bytes=48 * 2**20),
        cost_estimate=pl.CostEstimate(flops=4_000_000_000, bytes_accessed=10_000_000, transcendentals=0),
    )(group_rows, raw_a, raw_b)


def last_kernel(
    n_dp,
    parts,
    s_keep_ref,
    s_got_ref,
    q_keep_ref,
    q_got_ref,
    vec_ref,
    down_ref,
    in_ref,
    out_ref,
    qkv_ref,
    vec_out_ref,
    s_send_ref,
    s_recv_ref,
    s_hold_ref,
    core_send_ref,
    core_recv_ref,
    q_send_refs,
    q_recv_refs,
    q_hold_refs,
    vec_hold_ref,
    vec_recv_ref,
    vec_core_ref,
    q_sems,
    v_sems,
    other_sems,
):
    bits = n_dp.bit_length() - 1
    me, head = lax.axis_index("dp"), lax.axis_index("head")
    other = (me, 1 - head)
    along = [(flip(me, k), head) for k in range(bits)]
    greet(along + [other])

    top = bit(me, bits - 1)
    for place in range(2):
        total = s_keep_ref[place].astype(f32) + s_got_ref[place].astype(f32)

        @pl.when(place == top)
        def _():
            s_hold_ref[...] = total

        @pl.when(place != top)
        def _():
            s_send_ref[...] = total.astype(bf16)

    s_copy = remote(s_send_ref, s_recv_ref, other_sems.at[0], other_sems.at[1], along[-1])
    s_copy.start()

    vec_hold_ref[0] = vec_ref[...]

    def vec_copy(k):
        return remote(vec_hold_ref.at[k], vec_recv_ref.at[k], v_sems.at[0, k], v_sems.at[1, k], along[k])

    second = (flip(me, 1) * (1 - head) + flip(me, 0) * head, head)
    second_bit = bit(me, 1) * (1 - head) + bit(me, 0) * head
    stages = [(second_bit, second)] + [(bit(me, k), along[k]) for k in range(2, bits)]

    def q_copy(s):
        return remote(q_send_refs[s], q_recv_refs[s], q_sems.at[0, s], q_sems.at[1, s], stages[s][1])

    def q_split(s, total_of):
        mine = stages[s][0]
        for p in range(q_send_refs[s].shape[0]):
            q_send_refs[s][p] = total_of(2 * p + (1 - mine)).astype(bf16)
        q_copy(s).start()
        for p in range(q_send_refs[s].shape[0]):
            q_hold_refs[s][p] = total_of(2 * p + mine)

    q_split(0, lambda i: q_keep_ref[i].astype(f32) + q_got_ref[i].astype(f32))
    vec_copy(0).start()

    for k in range(bits):
        vec_copy(k).wait()
        total = vec_hold_ref[k] + vec_recv_ref[k]
        if k < bits - 1:
            vec_hold_ref[k + 1] = total
            vec_copy(k + 1).start()
        else:
            vec_out_ref[...] = total
        if k >= 1 and k < len(stages):
            q_copy(k - 1).wait()
            q_split(k, lambda i, k=k: q_hold_refs[k - 1][i] + q_recv_refs[k - 1][i].astype(f32))
    core_vec = remote(vec_out_ref.at[pl.ds(8, 8)], vec_core_ref, other_sems.at[2], other_sems.at[3], other)
    core_vec.start()

    s_copy.wait()
    rows = out_ref.shape[0]
    down_rows = down_ref.shape[0]
    cols = s_hold_ref.shape[1]

    s_hold_ref[...] = s_hold_ref[...] + s_recv_ref[...].astype(f32)

    def piece(start, count, who):
        return s_hold_ref[pl.ds(pl.multiple_of(start + who * count, 8), count), :]

    pieces = [(0, down_rows)] + [(2 * down_rows + 2 * rows * c, rows) for c in range(parts + 1)]
    at = 0
    for start, count in pieces:
        core_send_ref[at : at + count, :] = piece(start, count, 1 - head)
        at += count
    core_copy = remote(core_send_ref, core_recv_ref, other_sems.at[4], other_sems.at[5], other)
    core_copy.start()
    my_half = pl.ds(pl.multiple_of(head * cols, LANES), cols)
    other_half = pl.ds(pl.multiple_of((1 - head) * cols, LANES), cols)

    def place_all(half, source):
        down_ref[:, half] = source(0)
        for c in range(parts):
            shifted = pl.ds(pl.multiple_of(2 * cols * c + half.start, LANES), cols)
            in_ref[:, shifted] = source(1 + c)
        out_ref[:, half] = source(1 + parts)

    place_all(my_half, lambda i: piece(*pieces[i], head))

    last = len(stages) - 1
    q_copy(last).wait()
    qkv_ref[...] = q_hold_refs[last][0] + q_recv_refs[last][0].astype(f32)

    core_vec.wait()
    row = lax.broadcasted_iota(jnp.int32, vec_core_ref.shape, 0)
    vec_out_ref[8:16] = vec_out_ref[8:16] + jnp.where(row >= 4, vec_core_ref[...], 0.0)
    core_copy.wait()
    starts = [0]
    for _, count in pieces:
        starts.append(starts[-1] + count)
    place_all(other_half, lambda i: core_recv_ref[starts[i] : starts[i + 1], :])


def last(n_dp, parts, s_keep, s_got, q_keep, q_got, vec):
    bits = n_dp.bit_length() - 1
    _, block_rows, cols = s_keep.shape
    q_rows, q_cols = q_keep.shape[1:]
    model_dim = vec.shape[1]
    rows = model_dim // (2 * n_dp)
    vmem = pl.BlockSpec(memory_space=pltpu.VMEM)
    counts = [n_dp // 4 >> s for s in range(bits - 1)]

    def stacks(kind):
        return tuple(pltpu.VMEM((count, q_rows, q_cols), kind) for count in counts)

    def shape(*dims):
        return jax.ShapeDtypeStruct(dims, f32)

    return pl.pallas_call(
        partial(last_kernel, n_dp, parts),
        in_specs=[vmem] * 5,
        out_specs=[vmem] * 5,
        scratch_shapes=[
            pltpu.VMEM((block_rows, cols), bf16),
            pltpu.VMEM((block_rows, cols), bf16),
            pltpu.VMEM((block_rows, cols), f32),
            pltpu.VMEM((block_rows // 2, cols), f32),
            pltpu.VMEM((block_rows // 2, cols), f32),
            stacks(bf16),
            stacks(bf16),
            stacks(f32),
            pltpu.VMEM((bits,) + vec.shape, f32),
            pltpu.VMEM((bits,) + vec.shape, f32),
            pltpu.VMEM((8, model_dim), f32),
            pltpu.SemaphoreType.DMA((2, bits - 1)),
            pltpu.SemaphoreType.DMA((2, bits)),
            pltpu.SemaphoreType.DMA((6,)),
        ],
        out_shape=[
            shape(parts * rows, model_dim),
            shape(rows, parts * model_dim),
            shape(rows, model_dim),
            shape(q_rows, q_cols),
            shape(*vec.shape),
        ],
        compiler_params=pltpu.CompilerParams(
            collective_id=1, has_side_effects=True, vmem_limit_bytes=32 * 2**20
        ),
        cost_estimate=pl.CostEstimate(flops=1_000_000_000, bytes_accessed=6_000_000, transcendentals=0),
    )(s_keep, s_got, q_keep, q_got, vec)


def take(array, index, axis=0):
    return lax.dynamic_index_in_dim(array, index, axis, keepdims=False)


class Links:
    def __init__(self, n_dp):
        self.n_dp = n_dp
        self.bits = n_dp.bit_length() - 1
        self.dp = lax.axis_index("dp")
        self.head = lax.axis_index("head")

    def bit(self, which):
        return (self.dp >> which) & 1

    def permute(self, array, partner):
        pairs = []
        for d in range(self.n_dp):
            for h in range(2):
                to_d, to_h = partner(d, h)
                pairs.append((2 * d + h, 2 * to_d + to_h))
        return lax.ppermute(array, AXES, pairs)

    def swap_head(self, array):
        return self.permute(array, lambda d, h: (d, 1 - h))

    def swap_bit(self, array, which):
        return self.permute(array, lambda d, h: (d ^ (1 << which), h))

    def scatter_heads(self, blocks):
        got = self.swap_head(take(blocks, 1 - self.head, 1))
        return (take(blocks, self.head, 1).astype(f32) + got.astype(f32)).astype(bf16)

    def scatter_dp(self, blocks):
        tail = blocks.shape[1:]
        b0, b1 = self.bit(0), self.bit(1)
        first = self.head == 0
        blocks = blocks.reshape((self.n_dp // 4, 4) + tail)

        def two(one, other):
            i = jnp.where(first, one, 2 * other)
            j = jnp.where(first, 2 + one, 2 * other + 1)
            return jnp.stack([take(blocks, i, 1), take(blocks, j, 1)], axis=1)

        got = self.permute(two(1 - b0, 1 - b1), lambda d, h: (d ^ (1 if h == 0 else 2), h))
        blocks = (two(b0, b1).astype(f32) + got.astype(f32)).astype(bf16)
        mine = jnp.where(first, b1, b0)
        got = self.permute(take(blocks, 1 - mine, 1), lambda d, h: (d ^ (2 if h == 0 else 1), h))
        blocks = take(blocks, mine, 1).astype(f32) + got.astype(f32)
        for which in range(2, self.bits):
            blocks = blocks.reshape((-1, 2) + tail)
            mine = self.bit(which)
            got = self.swap_bit(take(blocks, 1 - mine, 1).astype(bf16), which)
            blocks = take(blocks, mine, 1) + got.astype(f32)
        return blocks.reshape(tail)

    def total(self, array):
        array = array + self.swap_head(array)
        for which in range(self.bits):
            array = array + self.swap_bit(array, which)
        return array


def shards(
    n_dp,
    tokens,
    lengths,
    w_qkv,
    bias_qv,
    w_out,
    bias_out,
    ln1_gain,
    ln1_bias,
    w_in,
    bias_in,
    w_down,
    bias_down,
    ln2_gain,
    ln2_bias,
    term_w,
    term_bias,
    grad_hidden,
    grad_term,
):
    links = Links(n_dp)
    head = links.head
    half, model_dim = tokens.shape
    row_len = 2 * half
    local_dim = w_qkv.shape[2]
    ffn_dim = w_in.shape[1]
    query_scale = HEAD_DIM ** (-0.5)

    boundary = jnp.cumsum(lengths[0])
    places = jnp.arange(row_len, dtype=jnp.int32)
    segment = jnp.sum((places[:, None] >= boundary[None, :]).astype(jnp.int32), axis=-1)
    seg_col = jnp.broadcast_to(segment[:, None], (row_len, LANES))
    seg_row = jnp.broadcast_to(segment[None, :], (8, row_len))

    def both(mine, theirs, axis):
        return jnp.where(
            head == 0,
            jnp.concatenate([mine, theirs], axis=axis),
            jnp.concatenate([theirs, mine], axis=axis),
        )

    group_rows = both(tokens, links.swap_head(tokens), 0)
    w_flat = w_qkv.reshape(model_dim, 3 * local_dim)
    projected = jnp.dot(group_rows, w_flat, preferred_element_type=f32)
    queries = ((projected[:, :local_dim] + bias_qv[:, 0]) * query_scale).astype(bf16)
    key_rows = projected[:, local_dim : 2 * local_dim].astype(bf16)
    value_rows = (projected[:, 2 * local_dim :] + bias_qv[:, 1]).astype(bf16)
    attended, logs = attend(lengths, queries, key_rows, value_rows, seg_col, seg_row)

    def my_half(rows):
        return lax.dynamic_slice_in_dim(rows, head * half, half, 0)

    def their_half(rows):
        return lax.dynamic_slice_in_dim(rows, (1 - head) * half, half, 0)

    vec = jnp.stack([bias_out, ln1_gain, ln1_bias, bias_down, ln2_gain, ln2_bias, term_w, jnp.zeros_like(term_w)])
    hidden_out, term_weight, left, right, resid_one_grad, my_cols, their_cols, sums, bias_in_local = middle(
        my_half(attended),
        links.swap_head(their_half(attended)),
        tokens,
        grad_hidden,
        grad_term[:, None],
        w_out,
        w_in,
        w_down,
        vec,
        bias_in[None, :],
        term_bias[None, :],
    )
    parts = ffn_dim // model_dim
    vec = jnp.concatenate([sums, bias_in_local.reshape(parts, model_dim)])
    vec = jnp.pad(vec, ((0, 16 - vec.shape[0]), (0, 0)))
    pairs = local_dim // LANES
    split = pairs - 1
    in_kernels = (model_dim // n_dp) % 16 == 0 and links.bits >= 3

    def back(grads, own_lengths, first_pair, count):
        return attend_back(
            own_lengths, queries, key_rows, value_rows, grads, logs, seg_col, seg_row, first_pair, count
        )

    def tokens_grad(raw_a, raw_b):
        w_a = w_qkv[:, :, : split * LANES].reshape(model_dim, -1)
        w_b = w_qkv[:, :, split * LANES :].reshape(model_dim, -1)
        grad = lax.dot_general(raw_a, w_a, NT, preferred_element_type=f32)
        grad = grad + lax.dot_general(raw_b, w_b, NT, preferred_element_type=f32)
        received = links.swap_head(their_half(grad).astype(bf16))
        return resid_one_grad + my_half(grad) + received.astype(f32)

    def value_sums(sums_a, sums_b):
        rows = [
            jnp.concatenate([x[:, c * x.shape[1] // 3 : (c + 1) * x.shape[1] // 3] for x in (sums_a, sums_b)], axis=1)
            for c in (0, 2)
        ]
        return lax.dynamic_update_slice(
            jnp.zeros((2, 2 * local_dim), f32), jnp.concatenate(rows), (jnp.int32(0), head * local_dim)
        )

    if in_kernels:
        s_keep, s_send, head_grad, vec = weights(n_dp, left, right, my_cols, their_cols, vec)
        s_got = links.permute(s_send, lambda d, h: (d ^ (1 if h == 0 else 2), h))
        raw_a, sums_a = back(head_grad, lengths, 0, split)
        s_keep, s_send = halve(jnp.where(head == 0, links.bit(1), links.bit(0)), s_keep, s_got)
        s_got = links.permute(s_send, lambda d, h: (d ^ (2 if h == 0 else 1), h))
        late_lengths, _ = lax.optimization_barrier((lengths, s_keep))
        raw_b, sums_b = back(head_grad, late_lengths, split, 1)
        for which in range(2, links.bits - 1):
            s_keep, s_send = halve(links.bit(which), s_keep, s_got)
            s_got = links.swap_bit(s_send, which)
        q_keep, q_send = projection(n_dp, group_rows, raw_a, raw_b)
        q_got = links.permute(q_send, lambda d, h: (d ^ (1 if h == 0 else 2), h))
        grad_tokens = tokens_grad(raw_a, raw_b)
        vec = lax.dynamic_update_slice(vec, value_sums(sums_a, sums_b), (12, 0))
        grad_down, grad_in, grad_out, grad_qkv, vectors = last(n_dp, parts, s_keep, s_got, q_keep, q_got, vec)
    else:
        head_grad = both(my_cols, links.swap_head(their_cols), 0)
        raw_a, sums_a = back(head_grad, lengths, 0, split)
        raw_b, sums_b = back(head_grad, lengths, split, 1)

        def product(i, j):
            return lax.dot_general(left[i], right[j], TN, preferred_element_type=f32).astype(bf16)

        def reduced(partial_sum):
            rows, cols = partial_sum.shape
            return links.scatter_dp(links.scatter_heads(partial_sum.reshape(n_dp, 2, rows // (2 * n_dp), cols)))

        grad_down = reduced(jnp.concatenate([product(i, 0) for i in range(parts)]))
        grad_in = reduced(jnp.concatenate([product(parts, 1 + i) for i in range(parts)], axis=1))
        grad_out = reduced(product(parts + 1, parts + 1))
        grad_tokens = tokens_grad(raw_a, raw_b)
        raw = [x[:, c * x.shape[1] // 3 : (c + 1) * x.shape[1] // 3] for c in range(3) for x in (raw_a, raw_b)]
        qkv_local = lax.dot_general(group_rows, jnp.concatenate(raw, axis=1), TN, preferred_element_type=f32)
        grad_qkv = links.scatter_dp(qkv_local.astype(bf16).reshape(n_dp, model_dim // n_dp, 3 * local_dim))
        vectors = links.total(lax.dynamic_update_slice(vec, value_sums(sums_a, sums_b), (12, 0)))
    grad_qkv = grad_qkv.reshape(model_dim // n_dp, 3, local_dim)

    place = 2 * links.dp + head
    width = model_dim // (2 * n_dp)
    mine = lax.dynamic_slice_in_dim(vectors, place * width, width, 1)
    in_width = ffn_dim // (2 * n_dp)
    bias_in_mine = lax.dynamic_slice_in_dim(vectors[8 : 8 + parts].reshape(-1), place * in_width, in_width, 0)
    bias_qv_mine = mine[12:14].T

    return (
        hidden_out,
        term_weight[:, 0],
        grad_tokens,
        grad_qkv,
        bias_qv_mine,
        grad_out,
        mine[0],
        mine[1],
        mine[2],
        grad_in,
        bias_in_mine,
        grad_down,
        mine[3],
        mine[4],
        mine[5],
        mine[6],
        vectors[7, :1],
    )


def solution(mesh):
    rows = P(AXES, None)
    return jax.shard_map(
        partial(shards, mesh.shape["dp"]),
        mesh=mesh,
        in_specs=(rows, P("dp", None), P(None, None, "head"), P("head", None))
        + (P(),) * 12
        + (rows, P(AXES)),
        out_specs=(
            rows,
            P(AXES),
            rows,
            P("dp", None, "head"),
            rows,
            rows,
            P(AXES),
            P(AXES),
            P(AXES),
            rows,
            P(AXES),
            rows,
            P(AXES),
            P(AXES),
            P(AXES),
            P(AXES),
            P(),
        ),
        check_vma=False,
    )
```

```python
from functools import partial

import jax
import jax.numpy as jnp
from jax import lax
from jax.experimental import pallas as pl
from jax.experimental.pallas import tpu as pltpu
from jax.sharding import PartitionSpec as P

HEAD_DIM = 64
LANES = 128
VMEM_LIMIT = 60 * 2**20
Q_ROWS = 256
PIECE = 32
Q_COLUMNS = 128
WIDTHS = (2, 3, 4, 5, 6, 8, 10)
AXES = ("dp", "head")

f32 = jnp.float32
bf16 = jnp.bfloat16
norm_eps = 1e-06
NT = (((1,), (1,)), ((), ()))
TN = (((0,), (0,)), ((), ()))


def key_range(lengths_ref, first, rows, row_len):
    start = jnp.int32(0)
    low = jnp.int32(0)
    high = jnp.int32(row_len)
    for j in range(lengths_ref.shape[1]):
        end = start + lengths_ref[0, j]
        low = jnp.where(start <= first, start, low)
        high = jnp.where(end >= first + rows, jnp.minimum(high, end), high)
        start = end
    low_block = low // LANES
    count = (high + LANES - 1) // LANES - low_block
    return low_block, count


def by_width(lengths_ref, first, rows, row_len, body):
    blocks = row_len // LANES
    low_block, count = key_range(lengths_ref, first, rows, row_len)
    widths = sorted({min(w, blocks) for w in WIDTHS})
    below = 0
    for width in widths:

        @pl.when((count > below) & (count <= width))
        def _(width=width):
            begin = jnp.minimum(low_block, blocks - width)
            body(pl.multiple_of(begin * LANES, LANES), width * LANES)

        below = width


def attend_kernel(
    lengths_ref, q_ref, k_ref, v_ref, segc_ref, segr_ref, o_ref, log_ref, mask_ref, cols_ref, s_ref, p_ref
):
    rows, local_dim = q_ref.shape
    row_len = k_ref.shape[0]
    first = pl.program_id(0) * rows
    lane = lax.broadcasted_iota(jnp.int32, (rows, LANES), 1)

    def body(begin, width):
        same = segc_ref[:, 0:1] == segr_ref[0:1, pl.ds(begin, width)]
        mask_ref[:, :width] = jnp.where(same, 0.0, -1e30)

        heads = local_dim // HEAD_DIM

        def score(i):
            cols = slice(i // 2 * LANES, i // 2 * LANES + LANES)
            q_pair = q_ref[:, cols]
            q_one = jnp.where((lane // HEAD_DIM) == i % 2, q_pair, jnp.zeros_like(q_pair))
            k_pair = k_ref[pl.ds(begin, width), cols]
            s_ref[i % 2, :, :width] = lax.dot_general(q_one, k_pair, NT, preferred_element_type=f32)

        def soft(i):
            for r in range(0, rows, PIECE):
                part = slice(r, r + PIECE)
                scores = s_ref[i % 2, part, :width] + mask_ref[part, :width]
                row_max = jnp.max(scores, axis=1, keepdims=True)
                powers = jnp.exp(scores - row_max)
                total = jnp.sum(powers, axis=1, keepdims=True)
                p_ref[i % 2, part, :width] = (powers * (1.0 / total)).astype(bf16)
                log_total = row_max + jnp.log(total)
                cols_ref[part] = jnp.where(lane[part] == i, log_total, cols_ref[part])

        def value(i):
            cols = slice(i // 2 * LANES, i // 2 * LANES + LANES)
            return jnp.dot(p_ref[i % 2, :, :width], v_ref[pl.ds(begin, width), cols], preferred_element_type=f32)

        score(0)
        held = None
        for i in range(heads):
            if i + 1 < heads:
                score(i + 1)
            soft(i)
            out = value(i)
            if i % 2 == 0:
                held = out
            else:
                cols = slice(i // 2 * LANES, i // 2 * LANES + LANES)
                o_ref[:, cols] = jnp.where(lane < HEAD_DIM, held, out).astype(bf16)

    by_width(lengths_ref, first, rows, row_len, body)
    log_ref[...] = cols_ref[...].T[: log_ref.shape[0]]


def attend(lengths, queries, key_rows, value_rows, seg_col, seg_row):
    row_len, local_dim = queries.shape
    rows = min(Q_ROWS, row_len)
    whole = pl.BlockSpec((row_len, local_dim), lambda i, n: (0, 0))
    block = pl.BlockSpec((rows, local_dim), lambda i, n: (i, 0))
    return pl.pallas_call(
        attend_kernel,
        grid_spec=pltpu.PrefetchScalarGridSpec(
            num_scalar_prefetch=1,
            grid=(row_len // rows,),
            in_specs=[
                block,
                whole,
                whole,
                pl.BlockSpec((rows, LANES), lambda i, n: (i, 0)),
                pl.BlockSpec((8, row_len), lambda i, n: (0, 0)),
            ],
            out_specs=[block, pl.BlockSpec((8, rows), lambda i, n: (0, i))],
            scratch_shapes=[
                pltpu.VMEM((rows, max(WIDTHS) * LANES), f32),
                pltpu.VMEM((rows, LANES), f32),
                pltpu.VMEM((2, rows, max(WIDTHS) * LANES), f32),
                pltpu.VMEM((2, rows, max(WIDTHS) * LANES), bf16),
            ],
        ),
        out_shape=[
            jax.ShapeDtypeStruct((row_len, local_dim), bf16),
            jax.ShapeDtypeStruct((8, row_len), f32),
        ],
        compiler_params=pltpu.CompilerParams(vmem_limit_bytes=VMEM_LIMIT),
        cost_estimate=pl.CostEstimate(flops=20_000_000_000, bytes_accessed=8_000_000, transcendentals=0),
    )(lengths, queries, key_rows, value_rows, seg_col, seg_row)


def attend_back_kernel(
    lengths_ref,
    q_ref,
    k_ref,
    v_ref,
    g_ref,
    log_ref,
    segc_ref,
    segr_ref,
    raw_ref,
    sums_ref,
    mask_ref,
    dk_ref,
    dv_ref,
    s_ref,
    d_ref,
    p_ref,
    e_ref,
    ones_ref,
):
    rows, local_dim = q_ref.shape
    row_len = k_ref.shape[0]
    step = pl.program_id(0)
    first = step * rows
    lane = lax.broadcasted_iota(jnp.int32, (rows, LANES), 1)

    @pl.when(step == 0)
    def _():
        dk_ref[...] = jnp.zeros_like(dk_ref)
        dv_ref[...] = jnp.zeros_like(dv_ref)

    def body(begin, width):
        keys = pl.ds(begin, width)
        same = segc_ref[keys, 0:1] == segr_ref[0:1, :]
        mask_ref[:width, :] = jnp.where(same, 0.0, -1e30)

        def pair_step(pair, carry):
            cols = pl.ds(pl.multiple_of(pair * LANES, LANES), LANES)

            def products(i):
                mine = (lane // HEAD_DIM) == i
                here = slice(i * rows, i * rows + rows)
                q_pair, g_pair = q_ref[:, cols], g_ref[:, cols]
                q_one = jnp.where(mine, q_pair, jnp.zeros_like(q_pair))
                g_one = jnp.where(mine, g_pair, jnp.zeros_like(g_pair))
                ones_ref[0, here] = q_one
                ones_ref[1, here] = g_one
                s_ref[i, :width] = lax.dot_general(k_ref[keys, cols], q_one, NT, preferred_element_type=f32)
                d_ref[i, :width] = lax.dot_general(v_ref[keys, cols], g_one, NT, preferred_element_type=f32)

            def soft(i):
                here = slice(i * rows, i * rows + rows)
                log_row = log_ref[pl.ds(2 * pair + i, 1), :]
                inner = jnp.zeros((8, rows), f32)
                for r in range(0, width, PIECE):
                    part = slice(r, r + PIECE)
                    probs = jnp.exp(s_ref[i, part] + mask_ref[part] - log_row)
                    s_ref[i, part] = probs
                    p_ref[part, here] = probs.astype(bf16)
                    inner = inner + jnp.sum((probs * d_ref[i, part]).reshape(PIECE // 8, 8, rows), axis=0)
                inner = jnp.sum(inner, axis=0, keepdims=True)
                for r in range(0, width, PIECE):
                    part = slice(r, r + PIECE)
                    e_ref[part, here] = (s_ref[i, part] * (d_ref[i, part] - inner)).astype(bf16)

            products(0)
            products(1)
            soft(0)
            soft(1)
            dv_ref[keys, cols] += jnp.dot(p_ref[:width], ones_ref[1], preferred_element_type=f32)
            dk_ref[keys, cols] += jnp.dot(e_ref[:width], ones_ref[0], preferred_element_type=f32)
            dq = lax.dot_general(e_ref[:width], k_ref[keys, cols], TN, preferred_element_type=f32)
            dq_low = jnp.where(lane < HEAD_DIM, dq[:rows], dq[rows:]).astype(bf16)
            raw_ref[pl.ds(pl.multiple_of(first, rows), rows), cols] = dq_low * jnp.asarray(HEAD_DIM**-0.5, bf16)
            return carry

        lax.fori_loop(0, local_dim // LANES, pair_step, 0)

    by_width(lengths_ref, first, rows, row_len, body)

    @pl.when(step == pl.num_programs(0) - 1)
    def _():
        raw_ref[:, local_dim : 2 * local_dim] = dk_ref[...].astype(bf16)
        raw_ref[:, 2 * local_dim :] = dv_ref[...].astype(bf16)
        sums_ref[...] = jnp.sum(raw_ref[...].astype(f32), axis=0, keepdims=True)


def attend_back(lengths, queries, key_rows, value_rows, grads, logs, seg_col, seg_row):
    row_len, local_dim = queries.shape
    rows = min(Q_ROWS, row_len)
    whole = pl.BlockSpec((row_len, local_dim), lambda i, n: (0, 0))
    block = pl.BlockSpec((rows, local_dim), lambda i, n: (i, 0))
    return pl.pallas_call(
        attend_back_kernel,
        grid_spec=pltpu.PrefetchScalarGridSpec(
            num_scalar_prefetch=1,
            grid=(row_len // rows,),
            in_specs=[
                block,
                whole,
                whole,
                block,
                pl.BlockSpec((8, rows), lambda i, n: (0, i)),
                pl.BlockSpec((row_len, LANES), lambda i, n: (0, 0)),
                pl.BlockSpec((8, rows), lambda i, n: (0, i)),
            ],
            out_specs=[
                pl.BlockSpec((row_len, 3 * local_dim), lambda i, n: (0, 0)),
                pl.BlockSpec((1, 3 * local_dim), lambda i, n: (0, 0)),
            ],
            scratch_shapes=[
                pltpu.VMEM((max(WIDTHS) * LANES, rows), f32),
                pltpu.VMEM((row_len, local_dim), f32),
                pltpu.VMEM((row_len, local_dim), f32),
                pltpu.VMEM((2, max(WIDTHS) * LANES, rows), f32),
                pltpu.VMEM((2, max(WIDTHS) * LANES, rows), f32),
                pltpu.VMEM((max(WIDTHS) * LANES, 2 * rows), bf16),
                pltpu.VMEM((max(WIDTHS) * LANES, 2 * rows), bf16),
                pltpu.VMEM((2, 2 * rows, LANES), bf16),
            ],
        ),
        out_shape=[
            jax.ShapeDtypeStruct((row_len, 3 * local_dim), bf16),
            jax.ShapeDtypeStruct((1, 3 * local_dim), f32),
        ],
        compiler_params=pltpu.CompilerParams(vmem_limit_bytes=VMEM_LIMIT),
        cost_estimate=pl.CostEstimate(flops=40_000_000_000, bytes_accessed=12_000_000, transcendentals=0),
    )(lengths, queries, key_rows, value_rows, grads, logs, seg_col, seg_row)


TILE = 256


def gelu_both(x):
    cdf = 0.5 + 0.5 * lax.erf(x * 0.7071067811865476)
    density = jnp.exp(-0.5 * x * x) * 0.3989422804014327
    return x * cdf, cdf + x * density


def normalize(resid):
    center = resid - jnp.mean(resid, axis=-1, keepdims=True)
    scale = lax.rsqrt(jnp.mean(center * center, axis=-1, keepdims=True) + norm_eps)
    return center * scale, scale


def normalize_back(grad, normed, scale):
    shift = jnp.mean(grad, axis=-1, keepdims=True)
    slope = jnp.mean(grad * normed, axis=-1, keepdims=True)
    return scale * (grad - shift - normed * slope)


def fold(x):
    return jnp.sum(x.astype(f32).reshape(x.shape[0] // 8, 8, x.shape[1]), axis=0)


def middle_kernel(
    mine_ref,
    theirs_ref,
    tokens_ref,
    hid_ref,
    term_ref,
    w_out_ref,
    w_in_ref,
    w_down_ref,
    vec_ref,
    bias_in_ref,
    term_bias_ref,
    hidden_ref,
    weight_ref,
    left_ref,
    right_ref,
    resid_ref,
    my_grad_ref,
    their_grad_ref,
    sums_ref,
    in_sums_ref,
    slope_ref,
    wide_ref,
    x_ref,
    normal_ref,
    scale_ref,
    fold_ref,
    in_fold_ref,
):
    head = lax.axis_index("head")
    local_dim = mine_ref.shape[1]
    model_dim = w_out_ref.shape[0]
    parts = w_in_ref.shape[1] // model_dim
    rows = tokens_ref.shape[0]
    pieces = [slice(r, r + PIECE) for r in range(0, rows, PIECE)]
    bias_out, ln1_gain, ln1_bias = vec_ref[0:1], vec_ref[1:2], vec_ref[2:3]
    bias_down, ln2_gain, ln2_bias, term_w = vec_ref[3:4], vec_ref[4:5], vec_ref[5:6], vec_ref[6:7]

    @pl.when(pl.program_id(0) == 0)
    def _():
        fold_ref[...] = jnp.zeros_like(fold_ref)
        in_fold_ref[...] = jnp.zeros_like(in_fold_ref)

    left_ref[parts + 1, :, pl.ds(pl.multiple_of(head * local_dim, LANES), local_dim)] = mine_ref[...]
    left_ref[parts + 1, :, pl.ds(pl.multiple_of((1 - head) * local_dim, LANES), local_dim)] = theirs_ref[...]
    x_ref[...] = jnp.dot(left_ref[parts + 1], w_out_ref[...], preferred_element_type=f32)
    for r in pieces:
        normal, scale = normalize(tokens_ref[r].astype(f32) + (x_ref[r] + bias_out))
        normed = normal * ln1_gain + ln1_bias
        normal_ref[r] = normal
        scale_ref[r] = scale
        left_ref[parts, r] = normed.astype(bf16)
        x_ref[r] = normed + bias_down

    def columns(c):
        return slice(c * model_dim, (c + 1) * model_dim)

    def rise(c):
        wide_ref[c % 2] = jnp.dot(left_ref[parts], w_in_ref[:, columns(c)], preferred_element_type=f32)

    rise(0)
    for c in range(parts):
        if c + 1 < parts:
            rise(c + 1)
        for r in pieces:
            value, slope = gelu_both(wide_ref[c % 2, r] + bias_in_ref[:, columns(c)])
            left_ref[c, r] = value.astype(bf16)
            slope_ref[r, columns(c)] = slope
        x_ref[...] += jnp.dot(left_ref[c], w_down_ref[columns(c), :], preferred_element_type=f32)

    for r in pieces:
        normal, scale = normalize(x_ref[r])
        normed = normal * ln2_gain + ln2_bias
        hidden_ref[r] = normed.astype(bf16)
        logit = jnp.sum(normed * term_w, axis=-1, keepdims=True) + term_bias_ref[0:1, 0:1]
        small = jnp.exp(-jnp.abs(logit))
        weight_ref[r] = jnp.maximum(logit, 0.0) + jnp.log1p(small)
        logit_grad = term_ref[r] * (jnp.where(logit >= 0.0, 1.0, small) / (1.0 + small))
        two_grad = hid_ref[r] + logit_grad * term_w
        resid_two = normalize_back(two_grad * ln2_gain, normal, scale)
        low = resid_two.astype(bf16)
        right_ref[0, r] = low
        x_ref[r] = resid_two
        fold_ref[3] += fold(low)
        fold_ref[4] += fold(two_grad * normal)
        fold_ref[5] += fold(two_grad)
        fold_ref[6] += fold(logit_grad * normed)
        fold_ref[7] += fold(jnp.broadcast_to(logit_grad, normal.shape))

    def fall(c):
        wide_ref[c % 2] = lax.dot_general(right_ref[0], w_down_ref[columns(c), :], NT, preferred_element_type=f32)

    fall(0)
    for c in range(parts):
        if c + 1 < parts:
            fall(c + 1)
        for r in pieces:
            low = (wide_ref[c % 2, r] * slope_ref[r, columns(c)]).astype(bf16)
            right_ref[1 + c, r] = low
            in_fold_ref[:, columns(c)] += fold(low)
        x_ref[...] += lax.dot_general(right_ref[1 + c], w_in_ref[:, columns(c)], NT, preferred_element_type=f32)

    for r in pieces:
        one_grad = x_ref[r]
        normal = normal_ref[r]
        resid_one = normalize_back(one_grad * ln1_gain, normal, scale_ref[r])
        resid_ref[r] = resid_one
        low = resid_one.astype(bf16)
        right_ref[parts + 1, r] = low
        fold_ref[0] += fold(low)
        fold_ref[1] += fold(one_grad * normal)
        fold_ref[2] += fold(one_grad)
    grads = lax.dot_general(right_ref[parts + 1], w_out_ref[...], NT, preferred_element_type=f32).astype(bf16)

    @pl.when(head == 0)
    def _():
        my_grad_ref[...] = grads[:, :local_dim]
        their_grad_ref[...] = grads[:, local_dim:]

    @pl.when(head == 1)
    def _():
        my_grad_ref[...] = grads[:, local_dim:]
        their_grad_ref[...] = grads[:, :local_dim]

    @pl.when(pl.program_id(0) == pl.num_programs(0) - 1)
    def _():
        sums_ref[...] = jnp.sum(fold_ref[...], axis=1)
        in_sums_ref[...] = jnp.sum(in_fold_ref[...], axis=0, keepdims=True)


def middle(mine, theirs, tokens, grad_hidden, grad_term, w_out, w_in, w_down, vec, bias_in, term_bias):
    half, model_dim = tokens.shape
    local_dim = mine.shape[1]
    ffn_dim = w_in.shape[1]
    rows = min(TILE, half)

    def tile(cols):
        return pl.BlockSpec((rows, cols), lambda i: (i, 0))

    def whole(*shape):
        return pl.BlockSpec(shape, lambda i: (0, 0), pipeline_mode=pl.Buffered(1))

    stacked = pl.BlockSpec((ffn_dim // model_dim + 2, rows, model_dim), lambda i: (0, i, 0))
    stack = jax.ShapeDtypeStruct((ffn_dim // model_dim + 2, half, model_dim), bf16)

    def full(cols, kind):
        return jax.ShapeDtypeStruct((half, cols), kind)

    return pl.pallas_call(
        middle_kernel,
        grid=(half // rows,),
        in_specs=[
            tile(local_dim),
            tile(local_dim),
            tile(model_dim),
            tile(model_dim),
            tile(1),
            whole(model_dim, model_dim),
            whole(model_dim, ffn_dim),
            whole(ffn_dim, model_dim),
            whole(8, model_dim),
            whole(1, ffn_dim),
            whole(1, 1),
        ],
        out_specs=[
            tile(model_dim),
            tile(1),
            stacked,
            stacked,
            tile(model_dim),
            tile(local_dim),
            tile(local_dim),
            pl.BlockSpec((8, model_dim), lambda i: (0, 0)),
            pl.BlockSpec((1, ffn_dim), lambda i: (0, 0)),
        ],
        scratch_shapes=[
            pltpu.VMEM((rows, ffn_dim), f32),
            pltpu.VMEM((2, rows, model_dim), f32),
            pltpu.VMEM((rows, model_dim), f32),
            pltpu.VMEM((rows, model_dim), f32),
            pltpu.VMEM((rows, 1), f32),
            pltpu.VMEM((8, 8, model_dim), f32),
            pltpu.VMEM((8, ffn_dim), f32),
        ],
        out_shape=[
            full(model_dim, bf16),
            full(1, f32),
            stack,
            stack,
            full(model_dim, f32),
            full(local_dim, bf16),
            full(local_dim, bf16),
            jax.ShapeDtypeStruct((8, model_dim), f32),
            jax.ShapeDtypeStruct((1, ffn_dim), f32),
        ],
        compiler_params=pltpu.CompilerParams(vmem_limit_bytes=VMEM_LIMIT),
        cost_estimate=pl.CostEstimate(flops=40_000_000_000, bytes_accessed=50_000_000, transcendentals=0),
    )(mine, theirs, tokens, grad_hidden, grad_term, w_out, w_in, w_down, vec, bias_in, term_bias)


def bit(place, which):
    return (place // 2**which) % 2


def flip(place, which):
    return place + (1 - 2 * bit(place, which)) * 2**which


def route(target, me, head):
    low, high = bit(target, 0), bit(target, 1)
    send = (1 - head) * ((low + bit(me, 0)) % 2) + head * ((high + bit(me, 1)) % 2)
    return send, 2 * (target // 4) + (1 - head) * high + head * low


def greet(partners):
    barrier = pltpu.get_barrier_semaphore()
    for partner in partners:
        pl.semaphore_signal(barrier, inc=1, device_id=partner, device_id_type=pl.DeviceIdType.MESH)
    pl.semaphore_wait(barrier, len(partners))


def remote(source, target, send_sem, recv_sem, partner):
    return pltpu.make_async_remote_copy(
        src_ref=source,
        dst_ref=target,
        send_sem=send_sem,
        recv_sem=recv_sem,
        device_id=partner,
        device_id_type=pl.DeviceIdType.MESH,
    )


def weights_kernel(
    n_dp,
    parts,
    left_ref,
    right_ref,
    my_cols_ref,
    their_cols_ref,
    vec_ref,
    keep_ref,
    send_ref,
    grads_ref,
    vec_out_ref,
    full_ref,
    recv_ref,
    both_ref,
    vec_recv_ref,
    send_sem,
    recv_sem,
    grad_send_sem,
    grad_recv_sem,
    vec_send_sem,
    vec_recv_sem,
    copy_sem,
):
    me, head = lax.axis_index("dp"), lax.axis_index("head")
    other = (me, 1 - head)
    step = pl.program_id(0)
    steps = 2 * parts + 1
    model_dim = left_ref.shape[2]
    cols = model_dim // 2
    half = my_cols_ref.shape[0]
    down_rows = parts * model_dim // n_dp
    rows = model_dim // n_dp
    my_rows = grads_ref.at[pl.ds(pl.multiple_of(head * half, half), half)]
    own_copy = pltpu.make_async_copy(my_cols_ref, my_rows, copy_sem.at[2])
    grad_copy = remote(their_cols_ref, my_rows, grad_send_sem, grad_recv_sem, other)
    vec_copy = remote(vec_ref, vec_recv_ref, vec_send_sem, vec_recv_sem, other)
    my_half = pl.ds(pl.multiple_of(head * cols, LANES), cols)
    other_half = pl.ds(pl.multiple_of((1 - head) * cols, LANES), cols)

    def exchange(k):
        return remote(full_ref.at[k % 2, :, other_half], recv_ref.at[k], send_sem.at[k], recv_sem.at[k], other)

    @pl.when(step == 0)
    def _():
        greet([other])
        grad_copy.start()
        vec_copy.start()
        own_copy.start()

    @pl.when(step >= 2)
    def _():
        exchange(step - 2).wait_send()

    full_ref[step % 2] = lax.dot_general(left_ref[0], right_ref[0], TN, preferred_element_type=f32).astype(bf16)
    exchange(step).start()

    def finish(k):
        exchange(k).wait_recv()

        def total(start, count):
            return (
                full_ref[k % 2, start : start + count, my_half].astype(f32)
                + recv_ref[k, start : start + count, :].astype(f32)
            ).astype(bf16)

        @pl.when(k < parts)
        def _():
            count = model_dim // down_rows
            for q in range(count):
                send, place = route(k * count + q, me, head)
                both_ref[send, place, :down_rows, :] = total(q * down_rows, down_rows)

        @pl.when(k >= parts)
        def _():
            start = pl.multiple_of(down_rows + (k - parts) * rows, 16)
            for d in range(n_dp):
                send, place = route(d, me, head)
                both_ref[send, place, pl.ds(start, rows), :] = total(d * rows, rows)

    @pl.when(step >= 1)
    def _():
        finish(step - 1)

    @pl.when(step == steps - 1)
    def _():
        finish(steps - 1)
        copies = [
            pltpu.make_async_copy(both_ref.at[0], keep_ref, copy_sem.at[0]),
            pltpu.make_async_copy(both_ref.at[1], send_ref, copy_sem.at[1]),
        ]
        for copy in copies:
            copy.start()
        vec_copy.wait()
        vec_out_ref[...] = vec_ref[...] + vec_recv_ref[...]
        grad_copy.wait()
        own_copy.wait()
        exchange(steps - 2).wait_send()
        exchange(steps - 1).wait_send()
        for copy in copies:
            copy.wait()


def weights(n_dp, left, right, my_cols, their_cols, vec):
    stack, half, model_dim = left.shape
    parts = stack - 2
    steps = 2 * parts + 1
    cols = model_dim // 2
    block_rows = (2 * parts + 1) * model_dim // n_dp
    anywhere = pl.BlockSpec(memory_space=pl.ANY)

    def left_map(j):
        return (jnp.where(j < parts, j, jnp.where(j < 2 * parts, parts, parts + 1)), 0, 0)

    def right_map(j):
        return (jnp.where(j < parts, 0, j - parts + 1), 0, 0)

    blocks = jax.ShapeDtypeStruct((n_dp // 2, block_rows, cols), bf16)
    return pl.pallas_call(
        partial(weights_kernel, n_dp, parts),
        grid=(steps,),
        in_specs=[
            pl.BlockSpec((1, half, model_dim), left_map),
            pl.BlockSpec((1, half, model_dim), right_map),
            anywhere,
            anywhere,
            pl.BlockSpec(vec.shape, lambda j: (0, 0)),
        ],
        out_specs=[anywhere, anywhere, anywhere, pl.BlockSpec(vec.shape, lambda j: (0, 0))],
        scratch_shapes=[
            pltpu.VMEM((2, model_dim, model_dim), bf16),
            pltpu.VMEM((steps, model_dim, cols), bf16),
            pltpu.VMEM((2,) + blocks.shape, bf16),
            pltpu.VMEM(vec.shape, f32),
            pltpu.SemaphoreType.DMA((steps,)),
            pltpu.SemaphoreType.DMA((steps,)),
            pltpu.SemaphoreType.DMA,
            pltpu.SemaphoreType.DMA,
            pltpu.SemaphoreType.DMA,
            pltpu.SemaphoreType.DMA,
            pltpu.SemaphoreType.DMA((3,)),
        ],
        out_shape=[
            blocks,
            blocks,
            jax.ShapeDtypeStruct((2 * half, my_cols.shape[1]), bf16),
            jax.ShapeDtypeStruct(vec.shape, f32),
        ],
        compiler_params=pltpu.CompilerParams(
            collective_id=0, has_side_effects=True, vmem_limit_bytes=VMEM_LIMIT
        ),
        cost_estimate=pl.CostEstimate(flops=15_000_000_000, bytes_accessed=20_000_000, transcendentals=0),
    )(left, right, my_cols, their_cols, vec)


def final_kernel(
    n_dp,
    chunks,
    s_keep_any,
    s_got_any,
    raw_any,
    rows_any,
    w_any,
    resid_any,
    vec_ref,
    raw_sums_ref,
    core_send_ref,
    core_recv_ref,
    qkv_ref,
    vec_out_ref,
    vec_core_ref,
    tokens_any,
    t_recv_any,
    s_keep_ref,
    s_got_ref,
    raw_ref,
    rows_ref,
    w_ref,
    resid_ref,
    s_send_ref,
    s_recv_ref,
    s_own_ref,
    s_out_ref,
    s_got_z_ref,
    s_sum_ref,
    q_grad_ref,
    q_both_ref,
    q_first_ref,
    q_send_ref,
    q_recv_ref,
    q_own_ref,
    q_out_ref,
    q_got_z_ref,
    t_send_ref,
    vec_hold_ref,
    vec_recv_ref,
    in_sems,
    s_sems,
    s_z_sems,
    q_first_sems,
    q_sems,
    q_z_sems,
    t_sems,
    core_sems,
    vec_sems,
    out_sem,
):
    me, head = lax.axis_index("dp"), lax.axis_index("head")
    line = n_dp // 4
    depth = line.bit_length() - 1
    z = me // 4
    other = (me, 1 - head)
    low = (flip(me, 0), head)
    high = (flip(me, 1), head)
    around = [(((z + j) % line) * 4 + me % 4, head) for j in range(1, line)]
    first = (flip(me, 0) * (1 - head) + flip(me, 1) * head, head)
    second = (flip(me, 1) * (1 - head) + flip(me, 0) * head, head)
    mine = bit(me, 1) * (1 - head) + bit(me, 0) * head
    half, model_dim = resid_ref.shape
    local_dim = raw_ref.shape[1] // 3
    size = s_keep_ref.shape[1] // chunks
    q_chunks, _, _, q_size, _ = q_both_ref.shape
    q_rows = q_chunks * q_size

    def piece(i):
        return slice(i * size, (i + 1) * size)

    s_loads = [
        pltpu.make_async_copy(s_keep_any, s_keep_ref, in_sems.at[0]),
        pltpu.make_async_copy(s_got_any, s_got_ref, in_sems.at[1]),
    ]
    q_loads = [
        pltpu.make_async_copy(rows_any, rows_ref, in_sems.at[2]),
        pltpu.make_async_copy(raw_any, raw_ref, in_sems.at[3]),
    ]
    t_loads = [
        pltpu.make_async_copy(w_any, w_ref, in_sems.at[4]),
        pltpu.make_async_copy(resid_any, resid_ref, in_sems.at[5]),
    ]
    for load in s_loads:
        load.start()
    greet([low, high, other] + around)

    vec_hold_ref[0] = vec_ref[...]
    here = pl.ds(pl.multiple_of(head * local_dim, LANES), local_dim)
    vec_hold_ref[0, 8:9, here] = raw_sums_ref[:, :local_dim]
    vec_hold_ref[0, 9:10, here] = raw_sums_ref[:, 2 * local_dim :]

    def vec_copy(k):
        to = (low, high)[k] if k < 2 else around[k - 2]
        source = vec_hold_ref.at[min(k, 2)]
        return remote(source, vec_recv_ref.at[k], vec_sems.at[0, k], vec_sems.at[1, k], to)

    vec_copy(0).start()

    def s_copy(i):
        return remote(s_send_ref.at[i], s_recv_ref.at[i], s_sems.at[0, i], s_sems.at[1, i], second)

    def s_total(block, i):
        return s_keep_ref[block, piece(i)].astype(f32) + s_got_ref[block, piece(i)].astype(f32)

    def s_prepare(i):
        def send_block(r, carry):
            s_send_ref[i, r] = s_total(2 * r + 1 - mine, i).astype(bf16)
            return carry

        lax.fori_loop(0, line, send_block, 0)

    for load in s_loads:
        load.wait()
    for load in q_loads:
        load.start()
    for load in t_loads:
        load.start()
    for i in range(chunks):
        s_prepare(i)
        s_copy(i).start()

    for load in q_loads:
        load.wait()

    def q_columns(j, carry):
        at = pl.ds(pl.multiple_of(j * Q_COLUMNS, LANES), Q_COLUMNS)
        grad = lax.dot_general(rows_ref[:, at], raw_ref[...], TN, preferred_element_type=f32)
        q_grad_ref[pl.ds(pl.multiple_of(j * Q_COLUMNS, LANES), Q_COLUMNS), :] = grad.astype(bf16)
        return carry

    lax.fori_loop(0, model_dim // Q_COLUMNS, q_columns, 0)

    def q_place(d, carry):
        send, place = route(d, me, head)
        for j in range(q_chunks):
            at = pl.ds(pl.multiple_of(d * q_rows + j * q_size, 16), q_size)
            q_both_ref[j, send, place] = q_grad_ref[at, :]
        return carry

    lax.fori_loop(0, n_dp, q_place, 0)

    def q_copy(j):
        return remote(q_both_ref.at[j, 1], q_first_ref.at[j], q_first_sems.at[0, j], q_first_sems.at[1, j], first)

    def q_second(j):
        return remote(q_send_ref.at[j], q_recv_ref.at[j], q_sems.at[0, j], q_sems.at[1, j], second)

    def fold_line(own_ref, hold_ref, got_ref, sems):
        def moved(k):
            count = line >> (k + 1)
            at = slice(line - 2 * count, line - count)
            return remote(hold_ref.at[at], got_ref.at[at], sems.at[0, k], sems.at[1, k], (flip(me, k + 2), head))

        def send(k):
            count = line >> (k + 1)
            keep = bit(me, k + 2)
            for q in range(count):
                hold_ref[line - 2 * count + q] = own_ref[2 * q + 1 - keep].astype(bf16)
            moved(k).start()

        def add(k):
            count = line >> (k + 1)
            keep = bit(me, k + 2)
            moved(k).wait()
            for q in range(count):
                own_ref[q] = own_ref[2 * q + keep] + got_ref[line - 2 * count + q].astype(f32)
            if k + 1 < depth:
                send(k + 1)

        return send, add

    s_line = [
        fold_line(s_own_ref.at[i], s_out_ref.at[i], s_got_z_ref.at[i], s_z_sems.at[i]) for i in range(chunks)
    ]
    q_line = [
        fold_line(q_own_ref.at[j], q_out_ref.at[j], q_got_z_ref.at[j], q_z_sems.at[j]) for j in range(q_chunks)
    ]

    def s_enter(i):
        s_copy(i).wait()

        def add_block(r, carry):
            s_own_ref[i, r] = s_total(2 * r + mine, i) + s_recv_ref[i, r].astype(f32)
            return carry

        lax.fori_loop(0, line, add_block, 0)
        s_line[i][0](0)

    def q_total(j, block):
        return q_both_ref[j, 0, block].astype(f32) + q_first_ref[j, block].astype(f32)

    def q_enter(j):
        q_copy(j).wait()

        def send_block(r, carry):
            q_send_ref[j, r] = q_total(j, 2 * r + 1 - mine).astype(bf16)
            return carry

        lax.fori_loop(0, line, send_block, 0)
        q_second(j).start()

        def own_block(r, carry):
            q_own_ref[j, r] = q_total(j, 2 * r + mine)
            return carry

        lax.fori_loop(0, line, own_block, 0)

    def q_turn(j):
        q_second(j).wait()

        def add_block(r, carry):
            q_own_ref[j, r] = q_own_ref[j, r] + q_recv_ref[j, r].astype(f32)
            return carry

        lax.fori_loop(0, line, add_block, 0)
        q_line[j][0](0)

    tile_rows = half // 4

    def token_rows(who, tile):
        start = pl.multiple_of(who * half + tile * tile_rows, tile_rows)
        return lax.dot_general(raw_ref[pl.ds(start, tile_rows), :], w_ref[...], NT, preferred_element_type=f32)

    t_copy = remote(t_send_ref, t_recv_any, t_sems.at[0], t_sems.at[1], other)

    def send_tile(tile, carry):
        at = pl.ds(pl.multiple_of(tile * tile_rows, tile_rows), tile_rows)
        t_send_ref[at, :] = token_rows(1 - head, tile).astype(bf16)
        return carry

    def own_tile(tile, carry):
        at = pl.ds(pl.multiple_of(tile * tile_rows, tile_rows), tile_rows)
        resid_ref[at, :] = resid_ref[at, :] + token_rows(head, tile)
        return carry

    for j in range(q_chunks):
        q_copy(j).start()
    s_enter(0)
    for load in t_loads:
        load.wait()
    lax.fori_loop(0, 4, send_tile, 0)
    t_copy.start()
    if chunks > 1:
        s_enter(1)
        s_line[0][1](0)
    lax.fori_loop(0, 4, own_tile, 0)
    t_out = pltpu.make_async_copy(resid_ref, tokens_any, out_sem)
    t_out.start()
    for i in range(2, chunks):
        s_enter(i)
        s_line[i - 1][1](0)
    vec_copy(0).wait()
    vec_hold_ref[1] = vec_hold_ref[0] + vec_recv_ref[0]
    vec_copy(1).start()
    q_enter(0)
    s_line[chunks - 1][1](0)
    for j in range(1, q_chunks):
        q_enter(j)
    vec_copy(1).wait()
    vec_hold_ref[2] = vec_hold_ref[1] + vec_recv_ref[1]
    for j in range(line - 1):
        vec_copy(2 + j).start()
    for j in range(q_chunks - 1):
        q_turn(j)
    for i in range(chunks):
        for k in range(1, depth):
            s_line[i][1](k)
        s_sum_ref[piece(i), :] = s_own_ref[i, 0]
    pieces = core_pieces(s_sum_ref.shape[0], q_rows)

    def gather(target_ref, who):
        at = 0
        for start, count in pieces:
            here = pl.ds(pl.multiple_of(start + who * count, 8), count)
            target_ref[at : at + count, :] = s_sum_ref[here, :]
            at += count

    gather(core_send_ref.at[1], 1 - head)
    core_copy = remote(core_send_ref.at[1], core_recv_ref, core_sems.at[0], core_sems.at[1], other)
    core_copy.start()
    gather(core_send_ref.at[0], head)
    q_turn(q_chunks - 1)
    for j in range(line - 1):
        vec_copy(2 + j).wait()
    total = vec_hold_ref[2]
    for j in range(line - 1):
        total = total + vec_recv_ref[2 + j]
    vec_out_ref[...] = total
    core_vec = remote(vec_out_ref.at[pl.ds(8, 8)], vec_core_ref, core_sems.at[2], core_sems.at[3], other)
    core_vec.start()
    for k in range(depth):
        for j in range(q_chunks):
            q_line[j][1](k)
    for j in range(q_chunks):
        qkv_ref[j * q_size : (j + 1) * q_size, :] = q_own_ref[j, 0]
    core_vec.wait()
    core_copy.wait()
    t_copy.wait()
    t_out.wait()


def core_pieces(block_rows, rows):
    parts = (block_rows // rows - 1) // 2
    return [(0, parts * rows // 2)] + [(parts * rows + rows * c, rows // 2) for c in range(parts + 1)]


def final(n_dp, s_keep, s_got, raw, group_rows, w_flat, resid, vec, raw_sums):
    line = n_dp // 4
    depth = line.bit_length() - 1
    blocks, block_rows, cols = s_keep.shape
    half, model_dim = resid.shape
    local_dim = raw.shape[1] // 3
    q_rows, q_cols = model_dim // n_dp, 3 * local_dim
    chunks = 3 if block_rows % 48 == 0 else 1
    size = block_rows // chunks
    q_chunks = q_rows // 16
    anywhere = pl.BlockSpec(memory_space=pl.ANY)
    vmem = pl.BlockSpec(memory_space=pltpu.VMEM)

    def low(*dims):
        return pltpu.VMEM(dims, bf16)

    def wide(*dims):
        return pltpu.VMEM(dims, f32)

    def shape(*dims):
        return jax.ShapeDtypeStruct(dims, f32)

    def sems(*dims):
        return pltpu.SemaphoreType.DMA(dims)

    return pl.pallas_call(
        partial(final_kernel, n_dp, chunks),
        in_specs=[anywhere] * 6 + [vmem] * 2,
        out_specs=[vmem] * 5 + [anywhere] * 2,
        scratch_shapes=[
            low(*s_keep.shape),
            low(*s_keep.shape),
            low(*raw.shape),
            low(*group_rows.shape),
            low(*w_flat.shape),
            wide(half, model_dim),
            low(chunks, line, size, cols),
            low(chunks, line, size, cols),
            wide(chunks, line, size, cols),
            low(chunks, line, size, cols),
            low(chunks, line - 1, size, cols),
            wide(block_rows, cols),
            low(model_dim, q_cols),
            low(q_chunks, 2, 2 * line, 16, q_cols),
            low(q_chunks, 2 * line, 16, q_cols),
            low(q_chunks, line, 16, q_cols),
            low(q_chunks, line, 16, q_cols),
            wide(q_chunks, line, 16, q_cols),
            low(q_chunks, line, 16, q_cols),
            low(q_chunks, line - 1, 16, q_cols),
            low(half, model_dim),
            wide(3, *vec.shape),
            wide(1 + line, *vec.shape),
            sems(6),
            sems(2, chunks),
            sems(chunks, 2, depth),
            sems(2, q_chunks),
            sems(2, q_chunks),
            sems(q_chunks, 2, depth),
            sems(2),
            sems(4),
            sems(2, 1 + line),
            pltpu.SemaphoreType.DMA,
        ],
        out_shape=[
            shape(2, block_rows // 2, cols),
            shape(block_rows // 2, cols),
            shape(q_rows, q_cols),
            shape(*vec.shape),
            shape(8, model_dim),
            shape(half, model_dim),
            jax.ShapeDtypeStruct((half, model_dim), bf16),
        ],
        compiler_params=pltpu.CompilerParams(
            collective_id=1, has_side_effects=True, vmem_limit_bytes=VMEM_LIMIT
        ),
        cost_estimate=pl.CostEstimate(flops=12_000_000_000, bytes_accessed=25_000_000, transcendentals=0),
    )(s_keep, s_got, raw, group_rows, w_flat, resid, vec, raw_sums)


def finish_kernel(
    n_dp,
    parts,
    own_ref,
    got_ref,
    kept_ref,
    core_ref,
    qkv_ref,
    vec_ref,
    vec_core_ref,
    tokens_ref,
    grad_qkv_ref,
    down_ref,
    in_ref,
    out_ref,
    qv_ref,
    in_bias_ref,
    term_ref,
    *vector_refs,
):
    tokens_ref[...] = own_ref[...] + got_ref[...].astype(f32)

    @pl.when(pl.program_id(0) == 0)
    def _():
        head = lax.axis_index("head")
        place = 2 * lax.axis_index("dp") + head
        cols = kept_ref.shape[2]
        model_dim = 2 * cols
        rows = out_ref.shape[0]
        width = model_dim // (2 * n_dp)
        starts = [0, parts * rows] + [parts * rows + rows * (c + 1) for c in range(parts + 1)]
        for who, source in ((head, kept_ref.at[0]), (1 - head, core_ref)):
            start = who * cols
            here = pl.ds(pl.multiple_of(start, LANES), cols)
            down_ref[:, here] = source[starts[0] : starts[1], :]
            for c in range(parts):
                shifted = pl.ds(pl.multiple_of(2 * cols * c + start, LANES), cols)
                in_ref[:, shifted] = source[starts[1 + c] : starts[2 + c], :]
            out_ref[:, here] = source[starts[1 + parts] : starts[2 + parts], :]
        for c in range(3):
            grad_qkv_ref[:, c, :] = qkv_ref[:, c * cols : (c + 1) * cols]
        shift = lax.rem(model_dim - place * width, model_dim)
        turned = pltpu.roll(vec_ref[0:8], shift, 1)
        for j, ref in enumerate(vector_refs):
            ref[...] = turned[j : j + 1, :width]
        term_ref[...] = vec_ref[7:8, :1]
        turned = pltpu.roll(vec_ref[8:16] + vec_core_ref[...], shift, 1)
        qv_ref[...] = turned[:, :LANES].T[:width, :2]
        in_width = parts * model_dim // (2 * n_dp)
        per_row = model_dim // in_width
        row = vec_ref[pl.ds(10 + place // per_row, 1), :]
        row = jnp.broadcast_to(row, (8, model_dim))
        turned = pltpu.roll(row, lax.rem(model_dim - (place % per_row) * in_width, model_dim), 1)
        in_bias_ref[...] = turned[0:1, :in_width]


def finish(n_dp, parts, kept, core, qkv, vec, vec_core, own, got):
    half, model_dim = own.shape
    q_rows = qkv.shape[0]
    width = model_dim // (2 * n_dp)
    rows = min(256, half)
    tile = pl.BlockSpec((rows, model_dim), lambda i: (i, 0))

    def whole(dims):
        return pl.BlockSpec(dims, lambda i: (0,) * len(dims))

    out = [
        (q_rows, 3, model_dim // 2),
        (parts * width, model_dim),
        (width, parts * model_dim),
        (width, model_dim),
        (width, 2),
        (1, parts * width),
        (1, 1),
    ] + [(1, width)] * 7
    return pl.pallas_call(
        partial(finish_kernel, n_dp, parts),
        grid=(half // rows,),
        in_specs=[tile, tile] + [whole(x.shape) for x in (kept, core, qkv, vec, vec_core)],
        out_specs=[tile] + [whole(dims) for dims in out],
        out_shape=[jax.ShapeDtypeStruct((half, model_dim), f32)] + [jax.ShapeDtypeStruct(dims, f32) for dims in out],
        compiler_params=pltpu.CompilerParams(vmem_limit_bytes=VMEM_LIMIT),
        cost_estimate=pl.CostEstimate(flops=1_000_000, bytes_accessed=10_000_000, transcendentals=0),
    )(own, got, kept, core, qkv, vec, vec_core)


def take(array, index, axis=0):
    return lax.dynamic_index_in_dim(array, index, axis, keepdims=False)


class Links:
    def __init__(self, n_dp):
        self.n_dp = n_dp
        self.bits = n_dp.bit_length() - 1
        self.dp = lax.axis_index("dp")
        self.head = lax.axis_index("head")

    def bit(self, which):
        return (self.dp >> which) & 1

    def permute(self, array, partner):
        pairs = []
        for d in range(self.n_dp):
            for h in range(2):
                to_d, to_h = partner(d, h)
                pairs.append((2 * d + h, 2 * to_d + to_h))
        return lax.ppermute(array, AXES, pairs)

    def swap_head(self, array):
        return self.permute(array, lambda d, h: (d, 1 - h))

    def swap_bit(self, array, which):
        return self.permute(array, lambda d, h: (d ^ (1 << which), h))

    def scatter_heads(self, blocks):
        got = self.swap_head(take(blocks, 1 - self.head, 1))
        return (take(blocks, self.head, 1).astype(f32) + got.astype(f32)).astype(bf16)

    def scatter_dp(self, blocks):
        tail = blocks.shape[1:]
        b0, b1 = self.bit(0), self.bit(1)
        first = self.head == 0
        blocks = blocks.reshape((self.n_dp // 4, 4) + tail)

        def two(one, other):
            i = jnp.where(first, one, 2 * other)
            j = jnp.where(first, 2 + one, 2 * other + 1)
            return jnp.stack([take(blocks, i, 1), take(blocks, j, 1)], axis=1)

        got = self.permute(two(1 - b0, 1 - b1), lambda d, h: (d ^ (1 if h == 0 else 2), h))
        blocks = (two(b0, b1).astype(f32) + got.astype(f32)).astype(bf16)
        mine = jnp.where(first, b1, b0)
        got = self.permute(take(blocks, 1 - mine, 1), lambda d, h: (d ^ (2 if h == 0 else 1), h))
        blocks = take(blocks, mine, 1).astype(f32) + got.astype(f32)
        for which in range(2, self.bits):
            blocks = blocks.reshape((-1, 2) + tail)
            mine = self.bit(which)
            got = self.swap_bit(take(blocks, 1 - mine, 1).astype(bf16), which)
            blocks = take(blocks, mine, 1) + got.astype(f32)
        return blocks.reshape(tail)

    def total(self, array):
        array = array + self.swap_head(array)
        for which in range(self.bits):
            array = array + self.swap_bit(array, which)
        return array


def shards(
    n_dp,
    tokens,
    lengths,
    w_qkv,
    bias_qv,
    w_out,
    bias_out,
    ln1_gain,
    ln1_bias,
    w_in,
    bias_in,
    w_down,
    bias_down,
    ln2_gain,
    ln2_bias,
    term_w,
    term_bias,
    grad_hidden,
    grad_term,
):
    links = Links(n_dp)
    head = links.head
    half, model_dim = tokens.shape
    row_len = 2 * half
    local_dim = w_qkv.shape[2]
    ffn_dim = w_in.shape[1]
    query_scale = HEAD_DIM ** (-0.5)

    boundary = jnp.cumsum(lengths[0])
    places = jnp.arange(row_len, dtype=jnp.int32)
    segment = jnp.sum((places[:, None] >= boundary[None, :]).astype(jnp.int32), axis=-1)
    seg_col = jnp.broadcast_to(segment[:, None], (row_len, LANES))
    seg_row = jnp.broadcast_to(segment[None, :], (8, row_len))

    def both(mine, theirs, axis):
        return jnp.where(
            head == 0,
            jnp.concatenate([mine, theirs], axis=axis),
            jnp.concatenate([theirs, mine], axis=axis),
        )

    group_rows = both(tokens, links.swap_head(tokens), 0)
    w_flat = w_qkv.reshape(model_dim, 3 * local_dim)
    projected = jnp.dot(group_rows, w_flat, preferred_element_type=f32)
    queries = ((projected[:, :local_dim] + bias_qv[:, 0]) * query_scale).astype(bf16)
    key_rows = projected[:, local_dim : 2 * local_dim].astype(bf16)
    value_rows = (projected[:, 2 * local_dim :] + bias_qv[:, 1]).astype(bf16)
    attended, logs = attend(lengths, queries, key_rows, value_rows, seg_col, seg_row)

    def my_half(rows):
        return lax.dynamic_slice_in_dim(rows, head * half, half, 0)

    def their_half(rows):
        return lax.dynamic_slice_in_dim(rows, (1 - head) * half, half, 0)

    vec = jnp.stack([bias_out, ln1_gain, ln1_bias, bias_down, ln2_gain, ln2_bias, term_w, jnp.zeros_like(term_w)])
    hidden_out, term_weight, left, right, resid_one_grad, my_cols, their_cols, sums, bias_in_local = middle(
        my_half(attended),
        links.swap_head(their_half(attended)),
        tokens,
        grad_hidden,
        grad_term[:, None],
        w_out,
        w_in,
        w_down,
        vec,
        bias_in[None, :],
        term_bias[None, :],
    )
    parts = ffn_dim // model_dim
    vec = jnp.concatenate([sums, jnp.zeros((2, model_dim), f32), bias_in_local.reshape(parts, model_dim)])
    vec = jnp.pad(vec, ((0, 16 - vec.shape[0]), (0, 0)))
    in_kernels = (model_dim // n_dp) % 16 == 0 and n_dp % 8 == 0

    def back(grads):
        return attend_back(lengths, queries, key_rows, value_rows, grads, logs, seg_col, seg_row)

    if in_kernels:
        s_keep, s_send, head_grad, vec = weights(n_dp, left, right, my_cols, their_cols, vec)
        s_got = links.permute(s_send, lambda d, h: (d ^ (1 if h == 0 else 2), h))
        raw, raw_sums = back(head_grad)
        kept, core, qkv, vec, vec_core, own, got = final(
            n_dp, s_keep, s_got, raw, group_rows, w_flat, resid_one_grad, vec, raw_sums
        )
        (grad_tokens, grad_qkv, grad_down, grad_in, grad_out, bias_qv_mine, bias_in_mine, term_total, *vectors) = finish(
            n_dp, parts, kept, core, qkv, vec, vec_core, own, got
        )
        bias_in_mine = bias_in_mine.reshape(-1)
        term_total = term_total.reshape(1)
        mine = [v.reshape(-1) for v in vectors]
    else:
        raw, raw_sums = back(both(my_cols, links.swap_head(their_cols), 0))

        def product(i, j):
            return lax.dot_general(left[i], right[j], TN, preferred_element_type=f32).astype(bf16)

        def reduced(partial_sum):
            rows, cols = partial_sum.shape
            return links.scatter_dp(links.scatter_heads(partial_sum.reshape(n_dp, 2, rows // (2 * n_dp), cols)))

        grad_down = reduced(jnp.concatenate([product(i, 0) for i in range(parts)]))
        grad_in = reduced(jnp.concatenate([product(parts, 1 + i) for i in range(parts)], axis=1))
        grad_out = reduced(product(parts + 1, parts + 1))
        grad = lax.dot_general(raw, w_flat, NT, preferred_element_type=f32)
        received = links.swap_head(their_half(grad).astype(bf16))
        grad_tokens = resid_one_grad + my_half(grad) + received.astype(f32)
        qkv_local = lax.dot_general(group_rows, raw, TN, preferred_element_type=f32).astype(bf16)
        grad_qkv = links.scatter_dp(qkv_local.reshape(n_dp, model_dim // n_dp, 3 * local_dim))
        value_sums = lax.dynamic_update_slice(
            jnp.zeros((2, 2 * local_dim), f32),
            jnp.concatenate([raw_sums[:, :local_dim], raw_sums[:, 2 * local_dim :]]),
            (jnp.int32(0), head * local_dim),
        )
        vectors = links.total(lax.dynamic_update_slice(vec, value_sums, (8, 0)))
        grad_qkv = grad_qkv.reshape(model_dim // n_dp, 3, local_dim)
        place = 2 * links.dp + head
        width = model_dim // (2 * n_dp)
        mine = lax.dynamic_slice_in_dim(vectors, place * width, width, 1)
        in_width = ffn_dim // (2 * n_dp)
        in_row = vectors[10 : 10 + parts].reshape(-1)
        bias_in_mine = lax.dynamic_slice_in_dim(in_row, place * in_width, in_width, 0)
        bias_qv_mine = mine[8:10].T
        term_total = vectors[7, :1]

    return (
        hidden_out,
        term_weight[:, 0],
        grad_tokens,
        grad_qkv,
        bias_qv_mine,
        grad_out,
        mine[0],
        mine[1],
        mine[2],
        grad_in,
        bias_in_mine,
        grad_down,
        mine[3],
        mine[4],
        mine[5],
        mine[6],
        term_total,
    )


def solution(mesh):
    rows = P(AXES, None)
    return jax.shard_map(
        partial(shards, mesh.shape["dp"]),
        mesh=mesh,
        in_specs=(rows, P("dp", None), P(None, None, "head"), P("head", None))
        + (P(),) * 12
        + (rows, P(AXES)),
        out_specs=(
            rows,
            P(AXES),
            rows,
            P("dp", None, "head"),
            rows,
            rows,
            P(AXES),
            P(AXES),
            P(AXES),
            rows,
            P(AXES),
            rows,
            P(AXES),
            P(AXES),
            P(AXES),
            P(AXES),
            P(),
        ),
        check_vma=False,
    )
```

```python
from functools import partial

import jax
import jax.numpy as jnp
from jax import lax
from jax.experimental import pallas as pl
from jax.experimental.pallas import tpu as pltpu
from jax.sharding import PartitionSpec as P

HEAD_DIM = 64
LANES = 128
VMEM_LIMIT = 60 * 2**20
Q_ROWS = 256
PIECE = 32
Q_COLUMNS = 128
WIDTHS = (2, 3, 4, 5, 6, 8, 10)
AXES = ("dp", "head")

f32 = jnp.float32
bf16 = jnp.bfloat16
norm_eps = 1e-06
NT = (((1,), (1,)), ((), ()))
TN = (((0,), (0,)), ((), ()))


def key_range(lengths_ref, first, rows, row_len):
    start = jnp.int32(0)
    low = jnp.int32(0)
    high = jnp.int32(row_len)
    for j in range(lengths_ref.shape[1]):
        end = start + lengths_ref[0, j]
        low = jnp.where(start <= first, start, low)
        high = jnp.where(end >= first + rows, jnp.minimum(high, end), high)
        start = end
    low_block = low // LANES
    count = (high + LANES - 1) // LANES - low_block
    return low_block, count


def by_width(lengths_ref, first, rows, row_len, body):
    blocks = row_len // LANES
    low_block, count = key_range(lengths_ref, first, rows, row_len)
    widths = sorted({min(w, blocks) for w in WIDTHS})
    below = 0
    for width in widths:

        @pl.when((count > below) & (count <= width))
        def _(width=width):
            begin = jnp.minimum(low_block, blocks - width)
            body(pl.multiple_of(begin * LANES, LANES), width * LANES)

        below = width


def query_block(step, steps, head):
    return lax.rem(step + (1 - head) * (steps // 2), steps)


def attend_kernel(
    lengths_ref,
    head_ref,
    q_ref,
    k_ref,
    v_ref,
    segc_ref,
    segr_ref,
    theirs_ref,
    mine_ref,
    log_ref,
    mask_ref,
    cols_ref,
    s_ref,
    p_ref,
    o_ref,
):
    rows, local_dim = q_ref.shape
    row_len = k_ref.shape[0]
    step, steps = pl.program_id(0), pl.num_programs(0)
    first = query_block(step, steps, head_ref[0]) * rows
    lane = lax.broadcasted_iota(jnp.int32, (rows, LANES), 1)

    def body(begin, width):
        same = segc_ref[:, 0:1] == segr_ref[0:1, pl.ds(begin, width)]
        mask_ref[:, :width] = jnp.where(same, 0.0, -1e30)

        heads = local_dim // HEAD_DIM

        def score(i):
            cols = slice(i // 2 * LANES, i // 2 * LANES + LANES)
            q_pair = q_ref[:, cols]
            q_one = jnp.where((lane // HEAD_DIM) == i % 2, q_pair, jnp.zeros_like(q_pair))
            k_pair = k_ref[pl.ds(begin, width), cols]
            s_ref[i % 2, :, :width] = lax.dot_general(q_one, k_pair, NT, preferred_element_type=f32)

        def soft(i):
            for r in range(0, rows, PIECE):
                part = slice(r, r + PIECE)
                scores = s_ref[i % 2, part, :width] + mask_ref[part, :width]
                row_max = jnp.max(scores, axis=1, keepdims=True)
                powers = jnp.exp(scores - row_max)
                total = jnp.sum(powers, axis=1, keepdims=True)
                p_ref[i % 2, part, :width] = (powers * (1.0 / total)).astype(bf16)
                log_total = row_max + jnp.log(total)
                cols_ref[part] = jnp.where(lane[part] == i, log_total, cols_ref[part])

        def value(i):
            cols = slice(i // 2 * LANES, i // 2 * LANES + LANES)
            return jnp.dot(p_ref[i % 2, :, :width], v_ref[pl.ds(begin, width), cols], preferred_element_type=f32)

        score(0)
        held = None
        for i in range(heads):
            if i + 1 < heads:
                score(i + 1)
            soft(i)
            out = value(i)
            if i % 2 == 0:
                held = out
            else:
                cols = slice(i // 2 * LANES, i // 2 * LANES + LANES)
                o_ref[:, cols] = jnp.where(lane < HEAD_DIM, held, out).astype(bf16)

    by_width(lengths_ref, first, rows, row_len, body)
    log_ref[...] = cols_ref[...].T[: log_ref.shape[0]]

    @pl.when(step < steps // 2)
    def _():
        theirs_ref[...] = o_ref[...]

    @pl.when(step >= steps // 2)
    def _():
        mine_ref[...] = o_ref[...]


def attend(lengths, head, queries, key_rows, value_rows, seg_col, seg_row):
    row_len, local_dim = queries.shape
    rows = min(Q_ROWS, row_len // 2)
    steps = row_len // rows
    whole = pl.BlockSpec((row_len, local_dim), lambda i, n, h: (0, 0))
    return pl.pallas_call(
        attend_kernel,
        grid_spec=pltpu.PrefetchScalarGridSpec(
            num_scalar_prefetch=2,
            grid=(steps,),
            in_specs=[
                pl.BlockSpec((rows, local_dim), lambda i, n, h: (query_block(i, steps, h[0]), 0)),
                whole,
                whole,
                pl.BlockSpec((rows, LANES), lambda i, n, h: (query_block(i, steps, h[0]), 0)),
                pl.BlockSpec((8, row_len), lambda i, n, h: (0, 0)),
            ],
            out_specs=[
                pl.BlockSpec((rows, local_dim), lambda i, n, h: (jnp.minimum(i, steps // 2 - 1), 0)),
                pl.BlockSpec((rows, local_dim), lambda i, n, h: (jnp.maximum(i - steps // 2, 0), 0)),
                pl.BlockSpec((8, rows), lambda i, n, h: (0, query_block(i, steps, h[0]))),
            ],
            scratch_shapes=[
                pltpu.VMEM((rows, max(WIDTHS) * LANES), f32),
                pltpu.VMEM((rows, LANES), f32),
                pltpu.VMEM((2, rows, max(WIDTHS) * LANES), f32),
                pltpu.VMEM((2, rows, max(WIDTHS) * LANES), bf16),
                pltpu.VMEM((rows, local_dim), bf16),
            ],
        ),
        out_shape=[
            jax.ShapeDtypeStruct((row_len // 2, local_dim), bf16),
            jax.ShapeDtypeStruct((row_len // 2, local_dim), bf16),
            jax.ShapeDtypeStruct((8, row_len), f32),
        ],
        compiler_params=pltpu.CompilerParams(vmem_limit_bytes=VMEM_LIMIT),
        cost_estimate=pl.CostEstimate(flops=20_000_000_000, bytes_accessed=8_000_000, transcendentals=0),
    )(lengths, head[None], queries, key_rows, value_rows, seg_col, seg_row)


def attend_back_kernel(
    lengths_ref,
    q_ref,
    k_ref,
    v_ref,
    g_ref,
    log_ref,
    segc_ref,
    segr_ref,
    raw_ref,
    sums_ref,
    mask_ref,
    dk_ref,
    dv_ref,
    s_ref,
    d_ref,
    p_ref,
    e_ref,
    ones_ref,
):
    rows, local_dim = q_ref.shape
    row_len = k_ref.shape[0]
    step = pl.program_id(0)
    first = step * rows
    lane = lax.broadcasted_iota(jnp.int32, (rows, LANES), 1)

    @pl.when(step == 0)
    def _():
        dk_ref[...] = jnp.zeros_like(dk_ref)
        dv_ref[...] = jnp.zeros_like(dv_ref)

    def body(begin, width):
        keys = pl.ds(begin, width)
        same = segc_ref[keys, 0:1] == segr_ref[0:1, :]
        mask_ref[:width, :] = jnp.where(same, 0.0, -1e30)

        def pair_step(pair, carry):
            cols = pl.ds(pl.multiple_of(pair * LANES, LANES), LANES)

            def products(i):
                mine = (lane // HEAD_DIM) == i
                here = slice(i * rows, i * rows + rows)
                q_pair, g_pair = q_ref[:, cols], g_ref[:, cols]
                q_one = jnp.where(mine, q_pair, jnp.zeros_like(q_pair))
                g_one = jnp.where(mine, g_pair, jnp.zeros_like(g_pair))
                ones_ref[0, here] = q_one
                ones_ref[1, here] = g_one
                s_ref[i, :width] = lax.dot_general(k_ref[keys, cols], q_one, NT, preferred_element_type=f32)
                d_ref[i, :width] = lax.dot_general(v_ref[keys, cols], g_one, NT, preferred_element_type=f32)

            def soft(i):
                here = slice(i * rows, i * rows + rows)
                log_row = log_ref[pl.ds(2 * pair + i, 1), :]
                inner = jnp.zeros((8, rows), f32)
                for r in range(0, width, PIECE):
                    part = slice(r, r + PIECE)
                    probs = jnp.exp(s_ref[i, part] + mask_ref[part] - log_row)
                    s_ref[i, part] = probs
                    p_ref[part, here] = probs.astype(bf16)
                    inner = inner + jnp.sum((probs * d_ref[i, part]).reshape(PIECE // 8, 8, rows), axis=0)
                inner = jnp.sum(inner, axis=0, keepdims=True)
                for r in range(0, width, PIECE):
                    part = slice(r, r + PIECE)
                    e_ref[part, here] = (s_ref[i, part] * (d_ref[i, part] - inner)).astype(bf16)

            products(0)
            products(1)
            soft(0)
            soft(1)
            dv_ref[keys, cols] += jnp.dot(p_ref[:width], ones_ref[1], preferred_element_type=f32)
            dk_ref[keys, cols] += jnp.dot(e_ref[:width], ones_ref[0], preferred_element_type=f32)
            dq = lax.dot_general(e_ref[:width], k_ref[keys, cols], TN, preferred_element_type=f32)
            dq_low = jnp.where(lane < HEAD_DIM, dq[:rows], dq[rows:]).astype(bf16)
            raw_ref[pl.ds(pl.multiple_of(first, rows), rows), cols] = dq_low * jnp.asarray(HEAD_DIM**-0.5, bf16)
            return carry

        lax.fori_loop(0, local_dim // LANES, pair_step, 0)

    by_width(lengths_ref, first, rows, row_len, body)

    @pl.when(step == pl.num_programs(0) - 1)
    def _():
        raw_ref[:, local_dim : 2 * local_dim] = dk_ref[...].astype(bf16)
        raw_ref[:, 2 * local_dim :] = dv_ref[...].astype(bf16)
        sums_ref[...] = jnp.sum(raw_ref[...].astype(f32), axis=0, keepdims=True)


def attend_back(lengths, queries, key_rows, value_rows, grads, logs, seg_col, seg_row):
    row_len, local_dim = queries.shape
    rows = min(Q_ROWS, row_len)
    whole = pl.BlockSpec((row_len, local_dim), lambda i, n: (0, 0))
    block = pl.BlockSpec((rows, local_dim), lambda i, n: (i, 0))
    return pl.pallas_call(
        attend_back_kernel,
        grid_spec=pltpu.PrefetchScalarGridSpec(
            num_scalar_prefetch=1,
            grid=(row_len // rows,),
            in_specs=[
                block,
                whole,
                whole,
                block,
                pl.BlockSpec((8, rows), lambda i, n: (0, i)),
                pl.BlockSpec((row_len, LANES), lambda i, n: (0, 0)),
                pl.BlockSpec((8, rows), lambda i, n: (0, i)),
            ],
            out_specs=[
                pl.BlockSpec((row_len, 3 * local_dim), lambda i, n: (0, 0)),
                pl.BlockSpec((1, 3 * local_dim), lambda i, n: (0, 0)),
            ],
            scratch_shapes=[
                pltpu.VMEM((max(WIDTHS) * LANES, rows), f32),
                pltpu.VMEM((row_len, local_dim), f32),
                pltpu.VMEM((row_len, local_dim), f32),
                pltpu.VMEM((2, max(WIDTHS) * LANES, rows), f32),
                pltpu.VMEM((2, max(WIDTHS) * LANES, rows), f32),
                pltpu.VMEM((max(WIDTHS) * LANES, 2 * rows), bf16),
                pltpu.VMEM((max(WIDTHS) * LANES, 2 * rows), bf16),
                pltpu.VMEM((2, 2 * rows, LANES), bf16),
            ],
        ),
        out_shape=[
            jax.ShapeDtypeStruct((row_len, 3 * local_dim), bf16),
            jax.ShapeDtypeStruct((1, 3 * local_dim), f32),
        ],
        compiler_params=pltpu.CompilerParams(vmem_limit_bytes=56 * 2**20),
        cost_estimate=pl.CostEstimate(flops=40_000_000_000, bytes_accessed=12_000_000, transcendentals=0),
    )(lengths, queries, key_rows, value_rows, grads, logs, seg_col, seg_row)


TILE = 256


def gelu_both(x):
    cdf = 0.5 + 0.5 * lax.erf(x * 0.7071067811865476)
    density = jnp.exp(-0.5 * x * x) * 0.3989422804014327
    return x * cdf, cdf + x * density


def normalize(resid):
    center = resid - jnp.mean(resid, axis=-1, keepdims=True)
    scale = lax.rsqrt(jnp.mean(center * center, axis=-1, keepdims=True) + norm_eps)
    return center * scale, scale


def normalize_back(grad, normed, scale):
    shift = jnp.mean(grad, axis=-1, keepdims=True)
    slope = jnp.mean(grad * normed, axis=-1, keepdims=True)
    return scale * (grad - shift - normed * slope)


def fold(x):
    return jnp.sum(x.astype(f32).reshape(x.shape[0] // 8, 8, x.shape[1]), axis=0)


def middle_kernel(
    mine_ref,
    theirs_ref,
    tokens_ref,
    hid_ref,
    term_ref,
    w_out_ref,
    w_in_ref,
    w_down_ref,
    vec_ref,
    bias_in_ref,
    term_bias_ref,
    hidden_ref,
    weight_ref,
    left_ref,
    right_ref,
    resid_ref,
    my_grad_ref,
    their_grad_ref,
    sums_ref,
    slope_ref,
    wide_ref,
    x_ref,
    normal_ref,
    scale_ref,
    fold_ref,
    in_fold_ref,
    term_cols_ref,
    term_in_ref,
):
    head = lax.axis_index("head")
    local_dim = mine_ref.shape[1]
    model_dim = w_out_ref.shape[0]
    parts = w_in_ref.shape[1] // model_dim
    rows = tokens_ref.shape[0]
    pieces = [slice(r, r + PIECE) for r in range(0, rows, PIECE)]
    bias_out, ln1_gain, ln1_bias = vec_ref[0:1], vec_ref[1:2], vec_ref[2:3]
    bias_down, ln2_gain, ln2_bias, term_w = vec_ref[3:4], vec_ref[4:5], vec_ref[5:6], vec_ref[6:7]

    @pl.when(pl.program_id(0) == 0)
    def _():
        fold_ref[...] = jnp.zeros_like(fold_ref)
        in_fold_ref[...] = jnp.zeros_like(in_fold_ref)

    term_in_ref[...] = jnp.broadcast_to(term_ref[...], (LANES, rows)).T
    left_ref[parts + 1, :, pl.ds(pl.multiple_of(head * local_dim, LANES), local_dim)] = mine_ref[...]
    left_ref[parts + 1, :, pl.ds(pl.multiple_of((1 - head) * local_dim, LANES), local_dim)] = theirs_ref[...]
    x_ref[...] = jnp.dot(left_ref[parts + 1], w_out_ref[...], preferred_element_type=f32)
    for r in pieces:
        normal, scale = normalize(tokens_ref[r].astype(f32) + (x_ref[r] + bias_out))
        normed = normal * ln1_gain + ln1_bias
        normal_ref[r] = normal
        scale_ref[r] = scale
        left_ref[parts, r] = normed.astype(bf16)
        x_ref[r] = normed + bias_down

    def columns(c):
        return slice(c * model_dim, (c + 1) * model_dim)

    def rise(c):
        wide_ref[c % 2] = jnp.dot(left_ref[parts], w_in_ref[:, columns(c)], preferred_element_type=f32)

    rise(0)
    for c in range(parts):
        if c + 1 < parts:
            rise(c + 1)
        for r in pieces:
            value, slope = gelu_both(wide_ref[c % 2, r] + bias_in_ref[:, columns(c)])
            left_ref[c, r] = value.astype(bf16)
            slope_ref[r, columns(c)] = slope
        x_ref[...] += jnp.dot(left_ref[c], w_down_ref[columns(c), :], preferred_element_type=f32)

    for r in pieces:
        normal, scale = normalize(x_ref[r])
        normed = normal * ln2_gain + ln2_bias
        hidden_ref[r] = normed.astype(bf16)
        logit = jnp.sum(normed * term_w, axis=-1, keepdims=True) + term_bias_ref[0:1, 0:1]
        small = jnp.exp(-jnp.abs(logit))
        term_cols_ref[r] = jnp.broadcast_to(jnp.maximum(logit, 0.0) + jnp.log1p(small), (PIECE, LANES))
        logit_grad = term_in_ref[r, 0:1] * (jnp.where(logit >= 0.0, 1.0, small) / (1.0 + small))
        two_grad = hid_ref[r] + logit_grad * term_w
        resid_two = normalize_back(two_grad * ln2_gain, normal, scale)
        low = resid_two.astype(bf16)
        right_ref[0, r] = low
        x_ref[r] = resid_two
        fold_ref[3] += fold(low)
        fold_ref[4] += fold(two_grad * normal)
        fold_ref[5] += fold(two_grad)
        fold_ref[6] += fold(logit_grad * normed)
        fold_ref[7] += fold(jnp.broadcast_to(logit_grad, normal.shape))

    weight_ref[...] = term_cols_ref[...].T[0:1]

    def fall(c):
        wide_ref[c % 2] = lax.dot_general(right_ref[0], w_down_ref[columns(c), :], NT, preferred_element_type=f32)

    fall(0)
    for c in range(parts):
        if c + 1 < parts:
            fall(c + 1)
        for r in pieces:
            low = (wide_ref[c % 2, r] * slope_ref[r, columns(c)]).astype(bf16)
            right_ref[1 + c, r] = low
            in_fold_ref[:, columns(c)] += fold(low)
        x_ref[...] += lax.dot_general(right_ref[1 + c], w_in_ref[:, columns(c)], NT, preferred_element_type=f32)

    for r in pieces:
        one_grad = x_ref[r]
        normal = normal_ref[r]
        resid_one = normalize_back(one_grad * ln1_gain, normal, scale_ref[r])
        resid_ref[r] = resid_one
        low = resid_one.astype(bf16)
        right_ref[parts + 1, r] = low
        fold_ref[0] += fold(low)
        fold_ref[1] += fold(one_grad * normal)
        fold_ref[2] += fold(one_grad)
    grads = lax.dot_general(right_ref[parts + 1], w_out_ref[...], NT, preferred_element_type=f32).astype(bf16)

    @pl.when(head == 0)
    def _():
        my_grad_ref[...] = grads[:, :local_dim]
        their_grad_ref[...] = grads[:, local_dim:]

    @pl.when(head == 1)
    def _():
        my_grad_ref[...] = grads[:, local_dim:]
        their_grad_ref[...] = grads[:, :local_dim]

    @pl.when(pl.program_id(0) == pl.num_programs(0) - 1)
    def _():
        sums_ref[...] = jnp.zeros_like(sums_ref)
        sums_ref[0:8] = jnp.sum(fold_ref[...], axis=1)
        for c in range(parts):
            sums_ref[10 + c : 11 + c] = jnp.sum(in_fold_ref[:, columns(c)], axis=0, keepdims=True)


def middle(mine, theirs, tokens, grad_hidden, grad_term, w_out, w_in, w_down, vec, bias_in, term_bias):
    half, model_dim = tokens.shape
    local_dim = mine.shape[1]
    ffn_dim = w_in.shape[1]
    rows = min(TILE, half)

    def tile(cols):
        return pl.BlockSpec((rows, cols), lambda i: (i, 0))

    def whole(*shape):
        return pl.BlockSpec(shape, lambda i: (0, 0), pipeline_mode=pl.Buffered(1))

    stacked = pl.BlockSpec((ffn_dim // model_dim + 2, rows, model_dim), lambda i: (0, i, 0))
    stack = jax.ShapeDtypeStruct((ffn_dim // model_dim + 2, half, model_dim), bf16)

    def full(cols, kind):
        return jax.ShapeDtypeStruct((half, cols), kind)

    return pl.pallas_call(
        middle_kernel,
        grid=(half // rows,),
        in_specs=[
            tile(local_dim),
            tile(local_dim),
            tile(model_dim),
            tile(model_dim),
            pl.BlockSpec((1, rows), lambda i: (0, i)),
            whole(model_dim, model_dim),
            whole(model_dim, ffn_dim),
            whole(ffn_dim, model_dim),
            whole(8, model_dim),
            whole(1, ffn_dim),
            whole(1, 1),
        ],
        out_specs=[
            tile(model_dim),
            pl.BlockSpec((1, rows), lambda i: (0, i)),
            stacked,
            stacked,
            tile(model_dim),
            tile(local_dim),
            tile(local_dim),
            pl.BlockSpec((16, model_dim), lambda i: (0, 0)),
        ],
        scratch_shapes=[
            pltpu.VMEM((rows, ffn_dim), f32),
            pltpu.VMEM((2, rows, model_dim), f32),
            pltpu.VMEM((rows, model_dim), f32),
            pltpu.VMEM((rows, model_dim), f32),
            pltpu.VMEM((rows, 1), f32),
            pltpu.VMEM((8, 8, model_dim), f32),
            pltpu.VMEM((8, ffn_dim), f32),
            pltpu.VMEM((rows, LANES), f32),
            pltpu.VMEM((rows, LANES), f32),
        ],
        out_shape=[
            full(model_dim, bf16),
            jax.ShapeDtypeStruct((1, half), f32),
            stack,
            stack,
            full(model_dim, f32),
            full(local_dim, bf16),
            full(local_dim, bf16),
            jax.ShapeDtypeStruct((16, model_dim), f32),
        ],
        compiler_params=pltpu.CompilerParams(vmem_limit_bytes=VMEM_LIMIT),
        cost_estimate=pl.CostEstimate(flops=40_000_000_000, bytes_accessed=50_000_000, transcendentals=0),
    )(mine, theirs, tokens, grad_hidden, grad_term, w_out, w_in, w_down, vec, bias_in, term_bias)


def bit(place, which):
    return (place // 2**which) % 2


def flip(place, which):
    return place + (1 - 2 * bit(place, which)) * 2**which


def route(target, me, head):
    low, high = bit(target, 0), bit(target, 1)
    send = (1 - head) * ((low + bit(me, 0)) % 2) + head * ((high + bit(me, 1)) % 2)
    return send, 2 * (target // 4) + (1 - head) * high + head * low


def greet(partners):
    barrier = pltpu.get_barrier_semaphore()
    for partner in partners:
        pl.semaphore_signal(barrier, inc=1, device_id=partner, device_id_type=pl.DeviceIdType.MESH)
    pl.semaphore_wait(barrier, len(partners))


def remote(source, target, send_sem, recv_sem, partner):
    return pltpu.make_async_remote_copy(
        src_ref=source,
        dst_ref=target,
        send_sem=send_sem,
        recv_sem=recv_sem,
        device_id=partner,
        device_id_type=pl.DeviceIdType.MESH,
    )


def project_kernel(
    tokens_any,
    w_ref,
    bias_ref,
    rows_any,
    q_any,
    k_any,
    v_any,
    rows_ref,
    q_ref,
    k_ref,
    v_ref,
    load_sem,
    swap_sems,
    out_sems,
):
    head = lax.axis_index("head")
    other = (lax.axis_index("dp"), 1 - head)
    half = tokens_any.shape[0]
    tile_rows = min(256, half)

    def side(who):
        return pl.ds(pl.multiple_of(who * half, half), half)

    load = pltpu.make_async_copy(tokens_any, rows_ref.at[side(head)], load_sem)
    load.start()
    greet([other])
    swap = remote(tokens_any, rows_ref.at[side(head)], swap_sems.at[0], swap_sems.at[1], other)
    swap.start()

    def work(who):
        def step(tile, carry):
            at = pl.ds(pl.multiple_of(who * half + tile * tile_rows, tile_rows), tile_rows)
            x = rows_ref[at, :]
            queries = jnp.dot(x, w_ref[0], preferred_element_type=f32)
            q_ref[at, :] = ((queries + bias_ref[0:1]) * HEAD_DIM ** (-0.5)).astype(bf16)
            k_ref[at, :] = jnp.dot(x, w_ref[1], preferred_element_type=f32).astype(bf16)
            v_ref[at, :] = (jnp.dot(x, w_ref[2], preferred_element_type=f32) + bias_ref[1:2]).astype(bf16)
            return carry

        lax.fori_loop(0, half // tile_rows, step, 0)
        outs = ((rows_ref, rows_any), (q_ref, q_any), (k_ref, k_any), (v_ref, v_any))
        return [(source.at[side(who)], target.at[side(who)]) for source, target in outs]

    load.wait()
    stores = [pltpu.make_async_copy(*pair, out_sems.at[0, j]) for j, pair in enumerate(work(head))]
    for store in stores:
        store.start()
    swap.wait()
    late = [pltpu.make_async_copy(*pair, out_sems.at[1, j]) for j, pair in enumerate(work(1 - head))]
    for store in late:
        store.start()
    for store in stores + late:
        store.wait()


def project(tokens, w_qkv, bias_qv):
    half, model_dim = tokens.shape
    local_dim = w_qkv.shape[2]
    anywhere = pl.BlockSpec(memory_space=pl.ANY)
    vmem = pl.BlockSpec(memory_space=pltpu.VMEM)
    shapes = [(2 * half, model_dim)] + [(2 * half, local_dim)] * 3
    return pl.pallas_call(
        project_kernel,
        in_specs=[anywhere, vmem, vmem],
        out_specs=[anywhere] * 4,
        scratch_shapes=[pltpu.VMEM(shape, bf16) for shape in shapes]
        + [pltpu.SemaphoreType.DMA, pltpu.SemaphoreType.DMA((2,)), pltpu.SemaphoreType.DMA((2, 4))],
        out_shape=[jax.ShapeDtypeStruct(shape, bf16) for shape in shapes],
        compiler_params=pltpu.CompilerParams(
            collective_id=2, has_side_effects=True, vmem_limit_bytes=VMEM_LIMIT
        ),
        cost_estimate=pl.CostEstimate(flops=4_000_000_000, bytes_accessed=12_000_000, transcendentals=0),
    )(tokens, w_qkv, bias_qv)


def weights_kernel(
    n_dp,
    parts,
    left_ref,
    right_ref,
    my_cols_ref,
    their_cols_ref,
    vec_ref,
    keep_any,
    send_any,
    down_keep_any,
    down_send_any,
    grads_any,
    vec_out_ref,
    full_ref,
    recv_ref,
    rest_ref,
    down_ref,
    down_recv_ref,
    down_out_ref,
    vec_recv_ref,
    send_sem,
    recv_sem,
    down_sems,
    grad_sems,
    vec_sems,
    copy_sem,
):
    me, head = lax.axis_index("dp"), lax.axis_index("head")
    other = (me, 1 - head)
    first = (flip(me, 0) * (1 - head) + flip(me, 1) * head, head)
    mine = bit(me, 1) * (1 - head) + bit(me, 0) * head
    step = pl.program_id(0)
    steps = 2 * parts + 1
    model_dim = left_ref.shape[2]
    cols = model_dim // 2
    half = my_cols_ref.shape[0]
    down_rows = parts * model_dim // n_dp
    rows = model_dim // n_dp
    my_rows = grads_any.at[pl.ds(pl.multiple_of(head * half, half), half)]
    own_copy = pltpu.make_async_copy(my_cols_ref, my_rows, copy_sem.at[4])
    grad_copy = remote(their_cols_ref, my_rows, grad_sems.at[0], grad_sems.at[1], other)
    vec_copy = remote(vec_ref, vec_recv_ref, vec_sems.at[0], vec_sems.at[1], other)
    def exchange(k):
        return remote(full_ref.at[k % 3, 1 - head], recv_ref.at[k], send_sem.at[k], recv_sem.at[k], other)

    def down_copy(k):
        at = pl.ds(2 * k, 2)
        return remote(down_ref.at[1, at], down_recv_ref.at[at], down_sems.at[0, k], down_sems.at[1, k], first)

    def multiply():
        whole = lax.dot_general(left_ref[0], right_ref[0], TN, preferred_element_type=f32).astype(bf16)
        full_ref[step % 3, 0] = whole[:, :cols]
        full_ref[step % 3, 1] = whole[:, cols:]

    def total(k, start, count):
        return (
            full_ref[k % 3, head, start : start + count].astype(f32)
            + recv_ref[k, start : start + count, :].astype(f32)
        ).astype(bf16)

    def down_finish(k):
        for q in range(4):
            send, place = route(4 * k + q, me, head)
            down_ref[send, place] = total(k, q * down_rows, down_rows)

    def rest_finish(k):
        start = pl.multiple_of((k - parts) * rows, 16)
        for d in range(n_dp):
            send, place = route(d, me, head)
            rest_ref[send, place, pl.ds(start, rows), :] = total(k, d * rows, rows)

    @pl.when(step >= 3)
    def _():
        exchange(step - 3).wait_send()

    @pl.when(step == 0)
    def _():
        greet([other, first])
        grad_copy.start()
        vec_copy.start()
        own_copy.start()

    @pl.when(step < 2)
    def _():
        multiply()
        exchange(step).start()

    @pl.when((step >= 2) & (step < parts + 2))
    def _():
        exchange(step - 2).wait_recv()
        multiply()
        down_finish(step - 2)
        exchange(step).start()
        down_copy(step - 2).start()

    @pl.when(step >= parts + 2)
    def _():
        exchange(step - 2).wait_recv()
        multiply()
        rest_finish(step - 2)
        exchange(step).start()

    @pl.when(step == steps - 1)
    def _():
        for k in range(steps - 2, steps):
            exchange(k).wait_recv()
            rest_finish(k)
        copies = [
            pltpu.make_async_copy(rest_ref.at[0], keep_any, copy_sem.at[0]),
            pltpu.make_async_copy(rest_ref.at[1], send_any, copy_sem.at[1]),
            pltpu.make_async_copy(down_out_ref.at[0], down_keep_any, copy_sem.at[2]),
            pltpu.make_async_copy(down_out_ref.at[1], down_send_any, copy_sem.at[3]),
        ]
        for copy in copies[:2]:
            copy.start()
        for k in range(parts):
            down_copy(k).wait()

        def split(r, carry):
            for j in range(2):
                block = 2 * r + j * (1 - mine) + (1 - j) * mine
                whole = down_ref[0, block].astype(f32) + down_recv_ref[block].astype(f32)
                down_out_ref[j, r] = whole.astype(bf16)
            return carry

        lax.fori_loop(0, parts, split, 0)
        for copy in copies[2:]:
            copy.start()
        vec_copy.wait()
        vec_out_ref[...] = vec_ref[...] + vec_recv_ref[...]
        grad_copy.wait()
        own_copy.wait()
        for k in range(steps - 3, steps):
            exchange(k).wait_send()
        for copy in copies:
            copy.wait()


def weights(n_dp, left, right, my_cols, their_cols, vec):
    stack, half, model_dim = left.shape
    parts = stack - 2
    steps = 2 * parts + 1
    cols = model_dim // 2
    down_rows = parts * model_dim // n_dp
    rest_rows = (parts + 1) * model_dim // n_dp
    anywhere = pl.BlockSpec(memory_space=pl.ANY)

    def left_map(j):
        return (jnp.where(j < parts, j, jnp.where(j < 2 * parts, parts, parts + 1)), 0, 0)

    def right_map(j):
        return (jnp.where(j < parts, 0, j - parts + 1), 0, 0)

    rest = jax.ShapeDtypeStruct((n_dp // 2, rest_rows, cols), bf16)
    down = jax.ShapeDtypeStruct((n_dp // 4, down_rows, cols), bf16)
    return pl.pallas_call(
        partial(weights_kernel, n_dp, parts),
        grid=(steps,),
        in_specs=[
            pl.BlockSpec((1, half, model_dim), left_map),
            pl.BlockSpec((1, half, model_dim), right_map),
            anywhere,
            anywhere,
            pl.BlockSpec(vec.shape, lambda j: (0, 0)),
        ],
        out_specs=[anywhere] * 5 + [pl.BlockSpec(vec.shape, lambda j: (0, 0))],
        scratch_shapes=[
            pltpu.VMEM((3, 2, model_dim, cols), bf16),
            pltpu.VMEM((steps, model_dim, cols), bf16),
            pltpu.VMEM((2,) + rest.shape, bf16),
            pltpu.VMEM((2, n_dp // 2, down_rows, cols), bf16),
            pltpu.VMEM((n_dp // 2, down_rows, cols), bf16),
            pltpu.VMEM((2,) + down.shape, bf16),
            pltpu.VMEM(vec.shape, f32),
            pltpu.SemaphoreType.DMA((steps,)),
            pltpu.SemaphoreType.DMA((steps,)),
            pltpu.SemaphoreType.DMA((2, parts)),
            pltpu.SemaphoreType.DMA((2,)),
            pltpu.SemaphoreType.DMA((2,)),
            pltpu.SemaphoreType.DMA((5,)),
        ],
        out_shape=[
            rest,
            rest,
            down,
            down,
            jax.ShapeDtypeStruct((2 * half, my_cols.shape[1]), bf16),
            jax.ShapeDtypeStruct(vec.shape, f32),
        ],
        compiler_params=pltpu.CompilerParams(
            collective_id=0, has_side_effects=True, vmem_limit_bytes=48 * 2**20
        ),
        cost_estimate=pl.CostEstimate(flops=15_000_000_000, bytes_accessed=20_000_000, transcendentals=0),
    )(left, right, my_cols, their_cols, vec)


def final_kernel(
    n_dp,
    chunks,
    d_keep_any,
    d_got_any,
    s_keep_any,
    s_got_any,
    raw_any,
    rows_any,
    w_any,
    resid_any,
    vec_ref,
    raw_sums_ref,
    core_send_ref,
    core_recv_ref,
    qkv_ref,
    vec_out_ref,
    vec_core_ref,
    tokens_any,
    t_recv_any,
    d_keep_ref,
    d_got_ref,
    d_own_ref,
    d_out_ref,
    d_got_z_ref,
    s_keep_ref,
    s_got_ref,
    raw_ref,
    rows_ref,
    w_ref,
    resid_ref,
    s_send_ref,
    s_recv_ref,
    s_own_ref,
    s_out_ref,
    s_got_z_ref,
    s_sum_ref,
    q_grad_ref,
    q_both_ref,
    q_first_ref,
    q_send_ref,
    q_recv_ref,
    q_own_ref,
    q_out_ref,
    q_got_z_ref,
    t_send_ref,
    vec_hold_ref,
    vec_recv_ref,
    in_sems,
    d_z_sems,
    s_sems,
    s_z_sems,
    q_first_sems,
    q_sems,
    q_z_sems,
    t_sems,
    core_sems,
    vec_sems,
    out_sem,
):
    me, head = lax.axis_index("dp"), lax.axis_index("head")
    line = n_dp // 4
    depth = line.bit_length() - 1
    z = me // 4
    other = (me, 1 - head)
    low = (flip(me, 0), head)
    high = (flip(me, 1), head)
    around = [(((z + j) % line) * 4 + me % 4, head) for j in range(1, line)]
    first = (flip(me, 0) * (1 - head) + flip(me, 1) * head, head)
    second = (flip(me, 1) * (1 - head) + flip(me, 0) * head, head)
    mine = bit(me, 1) * (1 - head) + bit(me, 0) * head
    half, model_dim = resid_ref.shape
    local_dim = raw_ref.shape[1] // 3
    size = s_keep_ref.shape[1] // chunks
    q_chunks, _, _, q_size, _ = q_both_ref.shape
    q_rows = q_chunks * q_size

    def piece(i):
        return slice(i * size, (i + 1) * size)

    s_loads = [
        pltpu.make_async_copy(s_keep_any, s_keep_ref, in_sems.at[0]),
        pltpu.make_async_copy(s_got_any, s_got_ref, in_sems.at[1]),
    ]
    q_loads = [
        pltpu.make_async_copy(rows_any, rows_ref, in_sems.at[2]),
        pltpu.make_async_copy(raw_any, raw_ref, in_sems.at[3]),
    ]
    t_loads = [
        pltpu.make_async_copy(w_any, w_ref, in_sems.at[4]),
        pltpu.make_async_copy(resid_any, resid_ref, in_sems.at[5]),
    ]
    d_loads = [
        pltpu.make_async_copy(d_keep_any, d_keep_ref, in_sems.at[6]),
        pltpu.make_async_copy(d_got_any, d_got_ref, in_sems.at[7]),
    ]
    for load in s_loads + d_loads:
        load.start()
    greet([low, high, other] + around)

    vec_hold_ref[0] = vec_ref[...]
    here = pl.ds(pl.multiple_of(head * local_dim, LANES), local_dim)
    vec_hold_ref[0, 8:9, here] = raw_sums_ref[:, :local_dim]
    vec_hold_ref[0, 9:10, here] = raw_sums_ref[:, 2 * local_dim :]

    def vec_copy(k):
        to = (low, high)[k] if k < 2 else around[k - 2]
        source = vec_hold_ref.at[min(k, 2)]
        return remote(source, vec_recv_ref.at[k], vec_sems.at[0, k], vec_sems.at[1, k], to)

    vec_copy(0).start()

    def fold_line(own_ref, hold_ref, got_ref, sems):
        def moved(k):
            count = line >> (k + 1)
            at = slice(line - 2 * count, line - count)
            return remote(hold_ref.at[at], got_ref.at[at], sems.at[0, k], sems.at[1, k], (flip(me, k + 2), head))

        def send(k):
            count = line >> (k + 1)
            keep = bit(me, k + 2)
            for q in range(count):
                hold_ref[line - 2 * count + q] = own_ref[2 * q + 1 - keep].astype(bf16)
            moved(k).start()

        def add(k):
            count = line >> (k + 1)
            keep = bit(me, k + 2)
            moved(k).wait()
            for q in range(count):
                own_ref[q] = own_ref[2 * q + keep] + got_ref[line - 2 * count + q].astype(f32)
            if k + 1 < depth:
                send(k + 1)

        return send, add

    d_line = fold_line(d_own_ref, d_out_ref, d_got_z_ref, d_z_sems)

    def s_copy(i):
        return remote(s_send_ref.at[i], s_recv_ref.at[i], s_sems.at[0, i], s_sems.at[1, i], second)

    def s_total(block, i):
        return s_keep_ref[block, piece(i)].astype(f32) + s_got_ref[block, piece(i)].astype(f32)

    def s_prepare(i):
        def send_block(r, carry):
            s_send_ref[i, r] = s_total(2 * r + 1 - mine, i).astype(bf16)
            return carry

        lax.fori_loop(0, line, send_block, 0)

    for load in s_loads:
        load.wait()
    for load in q_loads:
        load.start()
    for load in t_loads:
        load.start()
    for i in range(chunks):
        s_prepare(i)
        s_copy(i).start()
    for load in d_loads:
        load.wait()

    def d_block(r, carry):
        d_own_ref[r] = d_keep_ref[r].astype(f32) + d_got_ref[r].astype(f32)
        return carry

    lax.fori_loop(0, line, d_block, 0)
    d_line[0](0)

    for load in q_loads:
        load.wait()

    def q_columns(j, carry):
        at = pl.ds(pl.multiple_of(j * Q_COLUMNS, LANES), Q_COLUMNS)
        grad = lax.dot_general(rows_ref[:, at], raw_ref[...], TN, preferred_element_type=f32)
        q_grad_ref[pl.ds(pl.multiple_of(j * Q_COLUMNS, LANES), Q_COLUMNS), :] = grad.astype(bf16)
        return carry

    lax.fori_loop(0, model_dim // Q_COLUMNS, q_columns, 0)
    d_line[1](0)

    def q_place(d, carry):
        send, place = route(d, me, head)
        for j in range(q_chunks):
            at = pl.ds(pl.multiple_of(d * q_rows + j * q_size, 16), q_size)
            q_both_ref[j, send, place] = q_grad_ref[at, :]
        return carry

    lax.fori_loop(0, n_dp, q_place, 0)

    def q_copy(j):
        return remote(q_both_ref.at[j, 1], q_first_ref.at[j], q_first_sems.at[0, j], q_first_sems.at[1, j], first)

    def q_second(j):
        return remote(q_send_ref.at[j], q_recv_ref.at[j], q_sems.at[0, j], q_sems.at[1, j], second)

    s_line = [
        fold_line(s_own_ref.at[i], s_out_ref.at[i], s_got_z_ref.at[i], s_z_sems.at[i]) for i in range(chunks)
    ]
    q_line = [
        fold_line(q_own_ref.at[j], q_out_ref.at[j], q_got_z_ref.at[j], q_z_sems.at[j]) for j in range(q_chunks)
    ]

    def s_enter(i):
        s_copy(i).wait()

        def add_block(r, carry):
            s_own_ref[i, r] = s_total(2 * r + mine, i) + s_recv_ref[i, r].astype(f32)
            return carry

        lax.fori_loop(0, line, add_block, 0)
        s_line[i][0](0)

    def q_total(j, block):
        return q_both_ref[j, 0, block].astype(f32) + q_first_ref[j, block].astype(f32)

    def q_enter(j):
        q_copy(j).wait()

        def send_block(r, carry):
            q_send_ref[j, r] = q_total(j, 2 * r + 1 - mine).astype(bf16)
            return carry

        lax.fori_loop(0, line, send_block, 0)
        q_second(j).start()

        def own_block(r, carry):
            q_own_ref[j, r] = q_total(j, 2 * r + mine)
            return carry

        lax.fori_loop(0, line, own_block, 0)

    def q_turn(j):
        q_second(j).wait()

        def add_block(r, carry):
            q_own_ref[j, r] = q_own_ref[j, r] + q_recv_ref[j, r].astype(f32)
            return carry

        lax.fori_loop(0, line, add_block, 0)
        q_line[j][0](0)

    tile_rows = half // 4

    def token_rows(who, tile):
        at = pl.ds(pl.multiple_of(who * half + tile * tile_rows, tile_rows), tile_rows)
        total = 0.0
        for c in range(3):
            part = raw_ref[at, c * local_dim : (c + 1) * local_dim]
            total = total + lax.dot_general(part, w_ref[c], NT, preferred_element_type=f32)
        return total

    t_copy = remote(t_send_ref, t_recv_any, t_sems.at[0], t_sems.at[1], other)

    def send_tile(tile, carry):
        at = pl.ds(pl.multiple_of(tile * tile_rows, tile_rows), tile_rows)
        t_send_ref[at, :] = token_rows(1 - head, tile).astype(bf16)
        return carry

    def own_tile(tile, carry):
        at = pl.ds(pl.multiple_of(tile * tile_rows, tile_rows), tile_rows)
        resid_ref[at, :] = resid_ref[at, :] + token_rows(head, tile)
        return carry

    for j in range(q_chunks):
        q_copy(j).start()
    s_enter(0)
    for load in t_loads:
        load.wait()
    lax.fori_loop(0, 4, send_tile, 0)
    t_copy.start()
    if chunks > 1:
        s_enter(1)
        s_line[0][1](0)
    lax.fori_loop(0, 4, own_tile, 0)
    t_out = pltpu.make_async_copy(resid_ref, tokens_any, out_sem)
    t_out.start()
    for i in range(2, chunks):
        s_enter(i)
        s_line[i - 1][1](0)
    vec_copy(0).wait()
    vec_hold_ref[1] = vec_hold_ref[0] + vec_recv_ref[0]
    vec_copy(1).start()
    q_enter(0)
    s_line[chunks - 1][1](0)
    for j in range(1, q_chunks):
        q_enter(j)
    vec_copy(1).wait()
    vec_hold_ref[2] = vec_hold_ref[1] + vec_recv_ref[1]
    for j in range(line - 1):
        vec_copy(2 + j).start()
    for j in range(q_chunks - 1):
        q_turn(j)
    d_rows = d_own_ref.shape[1]
    for k in range(1, depth):
        d_line[1](k)
    s_sum_ref[:d_rows, :] = d_own_ref[0]
    for i in range(chunks):
        for k in range(1, depth):
            s_line[i][1](k)
        s_sum_ref[d_rows + i * size : d_rows + (i + 1) * size, :] = s_own_ref[i, 0]
    pieces = core_pieces(s_sum_ref.shape[0], q_rows)

    def gather(target_ref, who):
        at = 0
        for start, count in pieces:
            here = pl.ds(pl.multiple_of(start + who * count, 8), count)
            target_ref[at : at + count, :] = s_sum_ref[here, :]
            at += count

    gather(core_send_ref.at[1], 1 - head)
    core_copy = remote(core_send_ref.at[1], core_recv_ref, core_sems.at[0], core_sems.at[1], other)
    core_copy.start()
    gather(core_send_ref.at[0], head)
    q_turn(q_chunks - 1)
    for j in range(line - 1):
        vec_copy(2 + j).wait()
    total = vec_hold_ref[2]
    for j in range(line - 1):
        total = total + vec_recv_ref[2 + j]
    vec_out_ref[...] = total
    core_vec = remote(vec_out_ref.at[pl.ds(8, 8)], vec_core_ref, core_sems.at[2], core_sems.at[3], other)
    core_vec.start()
    for k in range(depth):
        for j in range(q_chunks):
            q_line[j][1](k)
    for j in range(q_chunks):
        qkv_ref[j * q_size : (j + 1) * q_size, :] = q_own_ref[j, 0]
    core_vec.wait()
    core_copy.wait()
    t_copy.wait()
    t_out.wait()


def core_pieces(block_rows, rows):
    parts = (block_rows // rows - 1) // 2
    return [(0, parts * rows // 2)] + [(parts * rows + rows * c, rows // 2) for c in range(parts + 1)]


def final(n_dp, d_keep, d_got, s_keep, s_got, raw, group_rows, w_flat, resid, vec, raw_sums):
    line = n_dp // 4
    depth = line.bit_length() - 1
    _, rest_rows, cols = s_keep.shape
    down_rows = d_keep.shape[1]
    block_rows = down_rows + rest_rows
    half, model_dim = resid.shape
    local_dim = raw.shape[1] // 3
    q_rows, q_cols = model_dim // n_dp, 3 * local_dim
    chunks = 3 if rest_rows % 48 == 0 else 1
    size = rest_rows // chunks
    q_chunks = q_rows // 16
    anywhere = pl.BlockSpec(memory_space=pl.ANY)
    vmem = pl.BlockSpec(memory_space=pltpu.VMEM)

    def low(*dims):
        return pltpu.VMEM(dims, bf16)

    def wide(*dims):
        return pltpu.VMEM(dims, f32)

    def shape(*dims):
        return jax.ShapeDtypeStruct(dims, f32)

    def sems(*dims):
        return pltpu.SemaphoreType.DMA(dims)

    return pl.pallas_call(
        partial(final_kernel, n_dp, chunks),
        in_specs=[anywhere] * 8 + [vmem] * 2,
        out_specs=[vmem] * 5 + [anywhere] * 2,
        scratch_shapes=[
            low(*d_keep.shape),
            low(*d_keep.shape),
            wide(*d_keep.shape),
            low(*d_keep.shape),
            low(line - 1, down_rows, cols),
            low(*s_keep.shape),
            low(*s_keep.shape),
            low(*raw.shape),
            low(*group_rows.shape),
            low(*w_flat.shape),
            wide(half, model_dim),
            low(chunks, line, size, cols),
            low(chunks, line, size, cols),
            wide(chunks, line, size, cols),
            low(chunks, line, size, cols),
            low(chunks, line - 1, size, cols),
            wide(block_rows, cols),
            low(model_dim, q_cols),
            low(q_chunks, 2, 2 * line, 16, q_cols),
            low(q_chunks, 2 * line, 16, q_cols),
            low(q_chunks, line, 16, q_cols),
            low(q_chunks, line, 16, q_cols),
            wide(q_chunks, line, 16, q_cols),
            low(q_chunks, line, 16, q_cols),
            low(q_chunks, line - 1, 16, q_cols),
            low(half, model_dim),
            wide(3, *vec.shape),
            wide(1 + line, *vec.shape),
            sems(8),
            sems(2, depth),
            sems(2, chunks),
            sems(chunks, 2, depth),
            sems(2, q_chunks),
            sems(2, q_chunks),
            sems(q_chunks, 2, depth),
            sems(2),
            sems(4),
            sems(2, 1 + line),
            pltpu.SemaphoreType.DMA,
        ],
        out_shape=[
            shape(2, block_rows // 2, cols),
            shape(block_rows // 2, cols),
            shape(q_rows, q_cols),
            shape(*vec.shape),
            shape(8, model_dim),
            shape(half, model_dim),
            jax.ShapeDtypeStruct((half, model_dim), bf16),
        ],
        compiler_params=pltpu.CompilerParams(
            collective_id=1, has_side_effects=True, vmem_limit_bytes=VMEM_LIMIT
        ),
        cost_estimate=pl.CostEstimate(flops=12_000_000_000, bytes_accessed=25_000_000, transcendentals=0),
    )(d_keep, d_got, s_keep, s_got, raw, group_rows, w_flat, resid, vec, raw_sums)


def finish_kernel(
    n_dp,
    parts,
    own_ref,
    got_ref,
    kept_ref,
    core_ref,
    qkv_ref,
    vec_ref,
    vec_core_ref,
    tokens_ref,
    grad_qkv_ref,
    down_ref,
    in_ref,
    out_ref,
    qv_ref,
    in_bias_ref,
    term_ref,
    *vector_refs,
):
    tokens_ref[...] = own_ref[...] + got_ref[...].astype(f32)

    @pl.when(pl.program_id(0) == 0)
    def _():
        head = lax.axis_index("head")
        place = 2 * lax.axis_index("dp") + head
        cols = kept_ref.shape[2]
        model_dim = 2 * cols
        rows = out_ref.shape[0]
        width = model_dim // (2 * n_dp)
        starts = [0, parts * rows] + [parts * rows + rows * (c + 1) for c in range(parts + 1)]
        for who, source in ((head, kept_ref.at[0]), (1 - head, core_ref)):
            start = who * cols
            here = pl.ds(pl.multiple_of(start, LANES), cols)
            down_ref[:, here] = source[starts[0] : starts[1], :]
            for c in range(parts):
                shifted = pl.ds(pl.multiple_of(2 * cols * c + start, LANES), cols)
                in_ref[:, shifted] = source[starts[1 + c] : starts[2 + c], :]
            out_ref[:, here] = source[starts[1 + parts] : starts[2 + parts], :]
        for c in range(3):
            grad_qkv_ref[c] = qkv_ref[:, c * cols : (c + 1) * cols]
        shift = lax.rem(model_dim - place * width, model_dim)
        turned = pltpu.roll(vec_ref[0:8], shift, 1)
        for j, ref in enumerate(vector_refs):
            ref[...] = turned[j : j + 1, :width]
        term_ref[...] = vec_ref[7:8, :1]
        turned = pltpu.roll(vec_ref[8:16] + vec_core_ref[...], shift, 1)
        qv_ref[...] = turned[:2, :width]
        in_width = parts * model_dim // (2 * n_dp)
        per_row = model_dim // in_width
        row = vec_ref[pl.ds(10 + place // per_row, 1), :]
        row = jnp.broadcast_to(row, (8, model_dim))
        turned = pltpu.roll(row, lax.rem(model_dim - (place % per_row) * in_width, model_dim), 1)
        in_bias_ref[...] = turned[0:1, :in_width]


def finish(n_dp, parts, kept, core, qkv, vec, vec_core, own, got):
    half, model_dim = own.shape
    q_rows = qkv.shape[0]
    width = model_dim // (2 * n_dp)
    rows = min(512, half)
    tile = pl.BlockSpec((rows, model_dim), lambda i: (i, 0))

    def whole(dims):
        return pl.BlockSpec(dims, lambda i: (0,) * len(dims))

    out = [
        (3, q_rows, model_dim // 2),
        (parts * width, model_dim),
        (width, parts * model_dim),
        (width, model_dim),
        (2, width),
        (1, parts * width),
        (1, 1),
    ] + [(1, width)] * 7
    return pl.pallas_call(
        partial(finish_kernel, n_dp, parts),
        grid=(half // rows,),
        in_specs=[tile, tile] + [whole(x.shape) for x in (kept, core, qkv, vec, vec_core)],
        out_specs=[tile] + [whole(dims) for dims in out],
        out_shape=[jax.ShapeDtypeStruct((half, model_dim), f32)] + [jax.ShapeDtypeStruct(dims, f32) for dims in out],
        compiler_params=pltpu.CompilerParams(vmem_limit_bytes=VMEM_LIMIT),
        cost_estimate=pl.CostEstimate(flops=1_000_000, bytes_accessed=10_000_000, transcendentals=0),
    )(own, got, kept, core, qkv, vec, vec_core)


def take(array, index, axis=0):
    return lax.dynamic_index_in_dim(array, index, axis, keepdims=False)


class Links:
    def __init__(self, n_dp):
        self.n_dp = n_dp
        self.bits = n_dp.bit_length() - 1
        self.dp = lax.axis_index("dp")
        self.head = lax.axis_index("head")

    def bit(self, which):
        return (self.dp >> which) & 1

    def permute(self, array, partner):
        pairs = []
        for d in range(self.n_dp):
            for h in range(2):
                to_d, to_h = partner(d, h)
                pairs.append((2 * d + h, 2 * to_d + to_h))
        return lax.ppermute(array, AXES, pairs)

    def swap_head(self, array):
        return self.permute(array, lambda d, h: (d, 1 - h))

    def swap_bit(self, array, which):
        return self.permute(array, lambda d, h: (d ^ (1 << which), h))

    def scatter_heads(self, blocks):
        got = self.swap_head(take(blocks, 1 - self.head, 1))
        return (take(blocks, self.head, 1).astype(f32) + got.astype(f32)).astype(bf16)

    def scatter_dp(self, blocks):
        tail = blocks.shape[1:]
        b0, b1 = self.bit(0), self.bit(1)
        first = self.head == 0
        blocks = blocks.reshape((self.n_dp // 4, 4) + tail)

        def two(one, other):
            i = jnp.where(first, one, 2 * other)
            j = jnp.where(first, 2 + one, 2 * other + 1)
            return jnp.stack([take(blocks, i, 1), take(blocks, j, 1)], axis=1)

        got = self.permute(two(1 - b0, 1 - b1), lambda d, h: (d ^ (1 if h == 0 else 2), h))
        blocks = (two(b0, b1).astype(f32) + got.astype(f32)).astype(bf16)
        mine = jnp.where(first, b1, b0)
        got = self.permute(take(blocks, 1 - mine, 1), lambda d, h: (d ^ (2 if h == 0 else 1), h))
        blocks = take(blocks, mine, 1).astype(f32) + got.astype(f32)
        for which in range(2, self.bits):
            blocks = blocks.reshape((-1, 2) + tail)
            mine = self.bit(which)
            got = self.swap_bit(take(blocks, 1 - mine, 1).astype(bf16), which)
            blocks = take(blocks, mine, 1) + got.astype(f32)
        return blocks.reshape(tail)

    def total(self, array):
        array = array + self.swap_head(array)
        for which in range(self.bits):
            array = array + self.swap_bit(array, which)
        return array


def shards(
    n_dp,
    tokens,
    lengths,
    w_qkv,
    bias_qv,
    w_out,
    bias_out,
    ln1_gain,
    ln1_bias,
    w_in,
    bias_in,
    w_down,
    bias_down,
    ln2_gain,
    ln2_bias,
    term_w,
    term_bias,
    grad_hidden,
    grad_term,
):
    links = Links(n_dp)
    head = links.head
    half, model_dim = tokens.shape
    row_len = 2 * half
    local_dim = w_qkv.shape[2]
    ffn_dim = w_in.shape[1]

    boundary = jnp.cumsum(lengths[0])
    places = jnp.arange(row_len, dtype=jnp.int32)
    segment = jnp.sum((places[:, None] >= boundary[None, :]).astype(jnp.int32), axis=-1)
    seg_col = jnp.broadcast_to(segment[:, None], (row_len, LANES))
    seg_row = jnp.broadcast_to(segment[None, :], (8, row_len))

    def both(mine, theirs, axis):
        return jnp.where(
            head == 0,
            jnp.concatenate([mine, theirs], axis=axis),
            jnp.concatenate([theirs, mine], axis=axis),
        )

    w_parts = jnp.transpose(w_qkv, (1, 0, 2))
    group_rows, queries, key_rows, value_rows = project(tokens, w_parts, bias_qv.T)
    theirs, mine, logs = attend(lengths, head, queries, key_rows, value_rows, seg_col, seg_row)

    def my_half(rows):
        return lax.dynamic_slice_in_dim(rows, head * half, half, 0)

    def their_half(rows):
        return lax.dynamic_slice_in_dim(rows, (1 - head) * half, half, 0)

    vec = jnp.stack([bias_out, ln1_gain, ln1_bias, bias_down, ln2_gain, ln2_bias, term_w, jnp.zeros_like(term_w)])
    hidden_out, term_weight, left, right, resid_one_grad, my_cols, their_cols, vec = middle(
        mine,
        links.swap_head(theirs),
        tokens,
        grad_hidden,
        grad_term[None, :],
        w_out,
        w_in,
        w_down,
        vec,
        bias_in[None, :],
        term_bias[None, :],
    )
    parts = ffn_dim // model_dim
    in_kernels = (model_dim // n_dp) % 16 == 0 and n_dp == 4 * parts

    def back(grads):
        return attend_back(lengths, queries, key_rows, value_rows, grads, logs, seg_col, seg_row)

    if in_kernels:
        s_keep, s_send, d_keep, d_send, head_grad, vec = weights(n_dp, left, right, my_cols, their_cols, vec)
        d_got = links.permute(d_send, lambda d, h: (d ^ (2 if h == 0 else 1), h))
        s_got = links.permute(s_send, lambda d, h: (d ^ (1 if h == 0 else 2), h))
        raw, raw_sums = back(head_grad)
        kept, core, qkv, vec, vec_core, own, got = final(
            n_dp, d_keep, d_got, s_keep, s_got, raw, group_rows, w_parts, resid_one_grad, vec, raw_sums
        )
        (grad_tokens, grad_qkv, grad_down, grad_in, grad_out, bias_qv_mine, bias_in_mine, term_total, *vectors) = finish(
            n_dp, parts, kept, core, qkv, vec, vec_core, own, got
        )
        grad_qkv = jnp.transpose(grad_qkv, (1, 0, 2))
        bias_qv_mine = bias_qv_mine.T
        bias_in_mine = bias_in_mine.reshape(-1)
        term_total = term_total.reshape(1)
        mine = [v.reshape(-1) for v in vectors]
    else:
        raw, raw_sums = back(both(my_cols, links.swap_head(their_cols), 0))

        def product(i, j):
            return lax.dot_general(left[i], right[j], TN, preferred_element_type=f32).astype(bf16)

        def reduced(partial_sum):
            rows, cols = partial_sum.shape
            return links.scatter_dp(links.scatter_heads(partial_sum.reshape(n_dp, 2, rows // (2 * n_dp), cols)))

        grad_down = reduced(jnp.concatenate([product(i, 0) for i in range(parts)]))
        grad_in = reduced(jnp.concatenate([product(parts, 1 + i) for i in range(parts)], axis=1))
        grad_out = reduced(product(parts + 1, parts + 1))
        w_flat = w_qkv.reshape(model_dim, 3 * local_dim)
        grad = lax.dot_general(raw, w_flat, NT, preferred_element_type=f32)
        received = links.swap_head(their_half(grad).astype(bf16))
        grad_tokens = resid_one_grad + my_half(grad) + received.astype(f32)
        qkv_local = lax.dot_general(group_rows, raw, TN, preferred_element_type=f32).astype(bf16)
        grad_qkv = links.scatter_dp(qkv_local.reshape(n_dp, model_dim // n_dp, 3 * local_dim))
        value_sums = lax.dynamic_update_slice(
            jnp.zeros((2, 2 * local_dim), f32),
            jnp.concatenate([raw_sums[:, :local_dim], raw_sums[:, 2 * local_dim :]]),
            (jnp.int32(0), head * local_dim),
        )
        vectors = links.total(lax.dynamic_update_slice(vec, value_sums, (8, 0)))
        grad_qkv = grad_qkv.reshape(model_dim // n_dp, 3, local_dim)
        place = 2 * links.dp + head
        width = model_dim // (2 * n_dp)
        mine = lax.dynamic_slice_in_dim(vectors, place * width, width, 1)
        in_width = ffn_dim // (2 * n_dp)
        in_row = vectors[10 : 10 + parts].reshape(-1)
        bias_in_mine = lax.dynamic_slice_in_dim(in_row, place * in_width, in_width, 0)
        bias_qv_mine = mine[8:10].T
        term_total = vectors[7, :1]

    return (
        hidden_out,
        term_weight.reshape(-1),
        grad_tokens,
        grad_qkv,
        bias_qv_mine,
        grad_out,
        mine[0],
        mine[1],
        mine[2],
        grad_in,
        bias_in_mine,
        grad_down,
        mine[3],
        mine[4],
        mine[5],
        mine[6],
        term_total,
    )


def solution(mesh):
    rows = P(AXES, None)
    return jax.shard_map(
        partial(shards, mesh.shape["dp"]),
        mesh=mesh,
        in_specs=(rows, P("dp", None), P(None, None, "head"), P("head", None))
        + (P(),) * 12
        + (rows, P(AXES)),
        out_specs=(
            rows,
            P(AXES),
            rows,
            P("dp", None, "head"),
            rows,
            rows,
            P(AXES),
            P(AXES),
            P(AXES),
            rows,
            P(AXES),
            rows,
            P(AXES),
            P(AXES),
            P(AXES),
            P(AXES),
            P(),
        ),
        check_vma=False,
    )
```

```python
from functools import partial

import jax
import jax.numpy as jnp
from jax import lax
from jax.experimental import pallas as pl
from jax.experimental.pallas import tpu as pltpu
from jax.sharding import PartitionSpec as P

HEAD_DIM = 64
LANES = 128
VMEM_LIMIT = 60 * 2**20
Q_ROWS = 256
PIECE = 32
Q_COLUMNS = 128
WIDTHS = (2, 3, 4, 5, 6, 8, 10)
BACK_WIDTHS = (2, 3, 4, 5, 6, 7, 8, 10)
AXES = ("dp", "head")

f32 = jnp.float32
bf16 = jnp.bfloat16
norm_eps = 1e-06
NT = (((1,), (1,)), ((), ()))
TN = (((0,), (0,)), ((), ()))


def key_range(lengths_ref, first, rows, row_len):
    start = jnp.int32(0)
    low = jnp.int32(0)
    high = jnp.int32(row_len)
    for j in range(lengths_ref.shape[1]):
        end = start + lengths_ref[0, j]
        low = jnp.where(start <= first, start, low)
        high = jnp.where(end >= first + rows, jnp.minimum(high, end), high)
        start = end
    low_block = low // LANES
    count = (high + LANES - 1) // LANES - low_block
    return low_block, count


def by_width(lengths_ref, first, rows, row_len, body, choices=WIDTHS):
    blocks = row_len // LANES
    low_block, count = key_range(lengths_ref, first, rows, row_len)
    widths = sorted({min(w, blocks) for w in choices})
    below = 0
    for width in widths:

        @pl.when((count > below) & (count <= width))
        def _(width=width):
            begin = jnp.minimum(low_block, blocks - width)
            body(pl.multiple_of(begin * LANES, LANES), width * LANES)

        below = width


def query_block(step, steps, head):
    return lax.rem(step + (1 - head) * (steps // 2), steps)


def attend_kernel(
    lengths_ref,
    head_ref,
    q_ref,
    k_ref,
    v_ref,
    segc_ref,
    segr_ref,
    theirs_ref,
    mine_ref,
    log_ref,
    mask_ref,
    cols_ref,
    s_ref,
    p_ref,
    o_ref,
):
    rows, local_dim = q_ref.shape
    row_len = k_ref.shape[0]
    step, steps = pl.program_id(0), pl.num_programs(0)
    first = query_block(step, steps, head_ref[0]) * rows
    lane = lax.broadcasted_iota(jnp.int32, (rows, LANES), 1)

    def body(begin, width):
        same = segc_ref[:, 0:1] == segr_ref[0:1, pl.ds(begin, width)]
        mask_ref[:, :width] = jnp.where(same, 0.0, -1e30)

        heads = local_dim // HEAD_DIM

        def score(i):
            cols = slice(i // 2 * LANES, i // 2 * LANES + LANES)
            q_pair = q_ref[:, cols]
            q_one = jnp.where((lane // HEAD_DIM) == i % 2, q_pair, jnp.zeros_like(q_pair))
            k_pair = k_ref[pl.ds(begin, width), cols]
            s_ref[i % 2, :, :width] = lax.dot_general(q_one, k_pair, NT, preferred_element_type=f32)

        def soft(i):
            for r in range(0, rows, PIECE):
                part = slice(r, r + PIECE)
                scores = s_ref[i % 2, part, :width] + mask_ref[part, :width]
                row_max = jnp.max(scores, axis=1, keepdims=True)
                powers = jnp.exp(scores - row_max)
                total = jnp.sum(powers, axis=1, keepdims=True)
                p_ref[i % 2, part, :width] = (powers * (1.0 / total)).astype(bf16)
                log_total = row_max + jnp.log(total)
                cols_ref[part] = jnp.where(lane[part] == i, log_total, cols_ref[part])

        def value(i):
            cols = slice(i // 2 * LANES, i // 2 * LANES + LANES)
            return jnp.dot(p_ref[i % 2, :, :width], v_ref[pl.ds(begin, width), cols], preferred_element_type=f32)

        score(0)
        held = None
        for i in range(heads):
            if i + 1 < heads:
                score(i + 1)
            soft(i)
            out = value(i)
            if i % 2 == 0:
                held = out
            else:
                cols = slice(i // 2 * LANES, i // 2 * LANES + LANES)
                o_ref[:, cols] = jnp.where(lane < HEAD_DIM, held, out).astype(bf16)

    by_width(lengths_ref, first, rows, row_len, body)
    log_ref[...] = cols_ref[...].T[: log_ref.shape[0]]

    @pl.when(step < steps // 2)
    def _():
        theirs_ref[...] = o_ref[...]

    @pl.when(step >= steps // 2)
    def _():
        mine_ref[...] = o_ref[...]


def attend(lengths, head, queries, key_rows, value_rows, seg_col, seg_row):
    row_len, local_dim = queries.shape
    rows = min(Q_ROWS, row_len // 2)
    steps = row_len // rows
    whole = pl.BlockSpec((row_len, local_dim), lambda i, n, h: (0, 0))
    return pl.pallas_call(
        attend_kernel,
        grid_spec=pltpu.PrefetchScalarGridSpec(
            num_scalar_prefetch=2,
            grid=(steps,),
            in_specs=[
                pl.BlockSpec((rows, local_dim), lambda i, n, h: (query_block(i, steps, h[0]), 0)),
                whole,
                whole,
                pl.BlockSpec((rows, LANES), lambda i, n, h: (query_block(i, steps, h[0]), 0)),
                pl.BlockSpec((8, row_len), lambda i, n, h: (0, 0)),
            ],
            out_specs=[
                pl.BlockSpec((rows, local_dim), lambda i, n, h: (jnp.minimum(i, steps // 2 - 1), 0)),
                pl.BlockSpec((rows, local_dim), lambda i, n, h: (jnp.maximum(i - steps // 2, 0), 0)),
                pl.BlockSpec((8, rows), lambda i, n, h: (0, query_block(i, steps, h[0]))),
            ],
            scratch_shapes=[
                pltpu.VMEM((rows, max(WIDTHS) * LANES), f32),
                pltpu.VMEM((rows, LANES), f32),
                pltpu.VMEM((2, rows, max(WIDTHS) * LANES), f32),
                pltpu.VMEM((2, rows, max(WIDTHS) * LANES), bf16),
                pltpu.VMEM((rows, local_dim), bf16),
            ],
        ),
        out_shape=[
            jax.ShapeDtypeStruct((row_len // 2, local_dim), bf16),
            jax.ShapeDtypeStruct((row_len // 2, local_dim), bf16),
            jax.ShapeDtypeStruct((8, row_len), f32),
        ],
        compiler_params=pltpu.CompilerParams(vmem_limit_bytes=VMEM_LIMIT),
        cost_estimate=pl.CostEstimate(flops=20_000_000_000, bytes_accessed=8_000_000, transcendentals=0),
    )(lengths, head[None], queries, key_rows, value_rows, seg_col, seg_row)


def attend_back_kernel(
    lengths_ref,
    q_ref,
    k_ref,
    v_ref,
    g_ref,
    log_ref,
    segc_ref,
    segr_ref,
    raw_ref,
    sums_ref,
    mask_ref,
    dk_ref,
    dv_ref,
    s_ref,
    d_ref,
    p_ref,
    e_ref,
    ones_ref,
):
    rows, local_dim = q_ref.shape
    row_len = k_ref.shape[0]
    step = pl.program_id(0)
    first = step * rows
    lane = lax.broadcasted_iota(jnp.int32, (rows, LANES), 1)

    @pl.when(step == 0)
    def _():
        dk_ref[...] = jnp.zeros_like(dk_ref)
        dv_ref[...] = jnp.zeros_like(dv_ref)

    def body(begin, width):
        keys = pl.ds(begin, width)
        same = segc_ref[keys, 0:1] == segr_ref[0:1, :]
        mask_ref[:width, :] = jnp.where(same, 0.0, -1e30)

        def pair_step(pair, carry):
            cols = pl.ds(pl.multiple_of(pair * LANES, LANES), LANES)

            def products(i):
                mine = (lane // HEAD_DIM) == i
                here = slice(i * rows, i * rows + rows)
                q_pair, g_pair = q_ref[:, cols], g_ref[:, cols]
                q_one = jnp.where(mine, q_pair, jnp.zeros_like(q_pair))
                g_one = jnp.where(mine, g_pair, jnp.zeros_like(g_pair))
                ones_ref[0, here] = q_one
                ones_ref[1, here] = g_one
                s_ref[i, :width] = lax.dot_general(k_ref[keys, cols], q_one, NT, preferred_element_type=f32)
                d_ref[i, :width] = lax.dot_general(v_ref[keys, cols], g_one, NT, preferred_element_type=f32)

            def soft(i):
                here = slice(i * rows, i * rows + rows)
                log_row = log_ref[pl.ds(2 * pair + i, 1), :]
                inner = jnp.zeros((8, rows), f32)
                for r in range(0, width, PIECE):
                    part = slice(r, r + PIECE)
                    probs = jnp.exp(s_ref[i, part] + mask_ref[part] - log_row)
                    s_ref[i, part] = probs
                    p_ref[part, here] = probs.astype(bf16)
                    inner = inner + jnp.sum((probs * d_ref[i, part]).reshape(PIECE // 8, 8, rows), axis=0)
                inner = jnp.sum(inner, axis=0, keepdims=True)
                for r in range(0, width, PIECE):
                    part = slice(r, r + PIECE)
                    e_ref[part, here] = (s_ref[i, part] * (d_ref[i, part] - inner)).astype(bf16)

            def gather(i):
                here = slice(i * rows, i * rows + rows)
                dv_ref[keys, cols] += jnp.dot(p_ref[:width, here], ones_ref[1, here], preferred_element_type=f32)
                dk_ref[keys, cols] += jnp.dot(e_ref[:width, here], ones_ref[0, here], preferred_element_type=f32)
                return lax.dot_general(e_ref[:width, here], k_ref[keys, cols], TN, preferred_element_type=f32)

            products(0)
            products(1)
            soft(0)
            dq_first = gather(0)
            soft(1)
            dq_second = gather(1)
            dq_low = jnp.where(lane < HEAD_DIM, dq_first, dq_second).astype(bf16)
            raw_ref[pl.ds(pl.multiple_of(first, rows), rows), cols] = dq_low * jnp.asarray(HEAD_DIM**-0.5, bf16)
            return carry

        lax.fori_loop(0, local_dim // LANES, pair_step, 0)

    by_width(lengths_ref, first, rows, row_len, body, BACK_WIDTHS)

    @pl.when(step == pl.num_programs(0) - 1)
    def _():
        raw_ref[:, local_dim : 2 * local_dim] = dk_ref[...].astype(bf16)
        raw_ref[:, 2 * local_dim :] = dv_ref[...].astype(bf16)
        sums_ref[...] = jnp.sum(raw_ref[...].astype(f32), axis=0, keepdims=True)


def attend_back(lengths, queries, key_rows, value_rows, grads, logs, seg_col, seg_row):
    row_len, local_dim = queries.shape
    rows = min(Q_ROWS, row_len)
    whole = pl.BlockSpec((row_len, local_dim), lambda i, n: (0, 0))
    block = pl.BlockSpec((rows, local_dim), lambda i, n: (i, 0))
    return pl.pallas_call(
        attend_back_kernel,
        grid_spec=pltpu.PrefetchScalarGridSpec(
            num_scalar_prefetch=1,
            grid=(row_len // rows,),
            in_specs=[
                block,
                whole,
                whole,
                block,
                pl.BlockSpec((8, rows), lambda i, n: (0, i)),
                pl.BlockSpec((row_len, LANES), lambda i, n: (0, 0)),
                pl.BlockSpec((8, rows), lambda i, n: (0, i)),
            ],
            out_specs=[
                pl.BlockSpec((row_len, 3 * local_dim), lambda i, n: (0, 0)),
                pl.BlockSpec((1, 3 * local_dim), lambda i, n: (0, 0)),
            ],
            scratch_shapes=[
                pltpu.VMEM((max(WIDTHS) * LANES, rows), f32),
                pltpu.VMEM((row_len, local_dim), f32),
                pltpu.VMEM((row_len, local_dim), f32),
                pltpu.VMEM((2, max(WIDTHS) * LANES, rows), f32),
                pltpu.VMEM((2, max(WIDTHS) * LANES, rows), f32),
                pltpu.VMEM((max(WIDTHS) * LANES, 2 * rows), bf16),
                pltpu.VMEM((max(WIDTHS) * LANES, 2 * rows), bf16),
                pltpu.VMEM((2, 2 * rows, LANES), bf16),
            ],
        ),
        out_shape=[
            jax.ShapeDtypeStruct((row_len, 3 * local_dim), bf16),
            jax.ShapeDtypeStruct((1, 3 * local_dim), f32),
        ],
        compiler_params=pltpu.CompilerParams(vmem_limit_bytes=VMEM_LIMIT),
        cost_estimate=pl.CostEstimate(flops=40_000_000_000, bytes_accessed=12_000_000, transcendentals=0),
    )(lengths, queries, key_rows, value_rows, grads, logs, seg_col, seg_row)


TILE = 256


def gelu_both(x):
    cdf = 0.5 + 0.5 * lax.erf(x * 0.7071067811865476)
    density = jnp.exp(-0.5 * x * x) * 0.3989422804014327
    return x * cdf, cdf + x * density


def normalize(resid):
    center = resid - jnp.mean(resid, axis=-1, keepdims=True)
    scale = lax.rsqrt(jnp.mean(center * center, axis=-1, keepdims=True) + norm_eps)
    return center * scale, scale


def normalize_back(grad, normed, scale):
    shift = jnp.mean(grad, axis=-1, keepdims=True)
    slope = jnp.mean(grad * normed, axis=-1, keepdims=True)
    return scale * (grad - shift - normed * slope)


def fold(x):
    return jnp.sum(x.astype(f32).reshape(x.shape[0] // 8, 8, x.shape[1]), axis=0)


def middle_kernel(
    mine_ref,
    theirs_ref,
    tokens_ref,
    hid_ref,
    term_ref,
    w_out_ref,
    w_in_ref,
    w_down_ref,
    vec_ref,
    bias_in_ref,
    term_bias_ref,
    hidden_ref,
    weight_ref,
    left_ref,
    right_ref,
    resid_ref,
    my_grad_ref,
    their_grad_ref,
    sums_ref,
    slope_ref,
    wide_ref,
    x_ref,
    normal_ref,
    scale_ref,
    fold_ref,
    in_fold_ref,
    term_cols_ref,
    term_in_ref,
):
    head = lax.axis_index("head")
    local_dim = mine_ref.shape[1]
    model_dim = w_out_ref.shape[0]
    parts = w_in_ref.shape[1] // model_dim
    rows = tokens_ref.shape[0]
    pieces = [slice(r, r + PIECE) for r in range(0, rows, PIECE)]
    bias_out, ln1_gain, ln1_bias = vec_ref[0:1], vec_ref[1:2], vec_ref[2:3]
    bias_down, ln2_gain, ln2_bias, term_w = vec_ref[3:4], vec_ref[4:5], vec_ref[5:6], vec_ref[6:7]

    @pl.when(pl.program_id(0) == 0)
    def _():
        fold_ref[...] = jnp.zeros_like(fold_ref)
        in_fold_ref[...] = jnp.zeros_like(in_fold_ref)

    term_in_ref[...] = jnp.broadcast_to(term_ref[...], (LANES, rows)).T
    left_ref[parts + 1, :, pl.ds(pl.multiple_of(head * local_dim, LANES), local_dim)] = mine_ref[...]
    left_ref[parts + 1, :, pl.ds(pl.multiple_of((1 - head) * local_dim, LANES), local_dim)] = theirs_ref[...]
    x_ref[...] = jnp.dot(left_ref[parts + 1], w_out_ref[...], preferred_element_type=f32)
    for r in pieces:
        normal, scale = normalize(tokens_ref[r].astype(f32) + (x_ref[r] + bias_out))
        normed = normal * ln1_gain + ln1_bias
        normal_ref[r] = normal
        scale_ref[r] = scale
        left_ref[parts, r] = normed.astype(bf16)
        x_ref[r] = normed + bias_down

    def columns(c):
        return slice(c * model_dim, (c + 1) * model_dim)

    def rise(c):
        wide_ref[c % 2] = jnp.dot(left_ref[parts], w_in_ref[:, columns(c)], preferred_element_type=f32)

    rise(0)
    for c in range(parts):
        if c + 1 < parts:
            rise(c + 1)
        for r in pieces:
            value, slope = gelu_both(wide_ref[c % 2, r] + bias_in_ref[:, columns(c)])
            left_ref[c, r] = value.astype(bf16)
            slope_ref[r, columns(c)] = slope
        x_ref[...] += jnp.dot(left_ref[c], w_down_ref[columns(c), :], preferred_element_type=f32)

    for r in pieces:
        normal, scale = normalize(x_ref[r])
        normed = normal * ln2_gain + ln2_bias
        hidden_ref[r] = normed.astype(bf16)
        logit = jnp.sum(normed * term_w, axis=-1, keepdims=True) + term_bias_ref[0:1, 0:1]
        small = jnp.exp(-jnp.abs(logit))
        term_cols_ref[r] = jnp.broadcast_to(jnp.maximum(logit, 0.0) + jnp.log1p(small), (PIECE, LANES))
        logit_grad = term_in_ref[r, 0:1] * (jnp.where(logit >= 0.0, 1.0, small) / (1.0 + small))
        two_grad = hid_ref[r] + logit_grad * term_w
        resid_two = normalize_back(two_grad * ln2_gain, normal, scale)
        low = resid_two.astype(bf16)
        right_ref[0, r] = low
        x_ref[r] = resid_two
        fold_ref[3] += fold(low)
        fold_ref[4] += fold(two_grad * normal)
        fold_ref[5] += fold(two_grad)
        fold_ref[6] += fold(logit_grad * normed)
        fold_ref[7] += fold(jnp.broadcast_to(logit_grad, normal.shape))

    weight_ref[...] = term_cols_ref[...].T[0:1]

    def fall(c):
        wide_ref[c % 2] = lax.dot_general(right_ref[0], w_down_ref[columns(c), :], NT, preferred_element_type=f32)

    fall(0)
    for c in range(parts):
        if c + 1 < parts:
            fall(c + 1)
        for r in pieces:
            low = (wide_ref[c % 2, r] * slope_ref[r, columns(c)]).astype(bf16)
            right_ref[1 + c, r] = low
            in_fold_ref[:, columns(c)] += fold(low)
        x_ref[...] += lax.dot_general(right_ref[1 + c], w_in_ref[:, columns(c)], NT, preferred_element_type=f32)

    for r in pieces:
        one_grad = x_ref[r]
        normal = normal_ref[r]
        resid_one = normalize_back(one_grad * ln1_gain, normal, scale_ref[r])
        resid_ref[r] = resid_one
        low = resid_one.astype(bf16)
        right_ref[parts + 1, r] = low
        fold_ref[0] += fold(low)
        fold_ref[1] += fold(one_grad * normal)
        fold_ref[2] += fold(one_grad)
    grads = lax.dot_general(right_ref[parts + 1], w_out_ref[...], NT, preferred_element_type=f32).astype(bf16)

    @pl.when(head == 0)
    def _():
        my_grad_ref[...] = grads[:, :local_dim]
        their_grad_ref[...] = grads[:, local_dim:]

    @pl.when(head == 1)
    def _():
        my_grad_ref[...] = grads[:, local_dim:]
        their_grad_ref[...] = grads[:, :local_dim]

    @pl.when(pl.program_id(0) == pl.num_programs(0) - 1)
    def _():
        sums_ref[...] = jnp.zeros_like(sums_ref)
        sums_ref[0:8] = jnp.sum(fold_ref[...], axis=1)
        for c in range(parts):
            sums_ref[10 + c : 11 + c] = jnp.sum(in_fold_ref[:, columns(c)], axis=0, keepdims=True)


def middle(mine, theirs, tokens, grad_hidden, grad_term, w_out, w_in, w_down, vec, bias_in, term_bias):
    half, model_dim = tokens.shape
    local_dim = mine.shape[1]
    ffn_dim = w_in.shape[1]
    rows = min(TILE, half)

    def tile(cols):
        return pl.BlockSpec((rows, cols), lambda i: (i, 0))

    def whole(*shape):
        return pl.BlockSpec(shape, lambda i: (0, 0), pipeline_mode=pl.Buffered(1))

    stacked = pl.BlockSpec((ffn_dim // model_dim + 2, rows, model_dim), lambda i: (0, i, 0))
    stack = jax.ShapeDtypeStruct((ffn_dim // model_dim + 2, half, model_dim), bf16)

    def full(cols, kind):
        return jax.ShapeDtypeStruct((half, cols), kind)

    return pl.pallas_call(
        middle_kernel,
        grid=(half // rows,),
        in_specs=[
            tile(local_dim),
            tile(local_dim),
            tile(model_dim),
            tile(model_dim),
            pl.BlockSpec((1, rows), lambda i: (0, i)),
            whole(model_dim, model_dim),
            whole(model_dim, ffn_dim),
            whole(ffn_dim, model_dim),
            whole(8, model_dim),
            whole(1, ffn_dim),
            whole(1, 1),
        ],
        out_specs=[
            tile(model_dim),
            pl.BlockSpec((1, rows), lambda i: (0, i)),
            stacked,
            stacked,
            tile(model_dim),
            tile(local_dim),
            tile(local_dim),
            pl.BlockSpec((16, model_dim), lambda i: (0, 0)),
        ],
        scratch_shapes=[
            pltpu.VMEM((rows, ffn_dim), f32),
            pltpu.VMEM((2, rows, model_dim), f32),
            pltpu.VMEM((rows, model_dim), f32),
            pltpu.VMEM((rows, model_dim), f32),
            pltpu.VMEM((rows, 1), f32),
            pltpu.VMEM((8, 8, model_dim), f32),
            pltpu.VMEM((8, ffn_dim), f32),
            pltpu.VMEM((rows, LANES), f32),
            pltpu.VMEM((rows, LANES), f32),
        ],
        out_shape=[
            full(model_dim, bf16),
            jax.ShapeDtypeStruct((1, half), f32),
            stack,
            stack,
            full(model_dim, f32),
            full(local_dim, bf16),
            full(local_dim, bf16),
            jax.ShapeDtypeStruct((16, model_dim), f32),
        ],
        compiler_params=pltpu.CompilerParams(vmem_limit_bytes=VMEM_LIMIT),
        cost_estimate=pl.CostEstimate(flops=40_000_000_000, bytes_accessed=50_000_000, transcendentals=0),
    )(mine, theirs, tokens, grad_hidden, grad_term, w_out, w_in, w_down, vec, bias_in, term_bias)


def bit(place, which):
    return (place // 2**which) % 2


def flip(place, which):
    return place + (1 - 2 * bit(place, which)) * 2**which


def route(target, me, head):
    low, high = bit(target, 0), bit(target, 1)
    send = (1 - head) * ((low + bit(me, 0)) % 2) + head * ((high + bit(me, 1)) % 2)
    return send, 2 * (target // 4) + (1 - head) * high + head * low


def greet(partners):
    barrier = pltpu.get_barrier_semaphore()
    for partner in partners:
        pl.semaphore_signal(barrier, inc=1, device_id=partner, device_id_type=pl.DeviceIdType.MESH)
    pl.semaphore_wait(barrier, len(partners))


def remote(source, target, send_sem, recv_sem, partner):
    return pltpu.make_async_remote_copy(
        src_ref=source,
        dst_ref=target,
        send_sem=send_sem,
        recv_sem=recv_sem,
        device_id=partner,
        device_id_type=pl.DeviceIdType.MESH,
    )


def project_kernel(
    tokens_any,
    w_any,
    bias_ref,
    rows_any,
    q_any,
    k_any,
    v_any,
    rows_ref,
    q_ref,
    k_ref,
    v_ref,
    w_ref,
    load_sem,
    w_sem,
    swap_sems,
    out_sems,
):
    head = lax.axis_index("head")
    other = (lax.axis_index("dp"), 1 - head)
    half = tokens_any.shape[0]
    tile_rows = min(256, half)

    def side(who):
        return pl.ds(pl.multiple_of(who * half, half), half)

    load = pltpu.make_async_copy(tokens_any, rows_ref.at[side(head)], load_sem)
    load.start()
    w_load = pltpu.make_async_copy(w_any, w_ref, w_sem)
    w_load.start()
    greet([other])
    swap = remote(tokens_any, rows_ref.at[side(head)], swap_sems.at[0], swap_sems.at[1], other)
    swap.start()

    def work(who):
        def step(tile, carry):
            at = pl.ds(pl.multiple_of(who * half + tile * tile_rows, tile_rows), tile_rows)
            x = rows_ref[at, :]
            queries = jnp.dot(x, w_ref[0], preferred_element_type=f32)
            q_ref[at, :] = ((queries + bias_ref[0:1]) * HEAD_DIM ** (-0.5)).astype(bf16)
            k_ref[at, :] = jnp.dot(x, w_ref[1], preferred_element_type=f32).astype(bf16)
            v_ref[at, :] = (jnp.dot(x, w_ref[2], preferred_element_type=f32) + bias_ref[1:2]).astype(bf16)
            return carry

        lax.fori_loop(0, half // tile_rows, step, 0)
        outs = ((rows_ref, rows_any), (q_ref, q_any), (k_ref, k_any), (v_ref, v_any))
        return [(source.at[side(who)], target.at[side(who)]) for source, target in outs]

    load.wait()
    w_load.wait()
    stores = [pltpu.make_async_copy(*pair, out_sems.at[0, j]) for j, pair in enumerate(work(head))]
    for store in stores:
        store.start()
    swap.wait()
    late = [pltpu.make_async_copy(*pair, out_sems.at[1, j]) for j, pair in enumerate(work(1 - head))]
    for store in late:
        store.start()
    for store in stores + late:
        store.wait()


def project(tokens, w_qkv, bias_qv):
    half, model_dim = tokens.shape
    local_dim = w_qkv.shape[2]
    anywhere = pl.BlockSpec(memory_space=pl.ANY)
    vmem = pl.BlockSpec(memory_space=pltpu.VMEM)
    shapes = [(2 * half, model_dim)] + [(2 * half, local_dim)] * 3
    return pl.pallas_call(
        project_kernel,
        in_specs=[anywhere, anywhere, vmem],
        out_specs=[anywhere] * 4,
        scratch_shapes=[pltpu.VMEM(shape, bf16) for shape in shapes]
        + [pltpu.VMEM(w_qkv.shape, bf16), pltpu.SemaphoreType.DMA, pltpu.SemaphoreType.DMA, pltpu.SemaphoreType.DMA((2,)), pltpu.SemaphoreType.DMA((2, 4))],
        out_shape=[jax.ShapeDtypeStruct(shape, bf16) for shape in shapes],
        compiler_params=pltpu.CompilerParams(
            collective_id=2, has_side_effects=True, vmem_limit_bytes=VMEM_LIMIT
        ),
        cost_estimate=pl.CostEstimate(flops=4_000_000_000, bytes_accessed=12_000_000, transcendentals=0),
    )(tokens, w_qkv, bias_qv)


def weights_kernel(
    n_dp,
    parts,
    left_ref,
    right_ref,
    my_cols_ref,
    their_cols_ref,
    vec_ref,
    keep_any,
    send_any,
    down_keep_any,
    down_send_any,
    grads_any,
    vec_out_ref,
    full_ref,
    recv_ref,
    rest_ref,
    down_ref,
    down_recv_ref,
    down_out_ref,
    vec_recv_ref,
    send_sem,
    recv_sem,
    down_sems,
    grad_sems,
    vec_sems,
    copy_sem,
):
    me, head = lax.axis_index("dp"), lax.axis_index("head")
    other = (me, 1 - head)
    first = (flip(me, 0) * (1 - head) + flip(me, 1) * head, head)
    mine = bit(me, 1) * (1 - head) + bit(me, 0) * head
    step = pl.program_id(0)
    steps = 2 * parts + 1
    model_dim = left_ref.shape[2]
    cols = model_dim // 2
    half = my_cols_ref.shape[0]
    down_rows = parts * model_dim // n_dp
    rows = model_dim // n_dp
    my_rows = grads_any.at[pl.ds(pl.multiple_of(head * half, half), half)]
    own_copy = pltpu.make_async_copy(my_cols_ref, my_rows, copy_sem.at[4])
    grad_copy = remote(their_cols_ref, my_rows, grad_sems.at[0], grad_sems.at[1], other)
    vec_copy = remote(vec_ref, vec_recv_ref, vec_sems.at[0], vec_sems.at[1], other)
    def exchange(k):
        return remote(full_ref.at[k % 3, 1 - head], recv_ref.at[k], send_sem.at[k], recv_sem.at[k], other)

    def down_copy(k):
        at = pl.ds(2 * k, 2)
        return remote(down_ref.at[1, at], down_recv_ref.at[at], down_sems.at[0, k], down_sems.at[1, k], first)

    def multiply():
        whole = lax.dot_general(left_ref[0], right_ref[0], TN, preferred_element_type=f32).astype(bf16)
        full_ref[step % 3, 0] = whole[:, :cols]
        full_ref[step % 3, 1] = whole[:, cols:]

    def total(k, start, count):
        return (
            full_ref[k % 3, head, start : start + count].astype(f32)
            + recv_ref[k, start : start + count, :].astype(f32)
        ).astype(bf16)

    def down_finish(k):
        for q in range(4):
            send, place = route(4 * k + q, me, head)
            down_ref[send, place] = total(k, q * down_rows, down_rows)

    def rest_finish(k):
        start = pl.multiple_of((k - parts) * rows, 16)
        for d in range(n_dp):
            send, place = route(d, me, head)
            rest_ref[send, place, pl.ds(start, rows), :] = total(k, d * rows, rows)

    @pl.when(step >= 3)
    def _():
        exchange(step - 3).wait_send()

    @pl.when(step == 0)
    def _():
        greet([other, first])
        grad_copy.start()
        vec_copy.start()
        own_copy.start()

    @pl.when(step < 2)
    def _():
        multiply()
        exchange(step).start()

    @pl.when((step >= 2) & (step < parts + 2))
    def _():
        exchange(step - 2).wait_recv()
        multiply()
        down_finish(step - 2)
        exchange(step).start()
        down_copy(step - 2).start()

    @pl.when(step >= parts + 2)
    def _():
        exchange(step - 2).wait_recv()
        multiply()
        rest_finish(step - 2)
        exchange(step).start()

    @pl.when(step == steps - 1)
    def _():
        for k in range(steps - 2, steps):
            exchange(k).wait_recv()
            rest_finish(k)
        copies = [
            pltpu.make_async_copy(rest_ref.at[0], keep_any, copy_sem.at[0]),
            pltpu.make_async_copy(rest_ref.at[1], send_any, copy_sem.at[1]),
            pltpu.make_async_copy(down_out_ref.at[0], down_keep_any, copy_sem.at[2]),
            pltpu.make_async_copy(down_out_ref.at[1], down_send_any, copy_sem.at[3]),
        ]
        for copy in copies[:2]:
            copy.start()
        for k in range(parts):
            down_copy(k).wait()

        def split(r, carry):
            for j in range(2):
                block = 2 * r + j * (1 - mine) + (1 - j) * mine
                whole = down_ref[0, block].astype(f32) + down_recv_ref[block].astype(f32)
                down_out_ref[j, r] = whole.astype(bf16)
            return carry

        lax.fori_loop(0, parts, split, 0)
        for copy in copies[2:]:
            copy.start()
        vec_copy.wait()
        vec_out_ref[...] = vec_ref[...] + vec_recv_ref[...]
        grad_copy.wait()
        own_copy.wait()
        for k in range(steps - 3, steps):
            exchange(k).wait_send()
        for copy in copies:
            copy.wait()


def weights(n_dp, left, right, my_cols, their_cols, vec):
    stack, half, model_dim = left.shape
    parts = stack - 2
    steps = 2 * parts + 1
    cols = model_dim // 2
    down_rows = parts * model_dim // n_dp
    rest_rows = (parts + 1) * model_dim // n_dp
    anywhere = pl.BlockSpec(memory_space=pl.ANY)

    def left_map(j):
        return (jnp.where(j < parts, j, jnp.where(j < 2 * parts, parts, parts + 1)), 0, 0)

    def right_map(j):
        return (jnp.where(j < parts, 0, j - parts + 1), 0, 0)

    rest = jax.ShapeDtypeStruct((n_dp // 2, rest_rows, cols), bf16)
    down = jax.ShapeDtypeStruct((n_dp // 4, down_rows, cols), bf16)
    return pl.pallas_call(
        partial(weights_kernel, n_dp, parts),
        grid=(steps,),
        in_specs=[
            pl.BlockSpec((1, half, model_dim), left_map),
            pl.BlockSpec((1, half, model_dim), right_map),
            pl.BlockSpec(my_cols.shape, lambda j: (0, 0), pipeline_mode=pl.Buffered(1)),
            pl.BlockSpec(my_cols.shape, lambda j: (0, 0), pipeline_mode=pl.Buffered(1)),
            pl.BlockSpec(vec.shape, lambda j: (0, 0)),
        ],
        out_specs=[anywhere] * 5 + [pl.BlockSpec(vec.shape, lambda j: (0, 0))],
        scratch_shapes=[
            pltpu.VMEM((3, 2, model_dim, cols), bf16),
            pltpu.VMEM((steps, model_dim, cols), bf16),
            pltpu.VMEM((2,) + rest.shape, bf16),
            pltpu.VMEM((2, n_dp // 2, down_rows, cols), bf16),
            pltpu.VMEM((n_dp // 2, down_rows, cols), bf16),
            pltpu.VMEM((2,) + down.shape, bf16),
            pltpu.VMEM(vec.shape, f32),
            pltpu.SemaphoreType.DMA((steps,)),
            pltpu.SemaphoreType.DMA((steps,)),
            pltpu.SemaphoreType.DMA((2, parts)),
            pltpu.SemaphoreType.DMA((2,)),
            pltpu.SemaphoreType.DMA((2,)),
            pltpu.SemaphoreType.DMA((5,)),
        ],
        out_shape=[
            rest,
            rest,
            down,
            down,
            jax.ShapeDtypeStruct((2 * half, my_cols.shape[1]), bf16),
            jax.ShapeDtypeStruct(vec.shape, f32),
        ],
        compiler_params=pltpu.CompilerParams(
            collective_id=0, has_side_effects=True, vmem_limit_bytes=VMEM_LIMIT
        ),
        cost_estimate=pl.CostEstimate(flops=15_000_000_000, bytes_accessed=20_000_000, transcendentals=0),
    )(left, right, my_cols, their_cols, vec)


def final_kernel(
    n_dp,
    chunks,
    d_keep_any,
    d_got_any,
    s_keep_any,
    s_got_any,
    raw_any,
    rows_any,
    w_any,
    resid_any,
    vec_ref,
    raw_sums_ref,
    core_send_ref,
    core_recv_ref,
    qkv_ref,
    vec_out_ref,
    vec_core_ref,
    tokens_any,
    t_recv_any,
    d_keep_ref,
    d_got_ref,
    d_own_ref,
    d_out_ref,
    d_got_z_ref,
    s_keep_ref,
    s_got_ref,
    raw_ref,
    rows_ref,
    w_ref,
    resid_ref,
    s_send_ref,
    s_recv_ref,
    s_own_ref,
    s_out_ref,
    s_got_z_ref,
    s_sum_ref,
    q_grad_ref,
    q_both_ref,
    q_first_ref,
    q_send_ref,
    q_recv_ref,
    q_own_ref,
    q_out_ref,
    q_got_z_ref,
    t_send_ref,
    vec_hold_ref,
    vec_recv_ref,
    in_sems,
    d_z_sems,
    s_sems,
    s_z_sems,
    q_first_sems,
    q_sems,
    q_z_sems,
    t_sems,
    core_sems,
    vec_sems,
    out_sem,
):
    me, head = lax.axis_index("dp"), lax.axis_index("head")
    line = n_dp // 4
    depth = line.bit_length() - 1
    z = me // 4
    other = (me, 1 - head)
    low = (flip(me, 0), head)
    high = (flip(me, 1), head)
    around = [(((z + j) % line) * 4 + me % 4, head) for j in range(1, line)]
    first = (flip(me, 0) * (1 - head) + flip(me, 1) * head, head)
    second = (flip(me, 1) * (1 - head) + flip(me, 0) * head, head)
    mine = bit(me, 1) * (1 - head) + bit(me, 0) * head
    half, model_dim = resid_ref.shape
    local_dim = raw_ref.shape[1] // 3
    size = s_keep_ref.shape[1] // chunks
    q_chunks, _, _, q_size, _ = q_both_ref.shape
    q_rows = q_chunks * q_size

    def piece(i):
        return slice(i * size, (i + 1) * size)

    s_loads = [
        pltpu.make_async_copy(s_keep_any, s_keep_ref, in_sems.at[0]),
        pltpu.make_async_copy(s_got_any, s_got_ref, in_sems.at[1]),
    ]
    q_loads = [
        pltpu.make_async_copy(rows_any, rows_ref, in_sems.at[2]),
        pltpu.make_async_copy(raw_any, raw_ref, in_sems.at[3]),
    ]
    t_loads = [
        pltpu.make_async_copy(w_any, w_ref, in_sems.at[4]),
        pltpu.make_async_copy(resid_any, resid_ref, in_sems.at[5]),
    ]
    d_loads = [
        pltpu.make_async_copy(d_keep_any, d_keep_ref, in_sems.at[6]),
        pltpu.make_async_copy(d_got_any, d_got_ref, in_sems.at[7]),
    ]
    for load in s_loads + d_loads:
        load.start()
    greet([low, high, other] + around)

    vec_hold_ref[0] = vec_ref[...]
    here = pl.ds(pl.multiple_of(head * local_dim, LANES), local_dim)
    vec_hold_ref[0, 8:9, here] = raw_sums_ref[:, :local_dim]
    vec_hold_ref[0, 9:10, here] = raw_sums_ref[:, 2 * local_dim :]

    def vec_copy(k):
        to = (low, high)[k] if k < 2 else around[k - 2]
        source = vec_hold_ref.at[min(k, 2)]
        return remote(source, vec_recv_ref.at[k], vec_sems.at[0, k], vec_sems.at[1, k], to)

    vec_copy(0).start()

    def fold_line(own_ref, hold_ref, got_ref, sems):
        def moved(k):
            count = line >> (k + 1)
            at = slice(line - 2 * count, line - count)
            return remote(hold_ref.at[at], got_ref.at[at], sems.at[0, k], sems.at[1, k], (flip(me, k + 2), head))

        def send(k):
            count = line >> (k + 1)
            keep = bit(me, k + 2)
            for q in range(count):
                hold_ref[line - 2 * count + q] = own_ref[2 * q + 1 - keep].astype(bf16)
            moved(k).start()

        def add(k):
            count = line >> (k + 1)
            keep = bit(me, k + 2)
            moved(k).wait()
            for q in range(count):
                own_ref[q] = own_ref[2 * q + keep] + got_ref[line - 2 * count + q].astype(f32)
            if k + 1 < depth:
                send(k + 1)

        return send, add

    d_line = fold_line(d_own_ref, d_out_ref, d_got_z_ref, d_z_sems)

    def s_copy(i):
        return remote(s_send_ref.at[i], s_recv_ref.at[i], s_sems.at[0, i], s_sems.at[1, i], second)

    def s_total(block, i):
        return s_keep_ref[block, piece(i)].astype(f32) + s_got_ref[block, piece(i)].astype(f32)

    def s_prepare(i):
        def send_block(r, carry):
            s_send_ref[i, r] = s_total(2 * r + 1 - mine, i).astype(bf16)
            return carry

        lax.fori_loop(0, line, send_block, 0)

    for load in s_loads:
        load.wait()
    for load in q_loads:
        load.start()
    for load in t_loads:
        load.start()
    for i in range(chunks):
        s_prepare(i)
        s_copy(i).start()
    for load in d_loads:
        load.wait()

    def d_block(r, carry):
        d_own_ref[r] = d_keep_ref[r].astype(f32) + d_got_ref[r].astype(f32)
        return carry

    lax.fori_loop(0, line, d_block, 0)
    d_line[0](0)

    for load in q_loads:
        load.wait()

    def q_columns(j, carry):
        at = pl.ds(pl.multiple_of(j * Q_COLUMNS, LANES), Q_COLUMNS)
        grad = lax.dot_general(rows_ref[:, at], raw_ref[...], TN, preferred_element_type=f32)
        q_grad_ref[pl.ds(pl.multiple_of(j * Q_COLUMNS, LANES), Q_COLUMNS), :] = grad.astype(bf16)
        return carry

    lax.fori_loop(0, model_dim // Q_COLUMNS, q_columns, 0)
    d_line[1](0)

    def q_place(d, carry):
        send, place = route(d, me, head)
        for j in range(q_chunks):
            at = pl.ds(pl.multiple_of(d * q_rows + j * q_size, 16), q_size)
            q_both_ref[j, send, place] = q_grad_ref[at, :]
        return carry

    lax.fori_loop(0, n_dp, q_place, 0)

    def q_copy(j):
        return remote(q_both_ref.at[j, 1], q_first_ref.at[j], q_first_sems.at[0, j], q_first_sems.at[1, j], first)

    def q_second(j):
        return remote(q_send_ref.at[j], q_recv_ref.at[j], q_sems.at[0, j], q_sems.at[1, j], second)

    s_line = [
        fold_line(s_own_ref.at[i], s_out_ref.at[i], s_got_z_ref.at[i], s_z_sems.at[i]) for i in range(chunks)
    ]
    q_line = [
        fold_line(q_own_ref.at[j], q_out_ref.at[j], q_got_z_ref.at[j], q_z_sems.at[j]) for j in range(q_chunks)
    ]

    def s_enter(i):
        s_copy(i).wait()

        def add_block(r, carry):
            s_own_ref[i, r] = s_total(2 * r + mine, i) + s_recv_ref[i, r].astype(f32)
            return carry

        lax.fori_loop(0, line, add_block, 0)
        s_line[i][0](0)

    def q_total(j, block):
        return q_both_ref[j, 0, block].astype(f32) + q_first_ref[j, block].astype(f32)

    def q_enter(j):
        q_copy(j).wait()

        def send_block(r, carry):
            q_send_ref[j, r] = q_total(j, 2 * r + 1 - mine).astype(bf16)
            return carry

        lax.fori_loop(0, line, send_block, 0)
        q_second(j).start()

        def own_block(r, carry):
            q_own_ref[j, r] = q_total(j, 2 * r + mine)
            return carry

        lax.fori_loop(0, line, own_block, 0)

    def q_turn(j):
        q_second(j).wait()

        def add_block(r, carry):
            q_own_ref[j, r] = q_own_ref[j, r] + q_recv_ref[j, r].astype(f32)
            return carry

        lax.fori_loop(0, line, add_block, 0)
        q_line[j][0](0)

    tile_rows = half // 4

    def token_rows(who, tile):
        at = pl.ds(pl.multiple_of(who * half + tile * tile_rows, tile_rows), tile_rows)
        total = 0.0
        for c in range(3):
            part = raw_ref[at, c * local_dim : (c + 1) * local_dim]
            total = total + lax.dot_general(part, w_ref[c], NT, preferred_element_type=f32)
        return total

    t_copy = remote(t_send_ref, t_recv_any, t_sems.at[0], t_sems.at[1], other)

    def send_tile(tile, carry):
        at = pl.ds(pl.multiple_of(tile * tile_rows, tile_rows), tile_rows)
        t_send_ref[at, :] = token_rows(1 - head, tile).astype(bf16)
        return carry

    def own_tile(tile, carry):
        at = pl.ds(pl.multiple_of(tile * tile_rows, tile_rows), tile_rows)
        resid_ref[at, :] = resid_ref[at, :] + token_rows(head, tile)
        return carry

    for j in range(q_chunks):
        q_copy(j).start()
    s_enter(0)
    for load in t_loads:
        load.wait()
    lax.fori_loop(0, 4, send_tile, 0)
    t_copy.start()
    if chunks > 1:
        s_enter(1)
        s_line[0][1](0)
    lax.fori_loop(0, 4, own_tile, 0)
    t_out = pltpu.make_async_copy(resid_ref, tokens_any, out_sem)
    t_out.start()
    for i in range(2, chunks):
        s_enter(i)
        s_line[i - 1][1](0)
    vec_copy(0).wait()
    vec_hold_ref[1] = vec_hold_ref[0] + vec_recv_ref[0]
    vec_copy(1).start()
    q_enter(0)
    s_line[chunks - 1][1](0)
    for j in range(1, q_chunks):
        q_enter(j)
    vec_copy(1).wait()
    vec_hold_ref[2] = vec_hold_ref[1] + vec_recv_ref[1]
    for j in range(line - 1):
        vec_copy(2 + j).start()
    for j in range(q_chunks - 1):
        q_turn(j)
    d_rows = d_own_ref.shape[1]
    for k in range(1, depth):
        d_line[1](k)
    s_sum_ref[:d_rows, :] = d_own_ref[0]
    for i in range(chunks):
        for k in range(1, depth):
            s_line[i][1](k)
        s_sum_ref[d_rows + i * size : d_rows + (i + 1) * size, :] = s_own_ref[i, 0]
    pieces = core_pieces(s_sum_ref.shape[0], q_rows)

    def gather(target_ref, who):
        at = 0
        for start, count in pieces:
            here = pl.ds(pl.multiple_of(start + who * count, 8), count)
            target_ref[at : at + count, :] = s_sum_ref[here, :]
            at += count

    gather(core_send_ref.at[1], 1 - head)
    core_copy = remote(core_send_ref.at[1], core_recv_ref, core_sems.at[0], core_sems.at[1], other)
    core_copy.start()
    gather(core_send_ref.at[0], head)
    q_turn(q_chunks - 1)
    for j in range(line - 1):
        vec_copy(2 + j).wait()
    total = vec_hold_ref[2]
    for j in range(line - 1):
        total = total + vec_recv_ref[2 + j]
    vec_out_ref[...] = total
    core_vec = remote(vec_out_ref.at[pl.ds(8, 8)], vec_core_ref, core_sems.at[2], core_sems.at[3], other)
    core_vec.start()
    for k in range(depth):
        for j in range(q_chunks):
            q_line[j][1](k)
    for j in range(q_chunks):
        qkv_ref[j * q_size : (j + 1) * q_size, :] = q_own_ref[j, 0]
    core_vec.wait()
    core_copy.wait()
    t_copy.wait()
    t_out.wait()


def core_pieces(block_rows, rows):
    parts = (block_rows // rows - 1) // 2
    return [(0, parts * rows // 2)] + [(parts * rows + rows * c, rows // 2) for c in range(parts + 1)]


def final(n_dp, d_keep, d_got, s_keep, s_got, raw, group_rows, w_flat, resid, vec, raw_sums):
    line = n_dp // 4
    depth = line.bit_length() - 1
    _, rest_rows, cols = s_keep.shape
    down_rows = d_keep.shape[1]
    block_rows = down_rows + rest_rows
    half, model_dim = resid.shape
    local_dim = raw.shape[1] // 3
    q_rows, q_cols = model_dim // n_dp, 3 * local_dim
    chunks = 3 if rest_rows % 48 == 0 else 1
    size = rest_rows // chunks
    q_chunks = q_rows // 16
    anywhere = pl.BlockSpec(memory_space=pl.ANY)
    vmem = pl.BlockSpec(memory_space=pltpu.VMEM)

    def low(*dims):
        return pltpu.VMEM(dims, bf16)

    def wide(*dims):
        return pltpu.VMEM(dims, f32)

    def shape(*dims):
        return jax.ShapeDtypeStruct(dims, f32)

    def sems(*dims):
        return pltpu.SemaphoreType.DMA(dims)

    return pl.pallas_call(
        partial(final_kernel, n_dp, chunks),
        in_specs=[anywhere] * 8 + [vmem] * 2,
        out_specs=[vmem] * 5 + [anywhere] * 2,
        scratch_shapes=[
            low(*d_keep.shape),
            low(*d_keep.shape),
            wide(*d_keep.shape),
            low(*d_keep.shape),
            low(line - 1, down_rows, cols),
            low(*s_keep.shape),
            low(*s_keep.shape),
            low(*raw.shape),
            low(*group_rows.shape),
            low(*w_flat.shape),
            wide(half, model_dim),
            low(chunks, line, size, cols),
            low(chunks, line, size, cols),
            wide(chunks, line, size, cols),
            low(chunks, line, size, cols),
            low(chunks, line - 1, size, cols),
            wide(block_rows, cols),
            low(model_dim, q_cols),
            low(q_chunks, 2, 2 * line, 16, q_cols),
            low(q_chunks, 2 * line, 16, q_cols),
            low(q_chunks, line, 16, q_cols),
            low(q_chunks, line, 16, q_cols),
            wide(q_chunks, line, 16, q_cols),
            low(q_chunks, line, 16, q_cols),
            low(q_chunks, line - 1, 16, q_cols),
            low(half, model_dim),
            wide(3, *vec.shape),
            wide(1 + line, *vec.shape),
            sems(8),
            sems(2, depth),
            sems(2, chunks),
            sems(chunks, 2, depth),
            sems(2, q_chunks),
            sems(2, q_chunks),
            sems(q_chunks, 2, depth),
            sems(2),
            sems(4),
            sems(2, 1 + line),
            pltpu.SemaphoreType.DMA,
        ],
        out_shape=[
            shape(2, block_rows // 2, cols),
            shape(block_rows // 2, cols),
            shape(q_rows, q_cols),
            shape(*vec.shape),
            shape(8, model_dim),
            shape(half, model_dim),
            jax.ShapeDtypeStruct((half, model_dim), bf16),
        ],
        compiler_params=pltpu.CompilerParams(
            collective_id=1, has_side_effects=True, vmem_limit_bytes=VMEM_LIMIT
        ),
        cost_estimate=pl.CostEstimate(flops=12_000_000_000, bytes_accessed=25_000_000, transcendentals=0),
    )(d_keep, d_got, s_keep, s_got, raw, group_rows, w_flat, resid, vec, raw_sums)


def finish_kernel(
    n_dp,
    parts,
    own_ref,
    got_ref,
    kept_ref,
    core_ref,
    qkv_ref,
    vec_ref,
    vec_core_ref,
    tokens_ref,
    grad_qkv_ref,
    down_ref,
    in_ref,
    out_ref,
    qv_ref,
    in_bias_ref,
    term_ref,
    *vector_refs,
):
    tokens_ref[...] = own_ref[...] + got_ref[...].astype(f32)

    @pl.when(pl.program_id(0) == 0)
    def _():
        head = lax.axis_index("head")
        place = 2 * lax.axis_index("dp") + head
        cols = kept_ref.shape[2]
        model_dim = 2 * cols
        rows = out_ref.shape[0]
        width = model_dim // (2 * n_dp)
        starts = [0, parts * rows] + [parts * rows + rows * (c + 1) for c in range(parts + 1)]
        for who, source in ((head, kept_ref.at[0]), (1 - head, core_ref)):
            start = who * cols
            here = pl.ds(pl.multiple_of(start, LANES), cols)
            down_ref[:, here] = source[starts[0] : starts[1], :]
            for c in range(parts):
                shifted = pl.ds(pl.multiple_of(2 * cols * c + start, LANES), cols)
                in_ref[:, shifted] = source[starts[1 + c] : starts[2 + c], :]
            out_ref[:, here] = source[starts[1 + parts] : starts[2 + parts], :]
        for c in range(3):
            grad_qkv_ref[c] = qkv_ref[:, c * cols : (c + 1) * cols]
        shift = lax.rem(model_dim - place * width, model_dim)
        turned = pltpu.roll(vec_ref[0:8], shift, 1)
        for j, ref in enumerate(vector_refs):
            ref[...] = turned[j : j + 1, :width]
        term_ref[...] = vec_ref[7:8, :1]
        turned = pltpu.roll(vec_ref[8:16] + vec_core_ref[...], shift, 1)
        qv_ref[...] = turned[:, :width]
        in_width = parts * model_dim // (2 * n_dp)
        per_row = model_dim // in_width
        row = vec_ref[pl.ds(10 + place // per_row, 1), :]
        row = jnp.broadcast_to(row, (8, model_dim))
        turned = pltpu.roll(row, lax.rem(model_dim - (place % per_row) * in_width, model_dim), 1)
        in_bias_ref[...] = turned[0:1, :in_width]


def finish(n_dp, parts, kept, core, qkv, vec, vec_core, own, got):
    half, model_dim = own.shape
    q_rows = qkv.shape[0]
    width = model_dim // (2 * n_dp)
    rows = min(512, half)
    tile = pl.BlockSpec((rows, model_dim), lambda i: (i, 0))

    def whole(dims):
        return pl.BlockSpec(dims, lambda i: (0,) * len(dims))

    out = [
        (3, q_rows, model_dim // 2),
        (parts * width, model_dim),
        (width, parts * model_dim),
        (width, model_dim),
        (8, width),
        (1, parts * width),
        (1, 1),
    ] + [(1, width)] * 7
    return pl.pallas_call(
        partial(finish_kernel, n_dp, parts),
        grid=(half // rows,),
        in_specs=[tile, tile] + [whole(x.shape) for x in (kept, core, qkv, vec, vec_core)],
        out_specs=[tile] + [whole(dims) for dims in out],
        out_shape=[jax.ShapeDtypeStruct((half, model_dim), f32)] + [jax.ShapeDtypeStruct(dims, f32) for dims in out],
        compiler_params=pltpu.CompilerParams(vmem_limit_bytes=VMEM_LIMIT),
        cost_estimate=pl.CostEstimate(flops=1_000_000, bytes_accessed=10_000_000, transcendentals=0),
    )(own, got, kept, core, qkv, vec, vec_core)


def take(array, index, axis=0):
    return lax.dynamic_index_in_dim(array, index, axis, keepdims=False)


class Links:
    def __init__(self, n_dp):
        self.n_dp = n_dp
        self.bits = n_dp.bit_length() - 1
        self.dp = lax.axis_index("dp")
        self.head = lax.axis_index("head")

    def bit(self, which):
        return (self.dp >> which) & 1

    def permute(self, array, partner):
        pairs = []
        for d in range(self.n_dp):
            for h in range(2):
                to_d, to_h = partner(d, h)
                pairs.append((2 * d + h, 2 * to_d + to_h))
        return lax.ppermute(array, AXES, pairs)

    def swap_head(self, array):
        return self.permute(array, lambda d, h: (d, 1 - h))

    def swap_bit(self, array, which):
        return self.permute(array, lambda d, h: (d ^ (1 << which), h))

    def scatter_heads(self, blocks):
        got = self.swap_head(take(blocks, 1 - self.head, 1))
        return (take(blocks, self.head, 1).astype(f32) + got.astype(f32)).astype(bf16)

    def scatter_dp(self, blocks):
        tail = blocks.shape[1:]
        b0, b1 = self.bit(0), self.bit(1)
        first = self.head == 0
        blocks = blocks.reshape((self.n_dp // 4, 4) + tail)

        def two(one, other):
            i = jnp.where(first, one, 2 * other)
            j = jnp.where(first, 2 + one, 2 * other + 1)
            return jnp.stack([take(blocks, i, 1), take(blocks, j, 1)], axis=1)

        got = self.permute(two(1 - b0, 1 - b1), lambda d, h: (d ^ (1 if h == 0 else 2), h))
        blocks = (two(b0, b1).astype(f32) + got.astype(f32)).astype(bf16)
        mine = jnp.where(first, b1, b0)
        got = self.permute(take(blocks, 1 - mine, 1), lambda d, h: (d ^ (2 if h == 0 else 1), h))
        blocks = take(blocks, mine, 1).astype(f32) + got.astype(f32)
        for which in range(2, self.bits):
            blocks = blocks.reshape((-1, 2) + tail)
            mine = self.bit(which)
            got = self.swap_bit(take(blocks, 1 - mine, 1).astype(bf16), which)
            blocks = take(blocks, mine, 1) + got.astype(f32)
        return blocks.reshape(tail)

    def total(self, array):
        array = array + self.swap_head(array)
        for which in range(self.bits):
            array = array + self.swap_bit(array, which)
        return array


def shards(
    n_dp,
    tokens,
    lengths,
    w_qkv,
    bias_qv,
    w_out,
    bias_out,
    ln1_gain,
    ln1_bias,
    w_in,
    bias_in,
    w_down,
    bias_down,
    ln2_gain,
    ln2_bias,
    term_w,
    term_bias,
    grad_hidden,
    grad_term,
):
    links = Links(n_dp)
    head = links.head
    half, model_dim = tokens.shape
    row_len = 2 * half
    local_dim = w_qkv.shape[2]
    ffn_dim = w_in.shape[1]

    boundary = jnp.cumsum(lengths[0])
    places = jnp.arange(row_len, dtype=jnp.int32)
    segment = jnp.sum((places[:, None] >= boundary[None, :]).astype(jnp.int32), axis=-1)
    seg_col = jnp.broadcast_to(segment[:, None], (row_len, LANES))
    seg_row = jnp.broadcast_to(segment[None, :], (8, row_len))

    def both(mine, theirs, axis):
        return jnp.where(
            head == 0,
            jnp.concatenate([mine, theirs], axis=axis),
            jnp.concatenate([theirs, mine], axis=axis),
        )

    w_parts = jnp.transpose(w_qkv, (1, 0, 2))
    group_rows, queries, key_rows, value_rows = project(tokens, w_parts, bias_qv.T)
    theirs, mine, logs = attend(lengths, head, queries, key_rows, value_rows, seg_col, seg_row)

    def my_half(rows):
        return lax.dynamic_slice_in_dim(rows, head * half, half, 0)

    def their_half(rows):
        return lax.dynamic_slice_in_dim(rows, (1 - head) * half, half, 0)

    vec = jnp.stack([bias_out, ln1_gain, ln1_bias, bias_down, ln2_gain, ln2_bias, term_w, jnp.zeros_like(term_w)])
    hidden_out, term_weight, left, right, resid_one_grad, my_cols, their_cols, vec = middle(
        mine,
        links.swap_head(theirs),
        tokens,
        grad_hidden,
        grad_term[None, :],
        w_out,
        w_in,
        w_down,
        vec,
        bias_in[None, :],
        term_bias[None, :],
    )
    parts = ffn_dim // model_dim
    in_kernels = (model_dim // n_dp) % 16 == 0 and n_dp == 4 * parts

    def back(grads):
        return attend_back(lengths, queries, key_rows, value_rows, grads, logs, seg_col, seg_row)

    if in_kernels:
        s_keep, s_send, d_keep, d_send, head_grad, vec = weights(n_dp, left, right, my_cols, their_cols, vec)
        d_got = links.permute(d_send, lambda d, h: (d ^ (2 if h == 0 else 1), h))
        s_got = links.permute(s_send, lambda d, h: (d ^ (1 if h == 0 else 2), h))
        raw, raw_sums = back(head_grad)
        kept, core, qkv, vec, vec_core, own, got = final(
            n_dp, d_keep, d_got, s_keep, s_got, raw, group_rows, w_parts, resid_one_grad, vec, raw_sums
        )
        (grad_tokens, grad_qkv, grad_down, grad_in, grad_out, bias_qv_mine, bias_in_mine, term_total, *vectors) = finish(
            n_dp, parts, kept, core, qkv, vec, vec_core, own, got
        )
        grad_qkv = jnp.transpose(grad_qkv, (1, 0, 2))
        bias_qv_mine = bias_qv_mine[:2].T
        bias_in_mine = bias_in_mine.reshape(-1)
        term_total = term_total.reshape(1)
        mine = [v.reshape(-1) for v in vectors]
    else:
        raw, raw_sums = back(both(my_cols, links.swap_head(their_cols), 0))

        def product(i, j):
            return lax.dot_general(left[i], right[j], TN, preferred_element_type=f32).astype(bf16)

        def reduced(partial_sum):
            rows, cols = partial_sum.shape
            return links.scatter_dp(links.scatter_heads(partial_sum.reshape(n_dp, 2, rows // (2 * n_dp), cols)))

        grad_down = reduced(jnp.concatenate([product(i, 0) for i in range(parts)]))
        grad_in = reduced(jnp.concatenate([product(parts, 1 + i) for i in range(parts)], axis=1))
        grad_out = reduced(product(parts + 1, parts + 1))
        w_flat = w_qkv.reshape(model_dim, 3 * local_dim)
        grad = lax.dot_general(raw, w_flat, NT, preferred_element_type=f32)
        received = links.swap_head(their_half(grad).astype(bf16))
        grad_tokens = resid_one_grad + my_half(grad) + received.astype(f32)
        qkv_local = lax.dot_general(group_rows, raw, TN, preferred_element_type=f32).astype(bf16)
        grad_qkv = links.scatter_dp(qkv_local.reshape(n_dp, model_dim // n_dp, 3 * local_dim))
        value_sums = lax.dynamic_update_slice(
            jnp.zeros((2, 2 * local_dim), f32),
            jnp.concatenate([raw_sums[:, :local_dim], raw_sums[:, 2 * local_dim :]]),
            (jnp.int32(0), head * local_dim),
        )
        vectors = links.total(lax.dynamic_update_slice(vec, value_sums, (8, 0)))
        grad_qkv = grad_qkv.reshape(model_dim // n_dp, 3, local_dim)
        place = 2 * links.dp + head
        width = model_dim // (2 * n_dp)
        mine = lax.dynamic_slice_in_dim(vectors, place * width, width, 1)
        in_width = ffn_dim // (2 * n_dp)
        in_row = vectors[10 : 10 + parts].reshape(-1)
        bias_in_mine = lax.dynamic_slice_in_dim(in_row, place * in_width, in_width, 0)
        bias_qv_mine = mine[8:10].T
        term_total = vectors[7, :1]

    return (
        hidden_out,
        term_weight.reshape(-1),
        grad_tokens,
        grad_qkv,
        bias_qv_mine,
        grad_out,
        mine[0],
        mine[1],
        mine[2],
        grad_in,
        bias_in_mine,
        grad_down,
        mine[3],
        mine[4],
        mine[5],
        mine[6],
        term_total,
    )


def solution(mesh):
    rows = P(AXES, None)
    return jax.shard_map(
        partial(shards, mesh.shape["dp"]),
        mesh=mesh,
        in_specs=(rows, P("dp", None), P(None, None, "head"), P("head", None))
        + (P(),) * 12
        + (rows, P(AXES)),
        out_specs=(
            rows,
            P(AXES),
            rows,
            P("dp", None, "head"),
            rows,
            rows,
            P(AXES),
            P(AXES),
            P(AXES),
            rows,
            P(AXES),
            rows,
            P(AXES),
            P(AXES),
            P(AXES),
            P(AXES),
            P(),
        ),
        check_vma=False,
    )
```

```python
from functools import partial

import jax
import jax.numpy as jnp
from jax import lax
from jax.experimental import pallas as pl
from jax.experimental.pallas import tpu as pltpu
from jax.sharding import PartitionSpec as P

HEAD_DIM = 64
LANES = 128
VMEM_LIMIT = 60 * 2**20
Q_ROWS = 256
PIECE = 32
Q_COLUMNS = 128
WIDTHS = (2, 3, 4, 5, 6, 8, 10)
BACK_WIDTHS = (2, 3, 4, 5, 6, 7, 8, 10)
AXES = ("dp", "head")

f32 = jnp.float32
bf16 = jnp.bfloat16
norm_eps = 1e-06
NT = (((1,), (1,)), ((), ()))
TN = (((0,), (0,)), ((), ()))


def key_range(lengths_ref, first, rows, row_len):
    start = jnp.int32(0)
    low = jnp.int32(0)
    high = jnp.int32(row_len)
    for j in range(lengths_ref.shape[1]):
        end = start + lengths_ref[0, j]
        low = jnp.where(start <= first, start, low)
        high = jnp.where(end >= first + rows, jnp.minimum(high, end), high)
        start = end
    low_block = low // LANES
    count = (high + LANES - 1) // LANES - low_block
    return low_block, count


def by_width(lengths_ref, first, rows, row_len, body, choices=WIDTHS):
    blocks = row_len // LANES
    low_block, count = key_range(lengths_ref, first, rows, row_len)
    widths = sorted({min(w, blocks) for w in choices})
    below = 0
    for width in widths:

        @pl.when((count > below) & (count <= width))
        def _(width=width):
            begin = jnp.minimum(low_block, blocks - width)
            body(pl.multiple_of(begin * LANES, LANES), width * LANES)

        below = width


def query_block(step, steps, head):
    return lax.rem(step + (1 - head) * (steps // 2), steps)


def attend_kernel(
    lengths_ref,
    head_ref,
    q_ref,
    k_ref,
    v_ref,
    segc_ref,
    segr_ref,
    theirs_ref,
    mine_ref,
    log_ref,
    mask_ref,
    cols_ref,
    s_ref,
    p_ref,
    o_ref,
):
    rows, local_dim = q_ref.shape
    row_len = k_ref.shape[0]
    step, steps = pl.program_id(0), pl.num_programs(0)
    first = query_block(step, steps, head_ref[0]) * rows
    lane = lax.broadcasted_iota(jnp.int32, (rows, LANES), 1)

    def body(begin, width):
        same = segc_ref[:, 0:1] == segr_ref[0:1, pl.ds(begin, width)]
        mask_ref[:, :width] = jnp.where(same, 0.0, -1e30)

        heads = local_dim // HEAD_DIM

        def score(i):
            cols = slice(i // 2 * LANES, i // 2 * LANES + LANES)
            q_pair = q_ref[:, cols]
            q_one = jnp.where((lane // HEAD_DIM) == i % 2, q_pair, jnp.zeros_like(q_pair))
            k_pair = k_ref[pl.ds(begin, width), cols]
            s_ref[i % 2, :, :width] = lax.dot_general(q_one, k_pair, NT, preferred_element_type=f32)

        def soft(i):
            for r in range(0, rows, PIECE):
                part = slice(r, r + PIECE)
                scores = s_ref[i % 2, part, :width] + mask_ref[part, :width]
                row_max = jnp.max(scores, axis=1, keepdims=True)
                powers = jnp.exp(scores - row_max)
                total = jnp.sum(powers, axis=1, keepdims=True)
                p_ref[i % 2, part, :width] = (powers * (1.0 / total)).astype(bf16)
                log_total = row_max + jnp.log(total)
                cols_ref[part] = jnp.where(lane[part] == i, log_total, cols_ref[part])

        def value(i):
            cols = slice(i // 2 * LANES, i // 2 * LANES + LANES)
            return jnp.dot(p_ref[i % 2, :, :width], v_ref[pl.ds(begin, width), cols], preferred_element_type=f32)

        score(0)
        held = None
        for i in range(heads):
            if i + 1 < heads:
                score(i + 1)
            soft(i)
            out = value(i)
            if i % 2 == 0:
                held = out
            else:
                cols = slice(i // 2 * LANES, i // 2 * LANES + LANES)
                o_ref[:, cols] = jnp.where(lane < HEAD_DIM, held, out).astype(bf16)

    by_width(lengths_ref, first, rows, row_len, body)
    log_ref[...] = cols_ref[...].T[: log_ref.shape[0]]

    @pl.when(step < steps // 2)
    def _():
        theirs_ref[...] = o_ref[...]

    @pl.when(step >= steps // 2)
    def _():
        mine_ref[...] = o_ref[...]


def attend(lengths, head, queries, key_rows, value_rows, seg_col, seg_row):
    row_len, local_dim = queries.shape
    rows = min(Q_ROWS, row_len // 2)
    steps = row_len // rows
    whole = pl.BlockSpec((row_len, local_dim), lambda i, n, h: (0, 0))
    return pl.pallas_call(
        attend_kernel,
        grid_spec=pltpu.PrefetchScalarGridSpec(
            num_scalar_prefetch=2,
            grid=(steps,),
            in_specs=[
                pl.BlockSpec((rows, local_dim), lambda i, n, h: (query_block(i, steps, h[0]), 0)),
                whole,
                whole,
                pl.BlockSpec((rows, LANES), lambda i, n, h: (query_block(i, steps, h[0]), 0)),
                pl.BlockSpec((8, row_len), lambda i, n, h: (0, 0)),
            ],
            out_specs=[
                pl.BlockSpec((rows, local_dim), lambda i, n, h: (jnp.minimum(i, steps // 2 - 1), 0)),
                pl.BlockSpec((rows, local_dim), lambda i, n, h: (jnp.maximum(i - steps // 2, 0), 0)),
                pl.BlockSpec((8, rows), lambda i, n, h: (0, query_block(i, steps, h[0]))),
            ],
            scratch_shapes=[
                pltpu.VMEM((rows, max(WIDTHS) * LANES), f32),
                pltpu.VMEM((rows, LANES), f32),
                pltpu.VMEM((2, rows, max(WIDTHS) * LANES), f32),
                pltpu.VMEM((2, rows, max(WIDTHS) * LANES), bf16),
                pltpu.VMEM((rows, local_dim), bf16),
            ],
        ),
        out_shape=[
            jax.ShapeDtypeStruct((row_len // 2, local_dim), bf16),
            jax.ShapeDtypeStruct((row_len // 2, local_dim), bf16),
            jax.ShapeDtypeStruct((8, row_len), f32),
        ],
        compiler_params=pltpu.CompilerParams(vmem_limit_bytes=VMEM_LIMIT),
        cost_estimate=pl.CostEstimate(flops=20_000_000_000, bytes_accessed=8_000_000, transcendentals=0),
    )(lengths, head[None], queries, key_rows, value_rows, seg_col, seg_row)


def attend_back_kernel(
    lengths_ref,
    q_ref,
    k_ref,
    v_ref,
    g_ref,
    log_ref,
    segc_ref,
    segr_ref,
    raw_ref,
    sums_ref,
    mask_ref,
    dk_ref,
    dv_ref,
    s_ref,
    d_ref,
    p_ref,
    e_ref,
    ones_ref,
):
    rows, local_dim = q_ref.shape
    row_len = k_ref.shape[0]
    step = pl.program_id(0)
    first = step * rows
    lane = lax.broadcasted_iota(jnp.int32, (rows, LANES), 1)

    @pl.when(step == 0)
    def _():
        dk_ref[...] = jnp.zeros_like(dk_ref)
        dv_ref[...] = jnp.zeros_like(dv_ref)

    def body(begin, width):
        keys = pl.ds(begin, width)
        same = segc_ref[keys, 0:1] == segr_ref[0:1, :]
        mask_ref[:width, :] = jnp.where(same, 0.0, -1e30)

        def pair_step(pair, carry):
            cols = pl.ds(pl.multiple_of(pair * LANES, LANES), LANES)

            def products(i):
                mine = (lane // HEAD_DIM) == i
                here = slice(i * rows, i * rows + rows)
                q_pair, g_pair = q_ref[:, cols], g_ref[:, cols]
                q_one = jnp.where(mine, q_pair, jnp.zeros_like(q_pair))
                g_one = jnp.where(mine, g_pair, jnp.zeros_like(g_pair))
                ones_ref[0, here] = q_one
                ones_ref[1, here] = g_one
                s_ref[i, :width] = lax.dot_general(k_ref[keys, cols], q_one, NT, preferred_element_type=f32)
                d_ref[i, :width] = lax.dot_general(v_ref[keys, cols], g_one, NT, preferred_element_type=f32)

            def soft(i):
                here = slice(i * rows, i * rows + rows)
                log_row = log_ref[pl.ds(2 * pair + i, 1), :]
                inner = jnp.zeros((8, rows), f32)
                for r in range(0, width, PIECE):
                    part = slice(r, r + PIECE)
                    probs = jnp.exp(s_ref[i, part] + mask_ref[part] - log_row)
                    s_ref[i, part] = probs
                    p_ref[part, here] = probs.astype(bf16)
                    inner = inner + jnp.sum((probs * d_ref[i, part]).reshape(PIECE // 8, 8, rows), axis=0)
                inner = jnp.sum(inner, axis=0, keepdims=True)
                for r in range(0, width, PIECE):
                    part = slice(r, r + PIECE)
                    e_ref[part, here] = (s_ref[i, part] * (d_ref[i, part] - inner)).astype(bf16)

            def gather(i):
                here = slice(i * rows, i * rows + rows)
                dv_ref[keys, cols] += jnp.dot(p_ref[:width, here], ones_ref[1, here], preferred_element_type=f32)
                dk_ref[keys, cols] += jnp.dot(e_ref[:width, here], ones_ref[0, here], preferred_element_type=f32)
                return lax.dot_general(e_ref[:width, here], k_ref[keys, cols], TN, preferred_element_type=f32)

            products(0)
            products(1)
            soft(0)
            dq_first = gather(0)
            soft(1)
            dq_second = gather(1)
            dq_low = jnp.where(lane < HEAD_DIM, dq_first, dq_second).astype(bf16)
            raw_ref[pl.ds(pl.multiple_of(first, rows), rows), cols] = dq_low * jnp.asarray(HEAD_DIM**-0.5, bf16)
            return carry

        lax.fori_loop(0, local_dim // LANES, pair_step, 0)

    by_width(lengths_ref, first, rows, row_len, body, BACK_WIDTHS)

    @pl.when(step == pl.num_programs(0) - 1)
    def _():
        raw_ref[:, local_dim : 2 * local_dim] = dk_ref[...].astype(bf16)
        raw_ref[:, 2 * local_dim :] = dv_ref[...].astype(bf16)
        sums_ref[...] = jnp.sum(raw_ref[...].astype(f32), axis=0, keepdims=True)


def attend_back(lengths, queries, key_rows, value_rows, grads, logs, seg_col, seg_row):
    row_len, local_dim = queries.shape
    rows = min(Q_ROWS, row_len)
    whole = pl.BlockSpec((row_len, local_dim), lambda i, n: (0, 0))
    block = pl.BlockSpec((rows, local_dim), lambda i, n: (i, 0))
    return pl.pallas_call(
        attend_back_kernel,
        grid_spec=pltpu.PrefetchScalarGridSpec(
            num_scalar_prefetch=1,
            grid=(row_len // rows,),
            in_specs=[
                block,
                whole,
                whole,
                block,
                pl.BlockSpec((8, rows), lambda i, n: (0, i)),
                pl.BlockSpec((row_len, LANES), lambda i, n: (0, 0)),
                pl.BlockSpec((8, rows), lambda i, n: (0, i)),
            ],
            out_specs=[
                pl.BlockSpec((row_len, 3 * local_dim), lambda i, n: (0, 0)),
                pl.BlockSpec((1, 3 * local_dim), lambda i, n: (0, 0)),
            ],
            scratch_shapes=[
                pltpu.VMEM((max(WIDTHS) * LANES, rows), f32),
                pltpu.VMEM((row_len, local_dim), f32),
                pltpu.VMEM((row_len, local_dim), f32),
                pltpu.VMEM((2, max(WIDTHS) * LANES, rows), f32),
                pltpu.VMEM((2, max(WIDTHS) * LANES, rows), f32),
                pltpu.VMEM((max(WIDTHS) * LANES, 2 * rows), bf16),
                pltpu.VMEM((max(WIDTHS) * LANES, 2 * rows), bf16),
                pltpu.VMEM((2, 2 * rows, LANES), bf16),
            ],
        ),
        out_shape=[
            jax.ShapeDtypeStruct((row_len, 3 * local_dim), bf16),
            jax.ShapeDtypeStruct((1, 3 * local_dim), f32),
        ],
        compiler_params=pltpu.CompilerParams(vmem_limit_bytes=VMEM_LIMIT),
        cost_estimate=pl.CostEstimate(flops=40_000_000_000, bytes_accessed=12_000_000, transcendentals=0),
    )(lengths, queries, key_rows, value_rows, grads, logs, seg_col, seg_row)


TILE = 256


def gelu_both(x):
    cdf = 0.5 + 0.5 * lax.erf(x * 0.7071067811865476)
    density = jnp.exp(-0.5 * x * x) * 0.3989422804014327
    return x * cdf, cdf + x * density


def normalize(resid):
    center = resid - jnp.mean(resid, axis=-1, keepdims=True)
    scale = lax.rsqrt(jnp.mean(center * center, axis=-1, keepdims=True) + norm_eps)
    return center * scale, scale


def normalize_back(grad, normed, scale):
    shift = jnp.mean(grad, axis=-1, keepdims=True)
    slope = jnp.mean(grad * normed, axis=-1, keepdims=True)
    return scale * (grad - shift - normed * slope)


def fold(x):
    return jnp.sum(x.astype(f32).reshape(x.shape[0] // 8, 8, x.shape[1]), axis=0)


def middle_kernel(
    mine_ref,
    theirs_ref,
    tokens_ref,
    hid_ref,
    term_ref,
    w_out_ref,
    w_in_ref,
    w_down_ref,
    vec_ref,
    bias_in_ref,
    term_bias_ref,
    hidden_ref,
    weight_ref,
    left_ref,
    right_ref,
    resid_ref,
    my_grad_ref,
    their_grad_ref,
    sums_ref,
    slope_ref,
    wide_ref,
    x_ref,
    normal_ref,
    scale_ref,
    fold_ref,
    in_fold_ref,
    term_cols_ref,
    term_in_ref,
):
    head = lax.axis_index("head")
    local_dim = mine_ref.shape[1]
    model_dim = w_out_ref.shape[0]
    parts = w_in_ref.shape[1] // model_dim
    rows = tokens_ref.shape[0]
    pieces = [slice(r, r + PIECE) for r in range(0, rows, PIECE)]
    bias_out, ln1_gain, ln1_bias = vec_ref[0:1], vec_ref[1:2], vec_ref[2:3]
    bias_down, ln2_gain, ln2_bias, term_w = vec_ref[3:4], vec_ref[4:5], vec_ref[5:6], vec_ref[6:7]

    @pl.when(pl.program_id(0) == 0)
    def _():
        fold_ref[...] = jnp.zeros_like(fold_ref)
        in_fold_ref[...] = jnp.zeros_like(in_fold_ref)

    term_in_ref[...] = jnp.broadcast_to(term_ref[...], (LANES, rows)).T
    left_ref[parts + 1, :, pl.ds(pl.multiple_of(head * local_dim, LANES), local_dim)] = mine_ref[...]
    left_ref[parts + 1, :, pl.ds(pl.multiple_of((1 - head) * local_dim, LANES), local_dim)] = theirs_ref[...]
    x_ref[...] = jnp.dot(left_ref[parts + 1], w_out_ref[...], preferred_element_type=f32)
    for r in pieces:
        normal, scale = normalize(tokens_ref[r].astype(f32) + (x_ref[r] + bias_out))
        normed = normal * ln1_gain + ln1_bias
        normal_ref[r] = normal
        scale_ref[r] = scale
        left_ref[parts, r] = normed.astype(bf16)
        x_ref[r] = normed + bias_down

    def columns(c):
        return slice(c * model_dim, (c + 1) * model_dim)

    def rise(c):
        wide_ref[c % 2] = jnp.dot(left_ref[parts], w_in_ref[:, columns(c)], preferred_element_type=f32)

    rise(0)
    for c in range(parts):
        if c + 1 < parts:
            rise(c + 1)
        for r in pieces:
            value, slope = gelu_both(wide_ref[c % 2, r] + bias_in_ref[:, columns(c)])
            left_ref[c, r] = value.astype(bf16)
            slope_ref[r, columns(c)] = slope
        x_ref[...] += jnp.dot(left_ref[c], w_down_ref[columns(c), :], preferred_element_type=f32)

    for r in pieces:
        normal, scale = normalize(x_ref[r])
        normed = normal * ln2_gain + ln2_bias
        hidden_ref[r] = normed.astype(bf16)
        logit = jnp.sum(normed * term_w, axis=-1, keepdims=True) + term_bias_ref[0:1, 0:1]
        small = jnp.exp(-jnp.abs(logit))
        term_cols_ref[r] = jnp.broadcast_to(jnp.maximum(logit, 0.0) + jnp.log1p(small), (PIECE, LANES))
        logit_grad = term_in_ref[r, 0:1] * (jnp.where(logit >= 0.0, 1.0, small) / (1.0 + small))
        two_grad = hid_ref[r] + logit_grad * term_w
        resid_two = normalize_back(two_grad * ln2_gain, normal, scale)
        low = resid_two.astype(bf16)
        right_ref[0, r] = low
        x_ref[r] = resid_two
        fold_ref[3] += fold(low)
        fold_ref[4] += fold(two_grad * normal)
        fold_ref[5] += fold(two_grad)
        fold_ref[6] += fold(logit_grad * normed)
        fold_ref[7] += fold(jnp.broadcast_to(logit_grad, normal.shape))

    weight_ref[...] = term_cols_ref[...].T[0:1]

    def fall(c):
        wide_ref[c % 2] = lax.dot_general(right_ref[0], w_down_ref[columns(c), :], NT, preferred_element_type=f32)

    fall(0)
    for c in range(parts):
        if c + 1 < parts:
            fall(c + 1)
        for r in pieces:
            low = (wide_ref[c % 2, r] * slope_ref[r, columns(c)]).astype(bf16)
            right_ref[1 + c, r] = low
            in_fold_ref[:, columns(c)] += fold(low)
        x_ref[...] += lax.dot_general(right_ref[1 + c], w_in_ref[:, columns(c)], NT, preferred_element_type=f32)

    for r in pieces:
        one_grad = x_ref[r]
        normal = normal_ref[r]
        resid_one = normalize_back(one_grad * ln1_gain, normal, scale_ref[r])
        resid_ref[r] = resid_one
        low = resid_one.astype(bf16)
        right_ref[parts + 1, r] = low
        fold_ref[0] += fold(low)
        fold_ref[1] += fold(one_grad * normal)
        fold_ref[2] += fold(one_grad)
    grads = lax.dot_general(right_ref[parts + 1], w_out_ref[...], NT, preferred_element_type=f32).astype(bf16)

    @pl.when(head == 0)
    def _():
        my_grad_ref[...] = grads[:, :local_dim]
        their_grad_ref[...] = grads[:, local_dim:]

    @pl.when(head == 1)
    def _():
        my_grad_ref[...] = grads[:, local_dim:]
        their_grad_ref[...] = grads[:, :local_dim]

    @pl.when(pl.program_id(0) == pl.num_programs(0) - 1)
    def _():
        sums_ref[...] = jnp.zeros_like(sums_ref)
        sums_ref[0:8] = jnp.sum(fold_ref[...], axis=1)
        for c in range(parts):
            sums_ref[10 + c : 11 + c] = jnp.sum(in_fold_ref[:, columns(c)], axis=0, keepdims=True)


def middle(mine, theirs, tokens, grad_hidden, grad_term, w_out, w_in, w_down, vec, bias_in, term_bias):
    half, model_dim = tokens.shape
    local_dim = mine.shape[1]
    ffn_dim = w_in.shape[1]
    rows = min(TILE, half)

    def tile(cols):
        return pl.BlockSpec((rows, cols), lambda i: (i, 0))

    def whole(*shape):
        return pl.BlockSpec(shape, lambda i: (0, 0), pipeline_mode=pl.Buffered(1))

    stacked = pl.BlockSpec((ffn_dim // model_dim + 2, rows, model_dim), lambda i: (0, i, 0))
    stack = jax.ShapeDtypeStruct((ffn_dim // model_dim + 2, half, model_dim), bf16)

    def full(cols, kind):
        return jax.ShapeDtypeStruct((half, cols), kind)

    return pl.pallas_call(
        middle_kernel,
        grid=(half // rows,),
        in_specs=[
            tile(local_dim),
            tile(local_dim),
            tile(model_dim),
            tile(model_dim),
            pl.BlockSpec((1, rows), lambda i: (0, i)),
            whole(model_dim, model_dim),
            whole(model_dim, ffn_dim),
            whole(ffn_dim, model_dim),
            whole(8, model_dim),
            whole(1, ffn_dim),
            whole(1, 1),
        ],
        out_specs=[
            tile(model_dim),
            pl.BlockSpec((1, rows), lambda i: (0, i)),
            stacked,
            stacked,
            tile(model_dim),
            tile(local_dim),
            tile(local_dim),
            pl.BlockSpec((16, model_dim), lambda i: (0, 0)),
        ],
        scratch_shapes=[
            pltpu.VMEM((rows, ffn_dim), f32),
            pltpu.VMEM((2, rows, model_dim), f32),
            pltpu.VMEM((rows, model_dim), f32),
            pltpu.VMEM((rows, model_dim), f32),
            pltpu.VMEM((rows, 1), f32),
            pltpu.VMEM((8, 8, model_dim), f32),
            pltpu.VMEM((8, ffn_dim), f32),
            pltpu.VMEM((rows, LANES), f32),
            pltpu.VMEM((rows, LANES), f32),
        ],
        out_shape=[
            full(model_dim, bf16),
            jax.ShapeDtypeStruct((1, half), f32),
            stack,
            stack,
            full(model_dim, f32),
            full(local_dim, bf16),
            full(local_dim, bf16),
            jax.ShapeDtypeStruct((16, model_dim), f32),
        ],
        compiler_params=pltpu.CompilerParams(vmem_limit_bytes=VMEM_LIMIT),
        cost_estimate=pl.CostEstimate(flops=40_000_000_000, bytes_accessed=50_000_000, transcendentals=0),
    )(mine, theirs, tokens, grad_hidden, grad_term, w_out, w_in, w_down, vec, bias_in, term_bias)


def bit(place, which):
    return (place // 2**which) % 2


def flip(place, which):
    return place + (1 - 2 * bit(place, which)) * 2**which


def route(target, me, head):
    low, high = bit(target, 0), bit(target, 1)
    send = (1 - head) * ((low + bit(me, 0)) % 2) + head * ((high + bit(me, 1)) % 2)
    return send, 2 * (target // 4) + (1 - head) * high + head * low


def greet(partners):
    barrier = pltpu.get_barrier_semaphore()
    for partner in partners:
        pl.semaphore_signal(barrier, inc=1, device_id=partner, device_id_type=pl.DeviceIdType.MESH)
    pl.semaphore_wait(barrier, len(partners))


def remote(source, target, send_sem, recv_sem, partner):
    return pltpu.make_async_remote_copy(
        src_ref=source,
        dst_ref=target,
        send_sem=send_sem,
        recv_sem=recv_sem,
        device_id=partner,
        device_id_type=pl.DeviceIdType.MESH,
    )


def weights_kernel(
    n_dp,
    parts,
    left_ref,
    right_ref,
    my_cols_ref,
    their_cols_ref,
    vec_ref,
    keep_any,
    send_any,
    down_keep_any,
    down_send_any,
    grads_any,
    vec_out_ref,
    full_ref,
    recv_ref,
    rest_ref,
    down_ref,
    down_recv_ref,
    down_out_ref,
    vec_recv_ref,
    send_sem,
    recv_sem,
    down_sems,
    grad_sems,
    vec_sems,
    copy_sem,
):
    me, head = lax.axis_index("dp"), lax.axis_index("head")
    other = (me, 1 - head)
    first = (flip(me, 0) * (1 - head) + flip(me, 1) * head, head)
    mine = bit(me, 1) * (1 - head) + bit(me, 0) * head
    step = pl.program_id(0)
    steps = 2 * parts + 1
    model_dim = left_ref.shape[2]
    cols = model_dim // 2
    half = my_cols_ref.shape[0]
    down_rows = parts * model_dim // n_dp
    rows = model_dim // n_dp
    my_rows = grads_any.at[pl.ds(pl.multiple_of(head * half, half), half)]
    own_copy = pltpu.make_async_copy(my_cols_ref, my_rows, copy_sem.at[4])
    grad_copy = remote(their_cols_ref, my_rows, grad_sems.at[0], grad_sems.at[1], other)
    vec_copy = remote(vec_ref, vec_recv_ref, vec_sems.at[0], vec_sems.at[1], other)
    def exchange(k):
        return remote(full_ref.at[k % 3, 1 - head], recv_ref.at[k], send_sem.at[k], recv_sem.at[k], other)

    def down_copy(k):
        at = pl.ds(2 * k, 2)
        return remote(down_ref.at[1, at], down_recv_ref.at[at], down_sems.at[0, k], down_sems.at[1, k], first)

    def multiply():
        whole = lax.dot_general(left_ref[0], right_ref[0], TN, preferred_element_type=f32).astype(bf16)
        full_ref[step % 3, 0] = whole[:, :cols]
        full_ref[step % 3, 1] = whole[:, cols:]

    def total(k, start, count):
        return (
            full_ref[k % 3, head, start : start + count].astype(f32)
            + recv_ref[k, start : start + count, :].astype(f32)
        ).astype(bf16)

    def down_finish(k):
        for q in range(4):
            send, place = route(4 * k + q, me, head)
            down_ref[send, place] = total(k, q * down_rows, down_rows)

    def rest_finish(k):
        start = pl.multiple_of((k - parts) * rows, 16)
        for d in range(n_dp):
            send, place = route(d, me, head)
            rest_ref[send, place, pl.ds(start, rows), :] = total(k, d * rows, rows)

    @pl.when(step >= 3)
    def _():
        exchange(step - 3).wait_send()

    @pl.when(step == 0)
    def _():
        greet([other, first])
        grad_copy.start()
        vec_copy.start()
        own_copy.start()

    @pl.when(step < 2)
    def _():
        multiply()
        exchange(step).start()

    @pl.when((step >= 2) & (step < parts + 2))
    def _():
        exchange(step - 2).wait_recv()
        multiply()
        down_finish(step - 2)
        exchange(step).start()
        down_copy(step - 2).start()

    @pl.when(step >= parts + 2)
    def _():
        exchange(step - 2).wait_recv()
        multiply()
        rest_finish(step - 2)
        exchange(step).start()

    @pl.when(step == steps - 1)
    def _():
        for k in range(steps - 2, steps):
            exchange(k).wait_recv()
            rest_finish(k)
        copies = [
            pltpu.make_async_copy(rest_ref.at[0], keep_any, copy_sem.at[0]),
            pltpu.make_async_copy(rest_ref.at[1], send_any, copy_sem.at[1]),
            pltpu.make_async_copy(down_out_ref.at[0], down_keep_any, copy_sem.at[2]),
            pltpu.make_async_copy(down_out_ref.at[1], down_send_any, copy_sem.at[3]),
        ]
        for copy in copies[:2]:
            copy.start()
        for k in range(parts):
            down_copy(k).wait()

        def split(r, carry):
            for j in range(2):
                block = 2 * r + j * (1 - mine) + (1 - j) * mine
                whole = down_ref[0, block].astype(f32) + down_recv_ref[block].astype(f32)
                down_out_ref[j, r] = whole.astype(bf16)
            return carry

        lax.fori_loop(0, parts, split, 0)
        for copy in copies[2:]:
            copy.start()
        vec_copy.wait()
        vec_out_ref[...] = vec_ref[...] + vec_recv_ref[...]
        grad_copy.wait()
        own_copy.wait()
        for k in range(steps - 3, steps):
            exchange(k).wait_send()
        for copy in copies:
            copy.wait()


def weights(n_dp, left, right, my_cols, their_cols, vec):
    stack, half, model_dim = left.shape
    parts = stack - 2
    steps = 2 * parts + 1
    cols = model_dim // 2
    down_rows = parts * model_dim // n_dp
    rest_rows = (parts + 1) * model_dim // n_dp
    anywhere = pl.BlockSpec(memory_space=pl.ANY)

    def left_map(j):
        return (jnp.where(j < parts, j, jnp.where(j < 2 * parts, parts, parts + 1)), 0, 0)

    def right_map(j):
        return (jnp.where(j < parts, 0, j - parts + 1), 0, 0)

    rest = jax.ShapeDtypeStruct((n_dp // 2, rest_rows, cols), bf16)
    down = jax.ShapeDtypeStruct((n_dp // 4, down_rows, cols), bf16)
    return pl.pallas_call(
        partial(weights_kernel, n_dp, parts),
        grid=(steps,),
        in_specs=[
            pl.BlockSpec((1, half, model_dim), left_map),
            pl.BlockSpec((1, half, model_dim), right_map),
            pl.BlockSpec(my_cols.shape, lambda j: (0, 0), pipeline_mode=pl.Buffered(1)),
            pl.BlockSpec(my_cols.shape, lambda j: (0, 0), pipeline_mode=pl.Buffered(1)),
            pl.BlockSpec(vec.shape, lambda j: (0, 0)),
        ],
        out_specs=[anywhere] * 5 + [pl.BlockSpec(vec.shape, lambda j: (0, 0))],
        scratch_shapes=[
            pltpu.VMEM((3, 2, model_dim, cols), bf16),
            pltpu.VMEM((steps, model_dim, cols), bf16),
            pltpu.VMEM((2,) + rest.shape, bf16),
            pltpu.VMEM((2, n_dp // 2, down_rows, cols), bf16),
            pltpu.VMEM((n_dp // 2, down_rows, cols), bf16),
            pltpu.VMEM((2,) + down.shape, bf16),
            pltpu.VMEM(vec.shape, f32),
            pltpu.SemaphoreType.DMA((steps,)),
            pltpu.SemaphoreType.DMA((steps,)),
            pltpu.SemaphoreType.DMA((2, parts)),
            pltpu.SemaphoreType.DMA((2,)),
            pltpu.SemaphoreType.DMA((2,)),
            pltpu.SemaphoreType.DMA((5,)),
        ],
        out_shape=[
            rest,
            rest,
            down,
            down,
            jax.ShapeDtypeStruct((2 * half, my_cols.shape[1]), bf16),
            jax.ShapeDtypeStruct(vec.shape, f32),
        ],
        compiler_params=pltpu.CompilerParams(
            collective_id=0, has_side_effects=True, vmem_limit_bytes=VMEM_LIMIT
        ),
        cost_estimate=pl.CostEstimate(flops=15_000_000_000, bytes_accessed=20_000_000, transcendentals=0),
    )(left, right, my_cols, their_cols, vec)


def final_kernel(
    n_dp,
    chunks,
    d_keep_any,
    d_got_any,
    s_keep_any,
    s_got_any,
    raw_any,
    rows_any,
    w_any,
    resid_any,
    vec_ref,
    raw_sums_ref,
    core_send_ref,
    core_recv_ref,
    qkv_ref,
    vec_out_ref,
    vec_core_ref,
    tokens_any,
    t_recv_any,
    d_keep_ref,
    d_got_ref,
    d_own_ref,
    d_out_ref,
    d_got_z_ref,
    s_keep_ref,
    s_got_ref,
    raw_ref,
    rows_ref,
    w_ref,
    resid_ref,
    s_send_ref,
    s_recv_ref,
    s_own_ref,
    s_out_ref,
    s_got_z_ref,
    s_sum_ref,
    q_grad_ref,
    q_both_ref,
    q_first_ref,
    q_send_ref,
    q_recv_ref,
    q_own_ref,
    q_out_ref,
    q_got_z_ref,
    t_send_ref,
    vec_hold_ref,
    vec_recv_ref,
    in_sems,
    d_z_sems,
    s_sems,
    s_z_sems,
    q_first_sems,
    q_sems,
    q_z_sems,
    t_sems,
    core_sems,
    vec_sems,
    out_sem,
):
    me, head = lax.axis_index("dp"), lax.axis_index("head")
    line = n_dp // 4
    depth = line.bit_length() - 1
    z = me // 4
    other = (me, 1 - head)
    low = (flip(me, 0), head)
    high = (flip(me, 1), head)
    around = [(((z + j) % line) * 4 + me % 4, head) for j in range(1, line)]
    first = (flip(me, 0) * (1 - head) + flip(me, 1) * head, head)
    second = (flip(me, 1) * (1 - head) + flip(me, 0) * head, head)
    mine = bit(me, 1) * (1 - head) + bit(me, 0) * head
    half, model_dim = resid_ref.shape
    local_dim = raw_ref.shape[1] // 3
    size = s_keep_ref.shape[1] // chunks
    q_chunks, _, _, q_size, _ = q_both_ref.shape
    q_rows = q_chunks * q_size

    def piece(i):
        return slice(i * size, (i + 1) * size)

    s_loads = [
        pltpu.make_async_copy(s_keep_any, s_keep_ref, in_sems.at[0]),
        pltpu.make_async_copy(s_got_any, s_got_ref, in_sems.at[1]),
    ]
    q_loads = [
        pltpu.make_async_copy(rows_any, rows_ref, in_sems.at[2]),
        pltpu.make_async_copy(raw_any, raw_ref, in_sems.at[3]),
    ]
    t_loads = [
        pltpu.make_async_copy(w_any, w_ref, in_sems.at[4]),
        pltpu.make_async_copy(resid_any, resid_ref, in_sems.at[5]),
    ]
    d_loads = [
        pltpu.make_async_copy(d_keep_any, d_keep_ref, in_sems.at[6]),
        pltpu.make_async_copy(d_got_any, d_got_ref, in_sems.at[7]),
    ]
    for load in s_loads + d_loads:
        load.start()
    greet([low, high, other] + around)

    vec_hold_ref[0] = vec_ref[...]
    here = pl.ds(pl.multiple_of(head * local_dim, LANES), local_dim)
    vec_hold_ref[0, 8:9, here] = raw_sums_ref[:, :local_dim]
    vec_hold_ref[0, 9:10, here] = raw_sums_ref[:, 2 * local_dim :]

    def vec_copy(k):
        to = (low, high)[k] if k < 2 else around[k - 2]
        source = vec_hold_ref.at[min(k, 2)]
        return remote(source, vec_recv_ref.at[k], vec_sems.at[0, k], vec_sems.at[1, k], to)

    vec_copy(0).start()

    def fold_line(own_ref, hold_ref, got_ref, sems):
        def moved(k):
            count = line >> (k + 1)
            at = slice(line - 2 * count, line - count)
            return remote(hold_ref.at[at], got_ref.at[at], sems.at[0, k], sems.at[1, k], (flip(me, k + 2), head))

        def send(k):
            count = line >> (k + 1)
            keep = bit(me, k + 2)
            for q in range(count):
                hold_ref[line - 2 * count + q] = own_ref[2 * q + 1 - keep].astype(bf16)
            moved(k).start()

        def add(k):
            count = line >> (k + 1)
            keep = bit(me, k + 2)
            moved(k).wait()
            for q in range(count):
                own_ref[q] = own_ref[2 * q + keep] + got_ref[line - 2 * count + q].astype(f32)
            if k + 1 < depth:
                send(k + 1)

        return send, add

    d_line = fold_line(d_own_ref, d_out_ref, d_got_z_ref, d_z_sems)

    def s_copy(i):
        return remote(s_send_ref.at[i], s_recv_ref.at[i], s_sems.at[0, i], s_sems.at[1, i], second)

    def s_total(block, i):
        return s_keep_ref[block, piece(i)].astype(f32) + s_got_ref[block, piece(i)].astype(f32)

    def s_prepare(i):
        def send_block(r, carry):
            s_send_ref[i, r] = s_total(2 * r + 1 - mine, i).astype(bf16)
            return carry

        lax.fori_loop(0, line, send_block, 0)

    for load in s_loads:
        load.wait()
    for load in q_loads:
        load.start()
    for load in t_loads:
        load.start()
    for i in range(chunks):
        s_prepare(i)
        s_copy(i).start()
    for load in d_loads:
        load.wait()

    def d_block(r, carry):
        d_own_ref[r] = d_keep_ref[r].astype(f32) + d_got_ref[r].astype(f32)
        return carry

    lax.fori_loop(0, line, d_block, 0)
    d_line[0](0)

    for load in q_loads:
        load.wait()

    def q_columns(j, carry):
        at = pl.ds(pl.multiple_of(j * Q_COLUMNS, LANES), Q_COLUMNS)
        grad = lax.dot_general(rows_ref[:, at], raw_ref[...], TN, preferred_element_type=f32)
        q_grad_ref[pl.ds(pl.multiple_of(j * Q_COLUMNS, LANES), Q_COLUMNS), :] = grad.astype(bf16)
        return carry

    lax.fori_loop(0, model_dim // Q_COLUMNS, q_columns, 0)
    d_line[1](0)

    def q_place(d, carry):
        send, place = route(d, me, head)
        for j in range(q_chunks):
            at = pl.ds(pl.multiple_of(d * q_rows + j * q_size, 16), q_size)
            q_both_ref[j, send, place] = q_grad_ref[at, :]
        return carry

    lax.fori_loop(0, n_dp, q_place, 0)

    def q_copy(j):
        return remote(q_both_ref.at[j, 1], q_first_ref.at[j], q_first_sems.at[0, j], q_first_sems.at[1, j], first)

    def q_second(j):
        return remote(q_send_ref.at[j], q_recv_ref.at[j], q_sems.at[0, j], q_sems.at[1, j], second)

    s_line = [
        fold_line(s_own_ref.at[i], s_out_ref.at[i], s_got_z_ref.at[i], s_z_sems.at[i]) for i in range(chunks)
    ]
    q_line = [
        fold_line(q_own_ref.at[j], q_out_ref.at[j], q_got_z_ref.at[j], q_z_sems.at[j]) for j in range(q_chunks)
    ]

    def s_enter(i):
        s_copy(i).wait()

        def add_block(r, carry):
            s_own_ref[i, r] = s_total(2 * r + mine, i) + s_recv_ref[i, r].astype(f32)
            return carry

        lax.fori_loop(0, line, add_block, 0)
        s_line[i][0](0)

    def q_total(j, block):
        return q_both_ref[j, 0, block].astype(f32) + q_first_ref[j, block].astype(f32)

    def q_enter(j):
        q_copy(j).wait()

        def send_block(r, carry):
            q_send_ref[j, r] = q_total(j, 2 * r + 1 - mine).astype(bf16)
            return carry

        lax.fori_loop(0, line, send_block, 0)
        q_second(j).start()

        def own_block(r, carry):
            q_own_ref[j, r] = q_total(j, 2 * r + mine)
            return carry

        lax.fori_loop(0, line, own_block, 0)

    def q_turn(j):
        q_second(j).wait()

        def add_block(r, carry):
            q_own_ref[j, r] = q_own_ref[j, r] + q_recv_ref[j, r].astype(f32)
            return carry

        lax.fori_loop(0, line, add_block, 0)
        q_line[j][0](0)

    tile_rows = half // 4

    def token_rows(who, tile):
        at = pl.ds(pl.multiple_of(who * half + tile * tile_rows, tile_rows), tile_rows)
        total = 0.0
        for c in range(3):
            part = raw_ref[at, c * local_dim : (c + 1) * local_dim]
            total = total + lax.dot_general(part, w_ref[c], NT, preferred_element_type=f32)
        return total

    t_copy = remote(t_send_ref, t_recv_any, t_sems.at[0], t_sems.at[1], other)

    def send_tile(tile, carry):
        at = pl.ds(pl.multiple_of(tile * tile_rows, tile_rows), tile_rows)
        t_send_ref[at, :] = token_rows(1 - head, tile).astype(bf16)
        return carry

    def own_tile(tile, carry):
        at = pl.ds(pl.multiple_of(tile * tile_rows, tile_rows), tile_rows)
        resid_ref[at, :] = resid_ref[at, :] + token_rows(head, tile)
        return carry

    for j in range(q_chunks):
        q_copy(j).start()
    s_enter(0)
    for load in t_loads:
        load.wait()
    lax.fori_loop(0, 4, send_tile, 0)
    t_copy.start()
    if chunks > 1:
        s_enter(1)
        s_line[0][1](0)
    lax.fori_loop(0, 4, own_tile, 0)
    t_out = pltpu.make_async_copy(resid_ref, tokens_any, out_sem)
    t_out.start()
    for i in range(2, chunks):
        s_enter(i)
        s_line[i - 1][1](0)
    vec_copy(0).wait()
    vec_hold_ref[1] = vec_hold_ref[0] + vec_recv_ref[0]
    vec_copy(1).start()
    q_enter(0)
    s_line[chunks - 1][1](0)
    for j in range(1, q_chunks):
        q_enter(j)
    vec_copy(1).wait()
    vec_hold_ref[2] = vec_hold_ref[1] + vec_recv_ref[1]
    for j in range(line - 1):
        vec_copy(2 + j).start()
    for j in range(q_chunks - 1):
        q_turn(j)
    d_rows = d_own_ref.shape[1]
    for k in range(1, depth):
        d_line[1](k)
    s_sum_ref[:d_rows, :] = d_own_ref[0]
    for i in range(chunks):
        for k in range(1, depth):
            s_line[i][1](k)
        s_sum_ref[d_rows + i * size : d_rows + (i + 1) * size, :] = s_own_ref[i, 0]
    pieces = core_pieces(s_sum_ref.shape[0], q_rows)

    def gather(target_ref, who):
        at = 0
        for start, count in pieces:
            here = pl.ds(pl.multiple_of(start + who * count, 8), count)
            target_ref[at : at + count, :] = s_sum_ref[here, :]
            at += count

    gather(core_send_ref.at[1], 1 - head)
    core_copy = remote(core_send_ref.at[1], core_recv_ref, core_sems.at[0], core_sems.at[1], other)
    core_copy.start()
    gather(core_send_ref.at[0], head)
    q_turn(q_chunks - 1)
    for j in range(line - 1):
        vec_copy(2 + j).wait()
    total = vec_hold_ref[2]
    for j in range(line - 1):
        total = total + vec_recv_ref[2 + j]
    vec_out_ref[...] = total
    core_vec = remote(vec_out_ref.at[pl.ds(8, 8)], vec_core_ref, core_sems.at[2], core_sems.at[3], other)
    core_vec.start()
    for k in range(depth):
        for j in range(q_chunks):
            q_line[j][1](k)
    for j in range(q_chunks):
        qkv_ref[j * q_size : (j + 1) * q_size, :] = q_own_ref[j, 0]
    core_vec.wait()
    core_copy.wait()
    t_copy.wait()
    t_out.wait()


def core_pieces(block_rows, rows):
    parts = (block_rows // rows - 1) // 2
    return [(0, parts * rows // 2)] + [(parts * rows + rows * c, rows // 2) for c in range(parts + 1)]


def final(n_dp, d_keep, d_got, s_keep, s_got, raw, group_rows, w_flat, resid, vec, raw_sums):
    line = n_dp // 4
    depth = line.bit_length() - 1
    _, rest_rows, cols = s_keep.shape
    down_rows = d_keep.shape[1]
    block_rows = down_rows + rest_rows
    half, model_dim = resid.shape
    local_dim = raw.shape[1] // 3
    q_rows, q_cols = model_dim // n_dp, 3 * local_dim
    chunks = 3 if rest_rows % 48 == 0 else 1
    size = rest_rows // chunks
    q_chunks = q_rows // 16
    anywhere = pl.BlockSpec(memory_space=pl.ANY)
    vmem = pl.BlockSpec(memory_space=pltpu.VMEM)

    def low(*dims):
        return pltpu.VMEM(dims, bf16)

    def wide(*dims):
        return pltpu.VMEM(dims, f32)

    def shape(*dims):
        return jax.ShapeDtypeStruct(dims, f32)

    def sems(*dims):
        return pltpu.SemaphoreType.DMA(dims)

    return pl.pallas_call(
        partial(final_kernel, n_dp, chunks),
        in_specs=[anywhere] * 8 + [vmem] * 2,
        out_specs=[vmem] * 5 + [anywhere] * 2,
        scratch_shapes=[
            low(*d_keep.shape),
            low(*d_keep.shape),
            wide(*d_keep.shape),
            low(*d_keep.shape),
            low(line - 1, down_rows, cols),
            low(*s_keep.shape),
            low(*s_keep.shape),
            low(*raw.shape),
            low(*group_rows.shape),
            low(*w_flat.shape),
            wide(half, model_dim),
            low(chunks, line, size, cols),
            low(chunks, line, size, cols),
            wide(chunks, line, size, cols),
            low(chunks, line, size, cols),
            low(chunks, line - 1, size, cols),
            wide(block_rows, cols),
            low(model_dim, q_cols),
            low(q_chunks, 2, 2 * line, 16, q_cols),
            low(q_chunks, 2 * line, 16, q_cols),
            low(q_chunks, line, 16, q_cols),
            low(q_chunks, line, 16, q_cols),
            wide(q_chunks, line, 16, q_cols),
            low(q_chunks, line, 16, q_cols),
            low(q_chunks, line - 1, 16, q_cols),
            low(half, model_dim),
            wide(3, *vec.shape),
            wide(1 + line, *vec.shape),
            sems(8),
            sems(2, depth),
            sems(2, chunks),
            sems(chunks, 2, depth),
            sems(2, q_chunks),
            sems(2, q_chunks),
            sems(q_chunks, 2, depth),
            sems(2),
            sems(4),
            sems(2, 1 + line),
            pltpu.SemaphoreType.DMA,
        ],
        out_shape=[
            shape(2, block_rows // 2, cols),
            shape(block_rows // 2, cols),
            shape(q_rows, q_cols),
            shape(*vec.shape),
            shape(8, model_dim),
            shape(half, model_dim),
            jax.ShapeDtypeStruct((half, model_dim), bf16),
        ],
        compiler_params=pltpu.CompilerParams(
            collective_id=1, has_side_effects=True, vmem_limit_bytes=VMEM_LIMIT
        ),
        cost_estimate=pl.CostEstimate(flops=12_000_000_000, bytes_accessed=25_000_000, transcendentals=0),
    )(d_keep, d_got, s_keep, s_got, raw, group_rows, w_flat, resid, vec, raw_sums)


def finish_kernel(
    n_dp,
    parts,
    own_ref,
    got_ref,
    kept_ref,
    core_ref,
    qkv_ref,
    vec_ref,
    vec_core_ref,
    tokens_ref,
    grad_qkv_ref,
    down_ref,
    in_ref,
    out_ref,
    qv_ref,
    in_bias_ref,
    term_ref,
    *vector_refs,
):
    tokens_ref[...] = own_ref[...] + got_ref[...].astype(f32)

    @pl.when(pl.program_id(0) == 0)
    def _():
        head = lax.axis_index("head")
        place = 2 * lax.axis_index("dp") + head
        cols = kept_ref.shape[2]
        model_dim = 2 * cols
        rows = out_ref.shape[0]
        width = model_dim // (2 * n_dp)
        starts = [0, parts * rows] + [parts * rows + rows * (c + 1) for c in range(parts + 1)]
        for who, source in ((head, kept_ref.at[0]), (1 - head, core_ref)):
            start = who * cols
            here = pl.ds(pl.multiple_of(start, LANES), cols)
            down_ref[:, here] = source[starts[0] : starts[1], :]
            for c in range(parts):
                shifted = pl.ds(pl.multiple_of(2 * cols * c + start, LANES), cols)
                in_ref[:, shifted] = source[starts[1 + c] : starts[2 + c], :]
            out_ref[:, here] = source[starts[1 + parts] : starts[2 + parts], :]
        for c in range(3):
            grad_qkv_ref[c] = qkv_ref[:, c * cols : (c + 1) * cols]
        shift = lax.rem(model_dim - place * width, model_dim)
        turned = pltpu.roll(vec_ref[0:8], shift, 1)
        for j, ref in enumerate(vector_refs):
            ref[...] = turned[j : j + 1, :width]
        term_ref[...] = vec_ref[7:8, :1]
        turned = pltpu.roll(vec_ref[8:16] + vec_core_ref[...], shift, 1)
        qv_ref[...] = turned[:2, :width]
        in_width = parts * model_dim // (2 * n_dp)
        per_row = model_dim // in_width
        row = vec_ref[pl.ds(10 + place // per_row, 1), :]
        row = jnp.broadcast_to(row, (8, model_dim))
        turned = pltpu.roll(row, lax.rem(model_dim - (place % per_row) * in_width, model_dim), 1)
        in_bias_ref[...] = turned[0:1, :in_width]


def finish(n_dp, parts, kept, core, qkv, vec, vec_core, own, got):
    half, model_dim = own.shape
    q_rows = qkv.shape[0]
    width = model_dim // (2 * n_dp)
    rows = min(512, half)
    tile = pl.BlockSpec((rows, model_dim), lambda i: (i, 0))

    def whole(dims):
        return pl.BlockSpec(dims, lambda i: (0,) * len(dims))

    out = [
        (3, q_rows, model_dim // 2),
        (parts * width, model_dim),
        (width, parts * model_dim),
        (width, model_dim),
        (2, width),
        (1, parts * width),
        (1, 1),
    ] + [(1, width)] * 7
    return pl.pallas_call(
        partial(finish_kernel, n_dp, parts),
        grid=(half // rows,),
        in_specs=[tile, tile] + [whole(x.shape) for x in (kept, core, qkv, vec, vec_core)],
        out_specs=[tile] + [whole(dims) for dims in out],
        out_shape=[jax.ShapeDtypeStruct((half, model_dim), f32)] + [jax.ShapeDtypeStruct(dims, f32) for dims in out],
        compiler_params=pltpu.CompilerParams(vmem_limit_bytes=VMEM_LIMIT),
        cost_estimate=pl.CostEstimate(flops=1_000_000, bytes_accessed=10_000_000, transcendentals=0),
    )(own, got, kept, core, qkv, vec, vec_core)


def take(array, index, axis=0):
    return lax.dynamic_index_in_dim(array, index, axis, keepdims=False)


class Links:
    def __init__(self, n_dp):
        self.n_dp = n_dp
        self.bits = n_dp.bit_length() - 1
        self.dp = lax.axis_index("dp")
        self.head = lax.axis_index("head")

    def bit(self, which):
        return (self.dp >> which) & 1

    def permute(self, array, partner):
        pairs = []
        for d in range(self.n_dp):
            for h in range(2):
                to_d, to_h = partner(d, h)
                pairs.append((2 * d + h, 2 * to_d + to_h))
        return lax.ppermute(array, AXES, pairs)

    def swap_head(self, array):
        return self.permute(array, lambda d, h: (d, 1 - h))

    def swap_bit(self, array, which):
        return self.permute(array, lambda d, h: (d ^ (1 << which), h))

    def scatter_heads(self, blocks):
        got = self.swap_head(take(blocks, 1 - self.head, 1))
        return (take(blocks, self.head, 1).astype(f32) + got.astype(f32)).astype(bf16)

    def scatter_dp(self, blocks):
        tail = blocks.shape[1:]
        b0, b1 = self.bit(0), self.bit(1)
        first = self.head == 0
        blocks = blocks.reshape((self.n_dp // 4, 4) + tail)

        def two(one, other):
            i = jnp.where(first, one, 2 * other)
            j = jnp.where(first, 2 + one, 2 * other + 1)
            return jnp.stack([take(blocks, i, 1), take(blocks, j, 1)], axis=1)

        got = self.permute(two(1 - b0, 1 - b1), lambda d, h: (d ^ (1 if h == 0 else 2), h))
        blocks = (two(b0, b1).astype(f32) + got.astype(f32)).astype(bf16)
        mine = jnp.where(first, b1, b0)
        got = self.permute(take(blocks, 1 - mine, 1), lambda d, h: (d ^ (2 if h == 0 else 1), h))
        blocks = take(blocks, mine, 1).astype(f32) + got.astype(f32)
        for which in range(2, self.bits):
            blocks = blocks.reshape((-1, 2) + tail)
            mine = self.bit(which)
            got = self.swap_bit(take(blocks, 1 - mine, 1).astype(bf16), which)
            blocks = take(blocks, mine, 1) + got.astype(f32)
        return blocks.reshape(tail)

    def total(self, array):
        array = array + self.swap_head(array)
        for which in range(self.bits):
            array = array + self.swap_bit(array, which)
        return array


def shards(
    n_dp,
    tokens,
    lengths,
    w_qkv,
    bias_qv,
    w_out,
    bias_out,
    ln1_gain,
    ln1_bias,
    w_in,
    bias_in,
    w_down,
    bias_down,
    ln2_gain,
    ln2_bias,
    term_w,
    term_bias,
    grad_hidden,
    grad_term,
):
    links = Links(n_dp)
    head = links.head
    half, model_dim = tokens.shape
    row_len = 2 * half
    local_dim = w_qkv.shape[2]
    ffn_dim = w_in.shape[1]

    boundary = jnp.cumsum(lengths[0])
    places = jnp.arange(row_len, dtype=jnp.int32)
    segment = jnp.sum((places[:, None] >= boundary[None, :]).astype(jnp.int32), axis=-1)
    seg_col = jnp.broadcast_to(segment[:, None], (row_len, LANES))
    seg_row = jnp.broadcast_to(segment[None, :], (8, row_len))

    def both(mine, theirs, axis):
        return jnp.where(
            head == 0,
            jnp.concatenate([mine, theirs], axis=axis),
            jnp.concatenate([theirs, mine], axis=axis),
        )

    w_parts = jnp.transpose(w_qkv, (1, 0, 2))
    group_rows = both(tokens, links.swap_head(tokens), 0)
    queries, key_rows, value_rows = [jnp.dot(group_rows, w_parts[c], preferred_element_type=f32) for c in range(3)]
    queries = ((queries + bias_qv[:, 0]) * HEAD_DIM ** (-0.5)).astype(bf16)
    key_rows = key_rows.astype(bf16)
    value_rows = (value_rows + bias_qv[:, 1]).astype(bf16)
    theirs, mine, logs = attend(lengths, head, queries, key_rows, value_rows, seg_col, seg_row)

    def my_half(rows):
        return lax.dynamic_slice_in_dim(rows, head * half, half, 0)

    def their_half(rows):
        return lax.dynamic_slice_in_dim(rows, (1 - head) * half, half, 0)

    vec = jnp.stack([bias_out, ln1_gain, ln1_bias, bias_down, ln2_gain, ln2_bias, term_w, jnp.zeros_like(term_w)])
    hidden_out, term_weight, left, right, resid_one_grad, my_cols, their_cols, vec = middle(
        mine,
        links.swap_head(theirs),
        tokens,
        grad_hidden,
        grad_term[None, :],
        w_out,
        w_in,
        w_down,
        vec,
        bias_in[None, :],
        term_bias[None, :],
    )
    parts = ffn_dim // model_dim
    in_kernels = (model_dim // n_dp) % 16 == 0 and n_dp == 4 * parts

    def back(grads):
        return attend_back(lengths, queries, key_rows, value_rows, grads, logs, seg_col, seg_row)

    if in_kernels:
        s_keep, s_send, d_keep, d_send, head_grad, vec = weights(n_dp, left, right, my_cols, their_cols, vec)
        d_got = links.permute(d_send, lambda d, h: (d ^ (2 if h == 0 else 1), h))
        s_got = links.permute(s_send, lambda d, h: (d ^ (1 if h == 0 else 2), h))
        raw, raw_sums = back(head_grad)
        kept, core, qkv, vec, vec_core, own, got = final(
            n_dp, d_keep, d_got, s_keep, s_got, raw, group_rows, w_parts, resid_one_grad, vec, raw_sums
        )
        (grad_tokens, grad_qkv, grad_down, grad_in, grad_out, bias_qv_mine, bias_in_mine, term_total, *vectors) = finish(
            n_dp, parts, kept, core, qkv, vec, vec_core, own, got
        )
        grad_qkv = jnp.transpose(grad_qkv, (1, 0, 2))
        bias_qv_mine = bias_qv_mine.T
        bias_in_mine = bias_in_mine.reshape(-1)
        term_total = term_total.reshape(1)
        mine = [v.reshape(-1) for v in vectors]
    else:
        raw, raw_sums = back(both(my_cols, links.swap_head(their_cols), 0))

        def product(i, j):
            return lax.dot_general(left[i], right[j], TN, preferred_element_type=f32).astype(bf16)

        def reduced(partial_sum):
            rows, cols = partial_sum.shape
            return links.scatter_dp(links.scatter_heads(partial_sum.reshape(n_dp, 2, rows // (2 * n_dp), cols)))

        grad_down = reduced(jnp.concatenate([product(i, 0) for i in range(parts)]))
        grad_in = reduced(jnp.concatenate([product(parts, 1 + i) for i in range(parts)], axis=1))
        grad_out = reduced(product(parts + 1, parts + 1))
        w_flat = w_qkv.reshape(model_dim, 3 * local_dim)
        grad = lax.dot_general(raw, w_flat, NT, preferred_element_type=f32)
        received = links.swap_head(their_half(grad).astype(bf16))
        grad_tokens = resid_one_grad + my_half(grad) + received.astype(f32)
        qkv_local = lax.dot_general(group_rows, raw, TN, preferred_element_type=f32).astype(bf16)
        grad_qkv = links.scatter_dp(qkv_local.reshape(n_dp, model_dim // n_dp, 3 * local_dim))
        value_sums = lax.dynamic_update_slice(
            jnp.zeros((2, 2 * local_dim), f32),
            jnp.concatenate([raw_sums[:, :local_dim], raw_sums[:, 2 * local_dim :]]),
            (jnp.int32(0), head * local_dim),
        )
        vectors = links.total(lax.dynamic_update_slice(vec, value_sums, (8, 0)))
        grad_qkv = grad_qkv.reshape(model_dim // n_dp, 3, local_dim)
        place = 2 * links.dp + head
        width = model_dim // (2 * n_dp)
        mine = lax.dynamic_slice_in_dim(vectors, place * width, width, 1)
        in_width = ffn_dim // (2 * n_dp)
        in_row = vectors[10 : 10 + parts].reshape(-1)
        bias_in_mine = lax.dynamic_slice_in_dim(in_row, place * in_width, in_width, 0)
        bias_qv_mine = mine[8:10].T
        term_total = vectors[7, :1]

    return (
        hidden_out,
        term_weight.reshape(-1),
        grad_tokens,
        grad_qkv,
        bias_qv_mine,
        grad_out,
        mine[0],
        mine[1],
        mine[2],
        grad_in,
        bias_in_mine,
        grad_down,
        mine[3],
        mine[4],
        mine[5],
        mine[6],
        term_total,
    )


def solution(mesh):
    rows = P(AXES, None)
    return jax.shard_map(
        partial(shards, mesh.shape["dp"]),
        mesh=mesh,
        in_specs=(rows, P("dp", None), P(None, None, "head"), P("head", None))
        + (P(),) * 12
        + (rows, P(AXES)),
        out_specs=(
            rows,
            P(AXES),
            rows,
            P("dp", None, "head"),
            rows,
            rows,
            P(AXES),
            P(AXES),
            P(AXES),
            rows,
            P(AXES),
            rows,
            P(AXES),
            P(AXES),
            P(AXES),
            P(AXES),
            P(),
        ),
        check_vma=False,
    )
```

```python
from functools import partial

import jax
import jax.numpy as jnp
from jax import lax
from jax.experimental import pallas as pl
from jax.experimental.pallas import tpu as pltpu
from jax.sharding import PartitionSpec as P

HEAD_DIM = 64
LANES = 128
VMEM_LIMIT = 60 * 2**20
Q_ROWS = 256
PIECE = 32
Q_COLUMNS = 128
WIDTHS = (2, 3, 4, 5, 6, 8, 10)
BACK_WIDTHS = (2, 3, 4, 5, 6, 7, 8, 10)
AXES = ("dp", "head")

f32 = jnp.float32
bf16 = jnp.bfloat16
norm_eps = 1e-06
NT = (((1,), (1,)), ((), ()))
TN = (((0,), (0,)), ((), ()))


def key_range(lengths_ref, first, rows, row_len):
    start = jnp.int32(0)
    low = jnp.int32(0)
    high = jnp.int32(row_len)
    for j in range(lengths_ref.shape[1]):
        end = start + lengths_ref[0, j]
        low = jnp.where(start <= first, start, low)
        high = jnp.where(end >= first + rows, jnp.minimum(high, end), high)
        start = end
    low_block = low // LANES
    count = (high + LANES - 1) // LANES - low_block
    return low_block, count


def by_width(lengths_ref, first, rows, row_len, body, choices=WIDTHS):
    blocks = row_len // LANES
    low_block, count = key_range(lengths_ref, first, rows, row_len)
    widths = sorted({min(w, blocks) for w in choices})
    below = 0
    for width in widths:

        @pl.when((count > below) & (count <= width))
        def _(width=width):
            begin = jnp.minimum(low_block, blocks - width)
            body(pl.multiple_of(begin * LANES, LANES), width * LANES)

        below = width


def query_block(step, steps, head):
    return lax.rem(step + (1 - head) * (steps // 2), steps)


def attend_kernel(
    lengths_ref,
    head_ref,
    q_ref,
    k_ref,
    v_ref,
    segc_ref,
    segr_ref,
    theirs_ref,
    mine_ref,
    log_ref,
    mask_ref,
    cols_ref,
    s_ref,
    p_ref,
    o_ref,
):
    rows, local_dim = q_ref.shape
    row_len = k_ref.shape[0]
    step, steps = pl.program_id(0), pl.num_programs(0)
    first = query_block(step, steps, head_ref[0]) * rows
    lane = lax.broadcasted_iota(jnp.int32, (rows, LANES), 1)

    def body(begin, width):
        same = segc_ref[:, 0:1] == segr_ref[0:1, pl.ds(begin, width)]
        mask_ref[:, :width] = jnp.where(same, 0.0, -1e30)

        heads = local_dim // HEAD_DIM

        def score(i):
            cols = slice(i // 2 * LANES, i // 2 * LANES + LANES)
            q_pair = q_ref[:, cols]
            q_one = jnp.where((lane // HEAD_DIM) == i % 2, q_pair, jnp.zeros_like(q_pair))
            k_pair = k_ref[pl.ds(begin, width), cols]
            s_ref[i % 2, :, :width] = lax.dot_general(q_one, k_pair, NT, preferred_element_type=f32)

        def soft(i):
            for r in range(0, rows, PIECE):
                part = slice(r, r + PIECE)
                scores = s_ref[i % 2, part, :width] + mask_ref[part, :width]
                row_max = jnp.max(scores, axis=1, keepdims=True)
                powers = jnp.exp(scores - row_max)
                total = jnp.sum(powers, axis=1, keepdims=True)
                p_ref[i % 2, part, :width] = (powers * (1.0 / total)).astype(bf16)
                log_total = row_max + jnp.log(total)
                cols_ref[part] = jnp.where(lane[part] == i, log_total, cols_ref[part])

        def value(i):
            cols = slice(i // 2 * LANES, i // 2 * LANES + LANES)
            return jnp.dot(p_ref[i % 2, :, :width], v_ref[pl.ds(begin, width), cols], preferred_element_type=f32)

        score(0)
        held = None
        for i in range(heads):
            if i + 1 < heads:
                score(i + 1)
            soft(i)
            out = value(i)
            if i % 2 == 0:
                held = out
            else:
                cols = slice(i // 2 * LANES, i // 2 * LANES + LANES)
                o_ref[:, cols] = jnp.where(lane < HEAD_DIM, held, out).astype(bf16)

    by_width(lengths_ref, first, rows, row_len, body)
    log_ref[...] = cols_ref[...].T[: log_ref.shape[0]]

    @pl.when(step < steps // 2)
    def _():
        theirs_ref[...] = o_ref[...]

    @pl.when(step >= steps // 2)
    def _():
        mine_ref[...] = o_ref[...]


def attend(lengths, head, queries, key_rows, value_rows, seg_col, seg_row):
    row_len, local_dim = queries.shape
    rows = min(Q_ROWS, row_len // 2)
    steps = row_len // rows
    whole = pl.BlockSpec((row_len, local_dim), lambda i, n, h: (0, 0))
    return pl.pallas_call(
        attend_kernel,
        grid_spec=pltpu.PrefetchScalarGridSpec(
            num_scalar_prefetch=2,
            grid=(steps,),
            in_specs=[
                pl.BlockSpec((rows, local_dim), lambda i, n, h: (query_block(i, steps, h[0]), 0)),
                whole,
                whole,
                pl.BlockSpec((rows, LANES), lambda i, n, h: (query_block(i, steps, h[0]), 0)),
                pl.BlockSpec((8, row_len), lambda i, n, h: (0, 0)),
            ],
            out_specs=[
                pl.BlockSpec((rows, local_dim), lambda i, n, h: (jnp.minimum(i, steps // 2 - 1), 0)),
                pl.BlockSpec((rows, local_dim), lambda i, n, h: (jnp.maximum(i - steps // 2, 0), 0)),
                pl.BlockSpec((8, rows), lambda i, n, h: (0, query_block(i, steps, h[0]))),
            ],
            scratch_shapes=[
                pltpu.VMEM((rows, max(WIDTHS) * LANES), f32),
                pltpu.VMEM((rows, LANES), f32),
                pltpu.VMEM((2, rows, max(WIDTHS) * LANES), f32),
                pltpu.VMEM((2, rows, max(WIDTHS) * LANES), bf16),
                pltpu.VMEM((rows, local_dim), bf16),
            ],
        ),
        out_shape=[
            jax.ShapeDtypeStruct((row_len // 2, local_dim), bf16),
            jax.ShapeDtypeStruct((row_len // 2, local_dim), bf16),
            jax.ShapeDtypeStruct((8, row_len), f32),
        ],
        compiler_params=pltpu.CompilerParams(vmem_limit_bytes=48 * 2**20),
        cost_estimate=pl.CostEstimate(flops=20_000_000_000, bytes_accessed=8_000_000, transcendentals=0),
    )(lengths, head[None], queries, key_rows, value_rows, seg_col, seg_row)


def attend_back_kernel(
    lengths_ref,
    q_ref,
    k_ref,
    v_ref,
    g_ref,
    log_ref,
    segc_ref,
    segr_ref,
    raw_ref,
    sums_ref,
    mask_ref,
    dk_ref,
    dv_ref,
    s_ref,
    d_ref,
    p_ref,
    e_ref,
    ones_ref,
):
    rows, local_dim = q_ref.shape
    row_len = k_ref.shape[0]
    step = pl.program_id(0)
    first = step * rows
    lane = lax.broadcasted_iota(jnp.int32, (rows, LANES), 1)

    @pl.when(step == 0)
    def _():
        dk_ref[...] = jnp.zeros_like(dk_ref)
        dv_ref[...] = jnp.zeros_like(dv_ref)

    def body(begin, width):
        keys = pl.ds(begin, width)
        same = segc_ref[keys, 0:1] == segr_ref[0:1, :]
        mask_ref[:width, :] = jnp.where(same, 0.0, -1e30)

        def pair_step(pair, carry):
            cols = pl.ds(pl.multiple_of(pair * LANES, LANES), LANES)

            def products(i):
                mine = (lane // HEAD_DIM) == i
                here = slice(i * rows, i * rows + rows)
                q_pair, g_pair = q_ref[:, cols], g_ref[:, cols]
                q_one = jnp.where(mine, q_pair, jnp.zeros_like(q_pair))
                g_one = jnp.where(mine, g_pair, jnp.zeros_like(g_pair))
                ones_ref[0, here] = q_one
                ones_ref[1, here] = g_one
                s_ref[i, :width] = lax.dot_general(k_ref[keys, cols], q_one, NT, preferred_element_type=f32)
                d_ref[i, :width] = lax.dot_general(v_ref[keys, cols], g_one, NT, preferred_element_type=f32)

            def soft(i):
                here = slice(i * rows, i * rows + rows)
                log_row = log_ref[pl.ds(2 * pair + i, 1), :]
                inner = jnp.zeros((8, rows), f32)
                for r in range(0, width, PIECE):
                    part = slice(r, r + PIECE)
                    probs = jnp.exp(s_ref[i, part] + mask_ref[part] - log_row)
                    s_ref[i, part] = probs
                    p_ref[part, here] = probs.astype(bf16)
                    inner = inner + jnp.sum((probs * d_ref[i, part]).reshape(PIECE // 8, 8, rows), axis=0)
                inner = jnp.sum(inner, axis=0, keepdims=True)
                for r in range(0, width, PIECE):
                    part = slice(r, r + PIECE)
                    e_ref[part, here] = (s_ref[i, part] * (d_ref[i, part] - inner)).astype(bf16)

            def gather(i):
                here = slice(i * rows, i * rows + rows)
                dv_ref[keys, cols] += jnp.dot(p_ref[:width, here], ones_ref[1, here], preferred_element_type=f32)
                dk_ref[keys, cols] += jnp.dot(e_ref[:width, here], ones_ref[0, here], preferred_element_type=f32)
                return lax.dot_general(e_ref[:width, here], k_ref[keys, cols], TN, preferred_element_type=f32)

            products(0)
            products(1)
            soft(0)
            dq_first = gather(0)
            soft(1)
            dq_second = gather(1)
            dq_low = jnp.where(lane < HEAD_DIM, dq_first, dq_second).astype(bf16)
            raw_ref[pl.ds(pl.multiple_of(first, rows), rows), cols] = dq_low * jnp.asarray(HEAD_DIM**-0.5, bf16)
            return carry

        lax.fori_loop(0, local_dim // LANES, pair_step, 0)

    by_width(lengths_ref, first, rows, row_len, body, BACK_WIDTHS)

    @pl.when(step == pl.num_programs(0) - 1)
    def _():
        raw_ref[:, local_dim : 2 * local_dim] = dk_ref[...].astype(bf16)
        raw_ref[:, 2 * local_dim :] = dv_ref[...].astype(bf16)
        sums_ref[...] = jnp.sum(raw_ref[...].astype(f32), axis=0, keepdims=True)


def attend_back(lengths, queries, key_rows, value_rows, grads, logs, seg_col, seg_row):
    row_len, local_dim = queries.shape
    rows = min(Q_ROWS, row_len)
    whole = pl.BlockSpec((row_len, local_dim), lambda i, n: (0, 0))
    block = pl.BlockSpec((rows, local_dim), lambda i, n: (i, 0))
    return pl.pallas_call(
        attend_back_kernel,
        grid_spec=pltpu.PrefetchScalarGridSpec(
            num_scalar_prefetch=1,
            grid=(row_len // rows,),
            in_specs=[
                block,
                whole,
                whole,
                block,
                pl.BlockSpec((8, rows), lambda i, n: (0, i)),
                pl.BlockSpec((row_len, LANES), lambda i, n: (0, 0)),
                pl.BlockSpec((8, rows), lambda i, n: (0, i)),
            ],
            out_specs=[
                pl.BlockSpec((row_len, 3 * local_dim), lambda i, n: (0, 0)),
                pl.BlockSpec((1, 3 * local_dim), lambda i, n: (0, 0)),
            ],
            scratch_shapes=[
                pltpu.VMEM((max(WIDTHS) * LANES, rows), f32),
                pltpu.VMEM((row_len, local_dim), f32),
                pltpu.VMEM((row_len, local_dim), f32),
                pltpu.VMEM((2, max(WIDTHS) * LANES, rows), f32),
                pltpu.VMEM((2, max(WIDTHS) * LANES, rows), f32),
                pltpu.VMEM((max(WIDTHS) * LANES, 2 * rows), bf16),
                pltpu.VMEM((max(WIDTHS) * LANES, 2 * rows), bf16),
                pltpu.VMEM((2, 2 * rows, LANES), bf16),
            ],
        ),
        out_shape=[
            jax.ShapeDtypeStruct((row_len, 3 * local_dim), bf16),
            jax.ShapeDtypeStruct((1, 3 * local_dim), f32),
        ],
        compiler_params=pltpu.CompilerParams(vmem_limit_bytes=VMEM_LIMIT),
        cost_estimate=pl.CostEstimate(flops=40_000_000_000, bytes_accessed=12_000_000, transcendentals=0),
    )(lengths, queries, key_rows, value_rows, grads, logs, seg_col, seg_row)


TILE = 256


def gelu_both(x):
    cdf = 0.5 + 0.5 * lax.erf(x * 0.7071067811865476)
    density = jnp.exp(-0.5 * x * x) * 0.3989422804014327
    return x * cdf, cdf + x * density


def normalize(resid):
    center = resid - jnp.mean(resid, axis=-1, keepdims=True)
    scale = lax.rsqrt(jnp.mean(center * center, axis=-1, keepdims=True) + norm_eps)
    return center * scale, scale


def normalize_back(grad, normed, scale):
    shift = jnp.mean(grad, axis=-1, keepdims=True)
    slope = jnp.mean(grad * normed, axis=-1, keepdims=True)
    return scale * (grad - shift - normed * slope)


def fold(x):
    return jnp.sum(x.astype(f32).reshape(x.shape[0] // 8, 8, x.shape[1]), axis=0)


def middle_kernel(
    mine_ref,
    theirs_ref,
    tokens_ref,
    hid_ref,
    term_ref,
    w_out_ref,
    w_in_ref,
    w_down_ref,
    vec_ref,
    bias_in_ref,
    term_bias_ref,
    hidden_ref,
    weight_ref,
    left_ref,
    right_ref,
    resid_ref,
    my_grad_ref,
    their_grad_ref,
    sums_ref,
    slope_ref,
    wide_ref,
    x_ref,
    normal_ref,
    scale_ref,
    fold_ref,
    in_fold_ref,
    term_cols_ref,
    term_in_ref,
):
    head = lax.axis_index("head")
    local_dim = mine_ref.shape[1]
    model_dim = w_out_ref.shape[0]
    parts = w_in_ref.shape[1] // model_dim
    rows = tokens_ref.shape[0]
    pieces = [slice(r, r + PIECE) for r in range(0, rows, PIECE)]
    bias_out, ln1_gain, ln1_bias = vec_ref[0:1], vec_ref[1:2], vec_ref[2:3]
    bias_down, ln2_gain, ln2_bias, term_w = vec_ref[3:4], vec_ref[4:5], vec_ref[5:6], vec_ref[6:7]

    @pl.when(pl.program_id(0) == 0)
    def _():
        fold_ref[...] = jnp.zeros_like(fold_ref)
        in_fold_ref[...] = jnp.zeros_like(in_fold_ref)

    term_in_ref[...] = jnp.broadcast_to(term_ref[...], (LANES, rows)).T
    left_ref[parts + 1, :, pl.ds(pl.multiple_of(head * local_dim, LANES), local_dim)] = mine_ref[...]
    left_ref[parts + 1, :, pl.ds(pl.multiple_of((1 - head) * local_dim, LANES), local_dim)] = theirs_ref[...]
    x_ref[...] = jnp.dot(left_ref[parts + 1], w_out_ref[...], preferred_element_type=f32)
    for r in pieces:
        normal, scale = normalize(tokens_ref[r].astype(f32) + (x_ref[r] + bias_out))
        normed = normal * ln1_gain + ln1_bias
        normal_ref[r] = normal
        scale_ref[r] = scale
        left_ref[parts, r] = normed.astype(bf16)
        x_ref[r] = normed + bias_down

    def columns(c):
        return slice(c * model_dim, (c + 1) * model_dim)

    def rise(c):
        wide_ref[c % 2] = jnp.dot(left_ref[parts], w_in_ref[:, columns(c)], preferred_element_type=f32)

    rise(0)
    for c in range(parts):
        if c + 1 < parts:
            rise(c + 1)
        for r in pieces:
            value, slope = gelu_both(wide_ref[c % 2, r] + bias_in_ref[:, columns(c)])
            left_ref[c, r] = value.astype(bf16)
            slope_ref[r, columns(c)] = slope
        x_ref[...] += jnp.dot(left_ref[c], w_down_ref[columns(c), :], preferred_element_type=f32)

    for r in pieces:
        normal, scale = normalize(x_ref[r])
        normed = normal * ln2_gain + ln2_bias
        hidden_ref[r] = normed.astype(bf16)
        logit = jnp.sum(normed * term_w, axis=-1, keepdims=True) + term_bias_ref[0:1, 0:1]
        small = jnp.exp(-jnp.abs(logit))
        term_cols_ref[r] = jnp.broadcast_to(jnp.maximum(logit, 0.0) + jnp.log1p(small), (PIECE, LANES))
        logit_grad = term_in_ref[r, 0:1] * (jnp.where(logit >= 0.0, 1.0, small) / (1.0 + small))
        two_grad = hid_ref[r] + logit_grad * term_w
        resid_two = normalize_back(two_grad * ln2_gain, normal, scale)
        low = resid_two.astype(bf16)
        right_ref[0, r] = low
        x_ref[r] = resid_two
        fold_ref[3] += fold(low)
        fold_ref[4] += fold(two_grad * normal)
        fold_ref[5] += fold(two_grad)
        fold_ref[6] += fold(logit_grad * normed)
        fold_ref[7] += fold(jnp.broadcast_to(logit_grad, normal.shape))

    weight_ref[...] = term_cols_ref[...].T[0:1]

    def fall(c):
        wide_ref[c % 2] = lax.dot_general(right_ref[0], w_down_ref[columns(c), :], NT, preferred_element_type=f32)

    fall(0)
    for c in range(parts):
        if c + 1 < parts:
            fall(c + 1)
        for r in pieces:
            low = (wide_ref[c % 2, r] * slope_ref[r, columns(c)]).astype(bf16)
            right_ref[1 + c, r] = low
            in_fold_ref[:, columns(c)] += fold(low)
        x_ref[...] += lax.dot_general(right_ref[1 + c], w_in_ref[:, columns(c)], NT, preferred_element_type=f32)

    for r in pieces:
        one_grad = x_ref[r]
        normal = normal_ref[r]
        resid_one = normalize_back(one_grad * ln1_gain, normal, scale_ref[r])
        resid_ref[r] = resid_one
        low = resid_one.astype(bf16)
        right_ref[parts + 1, r] = low
        fold_ref[0] += fold(low)
        fold_ref[1] += fold(one_grad * normal)
        fold_ref[2] += fold(one_grad)
    grads = lax.dot_general(right_ref[parts + 1], w_out_ref[...], NT, preferred_element_type=f32).astype(bf16)

    @pl.when(head == 0)
    def _():
        my_grad_ref[...] = grads[:, :local_dim]
        their_grad_ref[...] = grads[:, local_dim:]

    @pl.when(head == 1)
    def _():
        my_grad_ref[...] = grads[:, local_dim:]
        their_grad_ref[...] = grads[:, :local_dim]

    @pl.when(pl.program_id(0) == pl.num_programs(0) - 1)
    def _():
        sums_ref[...] = jnp.zeros_like(sums_ref)
        sums_ref[0:8] = jnp.sum(fold_ref[...], axis=1)
        for c in range(parts):
            sums_ref[10 + c : 11 + c] = jnp.sum(in_fold_ref[:, columns(c)], axis=0, keepdims=True)


def middle(mine, theirs, tokens, grad_hidden, grad_term, w_out, w_in, w_down, vec, bias_in, term_bias):
    half, model_dim = tokens.shape
    local_dim = mine.shape[1]
    ffn_dim = w_in.shape[1]
    rows = min(TILE, half)

    def tile(cols):
        return pl.BlockSpec((rows, cols), lambda i: (i, 0))

    def whole(*shape):
        return pl.BlockSpec(shape, lambda i: (0, 0), pipeline_mode=pl.Buffered(1))

    stacked = pl.BlockSpec((ffn_dim // model_dim + 2, rows, model_dim), lambda i: (0, i, 0))
    stack = jax.ShapeDtypeStruct((ffn_dim // model_dim + 2, half, model_dim), bf16)

    def full(cols, kind):
        return jax.ShapeDtypeStruct((half, cols), kind)

    return pl.pallas_call(
        middle_kernel,
        grid=(half // rows,),
        in_specs=[
            tile(local_dim),
            tile(local_dim),
            tile(model_dim),
            tile(model_dim),
            pl.BlockSpec((1, rows), lambda i: (0, i)),
            whole(model_dim, model_dim),
            whole(model_dim, ffn_dim),
            whole(ffn_dim, model_dim),
            whole(8, model_dim),
            whole(1, ffn_dim),
            whole(1, 1),
        ],
        out_specs=[
            tile(model_dim),
            pl.BlockSpec((1, rows), lambda i: (0, i)),
            stacked,
            stacked,
            tile(model_dim),
            tile(local_dim),
            tile(local_dim),
            pl.BlockSpec((16, model_dim), lambda i: (0, 0)),
        ],
        scratch_shapes=[
            pltpu.VMEM((rows, ffn_dim), f32),
            pltpu.VMEM((2, rows, model_dim), f32),
            pltpu.VMEM((rows, model_dim), f32),
            pltpu.VMEM((rows, model_dim), f32),
            pltpu.VMEM((rows, 1), f32),
            pltpu.VMEM((8, 8, model_dim), f32),
            pltpu.VMEM((8, ffn_dim), f32),
            pltpu.VMEM((rows, LANES), f32),
            pltpu.VMEM((rows, LANES), f32),
        ],
        out_shape=[
            full(model_dim, bf16),
            jax.ShapeDtypeStruct((1, half), f32),
            stack,
            stack,
            full(model_dim, f32),
            full(local_dim, bf16),
            full(local_dim, bf16),
            jax.ShapeDtypeStruct((16, model_dim), f32),
        ],
        compiler_params=pltpu.CompilerParams(vmem_limit_bytes=VMEM_LIMIT),
        cost_estimate=pl.CostEstimate(flops=40_000_000_000, bytes_accessed=50_000_000, transcendentals=0),
    )(mine, theirs, tokens, grad_hidden, grad_term, w_out, w_in, w_down, vec, bias_in, term_bias)


def bit(place, which):
    return (place // 2**which) % 2


def flip(place, which):
    return place + (1 - 2 * bit(place, which)) * 2**which


def route(target, me, head):
    low, high = bit(target, 0), bit(target, 1)
    send = (1 - head) * ((low + bit(me, 0)) % 2) + head * ((high + bit(me, 1)) % 2)
    return send, 2 * (target // 4) + (1 - head) * high + head * low


def greet(partners):
    barrier = pltpu.get_barrier_semaphore()
    for partner in partners:
        pl.semaphore_signal(barrier, inc=1, device_id=partner, device_id_type=pl.DeviceIdType.MESH)
    pl.semaphore_wait(barrier, len(partners))


def remote(source, target, send_sem, recv_sem, partner):
    return pltpu.make_async_remote_copy(
        src_ref=source,
        dst_ref=target,
        send_sem=send_sem,
        recv_sem=recv_sem,
        device_id=partner,
        device_id_type=pl.DeviceIdType.MESH,
    )


def weights_kernel(
    n_dp,
    parts,
    left_ref,
    right_ref,
    my_cols_ref,
    their_cols_ref,
    vec_ref,
    keep_any,
    send_any,
    down_keep_any,
    down_send_any,
    grads_any,
    vec_out_ref,
    full_ref,
    recv_ref,
    rest_ref,
    down_ref,
    down_recv_ref,
    down_out_ref,
    vec_recv_ref,
    send_sem,
    recv_sem,
    down_sems,
    grad_sems,
    vec_sems,
    copy_sem,
):
    me, head = lax.axis_index("dp"), lax.axis_index("head")
    other = (me, 1 - head)
    first = (flip(me, 0) * (1 - head) + flip(me, 1) * head, head)
    mine = bit(me, 1) * (1 - head) + bit(me, 0) * head
    step = pl.program_id(0)
    steps = 2 * parts + 1
    model_dim = left_ref.shape[2]
    cols = model_dim // 2
    half = my_cols_ref.shape[0]
    down_rows = parts * model_dim // n_dp
    rows = model_dim // n_dp
    my_rows = grads_any.at[pl.ds(pl.multiple_of(head * half, half), half)]
    own_copy = pltpu.make_async_copy(my_cols_ref, my_rows, copy_sem.at[4])
    grad_copy = remote(their_cols_ref, my_rows, grad_sems.at[0], grad_sems.at[1], other)
    vec_copy = remote(vec_ref, vec_recv_ref, vec_sems.at[0], vec_sems.at[1], other)
    def exchange(k):
        return remote(full_ref.at[k % 3, 1 - head], recv_ref.at[k], send_sem.at[k], recv_sem.at[k], other)

    def down_copy(k):
        at = pl.ds(2 * k, 2)
        return remote(down_ref.at[1, at], down_recv_ref.at[at], down_sems.at[0, k], down_sems.at[1, k], first)

    def multiply():
        whole = lax.dot_general(left_ref[0], right_ref[0], TN, preferred_element_type=f32).astype(bf16)
        full_ref[step % 3, 0] = whole[:, :cols]
        full_ref[step % 3, 1] = whole[:, cols:]

    def total(k, start, count):
        return (
            full_ref[k % 3, head, start : start + count].astype(f32)
            + recv_ref[k, start : start + count, :].astype(f32)
        ).astype(bf16)

    def down_finish(k):
        for q in range(4):
            send, place = route(4 * k + q, me, head)
            down_ref[send, place] = total(k, q * down_rows, down_rows)

    def rest_finish(k):
        start = pl.multiple_of((k - parts) * rows, 16)
        for d in range(n_dp):
            send, place = route(d, me, head)
            rest_ref[send, place, pl.ds(start, rows), :] = total(k, d * rows, rows)

    @pl.when(step >= 3)
    def _():
        exchange(step - 3).wait_send()

    @pl.when(step == 0)
    def _():
        greet([other, first])
        grad_copy.start()
        vec_copy.start()
        own_copy.start()

    @pl.when(step < 2)
    def _():
        multiply()
        exchange(step).start()

    @pl.when((step >= 2) & (step < parts + 2))
    def _():
        exchange(step - 2).wait_recv()
        multiply()
        down_finish(step - 2)
        exchange(step).start()
        down_copy(step - 2).start()

    @pl.when(step >= parts + 2)
    def _():
        exchange(step - 2).wait_recv()
        multiply()
        rest_finish(step - 2)
        exchange(step).start()

    @pl.when(step == steps - 1)
    def _():
        for k in range(steps - 2, steps):
            exchange(k).wait_recv()
            rest_finish(k)
        copies = [
            pltpu.make_async_copy(rest_ref.at[0], keep_any, copy_sem.at[0]),
            pltpu.make_async_copy(rest_ref.at[1], send_any, copy_sem.at[1]),
            pltpu.make_async_copy(down_out_ref.at[0], down_keep_any, copy_sem.at[2]),
            pltpu.make_async_copy(down_out_ref.at[1], down_send_any, copy_sem.at[3]),
        ]
        for copy in copies[:2]:
            copy.start()
        for k in range(parts):
            down_copy(k).wait()

        def split(r, carry):
            for j in range(2):
                block = 2 * r + j * (1 - mine) + (1 - j) * mine
                whole = down_ref[0, block].astype(f32) + down_recv_ref[block].astype(f32)
                down_out_ref[j, r] = whole.astype(bf16)
            return carry

        lax.fori_loop(0, parts, split, 0)
        for copy in copies[2:]:
            copy.start()
        vec_copy.wait()
        vec_out_ref[...] = vec_ref[...] + vec_recv_ref[...]
        grad_copy.wait()
        own_copy.wait()
        for k in range(steps - 3, steps):
            exchange(k).wait_send()
        for copy in copies:
            copy.wait()


def weights(n_dp, left, right, my_cols, their_cols, vec):
    stack, half, model_dim = left.shape
    parts = stack - 2
    steps = 2 * parts + 1
    cols = model_dim // 2
    down_rows = parts * model_dim // n_dp
    rest_rows = (parts + 1) * model_dim // n_dp
    anywhere = pl.BlockSpec(memory_space=pl.ANY)

    def left_map(j):
        return (jnp.where(j < parts, j, jnp.where(j < 2 * parts, parts, parts + 1)), 0, 0)

    def right_map(j):
        return (jnp.where(j < parts, 0, j - parts + 1), 0, 0)

    rest = jax.ShapeDtypeStruct((n_dp // 2, rest_rows, cols), bf16)
    down = jax.ShapeDtypeStruct((n_dp // 4, down_rows, cols), bf16)
    return pl.pallas_call(
        partial(weights_kernel, n_dp, parts),
        grid=(steps,),
        in_specs=[
            pl.BlockSpec((1, half, model_dim), left_map),
            pl.BlockSpec((1, half, model_dim), right_map),
            pl.BlockSpec(my_cols.shape, lambda j: (0, 0), pipeline_mode=pl.Buffered(1)),
            pl.BlockSpec(my_cols.shape, lambda j: (0, 0), pipeline_mode=pl.Buffered(1)),
            pl.BlockSpec(vec.shape, lambda j: (0, 0)),
        ],
        out_specs=[anywhere] * 5 + [pl.BlockSpec(vec.shape, lambda j: (0, 0))],
        scratch_shapes=[
            pltpu.VMEM((3, 2, model_dim, cols), bf16),
            pltpu.VMEM((steps, model_dim, cols), bf16),
            pltpu.VMEM((2,) + rest.shape, bf16),
            pltpu.VMEM((2, n_dp // 2, down_rows, cols), bf16),
            pltpu.VMEM((n_dp // 2, down_rows, cols), bf16),
            pltpu.VMEM((2,) + down.shape, bf16),
            pltpu.VMEM(vec.shape, f32),
            pltpu.SemaphoreType.DMA((steps,)),
            pltpu.SemaphoreType.DMA((steps,)),
            pltpu.SemaphoreType.DMA((2, parts)),
            pltpu.SemaphoreType.DMA((2,)),
            pltpu.SemaphoreType.DMA((2,)),
            pltpu.SemaphoreType.DMA((5,)),
        ],
        out_shape=[
            rest,
            rest,
            down,
            down,
            jax.ShapeDtypeStruct((2 * half, my_cols.shape[1]), bf16),
            jax.ShapeDtypeStruct(vec.shape, f32),
        ],
        compiler_params=pltpu.CompilerParams(
            collective_id=0, has_side_effects=True, vmem_limit_bytes=VMEM_LIMIT
        ),
        cost_estimate=pl.CostEstimate(flops=15_000_000_000, bytes_accessed=20_000_000, transcendentals=0),
    )(left, right, my_cols, their_cols, vec)


def final_kernel(
    n_dp,
    chunks,
    d_keep_any,
    d_got_any,
    s_keep_any,
    s_got_any,
    raw_any,
    rows_any,
    w_any,
    resid_any,
    vec_ref,
    raw_sums_ref,
    core_send_ref,
    core_recv_ref,
    qkv_ref,
    vec_out_ref,
    vec_core_ref,
    tokens_any,
    t_recv_any,
    d_keep_ref,
    d_got_ref,
    d_own_ref,
    d_out_ref,
    d_got_z_ref,
    s_keep_ref,
    s_got_ref,
    raw_ref,
    rows_ref,
    w_ref,
    resid_ref,
    s_send_ref,
    s_recv_ref,
    s_own_ref,
    s_out_ref,
    s_got_z_ref,
    s_sum_ref,
    q_grad_ref,
    q_both_ref,
    q_first_ref,
    q_send_ref,
    q_recv_ref,
    q_own_ref,
    q_out_ref,
    q_got_z_ref,
    t_send_ref,
    vec_hold_ref,
    vec_recv_ref,
    in_sems,
    d_z_sems,
    s_sems,
    s_z_sems,
    q_first_sems,
    q_sems,
    q_z_sems,
    t_sems,
    core_sems,
    vec_sems,
    out_sem,
):
    me, head = lax.axis_index("dp"), lax.axis_index("head")
    line = n_dp // 4
    depth = line.bit_length() - 1
    z = me // 4
    other = (me, 1 - head)
    low = (flip(me, 0), head)
    high = (flip(me, 1), head)
    around = [(((z + j) % line) * 4 + me % 4, head) for j in range(1, line)]
    first = (flip(me, 0) * (1 - head) + flip(me, 1) * head, head)
    second = (flip(me, 1) * (1 - head) + flip(me, 0) * head, head)
    mine = bit(me, 1) * (1 - head) + bit(me, 0) * head
    half, model_dim = resid_ref.shape
    local_dim = raw_ref.shape[1] // 3
    size = s_keep_ref.shape[1] // chunks
    q_chunks, _, _, q_size, _ = q_both_ref.shape
    q_rows = q_chunks * q_size

    def piece(i):
        return slice(i * size, (i + 1) * size)

    s_loads = [
        pltpu.make_async_copy(s_keep_any, s_keep_ref, in_sems.at[0]),
        pltpu.make_async_copy(s_got_any, s_got_ref, in_sems.at[1]),
    ]
    q_loads = [
        pltpu.make_async_copy(rows_any, rows_ref, in_sems.at[2]),
        pltpu.make_async_copy(raw_any, raw_ref, in_sems.at[3]),
    ]
    t_loads = [
        pltpu.make_async_copy(w_any, w_ref, in_sems.at[4]),
        pltpu.make_async_copy(resid_any, resid_ref, in_sems.at[5]),
    ]
    d_loads = [
        pltpu.make_async_copy(d_keep_any, d_keep_ref, in_sems.at[6]),
        pltpu.make_async_copy(d_got_any, d_got_ref, in_sems.at[7]),
    ]
    for load in d_loads + s_loads:
        load.start()
    greet([low, high, other] + around)

    vec_hold_ref[0] = vec_ref[...]
    here = pl.ds(pl.multiple_of(head * local_dim, LANES), local_dim)
    vec_hold_ref[0, 8:9, here] = raw_sums_ref[:, :local_dim]
    vec_hold_ref[0, 9:10, here] = raw_sums_ref[:, 2 * local_dim :]

    def vec_copy(k):
        to = (low, high)[k] if k < 2 else around[k - 2]
        source = vec_hold_ref.at[min(k, 2)]
        return remote(source, vec_recv_ref.at[k], vec_sems.at[0, k], vec_sems.at[1, k], to)

    vec_copy(0).start()

    def fold_line(own_ref, hold_ref, got_ref, sems):
        def moved(k):
            count = line >> (k + 1)
            at = slice(line - 2 * count, line - count)
            return remote(hold_ref.at[at], got_ref.at[at], sems.at[0, k], sems.at[1, k], (flip(me, k + 2), head))

        def send(k):
            count = line >> (k + 1)
            keep = bit(me, k + 2)
            for q in range(count):
                hold_ref[line - 2 * count + q] = own_ref[2 * q + 1 - keep].astype(bf16)
            moved(k).start()

        def add(k):
            count = line >> (k + 1)
            keep = bit(me, k + 2)
            moved(k).wait()
            for q in range(count):
                own_ref[q] = own_ref[2 * q + keep] + got_ref[line - 2 * count + q].astype(f32)
            if k + 1 < depth:
                send(k + 1)

        return send, add

    d_line = fold_line(d_own_ref, d_out_ref, d_got_z_ref, d_z_sems)

    def s_copy(i):
        return remote(s_send_ref.at[i], s_recv_ref.at[i], s_sems.at[0, i], s_sems.at[1, i], second)

    def s_total(block, i):
        return s_keep_ref[block, piece(i)].astype(f32) + s_got_ref[block, piece(i)].astype(f32)

    def s_prepare(i):
        def send_block(r, carry):
            s_send_ref[i, r] = s_total(2 * r + 1 - mine, i).astype(bf16)
            return carry

        lax.fori_loop(0, line, send_block, 0)

    for load in s_loads:
        load.wait()
    for load in q_loads:
        load.start()
    for load in t_loads:
        load.start()
    for i in range(chunks):
        s_prepare(i)
        s_copy(i).start()
    for load in d_loads:
        load.wait()

    def d_block(r, carry):
        d_own_ref[r] = d_keep_ref[r].astype(f32) + d_got_ref[r].astype(f32)
        return carry

    lax.fori_loop(0, line, d_block, 0)
    d_line[0](0)

    for load in q_loads:
        load.wait()

    def q_columns(j, carry):
        at = pl.ds(pl.multiple_of(j * Q_COLUMNS, LANES), Q_COLUMNS)
        grad = lax.dot_general(rows_ref[:, at], raw_ref[...], TN, preferred_element_type=f32)
        q_grad_ref[pl.ds(pl.multiple_of(j * Q_COLUMNS, LANES), Q_COLUMNS), :] = grad.astype(bf16)
        return carry

    lax.fori_loop(0, model_dim // Q_COLUMNS, q_columns, 0)
    d_line[1](0)

    def q_place(d, carry):
        send, place = route(d, me, head)
        for j in range(q_chunks):
            at = pl.ds(pl.multiple_of(d * q_rows + j * q_size, 16), q_size)
            q_both_ref[j, send, place] = q_grad_ref[at, :]
        return carry

    lax.fori_loop(0, n_dp, q_place, 0)

    def q_copy(j):
        return remote(q_both_ref.at[j, 1], q_first_ref.at[j], q_first_sems.at[0, j], q_first_sems.at[1, j], first)

    def q_second(j):
        return remote(q_send_ref.at[j], q_recv_ref.at[j], q_sems.at[0, j], q_sems.at[1, j], second)

    s_line = [
        fold_line(s_own_ref.at[i], s_out_ref.at[i], s_got_z_ref.at[i], s_z_sems.at[i]) for i in range(chunks)
    ]
    q_line = [
        fold_line(q_own_ref.at[j], q_out_ref.at[j], q_got_z_ref.at[j], q_z_sems.at[j]) for j in range(q_chunks)
    ]

    def s_enter(i):
        s_copy(i).wait()

        def add_block(r, carry):
            s_own_ref[i, r] = s_total(2 * r + mine, i) + s_recv_ref[i, r].astype(f32)
            return carry

        lax.fori_loop(0, line, add_block, 0)
        s_line[i][0](0)

    def q_total(j, block):
        return q_both_ref[j, 0, block].astype(f32) + q_first_ref[j, block].astype(f32)

    def q_enter(j):
        q_copy(j).wait()

        def send_block(r, carry):
            q_send_ref[j, r] = q_total(j, 2 * r + 1 - mine).astype(bf16)
            return carry

        lax.fori_loop(0, line, send_block, 0)
        q_second(j).start()

        def own_block(r, carry):
            q_own_ref[j, r] = q_total(j, 2 * r + mine)
            return carry

        lax.fori_loop(0, line, own_block, 0)

    def q_turn(j):
        q_second(j).wait()

        def add_block(r, carry):
            q_own_ref[j, r] = q_own_ref[j, r] + q_recv_ref[j, r].astype(f32)
            return carry

        lax.fori_loop(0, line, add_block, 0)
        q_line[j][0](0)

    tile_rows = half // 4

    def token_rows(who, tile):
        at = pl.ds(pl.multiple_of(who * half + tile * tile_rows, tile_rows), tile_rows)
        total = 0.0
        for c in range(3):
            part = raw_ref[at, c * local_dim : (c + 1) * local_dim]
            total = total + lax.dot_general(part, w_ref[c], NT, preferred_element_type=f32)
        return total

    t_copy = remote(t_send_ref, t_recv_any, t_sems.at[0], t_sems.at[1], other)

    def send_tile(tile, carry):
        at = pl.ds(pl.multiple_of(tile * tile_rows, tile_rows), tile_rows)
        t_send_ref[at, :] = token_rows(1 - head, tile).astype(bf16)
        return carry

    def own_tile(tile, carry):
        at = pl.ds(pl.multiple_of(tile * tile_rows, tile_rows), tile_rows)
        resid_ref[at, :] = resid_ref[at, :] + token_rows(head, tile)
        return carry

    for j in range(q_chunks):
        q_copy(j).start()
    for i in range(chunks):
        s_enter(i)
    for load in t_loads:
        load.wait()
    lax.fori_loop(0, 4, send_tile, 0)
    t_copy.start()
    for i in range(chunks - 1):
        s_line[i][1](0)
    lax.fori_loop(0, 4, own_tile, 0)
    t_out = pltpu.make_async_copy(resid_ref, tokens_any, out_sem)
    t_out.start()
    vec_copy(0).wait()
    vec_hold_ref[1] = vec_hold_ref[0] + vec_recv_ref[0]
    vec_copy(1).start()
    q_enter(0)
    s_line[chunks - 1][1](0)
    for j in range(1, q_chunks):
        q_enter(j)
    vec_copy(1).wait()
    vec_hold_ref[2] = vec_hold_ref[1] + vec_recv_ref[1]
    for j in range(line - 1):
        vec_copy(2 + j).start()
    for j in range(q_chunks - 1):
        q_turn(j)
    d_rows = d_own_ref.shape[1]
    for k in range(1, depth):
        d_line[1](k)
    s_sum_ref[:d_rows, :] = d_own_ref[0]
    for i in range(chunks):
        for k in range(1, depth):
            s_line[i][1](k)
        s_sum_ref[d_rows + i * size : d_rows + (i + 1) * size, :] = s_own_ref[i, 0]
    pieces = core_pieces(s_sum_ref.shape[0], q_rows)

    def gather(target_ref, who):
        at = 0
        for start, count in pieces:
            here = pl.ds(pl.multiple_of(start + who * count, 8), count)
            target_ref[at : at + count, :] = s_sum_ref[here, :]
            at += count

    gather(core_send_ref.at[1], 1 - head)
    core_copy = remote(core_send_ref.at[1], core_recv_ref, core_sems.at[0], core_sems.at[1], other)
    core_copy.start()
    gather(core_send_ref.at[0], head)
    q_turn(q_chunks - 1)
    for j in range(line - 1):
        vec_copy(2 + j).wait()
    total = vec_hold_ref[2]
    for j in range(line - 1):
        total = total + vec_recv_ref[2 + j]
    vec_out_ref[...] = total
    core_vec = remote(vec_out_ref.at[pl.ds(8, 8)], vec_core_ref, core_sems.at[2], core_sems.at[3], other)
    core_vec.start()
    for k in range(depth):
        for j in range(q_chunks):
            q_line[j][1](k)
    for j in range(q_chunks):
        qkv_ref[j * q_size : (j + 1) * q_size, :] = q_own_ref[j, 0]
    core_vec.wait()
    core_copy.wait()
    t_copy.wait()
    t_out.wait()


def core_pieces(block_rows, rows):
    parts = (block_rows // rows - 1) // 2
    return [(0, parts * rows // 2)] + [(parts * rows + rows * c, rows // 2) for c in range(parts + 1)]


def final(n_dp, d_keep, d_got, s_keep, s_got, raw, group_rows, w_flat, resid, vec, raw_sums):
    line = n_dp // 4
    depth = line.bit_length() - 1
    _, rest_rows, cols = s_keep.shape
    down_rows = d_keep.shape[1]
    block_rows = down_rows + rest_rows
    half, model_dim = resid.shape
    local_dim = raw.shape[1] // 3
    q_rows, q_cols = model_dim // n_dp, 3 * local_dim
    chunks = 3 if rest_rows % 48 == 0 else 1
    size = rest_rows // chunks
    q_chunks = q_rows // 16
    anywhere = pl.BlockSpec(memory_space=pl.ANY)
    vmem = pl.BlockSpec(memory_space=pltpu.VMEM)

    def low(*dims):
        return pltpu.VMEM(dims, bf16)

    def wide(*dims):
        return pltpu.VMEM(dims, f32)

    def shape(*dims):
        return jax.ShapeDtypeStruct(dims, f32)

    def sems(*dims):
        return pltpu.SemaphoreType.DMA(dims)

    return pl.pallas_call(
        partial(final_kernel, n_dp, chunks),
        in_specs=[anywhere] * 8 + [vmem] * 2,
        out_specs=[vmem] * 5 + [anywhere] * 2,
        scratch_shapes=[
            low(*d_keep.shape),
            low(*d_keep.shape),
            wide(*d_keep.shape),
            low(*d_keep.shape),
            low(line - 1, down_rows, cols),
            low(*s_keep.shape),
            low(*s_keep.shape),
            low(*raw.shape),
            low(*group_rows.shape),
            low(*w_flat.shape),
            wide(half, model_dim),
            low(chunks, line, size, cols),
            low(chunks, line, size, cols),
            wide(chunks, line, size, cols),
            low(chunks, line, size, cols),
            low(chunks, line - 1, size, cols),
            wide(block_rows, cols),
            low(model_dim, q_cols),
            low(q_chunks, 2, 2 * line, 16, q_cols),
            low(q_chunks, 2 * line, 16, q_cols),
            low(q_chunks, line, 16, q_cols),
            low(q_chunks, line, 16, q_cols),
            wide(q_chunks, line, 16, q_cols),
            low(q_chunks, line, 16, q_cols),
            low(q_chunks, line - 1, 16, q_cols),
            low(half, model_dim),
            wide(3, *vec.shape),
            wide(1 + line, *vec.shape),
            sems(8),
            sems(2, depth),
            sems(2, chunks),
            sems(chunks, 2, depth),
            sems(2, q_chunks),
            sems(2, q_chunks),
            sems(q_chunks, 2, depth),
            sems(2),
            sems(4),
            sems(2, 1 + line),
            pltpu.SemaphoreType.DMA,
        ],
        out_shape=[
            shape(2, block_rows // 2, cols),
            shape(block_rows // 2, cols),
            shape(q_rows, q_cols),
            shape(*vec.shape),
            shape(8, model_dim),
            shape(half, model_dim),
            jax.ShapeDtypeStruct((half, model_dim), bf16),
        ],
        compiler_params=pltpu.CompilerParams(
            collective_id=1, has_side_effects=True, vmem_limit_bytes=VMEM_LIMIT
        ),
        cost_estimate=pl.CostEstimate(flops=12_000_000_000, bytes_accessed=25_000_000, transcendentals=0),
    )(d_keep, d_got, s_keep, s_got, raw, group_rows, w_flat, resid, vec, raw_sums)


def finish_kernel(
    n_dp,
    parts,
    own_ref,
    got_ref,
    kept_ref,
    core_ref,
    qkv_ref,
    vec_ref,
    vec_core_ref,
    tokens_ref,
    grad_qkv_ref,
    down_ref,
    in_ref,
    out_ref,
    qv_ref,
    in_bias_ref,
    term_ref,
    *vector_refs,
):
    tokens_ref[...] = own_ref[...] + got_ref[...].astype(f32)

    @pl.when(pl.program_id(0) == 0)
    def _():
        head = lax.axis_index("head")
        place = 2 * lax.axis_index("dp") + head
        cols = kept_ref.shape[2]
        model_dim = 2 * cols
        rows = out_ref.shape[0]
        width = model_dim // (2 * n_dp)
        starts = [0, parts * rows] + [parts * rows + rows * (c + 1) for c in range(parts + 1)]
        for who, source in ((head, kept_ref.at[0]), (1 - head, core_ref)):
            start = who * cols
            here = pl.ds(pl.multiple_of(start, LANES), cols)
            down_ref[:, here] = source[starts[0] : starts[1], :]
            for c in range(parts):
                shifted = pl.ds(pl.multiple_of(2 * cols * c + start, LANES), cols)
                in_ref[:, shifted] = source[starts[1 + c] : starts[2 + c], :]
            out_ref[:, here] = source[starts[1 + parts] : starts[2 + parts], :]
        for c in range(3):
            grad_qkv_ref[c] = qkv_ref[:, c * cols : (c + 1) * cols]
        shift = lax.rem(model_dim - place * width, model_dim)
        turned = pltpu.roll(vec_ref[0:8], shift, 1)
        for j, ref in enumerate(vector_refs):
            ref[...] = turned[j : j + 1, :width]
        term_ref[...] = vec_ref[7:8, :1]
        turned = pltpu.roll(vec_ref[8:16] + vec_core_ref[...], shift, 1)
        qv_ref[...] = turned[:2, :width]
        in_width = parts * model_dim // (2 * n_dp)
        per_row = model_dim // in_width
        row = vec_ref[pl.ds(10 + place // per_row, 1), :]
        row = jnp.broadcast_to(row, (8, model_dim))
        turned = pltpu.roll(row, lax.rem(model_dim - (place % per_row) * in_width, model_dim), 1)
        in_bias_ref[...] = turned[0:1, :in_width]


def finish(n_dp, parts, kept, core, qkv, vec, vec_core, own, got):
    half, model_dim = own.shape
    q_rows = qkv.shape[0]
    width = model_dim // (2 * n_dp)
    rows = min(512, half)
    tile = pl.BlockSpec((rows, model_dim), lambda i: (i, 0))

    def whole(dims):
        return pl.BlockSpec(dims, lambda i: (0,) * len(dims))

    out = [
        (3, q_rows, model_dim // 2),
        (parts * width, model_dim),
        (width, parts * model_dim),
        (width, model_dim),
        (2, width),
        (1, parts * width),
        (1, 1),
    ] + [(1, width)] * 7
    return pl.pallas_call(
        partial(finish_kernel, n_dp, parts),
        grid=(half // rows,),
        in_specs=[tile, tile] + [whole(x.shape) for x in (kept, core, qkv, vec, vec_core)],
        out_specs=[tile] + [whole(dims) for dims in out],
        out_shape=[jax.ShapeDtypeStruct((half, model_dim), f32)] + [jax.ShapeDtypeStruct(dims, f32) for dims in out],
        compiler_params=pltpu.CompilerParams(vmem_limit_bytes=VMEM_LIMIT),
        cost_estimate=pl.CostEstimate(flops=1_000_000, bytes_accessed=10_000_000, transcendentals=0),
    )(own, got, kept, core, qkv, vec, vec_core)


def take(array, index, axis=0):
    return lax.dynamic_index_in_dim(array, index, axis, keepdims=False)


class Links:
    def __init__(self, n_dp):
        self.n_dp = n_dp
        self.bits = n_dp.bit_length() - 1
        self.dp = lax.axis_index("dp")
        self.head = lax.axis_index("head")

    def bit(self, which):
        return (self.dp >> which) & 1

    def permute(self, array, partner):
        pairs = []
        for d in range(self.n_dp):
            for h in range(2):
                to_d, to_h = partner(d, h)
                pairs.append((2 * d + h, 2 * to_d + to_h))
        return lax.ppermute(array, AXES, pairs)

    def swap_head(self, array):
        return self.permute(array, lambda d, h: (d, 1 - h))

    def swap_bit(self, array, which):
        return self.permute(array, lambda d, h: (d ^ (1 << which), h))

    def scatter_heads(self, blocks):
        got = self.swap_head(take(blocks, 1 - self.head, 1))
        return (take(blocks, self.head, 1).astype(f32) + got.astype(f32)).astype(bf16)

    def scatter_dp(self, blocks):
        tail = blocks.shape[1:]
        b0, b1 = self.bit(0), self.bit(1)
        first = self.head == 0
        blocks = blocks.reshape((self.n_dp // 4, 4) + tail)

        def two(one, other):
            i = jnp.where(first, one, 2 * other)
            j = jnp.where(first, 2 + one, 2 * other + 1)
            return jnp.stack([take(blocks, i, 1), take(blocks, j, 1)], axis=1)

        got = self.permute(two(1 - b0, 1 - b1), lambda d, h: (d ^ (1 if h == 0 else 2), h))
        blocks = (two(b0, b1).astype(f32) + got.astype(f32)).astype(bf16)
        mine = jnp.where(first, b1, b0)
        got = self.permute(take(blocks, 1 - mine, 1), lambda d, h: (d ^ (2 if h == 0 else 1), h))
        blocks = take(blocks, mine, 1).astype(f32) + got.astype(f32)
        for which in range(2, self.bits):
            blocks = blocks.reshape((-1, 2) + tail)
            mine = self.bit(which)
            got = self.swap_bit(take(blocks, 1 - mine, 1).astype(bf16), which)
            blocks = take(blocks, mine, 1) + got.astype(f32)
        return blocks.reshape(tail)

    def total(self, array):
        array = array + self.swap_head(array)
        for which in range(self.bits):
            array = array + self.swap_bit(array, which)
        return array


def shards(
    n_dp,
    tokens,
    lengths,
    w_qkv,
    bias_qv,
    w_out,
    bias_out,
    ln1_gain,
    ln1_bias,
    w_in,
    bias_in,
    w_down,
    bias_down,
    ln2_gain,
    ln2_bias,
    term_w,
    term_bias,
    grad_hidden,
    grad_term,
):
    links = Links(n_dp)
    head = links.head
    half, model_dim = tokens.shape
    row_len = 2 * half
    local_dim = w_qkv.shape[2]
    ffn_dim = w_in.shape[1]

    boundary = jnp.cumsum(lengths[0])
    places = jnp.arange(row_len, dtype=jnp.int32)
    segment = jnp.sum((places[:, None] >= boundary[None, :]).astype(jnp.int32), axis=-1)
    seg_col = jnp.broadcast_to(segment[:, None], (row_len, LANES))
    seg_row = jnp.broadcast_to(segment[None, :], (8, row_len))

    def both(mine, theirs, axis):
        return jnp.where(
            head == 0,
            jnp.concatenate([mine, theirs], axis=axis),
            jnp.concatenate([theirs, mine], axis=axis),
        )

    w_parts = jnp.transpose(w_qkv, (1, 0, 2))
    group_rows = both(tokens, links.swap_head(tokens), 0)
    queries, key_rows, value_rows = [jnp.dot(group_rows, w_parts[c], preferred_element_type=f32) for c in range(3)]
    queries = ((queries + bias_qv[:, 0]) * HEAD_DIM ** (-0.5)).astype(bf16)
    key_rows = key_rows.astype(bf16)
    value_rows = (value_rows + bias_qv[:, 1]).astype(bf16)
    theirs, mine, logs = attend(lengths, head, queries, key_rows, value_rows, seg_col, seg_row)

    def my_half(rows):
        return lax.dynamic_slice_in_dim(rows, head * half, half, 0)

    def their_half(rows):
        return lax.dynamic_slice_in_dim(rows, (1 - head) * half, half, 0)

    vec = jnp.stack([bias_out, ln1_gain, ln1_bias, bias_down, ln2_gain, ln2_bias, term_w, jnp.zeros_like(term_w)])
    hidden_out, term_weight, left, right, resid_one_grad, my_cols, their_cols, vec = middle(
        mine,
        links.swap_head(theirs),
        tokens,
        grad_hidden,
        grad_term[None, :],
        w_out,
        w_in,
        w_down,
        vec,
        bias_in[None, :],
        term_bias[None, :],
    )
    parts = ffn_dim // model_dim
    in_kernels = (model_dim // n_dp) % 16 == 0 and n_dp == 4 * parts

    def back(grads):
        return attend_back(lengths, queries, key_rows, value_rows, grads, logs, seg_col, seg_row)

    if in_kernels:
        s_keep, s_send, d_keep, d_send, head_grad, vec = weights(n_dp, left, right, my_cols, their_cols, vec)
        d_got = links.permute(d_send, lambda d, h: (d ^ (2 if h == 0 else 1), h))
        s_got = links.permute(s_send, lambda d, h: (d ^ (1 if h == 0 else 2), h))
        raw, raw_sums = back(head_grad)
        kept, core, qkv, vec, vec_core, own, got = final(
            n_dp, d_keep, d_got, s_keep, s_got, raw, group_rows, w_parts, resid_one_grad, vec, raw_sums
        )
        (grad_tokens, grad_qkv, grad_down, grad_in, grad_out, bias_qv_mine, bias_in_mine, term_total, *vectors) = finish(
            n_dp, parts, kept, core, qkv, vec, vec_core, own, got
        )
        grad_qkv = jnp.transpose(grad_qkv, (1, 0, 2))
        bias_qv_mine = bias_qv_mine.T
        bias_in_mine = bias_in_mine.reshape(-1)
        term_total = term_total.reshape(1)
        mine = [v.reshape(-1) for v in vectors]
    else:
        raw, raw_sums = back(both(my_cols, links.swap_head(their_cols), 0))

        def product(i, j):
            return lax.dot_general(left[i], right[j], TN, preferred_element_type=f32).astype(bf16)

        def reduced(partial_sum):
            rows, cols = partial_sum.shape
            return links.scatter_dp(links.scatter_heads(partial_sum.reshape(n_dp, 2, rows // (2 * n_dp), cols)))

        grad_down = reduced(jnp.concatenate([product(i, 0) for i in range(parts)]))
        grad_in = reduced(jnp.concatenate([product(parts, 1 + i) for i in range(parts)], axis=1))
        grad_out = reduced(product(parts + 1, parts + 1))
        w_flat = w_qkv.reshape(model_dim, 3 * local_dim)
        grad = lax.dot_general(raw, w_flat, NT, preferred_element_type=f32)
        received = links.swap_head(their_half(grad).astype(bf16))
        grad_tokens = resid_one_grad + my_half(grad) + received.astype(f32)
        qkv_local = lax.dot_general(group_rows, raw, TN, preferred_element_type=f32).astype(bf16)
        grad_qkv = links.scatter_dp(qkv_local.reshape(n_dp, model_dim // n_dp, 3 * local_dim))
        value_sums = lax.dynamic_update_slice(
            jnp.zeros((2, 2 * local_dim), f32),
            jnp.concatenate([raw_sums[:, :local_dim], raw_sums[:, 2 * local_dim :]]),
            (jnp.int32(0), head * local_dim),
        )
        vectors = links.total(lax.dynamic_update_slice(vec, value_sums, (8, 0)))
        grad_qkv = grad_qkv.reshape(model_dim // n_dp, 3, local_dim)
        place = 2 * links.dp + head
        width = model_dim // (2 * n_dp)
        mine = lax.dynamic_slice_in_dim(vectors, place * width, width, 1)
        in_width = ffn_dim // (2 * n_dp)
        in_row = vectors[10 : 10 + parts].reshape(-1)
        bias_in_mine = lax.dynamic_slice_in_dim(in_row, place * in_width, in_width, 0)
        bias_qv_mine = mine[8:10].T
        term_total = vectors[7, :1]

    return (
        hidden_out,
        term_weight.reshape(-1),
        grad_tokens,
        grad_qkv,
        bias_qv_mine,
        grad_out,
        mine[0],
        mine[1],
        mine[2],
        grad_in,
        bias_in_mine,
        grad_down,
        mine[3],
        mine[4],
        mine[5],
        mine[6],
        term_total,
    )


def solution(mesh):
    rows = P(AXES, None)
    return jax.shard_map(
        partial(shards, mesh.shape["dp"]),
        mesh=mesh,
        in_specs=(rows, P("dp", None), P(None, None, "head"), P("head", None))
        + (P(),) * 12
        + (rows, P(AXES)),
        out_specs=(
            rows,
            P(AXES),
            rows,
            P("dp", None, "head"),
            rows,
            rows,
            P(AXES),
            P(AXES),
            P(AXES),
            rows,
            P(AXES),
            rows,
            P(AXES),
            P(AXES),
            P(AXES),
            P(AXES),
            P(),
        ),
        check_vma=False,
    )
```

```python
from functools import partial

import jax
import jax.numpy as jnp
from jax import lax
from jax.experimental import pallas as pl
from jax.experimental.pallas import tpu as pltpu
from jax.sharding import PartitionSpec as P

HEAD_DIM = 64
LANES = 128
VMEM_LIMIT = 60 * 2**20
Q_ROWS = 256
PIECE = 32
Q_COLUMNS = 128
WIDTHS = (2, 3, 4, 5, 6, 8, 10)
BACK_WIDTHS = (2, 3, 4, 5, 6, 7, 8, 10)
AXES = ("dp", "head")

f32 = jnp.float32
bf16 = jnp.bfloat16
norm_eps = 1e-06
NT = (((1,), (1,)), ((), ()))
TN = (((0,), (0,)), ((), ()))


def key_range(lengths_ref, first, rows, row_len):
    start = jnp.int32(0)
    low = jnp.int32(0)
    high = jnp.int32(row_len)
    for j in range(lengths_ref.shape[1]):
        end = start + lengths_ref[0, j]
        low = jnp.where(start <= first, start, low)
        high = jnp.where(end >= first + rows, jnp.minimum(high, end), high)
        start = end
    low_block = low // LANES
    count = (high + LANES - 1) // LANES - low_block
    return low_block, count


def by_width(lengths_ref, first, rows, row_len, body, choices=WIDTHS):
    blocks = row_len // LANES
    low_block, count = key_range(lengths_ref, first, rows, row_len)
    widths = sorted({min(w, blocks) for w in choices})
    below = 0
    for width in widths:

        @pl.when((count > below) & (count <= width))
        def _(width=width):
            begin = jnp.minimum(low_block, blocks - width)
            body(pl.multiple_of(begin * LANES, LANES), width * LANES)

        below = width


def query_block(step, steps, head):
    return lax.rem(step + (1 - head) * (steps // 2), steps)


def attend_kernel(
    lengths_ref,
    head_ref,
    q_ref,
    k_ref,
    v_ref,
    segc_ref,
    segr_ref,
    theirs_ref,
    mine_ref,
    log_ref,
    mask_ref,
    cols_ref,
    s_ref,
    p_ref,
    o_ref,
):
    rows, local_dim = q_ref.shape
    row_len = k_ref.shape[0]
    step, steps = pl.program_id(0), pl.num_programs(0)
    first = query_block(step, steps, head_ref[0]) * rows
    lane = lax.broadcasted_iota(jnp.int32, (rows, LANES), 1)

    def body(begin, width):
        same = segc_ref[:, 0:1] == segr_ref[0:1, pl.ds(begin, width)]
        mask_ref[:, :width] = jnp.where(same, 0.0, -1e30)

        heads = local_dim // HEAD_DIM

        def score(i):
            cols = slice(i // 2 * LANES, i // 2 * LANES + LANES)
            q_pair = q_ref[:, cols]
            q_one = jnp.where((lane // HEAD_DIM) == i % 2, q_pair, jnp.zeros_like(q_pair))
            k_pair = k_ref[pl.ds(begin, width), cols]
            s_ref[i % 2, :, :width] = lax.dot_general(q_one, k_pair, NT, preferred_element_type=f32)

        def soft(i):
            for r in range(0, rows, PIECE):
                part = slice(r, r + PIECE)
                scores = s_ref[i % 2, part, :width] + mask_ref[part, :width]
                row_max = jnp.max(scores, axis=1, keepdims=True)
                powers = jnp.exp(scores - row_max)
                total = jnp.sum(powers, axis=1, keepdims=True)
                p_ref[i % 2, part, :width] = (powers * (1.0 / total)).astype(bf16)
                log_total = row_max + jnp.log(total)
                cols_ref[part] = jnp.where(lane[part] == i, log_total, cols_ref[part])

        def value(i):
            cols = slice(i // 2 * LANES, i // 2 * LANES + LANES)
            return jnp.dot(p_ref[i % 2, :, :width], v_ref[pl.ds(begin, width), cols], preferred_element_type=f32)

        score(0)
        held = None
        for i in range(heads):
            if i + 1 < heads:
                score(i + 1)
            soft(i)
            out = value(i)
            if i % 2 == 0:
                held = out
            else:
                cols = slice(i // 2 * LANES, i // 2 * LANES + LANES)
                o_ref[:, cols] = jnp.where(lane < HEAD_DIM, held, out).astype(bf16)

    by_width(lengths_ref, first, rows, row_len, body)
    log_ref[...] = cols_ref[...].T[: log_ref.shape[0]]

    @pl.when(step < steps // 2)
    def _():
        theirs_ref[...] = o_ref[...]

    @pl.when(step >= steps // 2)
    def _():
        mine_ref[...] = o_ref[...]


def attend(lengths, head, queries, key_rows, value_rows, seg_col, seg_row):
    row_len, local_dim = queries.shape
    rows = min(Q_ROWS, row_len // 2)
    steps = row_len // rows
    whole = pl.BlockSpec((row_len, local_dim), lambda i, n, h: (0, 0))
    return pl.pallas_call(
        attend_kernel,
        grid_spec=pltpu.PrefetchScalarGridSpec(
            num_scalar_prefetch=2,
            grid=(steps,),
            in_specs=[
                pl.BlockSpec((rows, local_dim), lambda i, n, h: (query_block(i, steps, h[0]), 0)),
                whole,
                whole,
                pl.BlockSpec((rows, LANES), lambda i, n, h: (query_block(i, steps, h[0]), 0)),
                pl.BlockSpec((8, row_len), lambda i, n, h: (0, 0)),
            ],
            out_specs=[
                pl.BlockSpec((rows, local_dim), lambda i, n, h: (jnp.minimum(i, steps // 2 - 1), 0)),
                pl.BlockSpec((rows, local_dim), lambda i, n, h: (jnp.maximum(i - steps // 2, 0), 0)),
                pl.BlockSpec((8, rows), lambda i, n, h: (0, query_block(i, steps, h[0]))),
            ],
            scratch_shapes=[
                pltpu.VMEM((rows, max(WIDTHS) * LANES), f32),
                pltpu.VMEM((rows, LANES), f32),
                pltpu.VMEM((2, rows, max(WIDTHS) * LANES), f32),
                pltpu.VMEM((2, rows, max(WIDTHS) * LANES), bf16),
                pltpu.VMEM((rows, local_dim), bf16),
            ],
        ),
        out_shape=[
            jax.ShapeDtypeStruct((row_len // 2, local_dim), bf16),
            jax.ShapeDtypeStruct((row_len // 2, local_dim), bf16),
            jax.ShapeDtypeStruct((8, row_len), f32),
        ],
        compiler_params=pltpu.CompilerParams(vmem_limit_bytes=32 * 2**20),
        cost_estimate=pl.CostEstimate(flops=20_000_000_000, bytes_accessed=8_000_000, transcendentals=0),
    )(lengths, head[None], queries, key_rows, value_rows, seg_col, seg_row)


def attend_back_kernel(
    lengths_ref,
    q_ref,
    k_ref,
    v_ref,
    g_ref,
    log_ref,
    segc_ref,
    segr_ref,
    raw_ref,
    sums_ref,
    mask_ref,
    dk_ref,
    dv_ref,
    s_ref,
    d_ref,
    p_ref,
    e_ref,
    ones_ref,
):
    rows, local_dim = q_ref.shape
    row_len = k_ref.shape[0]
    step = pl.program_id(0)
    first = step * rows
    lane = lax.broadcasted_iota(jnp.int32, (rows, LANES), 1)

    @pl.when(step == 0)
    def _():
        dk_ref[...] = jnp.zeros_like(dk_ref)
        dv_ref[...] = jnp.zeros_like(dv_ref)

    def body(begin, width):
        keys = pl.ds(begin, width)
        same = segc_ref[keys, 0:1] == segr_ref[0:1, :]
        mask_ref[:width, :] = jnp.where(same, 0.0, -1e30)

        def pair_step(pair, carry):
            cols = pl.ds(pl.multiple_of(pair * LANES, LANES), LANES)

            def products(i):
                mine = (lane // HEAD_DIM) == i
                here = slice(i * rows, i * rows + rows)
                q_pair, g_pair = q_ref[:, cols], g_ref[:, cols]
                q_one = jnp.where(mine, q_pair, jnp.zeros_like(q_pair))
                g_one = jnp.where(mine, g_pair, jnp.zeros_like(g_pair))
                ones_ref[0, here] = q_one
                ones_ref[1, here] = g_one
                s_ref[i, :width] = lax.dot_general(k_ref[keys, cols], q_one, NT, preferred_element_type=f32)
                d_ref[i, :width] = lax.dot_general(v_ref[keys, cols], g_one, NT, preferred_element_type=f32)

            def soft(i):
                here = slice(i * rows, i * rows + rows)
                log_row = log_ref[pl.ds(2 * pair + i, 1), :]
                inner = jnp.zeros((8, rows), f32)
                for r in range(0, width, PIECE):
                    part = slice(r, r + PIECE)
                    probs = jnp.exp(s_ref[i, part] + mask_ref[part] - log_row)
                    s_ref[i, part] = probs
                    p_ref[part, here] = probs.astype(bf16)
                    inner = inner + jnp.sum((probs * d_ref[i, part]).reshape(PIECE // 8, 8, rows), axis=0)
                inner = jnp.sum(inner, axis=0, keepdims=True)
                for r in range(0, width, PIECE):
                    part = slice(r, r + PIECE)
                    e_ref[part, here] = (s_ref[i, part] * (d_ref[i, part] - inner)).astype(bf16)

            def gather(i):
                here = slice(i * rows, i * rows + rows)
                dv_ref[keys, cols] += jnp.dot(p_ref[:width, here], ones_ref[1, here], preferred_element_type=f32)
                dk_ref[keys, cols] += jnp.dot(e_ref[:width, here], ones_ref[0, here], preferred_element_type=f32)
                return lax.dot_general(e_ref[:width, here], k_ref[keys, cols], TN, preferred_element_type=f32)

            products(0)
            products(1)
            soft(0)
            dq_first = gather(0)
            soft(1)
            dq_second = gather(1)
            dq_low = jnp.where(lane < HEAD_DIM, dq_first, dq_second).astype(bf16)
            raw_ref[pl.ds(pl.multiple_of(first, rows), rows), cols] = dq_low * jnp.asarray(HEAD_DIM**-0.5, bf16)
            return carry

        lax.fori_loop(0, local_dim // LANES, pair_step, 0)

    by_width(lengths_ref, first, rows, row_len, body, BACK_WIDTHS)

    @pl.when(step == pl.num_programs(0) - 1)
    def _():
        raw_ref[:, local_dim : 2 * local_dim] = dk_ref[...].astype(bf16)
        raw_ref[:, 2 * local_dim :] = dv_ref[...].astype(bf16)
        sums_ref[...] = jnp.sum(raw_ref[...].astype(f32), axis=0, keepdims=True)


def attend_back(lengths, queries, key_rows, value_rows, grads, logs, seg_col, seg_row):
    row_len, local_dim = queries.shape
    rows = min(Q_ROWS, row_len)
    whole = pl.BlockSpec((row_len, local_dim), lambda i, n: (0, 0))
    block = pl.BlockSpec((rows, local_dim), lambda i, n: (i, 0))
    return pl.pallas_call(
        attend_back_kernel,
        grid_spec=pltpu.PrefetchScalarGridSpec(
            num_scalar_prefetch=1,
            grid=(row_len // rows,),
            in_specs=[
                block,
                whole,
                whole,
                block,
                pl.BlockSpec((8, rows), lambda i, n: (0, i)),
                pl.BlockSpec((row_len, LANES), lambda i, n: (0, 0)),
                pl.BlockSpec((8, rows), lambda i, n: (0, i)),
            ],
            out_specs=[
                pl.BlockSpec((row_len, 3 * local_dim), lambda i, n: (0, 0)),
                pl.BlockSpec((1, 3 * local_dim), lambda i, n: (0, 0)),
            ],
            scratch_shapes=[
                pltpu.VMEM((max(WIDTHS) * LANES, rows), f32),
                pltpu.VMEM((row_len, local_dim), f32),
                pltpu.VMEM((row_len, local_dim), f32),
                pltpu.VMEM((2, max(WIDTHS) * LANES, rows), f32),
                pltpu.VMEM((2, max(WIDTHS) * LANES, rows), f32),
                pltpu.VMEM((max(WIDTHS) * LANES, 2 * rows), bf16),
                pltpu.VMEM((max(WIDTHS) * LANES, 2 * rows), bf16),
                pltpu.VMEM((2, 2 * rows, LANES), bf16),
            ],
        ),
        out_shape=[
            jax.ShapeDtypeStruct((row_len, 3 * local_dim), bf16),
            jax.ShapeDtypeStruct((1, 3 * local_dim), f32),
        ],
        compiler_params=pltpu.CompilerParams(vmem_limit_bytes=VMEM_LIMIT),
        cost_estimate=pl.CostEstimate(flops=40_000_000_000, bytes_accessed=12_000_000, transcendentals=0),
    )(lengths, queries, key_rows, value_rows, grads, logs, seg_col, seg_row)


TILE = 256


def gelu_both(x):
    cdf = 0.5 + 0.5 * lax.erf(x * 0.7071067811865476)
    density = jnp.exp(-0.5 * x * x) * 0.3989422804014327
    return x * cdf, cdf + x * density


def normalize(resid):
    center = resid - jnp.mean(resid, axis=-1, keepdims=True)
    scale = lax.rsqrt(jnp.mean(center * center, axis=-1, keepdims=True) + norm_eps)
    return center * scale, scale


def normalize_back(grad, normed, scale):
    shift = jnp.mean(grad, axis=-1, keepdims=True)
    slope = jnp.mean(grad * normed, axis=-1, keepdims=True)
    return scale * (grad - shift - normed * slope)


def fold(x):
    return jnp.sum(x.astype(f32).reshape(x.shape[0] // 8, 8, x.shape[1]), axis=0)


def middle_kernel(
    mine_ref,
    theirs_ref,
    tokens_ref,
    hid_ref,
    term_ref,
    w_out_ref,
    w_in_ref,
    w_down_ref,
    vec_ref,
    bias_in_ref,
    term_bias_ref,
    hidden_ref,
    weight_ref,
    left_ref,
    right_ref,
    resid_ref,
    my_grad_ref,
    their_grad_ref,
    sums_ref,
    slope_ref,
    wide_ref,
    x_ref,
    normal_ref,
    scale_ref,
    fold_ref,
    in_fold_ref,
    term_cols_ref,
    term_in_ref,
):
    head = lax.axis_index("head")
    local_dim = mine_ref.shape[1]
    model_dim = w_out_ref.shape[0]
    parts = w_in_ref.shape[1] // model_dim
    rows = tokens_ref.shape[0]
    pieces = [slice(r, r + PIECE) for r in range(0, rows, PIECE)]
    bias_out, ln1_gain, ln1_bias = vec_ref[0:1], vec_ref[1:2], vec_ref[2:3]
    bias_down, ln2_gain, ln2_bias, term_w = vec_ref[3:4], vec_ref[4:5], vec_ref[5:6], vec_ref[6:7]

    @pl.when(pl.program_id(0) == 0)
    def _():
        fold_ref[...] = jnp.zeros_like(fold_ref)
        in_fold_ref[...] = jnp.zeros_like(in_fold_ref)

    term_in_ref[...] = jnp.broadcast_to(term_ref[...], (LANES, rows)).T
    left_ref[parts + 1, :, pl.ds(pl.multiple_of(head * local_dim, LANES), local_dim)] = mine_ref[...]
    left_ref[parts + 1, :, pl.ds(pl.multiple_of((1 - head) * local_dim, LANES), local_dim)] = theirs_ref[...]
    x_ref[...] = jnp.dot(left_ref[parts + 1], w_out_ref[...], preferred_element_type=f32)
    for r in pieces:
        normal, scale = normalize(tokens_ref[r].astype(f32) + (x_ref[r] + bias_out))
        normed = normal * ln1_gain + ln1_bias
        normal_ref[r] = normal
        scale_ref[r] = scale
        left_ref[parts, r] = normed.astype(bf16)
        x_ref[r] = normed + bias_down

    def columns(c):
        return slice(c * model_dim, (c + 1) * model_dim)

    def rise(c):
        wide_ref[c % 2] = jnp.dot(left_ref[parts], w_in_ref[:, columns(c)], preferred_element_type=f32)

    rise(0)
    for c in range(parts):
        if c + 1 < parts:
            rise(c + 1)
        for r in pieces:
            value, slope = gelu_both(wide_ref[c % 2, r] + bias_in_ref[:, columns(c)])
            left_ref[c, r] = value.astype(bf16)
            slope_ref[r, columns(c)] = slope
        x_ref[...] += jnp.dot(left_ref[c], w_down_ref[columns(c), :], preferred_element_type=f32)

    for r in pieces:
        normal, scale = normalize(x_ref[r])
        normed = normal * ln2_gain + ln2_bias
        hidden_ref[r] = normed.astype(bf16)
        logit = jnp.sum(normed * term_w, axis=-1, keepdims=True) + term_bias_ref[0:1, 0:1]
        small = jnp.exp(-jnp.abs(logit))
        term_cols_ref[r] = jnp.broadcast_to(jnp.maximum(logit, 0.0) + jnp.log1p(small), (PIECE, LANES))
        logit_grad = term_in_ref[r, 0:1] * (jnp.where(logit >= 0.0, 1.0, small) / (1.0 + small))
        two_grad = hid_ref[r] + logit_grad * term_w
        resid_two = normalize_back(two_grad * ln2_gain, normal, scale)
        low = resid_two.astype(bf16)
        right_ref[0, r] = low
        x_ref[r] = resid_two
        fold_ref[3] += fold(low)
        fold_ref[4] += fold(two_grad * normal)
        fold_ref[5] += fold(two_grad)
        fold_ref[6] += fold(logit_grad * normed)
        fold_ref[7] += fold(jnp.broadcast_to(logit_grad, normal.shape))

    weight_ref[...] = term_cols_ref[...].T[0:1]

    def fall(c):
        wide_ref[c % 2] = lax.dot_general(right_ref[0], w_down_ref[columns(c), :], NT, preferred_element_type=f32)

    fall(0)
    for c in range(parts):
        if c + 1 < parts:
            fall(c + 1)
        for r in pieces:
            low = (wide_ref[c % 2, r] * slope_ref[r, columns(c)]).astype(bf16)
            right_ref[1 + c, r] = low
            in_fold_ref[:, columns(c)] += fold(low)
        x_ref[...] += lax.dot_general(right_ref[1 + c], w_in_ref[:, columns(c)], NT, preferred_element_type=f32)

    for r in pieces:
        one_grad = x_ref[r]
        normal = normal_ref[r]
        resid_one = normalize_back(one_grad * ln1_gain, normal, scale_ref[r])
        resid_ref[r] = resid_one
        low = resid_one.astype(bf16)
        right_ref[parts + 1, r] = low
        fold_ref[0] += fold(low)
        fold_ref[1] += fold(one_grad * normal)
        fold_ref[2] += fold(one_grad)
    grads = lax.dot_general(right_ref[parts + 1], w_out_ref[...], NT, preferred_element_type=f32).astype(bf16)

    @pl.when(head == 0)
    def _():
        my_grad_ref[...] = grads[:, :local_dim]
        their_grad_ref[...] = grads[:, local_dim:]

    @pl.when(head == 1)
    def _():
        my_grad_ref[...] = grads[:, local_dim:]
        their_grad_ref[...] = grads[:, :local_dim]

    @pl.when(pl.program_id(0) == pl.num_programs(0) - 1)
    def _():
        sums_ref[...] = jnp.zeros_like(sums_ref)
        sums_ref[0:8] = jnp.sum(fold_ref[...], axis=1)
        for c in range(parts):
            sums_ref[10 + c : 11 + c] = jnp.sum(in_fold_ref[:, columns(c)], axis=0, keepdims=True)


def middle(mine, theirs, tokens, grad_hidden, grad_term, w_out, w_in, w_down, vec, bias_in, term_bias):
    half, model_dim = tokens.shape
    local_dim = mine.shape[1]
    ffn_dim = w_in.shape[1]
    rows = min(TILE, half)

    def tile(cols):
        return pl.BlockSpec((rows, cols), lambda i: (i, 0))

    def whole(*shape):
        return pl.BlockSpec(shape, lambda i: (0, 0), pipeline_mode=pl.Buffered(1))

    stacked = pl.BlockSpec((ffn_dim // model_dim + 2, rows, model_dim), lambda i: (0, i, 0))
    stack = jax.ShapeDtypeStruct((ffn_dim // model_dim + 2, half, model_dim), bf16)

    def full(cols, kind):
        return jax.ShapeDtypeStruct((half, cols), kind)

    return pl.pallas_call(
        middle_kernel,
        grid=(half // rows,),
        in_specs=[
            tile(local_dim),
            tile(local_dim),
            tile(model_dim),
            tile(model_dim),
            pl.BlockSpec((1, rows), lambda i: (0, i)),
            whole(model_dim, model_dim),
            whole(model_dim, ffn_dim),
            whole(ffn_dim, model_dim),
            whole(8, model_dim),
            whole(1, ffn_dim),
            whole(1, 1),
        ],
        out_specs=[
            tile(model_dim),
            pl.BlockSpec((1, rows), lambda i: (0, i)),
            stacked,
            stacked,
            tile(model_dim),
            tile(local_dim),
            tile(local_dim),
            pl.BlockSpec((16, model_dim), lambda i: (0, 0)),
        ],
        scratch_shapes=[
            pltpu.VMEM((rows, ffn_dim), f32),
            pltpu.VMEM((2, rows, model_dim), f32),
            pltpu.VMEM((rows, model_dim), f32),
            pltpu.VMEM((rows, model_dim), f32),
            pltpu.VMEM((rows, 1), f32),
            pltpu.VMEM((8, 8, model_dim), f32),
            pltpu.VMEM((8, ffn_dim), f32),
            pltpu.VMEM((rows, LANES), f32),
            pltpu.VMEM((rows, LANES), f32),
        ],
        out_shape=[
            full(model_dim, bf16),
            jax.ShapeDtypeStruct((1, half), f32),
            stack,
            stack,
            full(model_dim, f32),
            full(local_dim, bf16),
            full(local_dim, bf16),
            jax.ShapeDtypeStruct((16, model_dim), f32),
        ],
        compiler_params=pltpu.CompilerParams(vmem_limit_bytes=VMEM_LIMIT),
        cost_estimate=pl.CostEstimate(flops=40_000_000_000, bytes_accessed=50_000_000, transcendentals=0),
    )(mine, theirs, tokens, grad_hidden, grad_term, w_out, w_in, w_down, vec, bias_in, term_bias)


def bit(place, which):
    return (place // 2**which) % 2


def flip(place, which):
    return place + (1 - 2 * bit(place, which)) * 2**which


def route(target, me, head):
    low, high = bit(target, 0), bit(target, 1)
    send = (1 - head) * ((low + bit(me, 0)) % 2) + head * ((high + bit(me, 1)) % 2)
    return send, 2 * (target // 4) + (1 - head) * high + head * low


def greet(partners):
    barrier = pltpu.get_barrier_semaphore()
    for partner in partners:
        pl.semaphore_signal(barrier, inc=1, device_id=partner, device_id_type=pl.DeviceIdType.MESH)
    pl.semaphore_wait(barrier, len(partners))


def remote(source, target, send_sem, recv_sem, partner):
    return pltpu.make_async_remote_copy(
        src_ref=source,
        dst_ref=target,
        send_sem=send_sem,
        recv_sem=recv_sem,
        device_id=partner,
        device_id_type=pl.DeviceIdType.MESH,
    )


def weights_kernel(
    n_dp,
    parts,
    left_ref,
    right_ref,
    my_cols_ref,
    their_cols_ref,
    vec_ref,
    keep_any,
    send_any,
    down_keep_any,
    down_send_any,
    grads_any,
    vec_out_ref,
    full_ref,
    recv_ref,
    rest_ref,
    down_ref,
    down_recv_ref,
    down_out_ref,
    vec_recv_ref,
    send_sem,
    recv_sem,
    down_sems,
    grad_sems,
    vec_sems,
    copy_sem,
):
    me, head = lax.axis_index("dp"), lax.axis_index("head")
    other = (me, 1 - head)
    first = (flip(me, 0) * (1 - head) + flip(me, 1) * head, head)
    mine = bit(me, 1) * (1 - head) + bit(me, 0) * head
    step = pl.program_id(0)
    steps = 2 * parts + 1
    model_dim = left_ref.shape[2]
    cols = model_dim // 2
    half = my_cols_ref.shape[0]
    down_rows = parts * model_dim // n_dp
    rows = model_dim // n_dp
    my_rows = grads_any.at[pl.ds(pl.multiple_of(head * half, half), half)]
    own_copy = pltpu.make_async_copy(my_cols_ref, my_rows, copy_sem.at[4])
    grad_copy = remote(their_cols_ref, my_rows, grad_sems.at[0], grad_sems.at[1], other)
    vec_copy = remote(vec_ref, vec_recv_ref, vec_sems.at[0], vec_sems.at[1], other)
    def exchange(k):
        return remote(full_ref.at[k % 3, 1 - head], recv_ref.at[k], send_sem.at[k], recv_sem.at[k], other)

    def down_copy(k):
        at = pl.ds(2 * k, 2)
        return remote(down_ref.at[1, at], down_recv_ref.at[at], down_sems.at[0, k], down_sems.at[1, k], first)

    def multiply():
        whole = lax.dot_general(left_ref[0], right_ref[0], TN, preferred_element_type=f32).astype(bf16)
        full_ref[step % 3, 0] = whole[:, :cols]
        full_ref[step % 3, 1] = whole[:, cols:]

    def total(k, start, count):
        return (
            full_ref[k % 3, head, start : start + count].astype(f32)
            + recv_ref[k, start : start + count, :].astype(f32)
        ).astype(bf16)

    def down_finish(k):
        for q in range(4):
            send, place = route(4 * k + q, me, head)
            down_ref[send, place] = total(k, q * down_rows, down_rows)

    def rest_finish(k):
        start = pl.multiple_of((k - parts) * rows, 16)
        for d in range(n_dp):
            send, place = route(d, me, head)
            rest_ref[send, place, pl.ds(start, rows), :] = total(k, d * rows, rows)

    @pl.when(step >= 3)
    def _():
        exchange(step - 3).wait_send()

    @pl.when(step == 0)
    def _():
        greet([other, first])
        grad_copy.start()
        vec_copy.start()
        own_copy.start()

    @pl.when(step < 2)
    def _():
        multiply()
        exchange(step).start()

    @pl.when((step >= 2) & (step < parts + 2))
    def _():
        exchange(step - 2).wait_recv()
        multiply()
        down_finish(step - 2)
        exchange(step).start()
        down_copy(step - 2).start()

    @pl.when(step >= parts + 2)
    def _():
        exchange(step - 2).wait_recv()
        multiply()
        rest_finish(step - 2)
        exchange(step).start()

    @pl.when(step == steps - 1)
    def _():
        for k in range(steps - 2, steps):
            exchange(k).wait_recv()
            rest_finish(k)
        copies = [
            pltpu.make_async_copy(rest_ref.at[0], keep_any, copy_sem.at[0]),
            pltpu.make_async_copy(rest_ref.at[1], send_any, copy_sem.at[1]),
            pltpu.make_async_copy(down_out_ref.at[0], down_keep_any, copy_sem.at[2]),
            pltpu.make_async_copy(down_out_ref.at[1], down_send_any, copy_sem.at[3]),
        ]
        for copy in copies[:2]:
            copy.start()
        for k in range(parts):
            down_copy(k).wait()

        def split(r, carry):
            for j in range(2):
                block = 2 * r + j * (1 - mine) + (1 - j) * mine
                whole = down_ref[0, block].astype(f32) + down_recv_ref[block].astype(f32)
                down_out_ref[j, r] = whole.astype(bf16)
            return carry

        lax.fori_loop(0, parts, split, 0)
        for copy in copies[2:]:
            copy.start()
        vec_copy.wait()
        vec_out_ref[...] = vec_ref[...] + vec_recv_ref[...]
        grad_copy.wait()
        own_copy.wait()
        for k in range(steps - 3, steps):
            exchange(k).wait_send()
        for copy in copies:
            copy.wait()


def weights(n_dp, left, right, my_cols, their_cols, vec):
    stack, half, model_dim = left.shape
    parts = stack - 2
    steps = 2 * parts + 1
    cols = model_dim // 2
    down_rows = parts * model_dim // n_dp
    rest_rows = (parts + 1) * model_dim // n_dp
    anywhere = pl.BlockSpec(memory_space=pl.ANY)

    def left_map(j):
        return (jnp.where(j < parts, j, jnp.where(j < 2 * parts, parts, parts + 1)), 0, 0)

    def right_map(j):
        return (jnp.where(j < parts, 0, j - parts + 1), 0, 0)

    rest = jax.ShapeDtypeStruct((n_dp // 2, rest_rows, cols), bf16)
    down = jax.ShapeDtypeStruct((n_dp // 4, down_rows, cols), bf16)
    return pl.pallas_call(
        partial(weights_kernel, n_dp, parts),
        grid=(steps,),
        in_specs=[
            pl.BlockSpec((1, half, model_dim), left_map),
            pl.BlockSpec((1, half, model_dim), right_map),
            pl.BlockSpec(my_cols.shape, lambda j: (0, 0), pipeline_mode=pl.Buffered(1)),
            pl.BlockSpec(my_cols.shape, lambda j: (0, 0), pipeline_mode=pl.Buffered(1)),
            pl.BlockSpec(vec.shape, lambda j: (0, 0)),
        ],
        out_specs=[anywhere] * 5 + [pl.BlockSpec(vec.shape, lambda j: (0, 0))],
        scratch_shapes=[
            pltpu.VMEM((3, 2, model_dim, cols), bf16),
            pltpu.VMEM((steps, model_dim, cols), bf16),
            pltpu.VMEM((2,) + rest.shape, bf16),
            pltpu.VMEM((2, n_dp // 2, down_rows, cols), bf16),
            pltpu.VMEM((n_dp // 2, down_rows, cols), bf16),
            pltpu.VMEM((2,) + down.shape, bf16),
            pltpu.VMEM(vec.shape, f32),
            pltpu.SemaphoreType.DMA((steps,)),
            pltpu.SemaphoreType.DMA((steps,)),
            pltpu.SemaphoreType.DMA((2, parts)),
            pltpu.SemaphoreType.DMA((2,)),
            pltpu.SemaphoreType.DMA((2,)),
            pltpu.SemaphoreType.DMA((5,)),
        ],
        out_shape=[
            rest,
            rest,
            down,
            down,
            jax.ShapeDtypeStruct((2 * half, my_cols.shape[1]), bf16),
            jax.ShapeDtypeStruct(vec.shape, f32),
        ],
        compiler_params=pltpu.CompilerParams(
            collective_id=0, has_side_effects=True, vmem_limit_bytes=VMEM_LIMIT
        ),
        cost_estimate=pl.CostEstimate(flops=15_000_000_000, bytes_accessed=20_000_000, transcendentals=0),
    )(left, right, my_cols, their_cols, vec)


def final_kernel(
    n_dp,
    chunks,
    d_keep_any,
    d_got_any,
    s_keep_any,
    s_got_any,
    raw_any,
    rows_any,
    w_any,
    resid_any,
    vec_ref,
    raw_sums_ref,
    core_send_ref,
    core_recv_ref,
    qkv_ref,
    vec_out_ref,
    vec_core_ref,
    tokens_any,
    t_recv_any,
    d_keep_ref,
    d_got_ref,
    d_own_ref,
    d_out_ref,
    d_got_z_ref,
    s_keep_ref,
    s_got_ref,
    raw_ref,
    rows_ref,
    w_ref,
    resid_ref,
    s_send_ref,
    s_recv_ref,
    s_own_ref,
    s_out_ref,
    s_got_z_ref,
    s_sum_ref,
    q_grad_ref,
    q_both_ref,
    q_first_ref,
    q_send_ref,
    q_recv_ref,
    q_own_ref,
    q_out_ref,
    q_got_z_ref,
    t_send_ref,
    vec_hold_ref,
    vec_recv_ref,
    in_sems,
    d_z_sems,
    s_sems,
    s_z_sems,
    q_first_sems,
    q_sems,
    q_z_sems,
    t_sems,
    core_sems,
    vec_sems,
    out_sem,
):
    me, head = lax.axis_index("dp"), lax.axis_index("head")
    line = n_dp // 4
    depth = line.bit_length() - 1
    z = me // 4
    other = (me, 1 - head)
    low = (flip(me, 0), head)
    high = (flip(me, 1), head)
    around = [(((z + j) % line) * 4 + me % 4, head) for j in range(1, line)]
    first = (flip(me, 0) * (1 - head) + flip(me, 1) * head, head)
    second = (flip(me, 1) * (1 - head) + flip(me, 0) * head, head)
    mine = bit(me, 1) * (1 - head) + bit(me, 0) * head
    half, model_dim = resid_ref.shape
    local_dim = raw_ref.shape[1] // 3
    size = s_keep_ref.shape[1] // chunks
    q_chunks, _, _, q_size, _ = q_both_ref.shape
    q_rows = q_chunks * q_size

    def piece(i):
        return slice(i * size, (i + 1) * size)

    s_loads = [
        pltpu.make_async_copy(s_keep_any, s_keep_ref, in_sems.at[0]),
        pltpu.make_async_copy(s_got_any, s_got_ref, in_sems.at[1]),
    ]
    q_loads = [
        pltpu.make_async_copy(rows_any, rows_ref, in_sems.at[2]),
        pltpu.make_async_copy(raw_any, raw_ref, in_sems.at[3]),
    ]
    t_loads = [
        pltpu.make_async_copy(w_any, w_ref, in_sems.at[4]),
        pltpu.make_async_copy(resid_any, resid_ref, in_sems.at[5]),
    ]
    d_loads = [
        pltpu.make_async_copy(d_keep_any, d_keep_ref, in_sems.at[6]),
        pltpu.make_async_copy(d_got_any, d_got_ref, in_sems.at[7]),
    ]
    for load in d_loads + s_loads:
        load.start()
    greet([low, high, other] + around)

    vec_hold_ref[0] = vec_ref[...]
    here = pl.ds(pl.multiple_of(head * local_dim, LANES), local_dim)
    vec_hold_ref[0, 8:9, here] = raw_sums_ref[:, :local_dim]
    vec_hold_ref[0, 9:10, here] = raw_sums_ref[:, 2 * local_dim :]

    def vec_copy(k):
        to = (low, high)[k] if k < 2 else around[k - 2]
        source = vec_hold_ref.at[min(k, 2)]
        return remote(source, vec_recv_ref.at[k], vec_sems.at[0, k], vec_sems.at[1, k], to)

    vec_copy(0).start()

    def fold_line(own_ref, hold_ref, got_ref, sems):
        def moved(k):
            count = line >> (k + 1)
            at = slice(line - 2 * count, line - count)
            return remote(hold_ref.at[at], got_ref.at[at], sems.at[0, k], sems.at[1, k], (flip(me, k + 2), head))

        def send(k):
            count = line >> (k + 1)
            keep = bit(me, k + 2)
            for q in range(count):
                hold_ref[line - 2 * count + q] = own_ref[2 * q + 1 - keep].astype(bf16)
            moved(k).start()

        def add(k):
            count = line >> (k + 1)
            keep = bit(me, k + 2)
            moved(k).wait()
            for q in range(count):
                own_ref[q] = own_ref[2 * q + keep] + got_ref[line - 2 * count + q].astype(f32)
            if k + 1 < depth:
                send(k + 1)

        return send, add

    d_line = fold_line(d_own_ref, d_out_ref, d_got_z_ref, d_z_sems)

    def s_copy(i):
        return remote(s_send_ref.at[i], s_recv_ref.at[i], s_sems.at[0, i], s_sems.at[1, i], second)

    def s_total(block, i):
        return s_keep_ref[block, piece(i)].astype(f32) + s_got_ref[block, piece(i)].astype(f32)

    def s_prepare(i):
        def send_block(r, carry):
            s_send_ref[i, r] = s_total(2 * r + 1 - mine, i).astype(bf16)
            return carry

        lax.fori_loop(0, line, send_block, 0)

    for load in s_loads:
        load.wait()
    for load in q_loads:
        load.start()
    for load in t_loads:
        load.start()
    for i in range(chunks):
        s_prepare(i)
        s_copy(i).start()
    for load in d_loads:
        load.wait()

    def d_block(r, carry):
        d_own_ref[r] = d_keep_ref[r].astype(f32) + d_got_ref[r].astype(f32)
        return carry

    lax.fori_loop(0, line, d_block, 0)
    d_line[0](0)

    for load in q_loads:
        load.wait()

    def q_columns(j, carry):
        at = pl.ds(pl.multiple_of(j * Q_COLUMNS, LANES), Q_COLUMNS)
        grad = lax.dot_general(rows_ref[:, at], raw_ref[...], TN, preferred_element_type=f32)
        q_grad_ref[pl.ds(pl.multiple_of(j * Q_COLUMNS, LANES), Q_COLUMNS), :] = grad.astype(bf16)
        return carry

    lax.fori_loop(0, model_dim // Q_COLUMNS, q_columns, 0)
    d_line[1](0)

    def q_place(d, carry):
        send, place = route(d, me, head)
        for j in range(q_chunks):
            at = pl.ds(pl.multiple_of(d * q_rows + j * q_size, 16), q_size)
            q_both_ref[j, send, place] = q_grad_ref[at, :]
        return carry

    lax.fori_loop(0, n_dp, q_place, 0)

    def q_copy(j):
        return remote(q_both_ref.at[j, 1], q_first_ref.at[j], q_first_sems.at[0, j], q_first_sems.at[1, j], first)

    def q_second(j):
        return remote(q_send_ref.at[j], q_recv_ref.at[j], q_sems.at[0, j], q_sems.at[1, j], second)

    s_line = [
        fold_line(s_own_ref.at[i], s_out_ref.at[i], s_got_z_ref.at[i], s_z_sems.at[i]) for i in range(chunks)
    ]
    q_line = [
        fold_line(q_own_ref.at[j], q_out_ref.at[j], q_got_z_ref.at[j], q_z_sems.at[j]) for j in range(q_chunks)
    ]

    def s_enter(i):
        s_copy(i).wait()

        def add_block(r, carry):
            s_own_ref[i, r] = s_total(2 * r + mine, i) + s_recv_ref[i, r].astype(f32)
            return carry

        lax.fori_loop(0, line, add_block, 0)
        s_line[i][0](0)

    def q_total(j, block):
        return q_both_ref[j, 0, block].astype(f32) + q_first_ref[j, block].astype(f32)

    def q_enter(j):
        q_copy(j).wait()

        def send_block(r, carry):
            q_send_ref[j, r] = q_total(j, 2 * r + 1 - mine).astype(bf16)
            return carry

        lax.fori_loop(0, line, send_block, 0)
        q_second(j).start()

        def own_block(r, carry):
            q_own_ref[j, r] = q_total(j, 2 * r + mine)
            return carry

        lax.fori_loop(0, line, own_block, 0)

    def q_turn(j):
        q_second(j).wait()

        def add_block(r, carry):
            q_own_ref[j, r] = q_own_ref[j, r] + q_recv_ref[j, r].astype(f32)
            return carry

        lax.fori_loop(0, line, add_block, 0)
        q_line[j][0](0)

    tile_rows = half // 4

    def token_rows(who, tile):
        at = pl.ds(pl.multiple_of(who * half + tile * tile_rows, tile_rows), tile_rows)
        total = 0.0
        for c in range(3):
            part = raw_ref[at, c * local_dim : (c + 1) * local_dim]
            total = total + lax.dot_general(part, w_ref[c], NT, preferred_element_type=f32)
        return total

    t_copy = remote(t_send_ref, t_recv_any, t_sems.at[0], t_sems.at[1], other)

    def send_tile(tile, carry):
        at = pl.ds(pl.multiple_of(tile * tile_rows, tile_rows), tile_rows)
        t_send_ref[at, :] = token_rows(1 - head, tile).astype(bf16)
        return carry

    def own_tile(tile, carry):
        at = pl.ds(pl.multiple_of(tile * tile_rows, tile_rows), tile_rows)
        resid_ref[at, :] = resid_ref[at, :] + token_rows(head, tile)
        return carry

    for j in range(q_chunks):
        q_copy(j).start()
    for i in range(chunks):
        s_enter(i)
    for load in t_loads:
        load.wait()
    lax.fori_loop(0, 4, send_tile, 0)
    t_copy.start()
    for i in range(chunks - 1):
        s_line[i][1](0)
    lax.fori_loop(0, 4, own_tile, 0)
    t_out = pltpu.make_async_copy(resid_ref, tokens_any, out_sem)
    t_out.start()
    vec_copy(0).wait()
    vec_hold_ref[1] = vec_hold_ref[0] + vec_recv_ref[0]
    vec_copy(1).start()
    q_enter(0)
    s_line[chunks - 1][1](0)
    for j in range(1, q_chunks):
        q_enter(j)
    vec_copy(1).wait()
    vec_hold_ref[2] = vec_hold_ref[1] + vec_recv_ref[1]
    for j in range(line - 1):
        vec_copy(2 + j).start()
    for j in range(q_chunks - 1):
        q_turn(j)
    d_rows = d_own_ref.shape[1]
    for k in range(1, depth):
        d_line[1](k)
    s_sum_ref[:d_rows, :] = d_own_ref[0]
    for i in range(chunks):
        for k in range(1, depth):
            s_line[i][1](k)
        s_sum_ref[d_rows + i * size : d_rows + (i + 1) * size, :] = s_own_ref[i, 0]
    pieces = core_pieces(s_sum_ref.shape[0], q_rows)

    def gather(target_ref, who):
        at = 0
        for start, count in pieces:
            here = pl.ds(pl.multiple_of(start + who * count, 8), count)
            target_ref[at : at + count, :] = s_sum_ref[here, :]
            at += count

    gather(core_send_ref.at[1], 1 - head)
    core_copy = remote(core_send_ref.at[1], core_recv_ref, core_sems.at[0], core_sems.at[1], other)
    core_copy.start()
    gather(core_send_ref.at[0], head)
    q_turn(q_chunks - 1)
    for j in range(line - 1):
        vec_copy(2 + j).wait()
    total = vec_hold_ref[2]
    for j in range(line - 1):
        total = total + vec_recv_ref[2 + j]
    vec_out_ref[...] = total
    core_vec = remote(vec_out_ref.at[pl.ds(8, 8)], vec_core_ref, core_sems.at[2], core_sems.at[3], other)
    core_vec.start()
    for k in range(depth):
        for j in range(q_chunks):
            q_line[j][1](k)
    for j in range(q_chunks):
        qkv_ref[j * q_size : (j + 1) * q_size, :] = q_own_ref[j, 0]
    core_vec.wait()
    core_copy.wait()
    t_copy.wait()
    t_out.wait()


def core_pieces(block_rows, rows):
    parts = (block_rows // rows - 1) // 2
    return [(0, parts * rows // 2)] + [(parts * rows + rows * c, rows // 2) for c in range(parts + 1)]


def final(n_dp, d_keep, d_got, s_keep, s_got, raw, group_rows, w_flat, resid, vec, raw_sums):
    line = n_dp // 4
    depth = line.bit_length() - 1
    _, rest_rows, cols = s_keep.shape
    down_rows = d_keep.shape[1]
    block_rows = down_rows + rest_rows
    half, model_dim = resid.shape
    local_dim = raw.shape[1] // 3
    q_rows, q_cols = model_dim // n_dp, 3 * local_dim
    chunks = 3 if rest_rows % 48 == 0 else 1
    size = rest_rows // chunks
    q_chunks = q_rows // 16
    anywhere = pl.BlockSpec(memory_space=pl.ANY)
    vmem = pl.BlockSpec(memory_space=pltpu.VMEM)

    def low(*dims):
        return pltpu.VMEM(dims, bf16)

    def wide(*dims):
        return pltpu.VMEM(dims, f32)

    def shape(*dims):
        return jax.ShapeDtypeStruct(dims, f32)

    def sems(*dims):
        return pltpu.SemaphoreType.DMA(dims)

    return pl.pallas_call(
        partial(final_kernel, n_dp, chunks),
        in_specs=[anywhere] * 8 + [vmem] * 2,
        out_specs=[vmem] * 5 + [anywhere] * 2,
        scratch_shapes=[
            low(*d_keep.shape),
            low(*d_keep.shape),
            wide(*d_keep.shape),
            low(*d_keep.shape),
            low(line - 1, down_rows, cols),
            low(*s_keep.shape),
            low(*s_keep.shape),
            low(*raw.shape),
            low(*group_rows.shape),
            low(*w_flat.shape),
            wide(half, model_dim),
            low(chunks, line, size, cols),
            low(chunks, line, size, cols),
            wide(chunks, line, size, cols),
            low(chunks, line, size, cols),
            low(chunks, line - 1, size, cols),
            wide(block_rows, cols),
            low(model_dim, q_cols),
            low(q_chunks, 2, 2 * line, 16, q_cols),
            low(q_chunks, 2 * line, 16, q_cols),
            low(q_chunks, line, 16, q_cols),
            low(q_chunks, line, 16, q_cols),
            wide(q_chunks, line, 16, q_cols),
            low(q_chunks, line, 16, q_cols),
            low(q_chunks, line - 1, 16, q_cols),
            low(half, model_dim),
            wide(3, *vec.shape),
            wide(1 + line, *vec.shape),
            sems(8),
            sems(2, depth),
            sems(2, chunks),
            sems(chunks, 2, depth),
            sems(2, q_chunks),
            sems(2, q_chunks),
            sems(q_chunks, 2, depth),
            sems(2),
            sems(4),
            sems(2, 1 + line),
            pltpu.SemaphoreType.DMA,
        ],
        out_shape=[
            shape(2, block_rows // 2, cols),
            shape(block_rows // 2, cols),
            shape(q_rows, q_cols),
            shape(*vec.shape),
            shape(8, model_dim),
            shape(half, model_dim),
            jax.ShapeDtypeStruct((half, model_dim), bf16),
        ],
        compiler_params=pltpu.CompilerParams(
            collective_id=1, has_side_effects=True, vmem_limit_bytes=VMEM_LIMIT
        ),
        cost_estimate=pl.CostEstimate(flops=12_000_000_000, bytes_accessed=25_000_000, transcendentals=0),
    )(d_keep, d_got, s_keep, s_got, raw, group_rows, w_flat, resid, vec, raw_sums)


def finish_kernel(
    n_dp,
    parts,
    own_ref,
    got_ref,
    kept_ref,
    core_ref,
    qkv_ref,
    vec_ref,
    vec_core_ref,
    tokens_ref,
    grad_qkv_ref,
    down_ref,
    in_ref,
    out_ref,
    qv_ref,
    in_bias_ref,
    term_ref,
    *vector_refs,
):
    tokens_ref[...] = own_ref[...] + got_ref[...].astype(f32)

    @pl.when(pl.program_id(0) == 0)
    def _():
        head = lax.axis_index("head")
        place = 2 * lax.axis_index("dp") + head
        cols = kept_ref.shape[2]
        model_dim = 2 * cols
        rows = out_ref.shape[0]
        width = model_dim // (2 * n_dp)
        starts = [0, parts * rows] + [parts * rows + rows * (c + 1) for c in range(parts + 1)]
        for who, source in ((head, kept_ref.at[0]), (1 - head, core_ref)):
            start = who * cols
            here = pl.ds(pl.multiple_of(start, LANES), cols)
            down_ref[:, here] = source[starts[0] : starts[1], :]
            for c in range(parts):
                shifted = pl.ds(pl.multiple_of(2 * cols * c + start, LANES), cols)
                in_ref[:, shifted] = source[starts[1 + c] : starts[2 + c], :]
            out_ref[:, here] = source[starts[1 + parts] : starts[2 + parts], :]
        for c in range(3):
            grad_qkv_ref[c] = qkv_ref[:, c * cols : (c + 1) * cols]
        shift = lax.rem(model_dim - place * width, model_dim)
        turned = pltpu.roll(vec_ref[0:8], shift, 1)
        for j, ref in enumerate(vector_refs):
            ref[...] = turned[j : j + 1, :width]
        term_ref[...] = vec_ref[7:8, :1]
        turned = pltpu.roll(vec_ref[8:16] + vec_core_ref[...], shift, 1)
        qv_ref[...] = turned[:2, :width]
        in_width = parts * model_dim // (2 * n_dp)
        per_row = model_dim // in_width
        row = vec_ref[pl.ds(10 + place // per_row, 1), :]
        row = jnp.broadcast_to(row, (8, model_dim))
        turned = pltpu.roll(row, lax.rem(model_dim - (place % per_row) * in_width, model_dim), 1)
        in_bias_ref[...] = turned[0:1, :in_width]


def finish(n_dp, parts, kept, core, qkv, vec, vec_core, own, got):
    half, model_dim = own.shape
    q_rows = qkv.shape[0]
    width = model_dim // (2 * n_dp)
    rows = min(512, half)
    tile = pl.BlockSpec((rows, model_dim), lambda i: (i, 0))

    def whole(dims):
        return pl.BlockSpec(dims, lambda i: (0,) * len(dims))

    out = [
        (3, q_rows, model_dim // 2),
        (parts * width, model_dim),
        (width, parts * model_dim),
        (width, model_dim),
        (2, width),
        (1, parts * width),
        (1, 1),
    ] + [(1, width)] * 7
    return pl.pallas_call(
        partial(finish_kernel, n_dp, parts),
        grid=(half // rows,),
        in_specs=[tile, tile] + [whole(x.shape) for x in (kept, core, qkv, vec, vec_core)],
        out_specs=[tile] + [whole(dims) for dims in out],
        out_shape=[jax.ShapeDtypeStruct((half, model_dim), f32)] + [jax.ShapeDtypeStruct(dims, f32) for dims in out],
        compiler_params=pltpu.CompilerParams(vmem_limit_bytes=VMEM_LIMIT),
        cost_estimate=pl.CostEstimate(flops=1_000_000, bytes_accessed=10_000_000, transcendentals=0),
    )(own, got, kept, core, qkv, vec, vec_core)


def take(array, index, axis=0):
    return lax.dynamic_index_in_dim(array, index, axis, keepdims=False)


class Links:
    def __init__(self, n_dp):
        self.n_dp = n_dp
        self.bits = n_dp.bit_length() - 1
        self.dp = lax.axis_index("dp")
        self.head = lax.axis_index("head")

    def bit(self, which):
        return (self.dp >> which) & 1

    def permute(self, array, partner):
        pairs = []
        for d in range(self.n_dp):
            for h in range(2):
                to_d, to_h = partner(d, h)
                pairs.append((2 * d + h, 2 * to_d + to_h))
        return lax.ppermute(array, AXES, pairs)

    def swap_head(self, array):
        return self.permute(array, lambda d, h: (d, 1 - h))

    def swap_bit(self, array, which):
        return self.permute(array, lambda d, h: (d ^ (1 << which), h))

    def scatter_heads(self, blocks):
        got = self.swap_head(take(blocks, 1 - self.head, 1))
        return (take(blocks, self.head, 1).astype(f32) + got.astype(f32)).astype(bf16)

    def scatter_dp(self, blocks):
        tail = blocks.shape[1:]
        b0, b1 = self.bit(0), self.bit(1)
        first = self.head == 0
        blocks = blocks.reshape((self.n_dp // 4, 4) + tail)

        def two(one, other):
            i = jnp.where(first, one, 2 * other)
            j = jnp.where(first, 2 + one, 2 * other + 1)
            return jnp.stack([take(blocks, i, 1), take(blocks, j, 1)], axis=1)

        got = self.permute(two(1 - b0, 1 - b1), lambda d, h: (d ^ (1 if h == 0 else 2), h))
        blocks = (two(b0, b1).astype(f32) + got.astype(f32)).astype(bf16)
        mine = jnp.where(first, b1, b0)
        got = self.permute(take(blocks, 1 - mine, 1), lambda d, h: (d ^ (2 if h == 0 else 1), h))
        blocks = take(blocks, mine, 1).astype(f32) + got.astype(f32)
        for which in range(2, self.bits):
            blocks = blocks.reshape((-1, 2) + tail)
            mine = self.bit(which)
            got = self.swap_bit(take(blocks, 1 - mine, 1).astype(bf16), which)
            blocks = take(blocks, mine, 1) + got.astype(f32)
        return blocks.reshape(tail)

    def total(self, array):
        array = array + self.swap_head(array)
        for which in range(self.bits):
            array = array + self.swap_bit(array, which)
        return array


def shards(
    n_dp,
    tokens,
    lengths,
    w_qkv,
    bias_qv,
    w_out,
    bias_out,
    ln1_gain,
    ln1_bias,
    w_in,
    bias_in,
    w_down,
    bias_down,
    ln2_gain,
    ln2_bias,
    term_w,
    term_bias,
    grad_hidden,
    grad_term,
):
    links = Links(n_dp)
    head = links.head
    half, model_dim = tokens.shape
    row_len = 2 * half
    local_dim = w_qkv.shape[2]
    ffn_dim = w_in.shape[1]

    boundary = jnp.cumsum(lengths[0])
    places = jnp.arange(row_len, dtype=jnp.int32)
    segment = jnp.sum((places[:, None] >= boundary[None, :]).astype(jnp.int32), axis=-1)
    seg_col = jnp.broadcast_to(segment[:, None], (row_len, LANES))
    seg_row = jnp.broadcast_to(segment[None, :], (8, row_len))

    def both(mine, theirs, axis):
        return jnp.where(
            head == 0,
            jnp.concatenate([mine, theirs], axis=axis),
            jnp.concatenate([theirs, mine], axis=axis),
        )

    w_parts = jnp.transpose(w_qkv, (1, 0, 2))
    group_rows = both(tokens, links.swap_head(tokens), 0)
    queries, key_rows, value_rows = [jnp.dot(group_rows, w_parts[c], preferred_element_type=f32) for c in range(3)]
    queries = ((queries + bias_qv[:, 0]) * HEAD_DIM ** (-0.5)).astype(bf16)
    key_rows = key_rows.astype(bf16)
    value_rows = (value_rows + bias_qv[:, 1]).astype(bf16)
    theirs, mine, logs = attend(lengths, head, queries, key_rows, value_rows, seg_col, seg_row)

    def my_half(rows):
        return lax.dynamic_slice_in_dim(rows, head * half, half, 0)

    def their_half(rows):
        return lax.dynamic_slice_in_dim(rows, (1 - head) * half, half, 0)

    vec = jnp.stack([bias_out, ln1_gain, ln1_bias, bias_down, ln2_gain, ln2_bias, term_w, jnp.zeros_like(term_w)])
    hidden_out, term_weight, left, right, resid_one_grad, my_cols, their_cols, vec = middle(
        mine,
        links.swap_head(theirs),
        tokens,
        grad_hidden,
        grad_term[None, :],
        w_out,
        w_in,
        w_down,
        vec,
        bias_in[None, :],
        term_bias[None, :],
    )
    parts = ffn_dim // model_dim
    in_kernels = (model_dim // n_dp) % 16 == 0 and n_dp == 4 * parts

    def back(grads):
        return attend_back(lengths, queries, key_rows, value_rows, grads, logs, seg_col, seg_row)

    if in_kernels:
        s_keep, s_send, d_keep, d_send, head_grad, vec = weights(n_dp, left, right, my_cols, their_cols, vec)
        d_got = links.permute(d_send, lambda d, h: (d ^ (2 if h == 0 else 1), h))
        s_got = links.permute(s_send, lambda d, h: (d ^ (1 if h == 0 else 2), h))
        raw, raw_sums = back(head_grad)
        kept, core, qkv, vec, vec_core, own, got = final(
            n_dp, d_keep, d_got, s_keep, s_got, raw, group_rows, w_parts, resid_one_grad, vec, raw_sums
        )
        (grad_tokens, grad_qkv, grad_down, grad_in, grad_out, bias_qv_mine, bias_in_mine, term_total, *vectors) = finish(
            n_dp, parts, kept, core, qkv, vec, vec_core, own, got
        )
        grad_qkv = jnp.transpose(grad_qkv, (1, 0, 2))
        bias_qv_mine = bias_qv_mine.T
        bias_in_mine = bias_in_mine.reshape(-1)
        term_total = term_total.reshape(1)
        mine = [v.reshape(-1) for v in vectors]
    else:
        raw, raw_sums = back(both(my_cols, links.swap_head(their_cols), 0))

        def product(i, j):
            return lax.dot_general(left[i], right[j], TN, preferred_element_type=f32).astype(bf16)

        def reduced(partial_sum):
            rows, cols = partial_sum.shape
            return links.scatter_dp(links.scatter_heads(partial_sum.reshape(n_dp, 2, rows // (2 * n_dp), cols)))

        grad_down = reduced(jnp.concatenate([product(i, 0) for i in range(parts)]))
        grad_in = reduced(jnp.concatenate([product(parts, 1 + i) for i in range(parts)], axis=1))
        grad_out = reduced(product(parts + 1, parts + 1))
        w_flat = w_qkv.reshape(model_dim, 3 * local_dim)
        grad = lax.dot_general(raw, w_flat, NT, preferred_element_type=f32)
        received = links.swap_head(their_half(grad).astype(bf16))
        grad_tokens = resid_one_grad + my_half(grad) + received.astype(f32)
        qkv_local = lax.dot_general(group_rows, raw, TN, preferred_element_type=f32).astype(bf16)
        grad_qkv = links.scatter_dp(qkv_local.reshape(n_dp, model_dim // n_dp, 3 * local_dim))
        value_sums = lax.dynamic_update_slice(
            jnp.zeros((2, 2 * local_dim), f32),
            jnp.concatenate([raw_sums[:, :local_dim], raw_sums[:, 2 * local_dim :]]),
            (jnp.int32(0), head * local_dim),
        )
        vectors = links.total(lax.dynamic_update_slice(vec, value_sums, (8, 0)))
        grad_qkv = grad_qkv.reshape(model_dim // n_dp, 3, local_dim)
        place = 2 * links.dp + head
        width = model_dim // (2 * n_dp)
        mine = lax.dynamic_slice_in_dim(vectors, place * width, width, 1)
        in_width = ffn_dim // (2 * n_dp)
        in_row = vectors[10 : 10 + parts].reshape(-1)
        bias_in_mine = lax.dynamic_slice_in_dim(in_row, place * in_width, in_width, 0)
        bias_qv_mine = mine[8:10].T
        term_total = vectors[7, :1]

    return (
        hidden_out,
        term_weight.reshape(-1),
        grad_tokens,
        grad_qkv,
        bias_qv_mine,
        grad_out,
        mine[0],
        mine[1],
        mine[2],
        grad_in,
        bias_in_mine,
        grad_down,
        mine[3],
        mine[4],
        mine[5],
        mine[6],
        term_total,
    )


def solution(mesh):
    rows = P(AXES, None)
    return jax.shard_map(
        partial(shards, mesh.shape["dp"]),
        mesh=mesh,
        in_specs=(rows, P("dp", None), P(None, None, "head"), P("head", None))
        + (P(),) * 12
        + (rows, P(AXES)),
        out_specs=(
            rows,
            P(AXES),
            rows,
            P("dp", None, "head"),
            rows,
            rows,
            P(AXES),
            P(AXES),
            P(AXES),
            rows,
            P(AXES),
            rows,
            P(AXES),
            P(AXES),
            P(AXES),
            P(AXES),
            P(),
        ),
        check_vma=False,
    )
```
